32 devices in a mesh: slab: 8 (over z, x), col: 4 (over y, core).
Axes of the slice: x: 2, y: 2, z: 4, core: 2. Of those that a mesh axis runs over, the one named last changes fastest.
Arguments:
- basis: bfloat16 [3, 64, 16, 32, 128], P(None, None, 'slab', 'col')
- cell_map: int32 [16, 32, 128], P('slab', 'col'), may hold values from 0 to 7
- table: float32 [8, 27], replicated, may hold values from 0 to 1, as said below
Outputs:
- next_block: bfloat16 [64, 16, 32, 128], P(None, 'slab', 'col')
- projections: float32 [2, 192, 64], replicated
- triangles: float32 [2, 64, 64], replicated
The draws below stay inside these ranges and needn't reach their ends.
Inputs may be any that keep to these rules, and one draw needn't show every extreme that they name: `table`: coefficients lie between 0 and 1; the centre one is the largest.
All inputs are finite; a program needn't handle non-finite values.
Results may differ from the reference program's by a relative error of at most 0.027.
Values may be sent and summed in bfloat16 or wider, within the bound.
No kernel may reach another device: no remote copies, remote signals or barrier semaphores. Data moves between devices by JAX's collectives and lax.ppermute only.
A program may use at most 64 MiB of HBM per device.

```python
import jax
import jax.numpy as jnp
from jax import lax

COLS = 64
BLOCKS = 3
CLASSES = 8
NX = 16
NY = 32
NZ = 128


def draw_table(key, part):
    key = jax.random.fold_in(key, 7)
    offsets = jnp.arange(27)
    dist = jnp.abs(offsets // 9 - 1) + jnp.abs(offsets // 3 % 3 - 1) + jnp.abs(offsets % 3 - 1)
    low = jnp.array([0.6, 0.05, 0.0, 0.0], jnp.float32)[dist]
    high = jnp.array([1.0, 0.25, 0.08, 0.03], jnp.float32)[dist]
    unit = jax.random.uniform(key, (CLASSES, 27), jnp.float32)
    return (low + (high - low) * unit).astype(jnp.float32)


def draw_basis(key, part):
    key = jax.random.fold_in(key, 11)
    key_codes, key_angles, key_signs = jax.random.split(key, 3)
    plane_cells = NX * NY
    columns_all = BLOCKS * COLS
    walsh_codes = (jax.random.permutation(key_codes, plane_cells - 1)[:columns_all] + 1).astype(jnp.int32)
    places = jnp.arange(plane_cells, dtype=jnp.int32)
    masked = walsh_codes[:, None] & places[None, :]
    parity = jnp.zeros((columns_all, plane_cells), jnp.int32)
    for bit in range(plane_cells.bit_length()):
        parity = parity ^ masked >> bit & 1
    rotated = (1.0 - 2.0 * parity.astype(jnp.float32)).reshape(BLOCKS, COLS, plane_cells)
    column_ids = jnp.arange(COLS, dtype=jnp.int32)
    level = 0
    while 1 << level < COLS:
        partner = column_ids ^ 1 << level
        lower_index = jnp.minimum(column_ids, partner)
        angles = jax.random.uniform(jax.random.fold_in(key_angles, level), (BLOCKS, COLS), jnp.float32, -3.14159265, 3.14159265)
        cosine = jnp.cos(angles[:, lower_index])
        sine = jnp.sin(angles[:, lower_index])
        factor = jnp.where((column_ids == lower_index)[None, :], -sine, sine)
        rotated = cosine[:, :, None] * rotated + factor[:, :, None] * rotated[:, partner]
        level = level + 1
    cell_signs = jnp.where(jax.random.bernoulli(key_signs, 0.5, (NX, NY, NZ)), 1.0, -1.0).astype(jnp.float32)
    orthogonal = rotated.reshape(BLOCKS, COLS, NX, NY, 1) * cell_signs[None, None]
    earlier = jnp.concatenate([jnp.zeros_like(orthogonal[:1]), orthogonal[:-1]], axis=0)
    return (orthogonal + 0.4 * earlier).astype(jnp.float32).astype(jnp.bfloat16)


def with_ends(values, rng, least, top_value):
    index_at = [jax.random.randint(jax.random.fold_in(rng, axis), (), 0, length) for axis, length in enumerate(values.shape)]
    main_axis = values.shape.index(max(values.shape))
    next_to = index_at[:main_axis] + [(index_at[main_axis] + 1) % values.shape[main_axis]] + index_at[main_axis + 1:]
    return values.at[tuple(index_at)].set(least).at[tuple(next_to)].set(top_value)


def setup_inputs(seed: int = 0) -> dict:
    seeds = jax.random.split(jax.random.key(seed), 4)
    return {
        "basis": draw_basis(jax.random.fold_in(seeds[3], 71), 0),
        "cell_map": with_ends(jax.random.randint(seeds[1], (NX, NY, NZ), 0, CLASSES), jax.random.fold_in(seeds[1], 1), 0, CLASSES - 1).astype(jnp.int32),
        "table": draw_table(jax.random.fold_in(seeds[3], 71), 0),
    }


def apply_stencil(block, coef):

    def one_column(field):
        padded = jnp.pad(field.astype(jnp.float32), 1)
        nx, ny, nz = field.shape
        total = jnp.zeros((nx, ny, nz), jnp.float32)
        for dx in range(3):
            for dy in range(3):
                for dz in range(3):
                    offset = 9 * dx + 3 * dy + dz
                    total = total + coef[offset] * padded[dx:dx + nx, dy:dy + ny, dz:dz + nz]
        return total.astype(jnp.bfloat16)
    return lax.map(one_column, block)

def gram_of(left, right, scale):
    return lax.dot_general(left.astype(jnp.float32), right.astype(jnp.float32), (((1,), (1,)), ((), ())), preferred_element_type=jnp.float32) * scale

def correct(stack, block, coeffs):
    moved = lax.dot_general(coeffs.astype(jnp.bfloat16).astype(jnp.float32), stack.astype(jnp.float32), (((0,), (0,)), ((), ())), preferred_element_type=jnp.float32)
    return (block.astype(jnp.float32) - moved).astype(jnp.bfloat16)

def orthonormalize(stack, block, scale):
    first = gram_of(stack, block, scale)
    block_one = correct(stack, block, first)
    second = gram_of(stack, block_one, scale)
    block_two = correct(stack, block_one, second)
    square = gram_of(block_two, block_two, scale)
    lower = jnp.linalg.cholesky(square)
    identity = jnp.eye(lower.shape[0], dtype=lower.dtype)
    inverse = lax.linalg.triangular_solve(lower, identity, left_side=True, lower=True)
    result = jnp.dot(inverse.astype(jnp.bfloat16).astype(jnp.float32), block_two.astype(jnp.float32), preferred_element_type=jnp.float32).astype(jnp.bfloat16)
    return (result, first + second, lower)

def reference(basis, cell_map, table):
    coef = jnp.moveaxis(table[cell_map], -1, 0)
    cells = NX * NY * NZ
    scale = 1.0 / cells
    flat = basis.reshape(BLOCKS * COLS, cells)
    image = apply_stencil(basis[2], coef).reshape(COLS, cells)
    block_one, proj_one, lower_one = orthonormalize(flat, image, scale)
    stack = jnp.concatenate([flat[COLS:], block_one], axis=0)
    image = apply_stencil(block_one.reshape(COLS, NX, NY, NZ), coef).reshape(COLS, cells)
    block_two, proj_two, lower_two = orthonormalize(stack, image, scale)
    return (block_two.reshape(COLS, NX, NY, NZ), jnp.stack([proj_one, proj_two]), jnp.stack([lower_one, lower_two]))
```

```python
import functools

import jax
import jax.numpy as jnp
from jax import lax
from jax.experimental import pallas as pl
from jax.experimental.pallas import tpu as pltpu
from jax.sharding import PartitionSpec as P

HIGHEST = lax.Precision.HIGHEST
NN = (((1,), (0,)), ((), ()))
NT = (((1,), (1,)), ((), ()))
ROWS = 16


def dot(left, right, dims=NN, precision=None):
    return lax.dot_general(
        left, right, dims, precision=precision, preferred_element_type=jnp.float32
    )


def exact(left, right, dims=NN):
    return dot(left, right, dims, HIGHEST)


def neighbours(block, span_x, span_y, depth):
    plane = span_y * depth

    def exchange(axis, upward, downward):
        count = lax.axis_size(axis)
        forward = [(i, i + 1) for i in range(count - 1)]
        backward = [(target, source) for source, target in forward]
        return lax.ppermute(upward, axis, forward), lax.ppermute(downward, axis, backward)

    xlo, xhi = exchange("slab", block[:, (span_x - 1) * plane :], block[:, :plane])

    def edge(row):
        at = row * depth
        parts = [xlo[:, at : at + depth]]
        parts += [block[:, x * plane + at : x * plane + at + depth] for x in range(span_x)]
        parts += [xhi[:, at : at + depth]]
        return jnp.concatenate(parts, axis=1)

    ylo, yhi = exchange("col", edge(span_y - 1), edge(0))
    return xlo, xhi, ylo, yhi


def coefficients_kernel(table, cells, coef):
    classes = table.shape[0]
    lanes = lax.broadcasted_iota(jnp.int32, cells.shape, 1)
    depth = cells.shape[1]
    here = cells[...]
    below = pltpu.roll(here, depth - 1, 1)
    above = pltpu.roll(here, 1, 1)
    maps = (below, here, above)
    keep = (lanes < depth - 1, None, lanes > 0)
    for dz in range(3):
        masks = [maps[dz] == k for k in range(1, classes)]
        for pair in range(9):
            offset = 3 * pair + dz
            value = jnp.full(cells.shape, table[0, offset], jnp.float32)
            for k in range(1, classes):
                value = jnp.where(masks[k - 1], table[k, offset], value)
            if keep[dz] is not None:
                value = jnp.where(keep[dz], value, 0.0)
            coef[offset] = value


def coefficients(table, cell_map):
    span_x, span_y, depth = cell_map.shape
    lines = span_x * span_y
    return pl.pallas_call(
        coefficients_kernel,
        out_shape=jax.ShapeDtypeStruct((27, lines, depth), jnp.float32),
        in_specs=[
            pl.BlockSpec(memory_space=pltpu.SMEM),
            pl.BlockSpec(memory_space=pltpu.VMEM),
        ],
        out_specs=pl.BlockSpec(memory_space=pltpu.VMEM),
        name="coefficients",
    )(table, cell_map.reshape(lines, depth))


def stencil_into(image, coef, block, xlo, xhi, ylo, yhi, span_x, span_y, depth):
    columns = block.shape[0]

    def tile(step, carry):
        rows = pl.ds(pl.multiple_of(step * ROWS, ROWS), ROWS)

        def line(x, y):
            if y < 0:
                ref, at = ylo, x + 1
            elif y >= span_y:
                ref, at = yhi, x + 1
            elif x < 0:
                ref, at = xlo, y
            elif x >= span_x:
                ref, at = xhi, y
            else:
                ref, at = block, x * span_y + y
            return ref[rows, at * depth : (at + 1) * depth].astype(jnp.float32)

        held = {y: [line(x, y) for x in range(-1, span_x + 1)] for y in (-1, 0)}
        for y in range(span_y):
            held[y + 1] = [line(x, y + 1) for x in range(-1, span_x + 1)]
            for x in range(span_x):
                at = x * span_y + y
                sums = [None, None, None]
                for dx in range(3):
                    for dy in range(3):
                        field = held[y + dy - 1][x + dx]
                        for dz in range(3):
                            term = coef[9 * dx + 3 * dy + dz, at : at + 1, :] * field
                            sums[dz] = term if sums[dz] is None else sums[dz] + term
                total = sums[1] + pltpu.roll(sums[0], 1, 1) + pltpu.roll(sums[2], depth - 1, 1)
                image[rows, at * depth : (at + 1) * depth] = total.astype(jnp.bfloat16)
            del held[y - 1]
        return carry

    lax.fori_loop(0, columns // ROWS, tile, 0)


def first_image_kernel(spans, coef, stack, xlo, xhi, ylo, yhi, image, cross, own):
    columns = image.shape[0]
    fields = stack.shape[0]
    block = stack.at[fields - columns : fields]
    stencil_into(image, coef, block, xlo, xhi, ylo, yhi, *spans)
    w = image[...]
    cross[:, :fields] = dot(w, stack[...], NT)
    cross[:, fields:] = dot(w, w, NT)
    own[...] = dot(stack[...], stack[...], NT)


def second_image_kernel(spans, coef, stack, block, xlo, xhi, ylo, yhi, image, cross):
    columns = image.shape[0]
    fields = stack.shape[0]
    stencil_into(image, coef, block, xlo, xhi, ylo, yhi, *spans)
    w = image[...]
    cross[:, : fields - columns] = dot(w, stack[columns:], NT)
    cross[:, fields - columns : fields] = dot(w, block[...], NT)
    cross[:, fields:] = dot(w, w, NT)


def factor(square):
    size = square.shape[0]
    lane = lax.broadcasted_iota(jnp.int32, (8, 2 * size), 1)
    sub = lax.broadcasted_iota(jnp.int32, (8, 2 * size), 0)
    blocks = []
    for b in range(size // 8):
        unit = (lax.broadcasted_iota(jnp.int32, (8, size), 1)
                == lax.broadcasted_iota(jnp.int32, (8, size), 0) + 8 * b).astype(jnp.float32)
        blocks.append(jnp.concatenate([square[8 * b : 8 * b + 8], unit], axis=1))
    for k in range(size):
        b, r = divmod(k, 8)
        row = blocks[b][r : r + 1, :]
        row = row * (1.0 / row[:, k : k + 1])
        for later in range(b, size // 8):
            column = blocks[later][:, k : k + 1]
            if later == b:
                column = jnp.where(sub[:, :1] > r, column, 0.0)
            blocks[later] = blocks[later] - column * row
    done = []
    for b, rows in enumerate(blocks):
        diagonal = jnp.sum(jnp.where(lane == sub + 8 * b, rows, 0.0), axis=1, keepdims=True)
        done.append(rows * lax.rsqrt(diagonal))
    whole = jnp.concatenate(done, axis=0)
    return whole[:, :size], whole[:, size:]


def project(cross, own, scale):
    fields = own.shape[0]
    first = cross[:, :fields] * scale
    square = cross[:, fields:] * scale
    first_low = first.astype(jnp.bfloat16)
    second = first - exact(first_low.astype(jnp.float32), own)
    second_low = second.astype(jnp.bfloat16)
    used = first_low.astype(jnp.float32) + second_low.astype(jnp.float32)
    rest = second - exact(second_low.astype(jnp.float32), own)
    square = square - exact(used, first, NT) - exact(rest, used, NT)
    return first_low, second_low, first + second, rest, square


def first_solve_kernel(scale, cross, own, stack, image, block, proj, low, own_next):
    columns = image.shape[0]
    gram = own[...] * scale
    first_low, second_low, both, rest, square = project(cross[...], gram, scale)
    proj[...] = both.T
    upper, inverse = factor(square)
    low[...] = upper.T
    inverse = inverse.astype(jnp.bfloat16)
    w = image[...].astype(jnp.float32) - dot(first_low, stack[...]) - dot(second_low, stack[...])
    block[...] = dot(inverse, w.astype(jnp.bfloat16)).astype(jnp.bfloat16)
    kept = stack.shape[0] - columns
    wide = inverse.astype(jnp.float32)
    mixed = exact(wide, rest[:, columns:])
    own_next[:kept, :kept] = gram[columns:, columns:]
    own_next[kept:, :kept] = mixed
    own_next[:kept, kept:] = mixed.T
    own_next[kept:, kept:] = exact(exact(wide, square), wide, NT)


def second_solve_kernel(scale, cross, own, stack, last, image, proj_in, low_in, block, proj, low):
    columns = image.shape[0]
    kept = stack.shape[0] - columns
    first_low, second_low, both, _, square = project(cross[...], own[...], scale)
    proj[0] = proj_in[...]
    proj[1] = both.T
    upper, inverse = factor(square)
    low[0] = low_in[...]
    low[1] = upper.T
    w = image[...].astype(jnp.float32)
    for part in (first_low, second_low):
        w = w - dot(part[:, :kept], stack[columns:]) - dot(part[:, kept:], last[...])
    block[...] = dot(inverse.astype(jnp.bfloat16), w.astype(jnp.bfloat16)).astype(jnp.bfloat16)


def whole_sum(parts):
    axes = ("slab", "col")
    count = lax.axis_size("slab") * lax.axis_size("col")
    flat = jnp.concatenate([part.reshape(count, -1) for part in parts], axis=1)
    shares = lax.all_to_all(flat, axes, 0, 0, tiled=True)
    share = jnp.sum(shares, axis=0, keepdims=True)
    flat = lax.all_to_all(jnp.broadcast_to(share, flat.shape), axes, 0, 0, tiled=True)
    done, at = [], 0
    for part in parts:
        width = part.size // count
        done.append(flat[:, at : at + width].reshape(part.shape))
        at += width
    return done


def call(kernel, name, outs, *args):
    return pl.pallas_call(
        kernel,
        out_shape=[jax.ShapeDtypeStruct(shape, dtype) for shape, dtype in outs],
        in_specs=[pl.BlockSpec(memory_space=pltpu.VMEM)] * len(args),
        out_specs=[pl.BlockSpec(memory_space=pltpu.VMEM)] * len(outs),
        compiler_params=pltpu.CompilerParams(vmem_limit_bytes=24 * 1024 * 1024),
        name=name,
    )(*args)


def shards(basis, cell_map, table):
    span_x, span_y, depth = cell_map.shape
    blocks, columns = basis.shape[:2]
    cells = span_x * span_y * depth
    fields = blocks * columns
    scale = 1.0 / (cells * lax.axis_size("slab") * lax.axis_size("col"))
    spans = (span_x, span_y, depth)
    f32, bf16 = jnp.float32, jnp.bfloat16

    stack = basis.reshape(fields, cells)
    coef = coefficients(table, cell_map)
    around = neighbours(stack[fields - columns :], *spans)
    image, cross, own = call(
        functools.partial(first_image_kernel, spans),
        "first_image",
        [((columns, cells), bf16), ((columns, fields + columns), f32), ((fields, fields), f32)],
        coef, stack, *around,
    )
    cross, own = whole_sum([cross, own])
    block, proj, low, own = call(
        functools.partial(first_solve_kernel, scale),
        "first_solve",
        [((columns, cells), bf16), ((fields, columns), f32), ((columns, columns), f32),
         ((fields, fields), f32)],
        cross, own, stack, image,
    )
    around = neighbours(block, *spans)
    image, cross = call(
        functools.partial(second_image_kernel, spans),
        "second_image",
        [((columns, cells), bf16), ((columns, fields + columns), f32)],
        coef, stack, block, *around,
    )
    (cross,) = whole_sum([cross])
    block, proj, low = call(
        functools.partial(second_solve_kernel, scale),
        "second_solve",
        [((columns, cells), bf16), ((2, fields, columns), f32), ((2, columns, columns), f32)],
        cross, own, stack, block, image, proj, low,
    )
    return block.reshape(columns, *spans), proj, low


def solution(mesh):
    placed = (P(None, None, "slab", "col", None), P("slab", "col", None), P())
    return jax.shard_map(
        shards,
        mesh=mesh,
        in_specs=placed,
        out_specs=(P(None, "slab", "col", None), P(), P()),
        check_vma=False,
    )
```

```python
import functools

import jax
import jax.numpy as jnp
from jax import lax
from jax.experimental import pallas as pl
from jax.experimental.pallas import tpu as pltpu
from jax.sharding import PartitionSpec as P

HIGHEST = lax.Precision.HIGHEST
NN = (((1,), (0,)), ((), ()))
NT = (((1,), (1,)), ((), ()))
ROWS = 16


def dot(left, right, dims=NN, precision=None):
    return lax.dot_general(
        left, right, dims, precision=precision, preferred_element_type=jnp.float32
    )


def exact(left, right, dims=NN):
    return dot(left, right, dims, HIGHEST)


def neighbours(block, span_x, span_y, depth):
    plane = span_y * depth

    def exchange(axis, upward, downward):
        count = lax.axis_size(axis)
        forward = [(i, i + 1) for i in range(count - 1)]
        backward = [(target, source) for source, target in forward]
        return lax.ppermute(upward, axis, forward), lax.ppermute(downward, axis, backward)

    xlo, xhi = exchange("slab", block[:, (span_x - 1) * plane :], block[:, :plane])

    def edge(row):
        at = row * depth
        parts = [xlo[:, at : at + depth]]
        parts += [block[:, x * plane + at : x * plane + at + depth] for x in range(span_x)]
        parts += [xhi[:, at : at + depth]]
        return jnp.concatenate(parts, axis=1)

    ylo, yhi = exchange("col", edge(span_y - 1), edge(0))
    return xlo, xhi, ylo, yhi


def coefficients_kernel(table, cells, coef):
    classes = table.shape[0]
    lanes = lax.broadcasted_iota(jnp.int32, cells.shape, 1)
    depth = cells.shape[1]
    here = cells[...]
    below = pltpu.roll(here, depth - 1, 1)
    above = pltpu.roll(here, 1, 1)
    maps = (below, here, above)
    keep = (lanes < depth - 1, None, lanes > 0)
    for dz in range(3):
        masks = [maps[dz] == k for k in range(1, classes)]
        for pair in range(9):
            offset = 3 * pair + dz
            value = jnp.full(cells.shape, table[0, offset], jnp.float32)
            for k in range(1, classes):
                value = jnp.where(masks[k - 1], table[k, offset], value)
            if keep[dz] is not None:
                value = jnp.where(keep[dz], value, 0.0)
            coef[offset] = value


def coefficients(table, cell_map):
    span_x, span_y, depth = cell_map.shape
    lines = span_x * span_y
    return pl.pallas_call(
        coefficients_kernel,
        out_shape=jax.ShapeDtypeStruct((27, lines, depth), jnp.float32),
        in_specs=[
            pl.BlockSpec(memory_space=pltpu.SMEM),
            pl.BlockSpec(memory_space=pltpu.VMEM),
        ],
        out_specs=pl.BlockSpec(memory_space=pltpu.VMEM),
        name="coefficients",
    )(table, cell_map.reshape(lines, depth))


def stencil_into(image, coef, block, xlo, xhi, ylo, yhi, span_x, span_y, depth):
    columns = block.shape[0]

    def tile(step, carry):
        rows = pl.ds(pl.multiple_of(step * ROWS, ROWS), ROWS)

        def line(x, y):
            if y < 0:
                ref, at = ylo, x + 1
            elif y >= span_y:
                ref, at = yhi, x + 1
            elif x < 0:
                ref, at = xlo, y
            elif x >= span_x:
                ref, at = xhi, y
            else:
                ref, at = block, x * span_y + y
            return ref[rows, at * depth : (at + 1) * depth].astype(jnp.float32)

        held = {y: [line(x, y) for x in range(-1, span_x + 1)] for y in (-1, 0)}
        for y in range(span_y):
            held[y + 1] = [line(x, y + 1) for x in range(-1, span_x + 1)]
            for x in range(span_x):
                at = x * span_y + y
                sums = [None, None, None]
                for dx in range(3):
                    for dy in range(3):
                        field = held[y + dy - 1][x + dx]
                        for dz in range(3):
                            term = coef[9 * dx + 3 * dy + dz, at : at + 1, :] * field
                            sums[dz] = term if sums[dz] is None else sums[dz] + term
                total = sums[1] + pltpu.roll(sums[0], 1, 1) + pltpu.roll(sums[2], depth - 1, 1)
                image[rows, at * depth : (at + 1) * depth] = total.astype(jnp.bfloat16)
            del held[y - 1]
        return carry

    lax.fori_loop(0, columns // ROWS, tile, 0)


def first_image_kernel(spans, coef, stack, xlo, xhi, ylo, yhi, image, cross):
    columns = image.shape[0]
    fields = stack.shape[0]
    block = stack.at[fields - columns : fields]
    stencil_into(image, coef, block, xlo, xhi, ylo, yhi, *spans)
    w = image[...]
    cross[:, :fields] = dot(w, stack[...], NT)
    cross[:, fields : fields + columns] = dot(w, w, NT)
    at = fields + columns
    for b in range(0, fields, columns):
        width = fields - b
        cross[:, at : at + width] = dot(stack[b : b + columns], stack[b:], NT)
        at += width


def second_image_kernel(spans, coef, stack, block, xlo, xhi, ylo, yhi, image, cross):
    columns = image.shape[0]
    fields = stack.shape[0]
    stencil_into(image, coef, block, xlo, xhi, ylo, yhi, *spans)
    w = image[...]
    cross[:, : fields - columns] = dot(w, stack[columns:], NT)
    cross[:, fields - columns : fields] = dot(w, block[...], NT)
    cross[:, fields:] = dot(w, w, NT)


def factor(square):
    size = square.shape[0]
    lane = lax.broadcasted_iota(jnp.int32, (8, 2 * size), 1)
    sub = lax.broadcasted_iota(jnp.int32, (8, 2 * size), 0)
    blocks = []
    for b in range(size // 8):
        unit = (lax.broadcasted_iota(jnp.int32, (8, size), 1)
                == lax.broadcasted_iota(jnp.int32, (8, size), 0) + 8 * b).astype(jnp.float32)
        blocks.append(jnp.concatenate([square[8 * b : 8 * b + 8], unit], axis=1))
    for k in range(size):
        b, r = divmod(k, 8)
        row = blocks[b][r : r + 1, :]
        row = row * (1.0 / row[:, k : k + 1])
        for later in range(b, size // 8):
            column = blocks[later][:, k : k + 1]
            if later == b:
                column = jnp.where(sub[:, :1] > r, column, 0.0)
            blocks[later] = blocks[later] - column * row
    done = []
    for b, rows in enumerate(blocks):
        diagonal = jnp.sum(jnp.where(lane == sub + 8 * b, rows, 0.0), axis=1, keepdims=True)
        done.append(rows * lax.rsqrt(diagonal))
    whole = jnp.concatenate(done, axis=0)
    return whole[:, :size], whole[:, size:]


def project(cross, own, scale):
    fields = own.shape[0]
    first = cross[:, :fields] * scale
    square = cross[:, fields:] * scale
    first_low = first.astype(jnp.bfloat16)
    second = first - exact(first_low.astype(jnp.float32), own)
    second_low = second.astype(jnp.bfloat16)
    used = first_low.astype(jnp.float32) + second_low.astype(jnp.float32)
    rest = second - exact(second_low.astype(jnp.float32), own)
    square = square - exact(used, first, NT) - exact(rest, used, NT)
    return first_low, second_low, first + second, rest, square


def unpacked(upper, columns, fields):
    rows, at = [], 0
    for b in range(0, fields, columns):
        rows.append((b, upper[:, at : at + fields - b]))
        at += fields - b
    whole = []
    for b, row in rows:
        left = [above[:, b - a : b - a + columns].T for a, above in rows if a < b]
        whole.append(jnp.concatenate(left + [row], axis=1))
    return jnp.concatenate(whole, axis=0)


def first_solve_kernel(scale, cross, stack, image, block, proj, low, own_next):
    columns = image.shape[0]
    fields = stack.shape[0]
    gram = unpacked(cross[:, fields + columns :] * scale, columns, fields)
    first_low, second_low, both, rest, square = project(
        cross[:, : fields + columns], gram, scale
    )
    proj[...] = both
    upper, inverse = factor(square)
    low[...] = upper.T
    inverse = inverse.astype(jnp.bfloat16)
    w = image[...].astype(jnp.float32) - dot(first_low, stack[...]) - dot(second_low, stack[...])
    block[...] = dot(inverse, w.astype(jnp.bfloat16)).astype(jnp.bfloat16)
    kept = stack.shape[0] - columns
    wide = inverse.astype(jnp.float32)
    mixed = exact(wide, rest[:, columns:])
    own_next[:kept, :kept] = gram[columns:, columns:]
    own_next[kept:, :kept] = mixed
    own_next[:kept, kept:] = mixed.T
    own_next[kept:, kept:] = exact(exact(wide, square), wide, NT)


def second_solve_kernel(scale, cross, own, stack, last, image, proj_in, low_in, block, proj, low):
    columns = image.shape[0]
    kept = stack.shape[0] - columns
    first_low, second_low, both, _, square = project(cross[...], own[...], scale)
    proj[0] = proj_in[...]
    proj[1] = both
    upper, inverse = factor(square)
    low[0] = low_in[...]
    low[1] = upper.T
    w = image[...].astype(jnp.float32)
    for part in (first_low, second_low):
        w = w - dot(part[:, :kept], stack[columns:]) - dot(part[:, kept:], last[...])
    block[...] = dot(inverse.astype(jnp.bfloat16), w.astype(jnp.bfloat16)).astype(jnp.bfloat16)


def exchange_shares(shares, axis):
    return lax.all_to_all(shares, axis, 0, 0, tiled=True)


def whole_sum(part):
    slabs, cols = lax.axis_size("slab"), lax.axis_size("col")
    rows, width = part.shape
    shape = (rows // slabs, width) if rows % slabs == 0 else (1, rows * width // slabs)
    share = jnp.sum(exchange_shares(part.reshape(slabs, *shape), "slab"), axis=0)
    share = jnp.sum(exchange_shares(jnp.broadcast_to(share, (cols, *shape)), "col"), axis=0)
    whole = exchange_shares(jnp.broadcast_to(share, (slabs, *shape)), "slab")
    return whole.reshape(part.shape)


def call(kernel, name, outs, *args):
    return pl.pallas_call(
        kernel,
        out_shape=[jax.ShapeDtypeStruct(shape, dtype) for shape, dtype in outs],
        in_specs=[pl.BlockSpec(memory_space=pltpu.VMEM)] * len(args),
        out_specs=[pl.BlockSpec(memory_space=pltpu.VMEM)] * len(outs),
        compiler_params=pltpu.CompilerParams(vmem_limit_bytes=24 * 1024 * 1024),
        name=name,
    )(*args)


def shards(basis, cell_map, table):
    span_x, span_y, depth = cell_map.shape
    blocks, columns = basis.shape[:2]
    cells = span_x * span_y * depth
    fields = blocks * columns
    scale = 1.0 / (cells * lax.axis_size("slab") * lax.axis_size("col"))
    spans = (span_x, span_y, depth)
    f32, bf16 = jnp.float32, jnp.bfloat16

    stack = basis.reshape(fields, cells)
    coef = coefficients(table, cell_map)
    around = neighbours(stack[fields - columns :], *spans)
    packed = fields + columns + columns * blocks * (blocks + 1) // 2
    image, cross = call(
        functools.partial(first_image_kernel, spans),
        "first_image",
        [((columns, cells), bf16), ((columns, packed), f32)],
        coef, stack, *around,
    )
    block, proj, low, own = call(
        functools.partial(first_solve_kernel, scale),
        "first_solve",
        [((columns, cells), bf16), ((columns, fields), f32), ((columns, columns), f32),
         ((fields, fields), f32)],
        whole_sum(cross), stack, image,
    )
    around = neighbours(block, *spans)
    image, cross = call(
        functools.partial(second_image_kernel, spans),
        "second_image",
        [((columns, cells), bf16), ((columns, fields + columns), f32)],
        coef, stack, block, *around,
    )
    block, proj, low = call(
        functools.partial(second_solve_kernel, scale),
        "second_solve",
        [((columns, cells), bf16), ((2, columns, fields), f32), ((2, columns, columns), f32)],
        whole_sum(cross), own, stack, block, image, proj, low,
    )
    return block.reshape(columns, *spans), jnp.swapaxes(proj, 1, 2), low


def solution(mesh):
    placed = (P(None, None, "slab", "col", None), P("slab", "col", None), P())
    return jax.shard_map(
        shards,
        mesh=mesh,
        in_specs=placed,
        out_specs=(P(None, "slab", "col", None), P(), P()),
        check_vma=False,
    )
```

```python
import functools

import jax
import jax.numpy as jnp
from jax import lax
from jax.experimental import pallas as pl
from jax.experimental.pallas import tpu as pltpu
from jax.sharding import PartitionSpec as P

HIGHEST = lax.Precision.HIGHEST
NN = (((1,), (0,)), ((), ()))
NT = (((1,), (1,)), ((), ()))
ROWS = 16


def dot(left, right, dims=NN, precision=None):
    return lax.dot_general(
        left, right, dims, precision=precision, preferred_element_type=jnp.float32
    )


def exact(left, right, dims=NN):
    return dot(left, right, dims, HIGHEST)


def neighbours(block, span_x, span_y, depth):
    plane = span_y * depth

    def exchange(axis, upward, downward):
        count = lax.axis_size(axis)
        forward = [(i, i + 1) for i in range(count - 1)]
        backward = [(target, source) for source, target in forward]
        return lax.ppermute(upward, axis, forward), lax.ppermute(downward, axis, backward)

    xlo, xhi = exchange("slab", block[:, (span_x - 1) * plane :], block[:, :plane])

    def edge(row):
        at = row * depth
        parts = [xlo[:, at : at + depth]]
        parts += [block[:, x * plane + at : x * plane + at + depth] for x in range(span_x)]
        parts += [xhi[:, at : at + depth]]
        return jnp.concatenate(parts, axis=1)

    ylo, yhi = exchange("col", edge(span_y - 1), edge(0))
    return xlo, xhi, ylo, yhi


def coefficients_kernel(table, cells, coef):
    classes = table.shape[0]
    lanes = lax.broadcasted_iota(jnp.int32, cells.shape, 1)
    depth = cells.shape[1]
    here = cells[...]
    below = pltpu.roll(here, depth - 1, 1)
    above = pltpu.roll(here, 1, 1)
    maps = (below, here, above)
    keep = (lanes < depth - 1, None, lanes > 0)
    for dz in range(3):
        masks = [maps[dz] == k for k in range(1, classes)]
        for pair in range(9):
            offset = 3 * pair + dz
            value = jnp.full(cells.shape, table[0, offset], jnp.float32)
            for k in range(1, classes):
                value = jnp.where(masks[k - 1], table[k, offset], value)
            if keep[dz] is not None:
                value = jnp.where(keep[dz], value, 0.0)
            coef[offset] = value


def coefficients(table, cell_map):
    span_x, span_y, depth = cell_map.shape
    lines = span_x * span_y
    return pl.pallas_call(
        coefficients_kernel,
        out_shape=jax.ShapeDtypeStruct((27, lines, depth), jnp.float32),
        in_specs=[
            pl.BlockSpec(memory_space=pltpu.SMEM),
            pl.BlockSpec(memory_space=pltpu.VMEM),
        ],
        out_specs=pl.BlockSpec(memory_space=pltpu.VMEM),
        name="coefficients",
    )(table, cell_map.reshape(lines, depth))


def stencil_into(image, coef, block, xlo, xhi, ylo, yhi, span_x, span_y, depth):
    columns = block.shape[0]

    def tile(step, carry):
        rows = pl.ds(pl.multiple_of(step * ROWS, ROWS), ROWS)

        def line(x, y):
            if y < 0:
                ref, at = ylo, x + 1
            elif y >= span_y:
                ref, at = yhi, x + 1
            elif x < 0:
                ref, at = xlo, y
            elif x >= span_x:
                ref, at = xhi, y
            else:
                ref, at = block, x * span_y + y
            return ref[rows, at * depth : (at + 1) * depth].astype(jnp.float32)

        held = {y: [line(x, y) for x in range(-1, span_x + 1)] for y in (-1, 0)}
        for y in range(span_y):
            held[y + 1] = [line(x, y + 1) for x in range(-1, span_x + 1)]
            for x in range(span_x):
                at = x * span_y + y
                sums = [None, None, None]
                for dx in range(3):
                    for dy in range(3):
                        field = held[y + dy - 1][x + dx]
                        for dz in range(3):
                            term = coef[9 * dx + 3 * dy + dz, at : at + 1, :] * field
                            sums[dz] = term if sums[dz] is None else sums[dz] + term
                total = sums[1] + pltpu.roll(sums[0], 1, 1) + pltpu.roll(sums[2], depth - 1, 1)
                image[rows, at * depth : (at + 1) * depth] = total.astype(jnp.bfloat16)
            del held[y - 1]
        return carry

    lax.fori_loop(0, columns // ROWS, tile, 0)


def first_image_kernel(spans, coef, stack, xlo, xhi, ylo, yhi, image, cross):
    columns = image.shape[0]
    fields = stack.shape[0]
    block = stack.at[fields - columns : fields]
    stencil_into(image, coef, block, xlo, xhi, ylo, yhi, *spans)
    w = image[...]
    cross[:, :fields] = dot(w, stack[...], NT)
    cross[:, fields : fields + columns] = dot(w, w, NT)
    at = fields + columns
    for b in range(0, fields, columns):
        width = fields - b
        cross[:, at : at + width] = dot(stack[b : b + columns], stack[b:], NT)
        at += width


def second_image_kernel(spans, coef, stack, block, xlo, xhi, ylo, yhi, image, cross):
    columns = image.shape[0]
    fields = stack.shape[0]
    stencil_into(image, coef, block, xlo, xhi, ylo, yhi, *spans)
    w = image[...]
    cross[:, : fields - columns] = dot(w, stack[columns:], NT)
    cross[:, fields - columns : fields] = dot(w, block[...], NT)
    cross[:, fields:] = dot(w, w, NT)


def factor(square):
    size = square.shape[0]
    lane = lax.broadcasted_iota(jnp.int32, (8, 2 * size), 1)
    sub = lax.broadcasted_iota(jnp.int32, (8, 2 * size), 0)
    blocks = []
    for b in range(size // 8):
        unit = (lax.broadcasted_iota(jnp.int32, (8, size), 1)
                == lax.broadcasted_iota(jnp.int32, (8, size), 0) + 8 * b).astype(jnp.float32)
        blocks.append(jnp.concatenate([square[8 * b : 8 * b + 8], unit], axis=1))
    for k in range(size):
        b, r = divmod(k, 8)
        row = blocks[b][r : r + 1, :]
        row = row * (1.0 / row[:, k : k + 1])
        for later in range(b, size // 8):
            column = blocks[later][:, k : k + 1]
            if later == b:
                column = jnp.where(sub[:, :1] > r, column, 0.0)
            blocks[later] = blocks[later] - column * row
    done = []
    for b, rows in enumerate(blocks):
        diagonal = jnp.sum(jnp.where(lane == sub + 8 * b, rows, 0.0), axis=1, keepdims=True)
        done.append(rows * lax.rsqrt(diagonal))
    whole = jnp.concatenate(done, axis=0)
    return whole[:, :size], whole[:, size:]


def project(cross, own, scale):
    fields = own.shape[0]
    first = cross[:, :fields] * scale
    square = cross[:, fields:] * scale
    first_low = first.astype(jnp.bfloat16)
    second = first - exact(first_low.astype(jnp.float32), own)
    second_low = second.astype(jnp.bfloat16)
    used = first_low.astype(jnp.float32) + second_low.astype(jnp.float32)
    rest = second - exact(second_low.astype(jnp.float32), own)
    square = square - exact(used, first, NT) - exact(rest, used, NT)
    return first_low, second_low, first + second, rest, square


def unpacked(upper, columns, fields):
    rows, at = [], 0
    for b in range(0, fields, columns):
        rows.append((b, upper[:, at : at + fields - b]))
        at += fields - b
    whole = []
    for b, row in rows:
        left = [above[:, b - a : b - a + columns].T for a, above in rows if a < b]
        whole.append(jnp.concatenate(left + [row], axis=1))
    return jnp.concatenate(whole, axis=0)


def first_solve_kernel(scale, cross, stack, image, block, proj, low, own_next):
    columns = image.shape[0]
    fields = stack.shape[0]
    gram = unpacked(cross[:, fields + columns :] * scale, columns, fields)
    first_low, second_low, both, rest, square = project(
        cross[:, : fields + columns], gram, scale
    )
    proj[...] = both
    upper, inverse = factor(square)
    low[...] = upper.T
    inverse = inverse.astype(jnp.bfloat16)
    w = image[...].astype(jnp.float32) - dot(first_low, stack[...]) - dot(second_low, stack[...])
    block[...] = dot(inverse, w.astype(jnp.bfloat16)).astype(jnp.bfloat16)
    kept = stack.shape[0] - columns
    wide = inverse.astype(jnp.float32)
    mixed = exact(wide, rest[:, columns:])
    own_next[:kept, :kept] = gram[columns:, columns:]
    own_next[kept:, :kept] = mixed
    own_next[:kept, kept:] = mixed.T
    own_next[kept:, kept:] = exact(exact(wide, square), wide, NT)


def second_solve_kernel(scale, cross, own, stack, last, image, proj_in, low_in, block, proj, low):
    columns = image.shape[0]
    kept = stack.shape[0] - columns
    first_low, second_low, both, _, square = project(cross[...], own[...], scale)
    proj[0] = proj_in[...]
    proj[1] = both
    upper, inverse = factor(square)
    low[0] = low_in[...]
    low[1] = upper.T
    w = image[...].astype(jnp.float32)
    for part in (first_low, second_low):
        w = w - dot(part[:, :kept], stack[columns:]) - dot(part[:, kept:], last[...])
    block[...] = dot(inverse.astype(jnp.bfloat16), w.astype(jnp.bfloat16)).astype(jnp.bfloat16)


def whole_sum(part):
    axes = ("slab", "col")
    count = lax.axis_size("slab") * lax.axis_size("col")
    shares = lax.all_to_all(part.reshape(count, -1), axes, 0, 0, tiled=True)
    share = jnp.sum(shares, axis=0, keepdims=True)
    return lax.all_gather(share, axes, axis=0, tiled=True).reshape(part.shape)


def call(kernel, name, outs, *args):
    return pl.pallas_call(
        kernel,
        out_shape=[jax.ShapeDtypeStruct(shape, dtype) for shape, dtype in outs],
        in_specs=[pl.BlockSpec(memory_space=pltpu.VMEM)] * len(args),
        out_specs=[pl.BlockSpec(memory_space=pltpu.VMEM)] * len(outs),
        compiler_params=pltpu.CompilerParams(vmem_limit_bytes=24 * 1024 * 1024),
        name=name,
    )(*args)


def shards(basis, cell_map, table):
    span_x, span_y, depth = cell_map.shape
    blocks, columns = basis.shape[:2]
    cells = span_x * span_y * depth
    fields = blocks * columns
    scale = 1.0 / (cells * lax.axis_size("slab") * lax.axis_size("col"))
    spans = (span_x, span_y, depth)
    f32, bf16 = jnp.float32, jnp.bfloat16

    stack = basis.reshape(fields, cells)
    coef = coefficients(table, cell_map)
    around = neighbours(stack[fields - columns :], *spans)
    packed = fields + columns + columns * blocks * (blocks + 1) // 2
    image, cross = call(
        functools.partial(first_image_kernel, spans),
        "first_image",
        [((columns, cells), bf16), ((columns, packed), f32)],
        coef, stack, *around,
    )
    block, proj, low, own = call(
        functools.partial(first_solve_kernel, scale),
        "first_solve",
        [((columns, cells), bf16), ((columns, fields), f32), ((columns, columns), f32),
         ((fields, fields), f32)],
        whole_sum(cross), stack, image,
    )
    around = neighbours(block, *spans)
    image, cross = call(
        functools.partial(second_image_kernel, spans),
        "second_image",
        [((columns, cells), bf16), ((columns, fields + columns), f32)],
        coef, stack, block, *around,
    )
    block, proj, low = call(
        functools.partial(second_solve_kernel, scale),
        "second_solve",
        [((columns, cells), bf16), ((2, columns, fields), f32), ((2, columns, columns), f32)],
        whole_sum(cross), own, stack, block, image, proj, low,
    )
    return block.reshape(columns, *spans), jnp.swapaxes(proj, 1, 2), low


def solution(mesh):
    placed = (P(None, None, "slab", "col", None), P("slab", "col", None), P())
    return jax.shard_map(
        shards,
        mesh=mesh,
        in_specs=placed,
        out_specs=(P(None, "slab", "col", None), P(), P()),
        check_vma=False,
    )
```

```python
import functools

import jax
import jax.numpy as jnp
from jax import lax
from jax.experimental import pallas as pl
from jax.experimental.pallas import tpu as pltpu
from jax.sharding import PartitionSpec as P

HIGHEST = lax.Precision.HIGHEST
NN = (((1,), (0,)), ((), ()))
NT = (((1,), (1,)), ((), ()))
ROWS = 16


def dot(left, right, dims=NN, precision=None):
    return lax.dot_general(
        left, right, dims, precision=precision, preferred_element_type=jnp.float32
    )


def exact(left, right, dims=NN):
    return dot(left, right, dims, HIGHEST)


def neighbours(block, span_x, span_y, depth):
    plane = span_y * depth

    def exchange(axis, upward, downward):
        count = lax.axis_size(axis)
        forward = [(i, i + 1) for i in range(count - 1)]
        backward = [(target, source) for source, target in forward]
        return lax.ppermute(upward, axis, forward), lax.ppermute(downward, axis, backward)

    xlo, xhi = exchange("slab", block[:, (span_x - 1) * plane :], block[:, :plane])

    def edge(row):
        at = row * depth
        parts = [xlo[:, at : at + depth]]
        parts += [block[:, x * plane + at : x * plane + at + depth] for x in range(span_x)]
        parts += [xhi[:, at : at + depth]]
        return jnp.concatenate(parts, axis=1)

    ylo, yhi = exchange("col", edge(span_y - 1), edge(0))
    return xlo, xhi, ylo, yhi


def coefficients_kernel(table, cells, coef):
    classes = table.shape[0]
    lanes = lax.broadcasted_iota(jnp.int32, cells.shape, 1)
    depth = cells.shape[1]
    here = cells[...]
    below = pltpu.roll(here, depth - 1, 1)
    above = pltpu.roll(here, 1, 1)
    maps = (below, here, above)
    keep = (lanes < depth - 1, None, lanes > 0)
    for dz in range(3):
        masks = [maps[dz] == k for k in range(1, classes)]
        for pair in range(9):
            offset = 3 * pair + dz
            value = jnp.full(cells.shape, table[0, offset], jnp.float32)
            for k in range(1, classes):
                value = jnp.where(masks[k - 1], table[k, offset], value)
            if keep[dz] is not None:
                value = jnp.where(keep[dz], value, 0.0)
            coef[offset] = value


def coefficients(table, cell_map):
    span_x, span_y, depth = cell_map.shape
    lines = span_x * span_y
    return pl.pallas_call(
        coefficients_kernel,
        out_shape=jax.ShapeDtypeStruct((27, lines, depth), jnp.float32),
        in_specs=[
            pl.BlockSpec(memory_space=pltpu.SMEM),
            pl.BlockSpec(memory_space=pltpu.VMEM),
        ],
        out_specs=pl.BlockSpec(memory_space=pltpu.VMEM),
        name="coefficients",
    )(table, cell_map.reshape(lines, depth))


def stencil_into(image, coef, block, xlo, xhi, ylo, yhi, span_x, span_y, depth):
    columns = block.shape[0]

    def tile(step, carry):
        rows = pl.ds(pl.multiple_of(step * ROWS, ROWS), ROWS)

        def line(x, y):
            if y < 0:
                ref, at = ylo, x + 1
            elif y >= span_y:
                ref, at = yhi, x + 1
            elif x < 0:
                ref, at = xlo, y
            elif x >= span_x:
                ref, at = xhi, y
            else:
                ref, at = block, x * span_y + y
            return ref[rows, at * depth : (at + 1) * depth].astype(jnp.float32)

        held = {y: [line(x, y) for x in range(-1, span_x + 1)] for y in (-1, 0)}
        for y in range(span_y):
            held[y + 1] = [line(x, y + 1) for x in range(-1, span_x + 1)]
            for x in range(span_x):
                at = x * span_y + y
                sums = [None, None, None]
                for dx in range(3):
                    for dy in range(3):
                        field = held[y + dy - 1][x + dx]
                        for dz in range(3):
                            term = coef[9 * dx + 3 * dy + dz, at : at + 1, :] * field
                            sums[dz] = term if sums[dz] is None else sums[dz] + term
                total = sums[1] + pltpu.roll(sums[0], 1, 1) + pltpu.roll(sums[2], depth - 1, 1)
                image[rows, at * depth : (at + 1) * depth] = total.astype(jnp.bfloat16)
            del held[y - 1]
        return carry

    lax.fori_loop(0, columns // ROWS, tile, 0)


def first_image_kernel(spans, coef, stack, xlo, xhi, ylo, yhi, image, cross):
    columns = image.shape[0]
    fields = stack.shape[0]
    block = stack.at[fields - columns : fields]
    stencil_into(image, coef, block, xlo, xhi, ylo, yhi, *spans)
    w = image[...]
    cross[:, :fields] = dot(w, stack[...], NT)
    cross[:, fields : fields + columns] = dot(w, w, NT)
    at = fields + columns
    for b in range(0, fields, columns):
        width = fields - b
        cross[:, at : at + width] = dot(stack[b : b + columns], stack[b:], NT)
        at += width


def second_image_kernel(spans, coef, stack, block, xlo, xhi, ylo, yhi, image, cross):
    columns = image.shape[0]
    fields = stack.shape[0]
    stencil_into(image, coef, block, xlo, xhi, ylo, yhi, *spans)
    w = image[...]
    cross[:, : fields - columns] = dot(w, stack[columns:], NT)
    cross[:, fields - columns : fields] = dot(w, block[...], NT)
    cross[:, fields:] = dot(w, w, NT)


def factor(square):
    size = square.shape[0]
    lane = lax.broadcasted_iota(jnp.int32, (8, 2 * size), 1)
    sub = lax.broadcasted_iota(jnp.int32, (8, 2 * size), 0)
    blocks = []
    for b in range(size // 8):
        unit = (lax.broadcasted_iota(jnp.int32, (8, size), 1)
                == lax.broadcasted_iota(jnp.int32, (8, size), 0) + 8 * b).astype(jnp.float32)
        blocks.append(jnp.concatenate([square[8 * b : 8 * b + 8], unit], axis=1))
    for k in range(size):
        b, r = divmod(k, 8)
        row = blocks[b][r : r + 1, :]
        row = row * (1.0 / row[:, k : k + 1])
        for later in range(b, size // 8):
            column = blocks[later][:, k : k + 1]
            if later == b:
                column = jnp.where(sub[:, :1] > r, column, 0.0)
            blocks[later] = blocks[later] - column * row
    done = []
    for b, rows in enumerate(blocks):
        diagonal = jnp.sum(jnp.where(lane == sub + 8 * b, rows, 0.0), axis=1, keepdims=True)
        done.append(rows * lax.rsqrt(diagonal))
    whole = jnp.concatenate(done, axis=0)
    return whole[:, :size], whole[:, size:]


def project(cross, own, scale):
    fields = own.shape[0]
    first = cross[:, :fields] * scale
    square = cross[:, fields:] * scale
    first_low = first.astype(jnp.bfloat16)
    second = first - exact(first_low.astype(jnp.float32), own)
    second_low = second.astype(jnp.bfloat16)
    used = first_low.astype(jnp.float32) + second_low.astype(jnp.float32)
    rest = second - exact(second_low.astype(jnp.float32), own)
    square = square - exact(used, first, NT) - exact(rest, used, NT)
    return first_low, second_low, first + second, rest, square


def unpacked(upper, columns, fields):
    rows, at = [], 0
    for b in range(0, fields, columns):
        rows.append((b, upper[:, at : at + fields - b]))
        at += fields - b
    whole = []
    for b, row in rows:
        left = [above[:, b - a : b - a + columns].T for a, above in rows if a < b]
        whole.append(jnp.concatenate(left + [row], axis=1))
    return jnp.concatenate(whole, axis=0)


def first_solve_kernel(scale, cross, stack, image, block, proj, low, own_next):
    columns = image.shape[0]
    fields = stack.shape[0]
    gram = unpacked(cross[:, fields + columns :] * scale, columns, fields)
    first_low, second_low, both, rest, square = project(
        cross[:, : fields + columns], gram, scale
    )
    proj[...] = both
    upper, inverse = factor(square)
    low[...] = upper.T
    inverse = inverse.astype(jnp.bfloat16)
    w = image[...].astype(jnp.float32) - dot(first_low, stack[...]) - dot(second_low, stack[...])
    block[...] = dot(inverse, w.astype(jnp.bfloat16)).astype(jnp.bfloat16)
    kept = stack.shape[0] - columns
    wide = inverse.astype(jnp.float32)
    mixed = exact(wide, rest[:, columns:])
    own_next[:kept, :kept] = gram[columns:, columns:]
    own_next[kept:, :kept] = mixed
    own_next[:kept, kept:] = mixed.T
    own_next[kept:, kept:] = exact(exact(wide, square), wide, NT)


def second_solve_kernel(scale, cross, own, stack, last, image, proj_in, low_in, block, proj, low):
    columns = image.shape[0]
    kept = stack.shape[0] - columns
    first_low, second_low, both, _, square = project(cross[...], own[...], scale)
    proj[0] = proj_in[...]
    proj[1] = both
    upper, inverse = factor(square)
    low[0] = low_in[...]
    low[1] = upper.T
    w = image[...].astype(jnp.float32)
    for part in (first_low, second_low):
        w = w - dot(part[:, :kept], stack[columns:]) - dot(part[:, kept:], last[...])
    block[...] = dot(inverse.astype(jnp.bfloat16), w.astype(jnp.bfloat16)).astype(jnp.bfloat16)


def partner(part, axis, bit):
    count = lax.axis_size(axis)
    return lax.ppermute(part, axis, [(i, i ^ bit) for i in range(count)])


def bits(axis, first=1):
    while first < lax.axis_size(axis):
        yield axis, first
        first *= 2


def whole_sum(part, split):
    if split:
        half = part.shape[0] // 2
        upper = lax.axis_index("col") % 2 == 1
        low, high = part[:half], part[half:]
        given = partner(jnp.where(upper, low, high), "col", 1)
        part = jnp.where(upper, high, low) + given
    for axis, bit in (*bits("col", 2 if split else 1), *bits("slab")):
        part = part + partner(part, axis, bit)
    if split:
        other = partner(part, "col", 1)
        low, high = jnp.where(upper, other, part), jnp.where(upper, part, other)
        part = jnp.concatenate([low, high], axis=0)
    return part


def call(kernel, name, outs, *args):
    return pl.pallas_call(
        kernel,
        out_shape=[jax.ShapeDtypeStruct(shape, dtype) for shape, dtype in outs],
        in_specs=[pl.BlockSpec(memory_space=pltpu.VMEM)] * len(args),
        out_specs=[pl.BlockSpec(memory_space=pltpu.VMEM)] * len(outs),
        compiler_params=pltpu.CompilerParams(vmem_limit_bytes=24 * 1024 * 1024),
        name=name,
    )(*args)


def shards(basis, cell_map, table):
    span_x, span_y, depth = cell_map.shape
    blocks, columns = basis.shape[:2]
    cells = span_x * span_y * depth
    fields = blocks * columns
    scale = 1.0 / (cells * lax.axis_size("slab") * lax.axis_size("col"))
    spans = (span_x, span_y, depth)
    f32, bf16 = jnp.float32, jnp.bfloat16

    stack = basis.reshape(fields, cells)
    coef = coefficients(table, cell_map)
    around = neighbours(stack[fields - columns :], *spans)
    packed = fields + columns + columns * blocks * (blocks + 1) // 2
    image, cross = call(
        functools.partial(first_image_kernel, spans),
        "first_image",
        [((columns, cells), bf16), ((columns, packed), f32)],
        coef, stack, *around,
    )
    block, proj, low, own = call(
        functools.partial(first_solve_kernel, scale),
        "first_solve",
        [((columns, cells), bf16), ((columns, fields), f32), ((columns, columns), f32),
         ((fields, fields), f32)],
        whole_sum(cross, True), stack, image,
    )
    around = neighbours(block, *spans)
    image, cross = call(
        functools.partial(second_image_kernel, spans),
        "second_image",
        [((columns, cells), bf16), ((columns, fields + columns), f32)],
        coef, stack, block, *around,
    )
    block, proj, low = call(
        functools.partial(second_solve_kernel, scale),
        "second_solve",
        [((columns, cells), bf16), ((2, columns, fields), f32), ((2, columns, columns), f32)],
        whole_sum(cross, False), own, stack, block, image, proj, low,
    )
    return block.reshape(columns, *spans), jnp.swapaxes(proj, 1, 2), low


def solution(mesh):
    placed = (P(None, None, "slab", "col", None), P("slab", "col", None), P())
    return jax.shard_map(
        shards,
        mesh=mesh,
        in_specs=placed,
        out_specs=(P(None, "slab", "col", None), P(), P()),
        check_vma=False,
    )
```

```python
import functools

import jax
import jax.numpy as jnp
from jax import lax
from jax.experimental import pallas as pl
from jax.experimental.pallas import tpu as pltpu
from jax.sharding import PartitionSpec as P

HIGHEST = lax.Precision.HIGHEST
NN = (((1,), (0,)), ((), ()))
NT = (((1,), (1,)), ((), ()))
ROWS = 16


def dot(left, right, dims=NN, precision=None):
    return lax.dot_general(
        left, right, dims, precision=precision, preferred_element_type=jnp.float32
    )


def exact(left, right, dims=NN):
    return dot(left, right, dims, HIGHEST)


def neighbours(block, span_x, span_y, depth):
    plane = span_y * depth

    def exchange(axis, upward, downward):
        count = lax.axis_size(axis)
        odd = lax.axis_index(axis) % 2 == 1
        pairs = [[(i, i + 1) for i in range(first, count - 1, 2)] for first in (0, 1)]
        swaps = [pair + [(b, a) for a, b in pair] for pair in pairs]
        inner = lax.ppermute(jnp.where(odd, downward, upward), axis, swaps[0])
        outer = lax.ppermute(jnp.where(odd, upward, downward), axis, swaps[1])
        return jnp.where(odd, inner, outer), jnp.where(odd, outer, inner)

    xlo, xhi = exchange("slab", block[:, (span_x - 1) * plane :], block[:, :plane])

    def edge(row):
        at = row * depth
        parts = [xlo[:, at : at + depth]]
        parts += [block[:, x * plane + at : x * plane + at + depth] for x in range(span_x)]
        parts += [xhi[:, at : at + depth]]
        return jnp.concatenate(parts, axis=1)

    ylo, yhi = exchange("col", edge(span_y - 1), edge(0))
    return xlo, xhi, ylo, yhi


def coefficients_kernel(table, cells, coef):
    classes = table.shape[0]
    lanes = lax.broadcasted_iota(jnp.int32, cells.shape, 1)
    depth = cells.shape[1]
    here = cells[...]
    below = pltpu.roll(here, depth - 1, 1)
    above = pltpu.roll(here, 1, 1)
    maps = (below, here, above)
    keep = (lanes < depth - 1, None, lanes > 0)
    for dz in range(3):
        masks = [maps[dz] == k for k in range(1, classes)]
        for pair in range(9):
            offset = 3 * pair + dz
            value = jnp.full(cells.shape, table[0, offset], jnp.float32)
            for k in range(1, classes):
                value = jnp.where(masks[k - 1], table[k, offset], value)
            if keep[dz] is not None:
                value = jnp.where(keep[dz], value, 0.0)
            coef[offset] = value


def coefficients(table, cell_map):
    span_x, span_y, depth = cell_map.shape
    lines = span_x * span_y
    return pl.pallas_call(
        coefficients_kernel,
        out_shape=jax.ShapeDtypeStruct((27, lines, depth), jnp.float32),
        in_specs=[
            pl.BlockSpec(memory_space=pltpu.SMEM),
            pl.BlockSpec(memory_space=pltpu.VMEM),
        ],
        out_specs=pl.BlockSpec(memory_space=pltpu.VMEM),
        name="coefficients",
    )(table, cell_map.reshape(lines, depth))


def stencil_into(image, coef, block, xlo, xhi, ylo, yhi, span_x, span_y, depth):
    columns = block.shape[0]

    def tile(step, carry):
        rows = pl.ds(pl.multiple_of(step * ROWS, ROWS), ROWS)

        def line(x, y):
            if y < 0:
                ref, at = ylo, x + 1
            elif y >= span_y:
                ref, at = yhi, x + 1
            elif x < 0:
                ref, at = xlo, y
            elif x >= span_x:
                ref, at = xhi, y
            else:
                ref, at = block, x * span_y + y
            return ref[rows, at * depth : (at + 1) * depth].astype(jnp.float32)

        held = {y: [line(x, y) for x in range(-1, span_x + 1)] for y in (-1, 0)}
        for y in range(span_y):
            held[y + 1] = [line(x, y + 1) for x in range(-1, span_x + 1)]
            for x in range(span_x):
                at = x * span_y + y
                sums = [None, None, None]
                for dx in range(3):
                    for dy in range(3):
                        field = held[y + dy - 1][x + dx]
                        for dz in range(3):
                            term = coef[9 * dx + 3 * dy + dz, at : at + 1, :] * field
                            sums[dz] = term if sums[dz] is None else sums[dz] + term
                total = sums[1] + pltpu.roll(sums[0], 1, 1) + pltpu.roll(sums[2], depth - 1, 1)
                image[rows, at * depth : (at + 1) * depth] = total.astype(jnp.bfloat16)
            del held[y - 1]
        return carry

    lax.fori_loop(0, columns // ROWS, tile, 0)


def first_image_kernel(spans, coef, stack, xlo, xhi, ylo, yhi, image, cross):
    columns = image.shape[0]
    fields = stack.shape[0]
    block = stack.at[fields - columns : fields]
    stencil_into(image, coef, block, xlo, xhi, ylo, yhi, *spans)
    w = image[...]
    cross[:, :fields] = dot(w, stack[...], NT)
    cross[:, fields : fields + columns] = dot(w, w, NT)
    at = fields + columns
    for b in range(0, fields, columns):
        width = fields - b
        cross[:, at : at + width] = dot(stack[b : b + columns], stack[b:], NT)
        at += width


def second_image_kernel(spans, coef, stack, block, xlo, xhi, ylo, yhi, image, cross):
    columns = image.shape[0]
    fields = stack.shape[0]
    stencil_into(image, coef, block, xlo, xhi, ylo, yhi, *spans)
    w = image[...]
    cross[:, : fields - columns] = dot(w, stack[columns:], NT)
    cross[:, fields - columns : fields] = dot(w, block[...], NT)
    cross[:, fields:] = dot(w, w, NT)


def factor(square):
    size = square.shape[0]
    lane = lax.broadcasted_iota(jnp.int32, (8, 2 * size), 1)
    sub = lax.broadcasted_iota(jnp.int32, (8, 2 * size), 0)
    blocks = []
    for b in range(size // 8):
        unit = (lax.broadcasted_iota(jnp.int32, (8, size), 1)
                == lax.broadcasted_iota(jnp.int32, (8, size), 0) + 8 * b).astype(jnp.float32)
        blocks.append(jnp.concatenate([square[8 * b : 8 * b + 8], unit], axis=1))
    for k in range(size):
        b, r = divmod(k, 8)
        row = blocks[b][r : r + 1, :]
        row = row * (1.0 / row[:, k : k + 1])
        for later in range(b, size // 8):
            column = blocks[later][:, k : k + 1]
            if later == b:
                column = jnp.where(sub[:, :1] > r, column, 0.0)
            blocks[later] = blocks[later] - column * row
    done = []
    for b, rows in enumerate(blocks):
        diagonal = jnp.sum(jnp.where(lane == sub + 8 * b, rows, 0.0), axis=1, keepdims=True)
        done.append(rows * lax.rsqrt(diagonal))
    whole = jnp.concatenate(done, axis=0)
    return whole[:, :size], whole[:, size:]


def project(cross, own, scale):
    fields = own.shape[0]
    first = cross[:, :fields] * scale
    square = cross[:, fields:] * scale
    first_low = first.astype(jnp.bfloat16)
    second = first - exact(first_low.astype(jnp.float32), own)
    second_low = second.astype(jnp.bfloat16)
    used = first_low.astype(jnp.float32) + second_low.astype(jnp.float32)
    rest = second - exact(second_low.astype(jnp.float32), own)
    square = square - exact(used, first, NT) - exact(rest, used, NT)
    return first_low, second_low, first + second, rest, square


def unpacked(upper, columns, fields):
    rows, at = [], 0
    for b in range(0, fields, columns):
        rows.append((b, upper[:, at : at + fields - b]))
        at += fields - b
    whole = []
    for b, row in rows:
        left = [above[:, b - a : b - a + columns].T for a, above in rows if a < b]
        whole.append(jnp.concatenate(left + [row], axis=1))
    return jnp.concatenate(whole, axis=0)


def first_solve_kernel(scale, cross, stack, image, block, proj, low, own_next):
    columns = image.shape[0]
    fields = stack.shape[0]
    gram = unpacked(cross[:, fields + columns :] * scale, columns, fields)
    first_low, second_low, both, rest, square = project(
        cross[:, : fields + columns], gram, scale
    )
    proj[...] = both
    upper, inverse = factor(square)
    low[...] = upper.T
    inverse = inverse.astype(jnp.bfloat16)
    w = image[...].astype(jnp.float32) - dot(first_low, stack[...]) - dot(second_low, stack[...])
    block[...] = dot(inverse, w.astype(jnp.bfloat16)).astype(jnp.bfloat16)
    kept = stack.shape[0] - columns
    wide = inverse.astype(jnp.float32)
    mixed = exact(wide, rest[:, columns:])
    own_next[:kept, :kept] = gram[columns:, columns:]
    own_next[kept:, :kept] = mixed
    own_next[:kept, kept:] = mixed.T
    own_next[kept:, kept:] = exact(exact(wide, square), wide, NT)


def second_solve_kernel(scale, cross, own, stack, last, image, proj_in, low_in, block, proj, low):
    columns = image.shape[0]
    kept = stack.shape[0] - columns
    first_low, second_low, both, _, square = project(cross[...], own[...], scale)
    proj[0] = proj_in[...]
    proj[1] = both
    upper, inverse = factor(square)
    low[0] = low_in[...]
    low[1] = upper.T
    w = image[...].astype(jnp.float32)
    for part in (first_low, second_low):
        w = w - dot(part[:, :kept], stack[columns:]) - dot(part[:, kept:], last[...])
    block[...] = dot(inverse.astype(jnp.bfloat16), w.astype(jnp.bfloat16)).astype(jnp.bfloat16)


def partner(part, mask):
    axes = ("slab", "col")
    count = lax.axis_size("slab") * lax.axis_size("col")
    return lax.ppermute(part, axes, [(i, i ^ mask) for i in range(count)])


def whole_sum(part):
    count = lax.axis_size("slab") * lax.axis_size("col")
    half = part.shape[0] // 2
    upper = lax.axis_index("col") % 2 == 1
    low, high = part[:half], part[half:]
    part = jnp.where(upper, high, low) + partner(jnp.where(upper, low, high), 1)
    bit = 2
    while bit < count:
        if 2 * bit < count:
            one, two, both = (partner(part, mask) for mask in (bit, 2 * bit, 3 * bit))
            part = (part + one) + (two + both)
        else:
            part = part + partner(part, bit)
        bit *= 4
    other = partner(part, 1)
    return jnp.concatenate([jnp.where(upper, other, part), jnp.where(upper, part, other)], axis=0)


def call(kernel, name, outs, *args):
    return pl.pallas_call(
        kernel,
        out_shape=[jax.ShapeDtypeStruct(shape, dtype) for shape, dtype in outs],
        in_specs=[pl.BlockSpec(memory_space=pltpu.VMEM)] * len(args),
        out_specs=[pl.BlockSpec(memory_space=pltpu.VMEM)] * len(outs),
        compiler_params=pltpu.CompilerParams(vmem_limit_bytes=24 * 1024 * 1024),
        name=name,
    )(*args)


def shards(basis, cell_map, table):
    span_x, span_y, depth = cell_map.shape
    blocks, columns = basis.shape[:2]
    cells = span_x * span_y * depth
    fields = blocks * columns
    scale = 1.0 / (cells * lax.axis_size("slab") * lax.axis_size("col"))
    spans = (span_x, span_y, depth)
    f32, bf16 = jnp.float32, jnp.bfloat16

    stack = basis.reshape(fields, cells)
    coef = coefficients(table, cell_map)
    around = neighbours(stack[fields - columns :], *spans)
    packed = fields + columns + columns * blocks * (blocks + 1) // 2
    image, cross = call(
        functools.partial(first_image_kernel, spans),
        "first_image",
        [((columns, cells), bf16), ((columns, packed), f32)],
        coef, stack, *around,
    )
    block, proj, low, own = call(
        functools.partial(first_solve_kernel, scale),
        "first_solve",
        [((columns, cells), bf16), ((columns, fields), f32), ((columns, columns), f32),
         ((fields, fields), f32)],
        whole_sum(cross), stack, image,
    )
    around = neighbours(block, *spans)
    image, cross = call(
        functools.partial(second_image_kernel, spans),
        "second_image",
        [((columns, cells), bf16), ((columns, fields + columns), f32)],
        coef, stack, block, *around,
    )
    block, proj, low = call(
        functools.partial(second_solve_kernel, scale),
        "second_solve",
        [((columns, cells), bf16), ((2, columns, fields), f32), ((2, columns, columns), f32)],
        whole_sum(cross), own, stack, block, image, proj, low,
    )
    return block.reshape(columns, *spans), jnp.swapaxes(proj, 1, 2), low


def solution(mesh):
    placed = (P(None, None, "slab", "col", None), P("slab", "col", None), P())
    return jax.shard_map(
        shards,
        mesh=mesh,
        in_specs=placed,
        out_specs=(P(None, "slab", "col", None), P(), P()),
        check_vma=False,
    )
```

```python
import functools

import jax
import jax.numpy as jnp
from jax import lax
from jax.experimental import pallas as pl
from jax.experimental.pallas import tpu as pltpu
from jax.sharding import PartitionSpec as P

HIGHEST = lax.Precision.HIGHEST
NN = (((1,), (0,)), ((), ()))
NT = (((1,), (1,)), ((), ()))
ROWS = 16


def dot(left, right, dims=NN, precision=None):
    return lax.dot_general(
        left, right, dims, precision=precision, preferred_element_type=jnp.float32
    )


def exact(left, right, dims=NN):
    return dot(left, right, dims, HIGHEST)


def neighbours(block, span_x, span_y, depth):
    plane = span_y * depth

    def exchange(axis, upward, downward):
        count = lax.axis_size(axis)
        odd = lax.axis_index(axis) % 2 == 1
        pairs = [[(i, i + 1) for i in range(first, count - 1, 2)] for first in (0, 1)]
        swaps = [pair + [(b, a) for a, b in pair] for pair in pairs]
        inner = lax.ppermute(jnp.where(odd, downward, upward), axis, swaps[0])
        outer = lax.ppermute(jnp.where(odd, upward, downward), axis, swaps[1])
        return jnp.where(odd, inner, outer), jnp.where(odd, outer, inner)

    xlo, xhi = exchange("slab", block[:, (span_x - 1) * plane :], block[:, :plane])

    def edge(row):
        at = row * depth
        parts = [xlo[:, at : at + depth]]
        parts += [block[:, x * plane + at : x * plane + at + depth] for x in range(span_x)]
        parts += [xhi[:, at : at + depth]]
        return jnp.concatenate(parts, axis=1)

    ylo, yhi = exchange("col", edge(span_y - 1), edge(0))
    return xlo, xhi, ylo, yhi


def coefficients_kernel(table, cells, coef):
    classes = table.shape[0]
    lanes = lax.broadcasted_iota(jnp.int32, cells.shape, 1)
    depth = cells.shape[1]
    here = cells[...]
    below = pltpu.roll(here, depth - 1, 1)
    above = pltpu.roll(here, 1, 1)
    maps = (below, here, above)
    keep = (lanes < depth - 1, None, lanes > 0)
    for dz in range(3):
        masks = [maps[dz] == k for k in range(1, classes)]
        for pair in range(9):
            offset = 3 * pair + dz
            value = jnp.full(cells.shape, table[0, offset], jnp.float32)
            for k in range(1, classes):
                value = jnp.where(masks[k - 1], table[k, offset], value)
            if keep[dz] is not None:
                value = jnp.where(keep[dz], value, 0.0)
            coef[offset] = value


def coefficients(table, cell_map):
    span_x, span_y, depth = cell_map.shape
    lines = span_x * span_y
    return pl.pallas_call(
        coefficients_kernel,
        out_shape=jax.ShapeDtypeStruct((27, lines, depth), jnp.float32),
        in_specs=[
            pl.BlockSpec(memory_space=pltpu.SMEM),
            pl.BlockSpec(memory_space=pltpu.VMEM),
        ],
        out_specs=pl.BlockSpec(memory_space=pltpu.VMEM),
        compiler_params=pltpu.CompilerParams(vmem_limit_bytes=4 * 1024 * 1024),
        name="coefficients",
    )(table, cell_map.reshape(lines, depth))


def stencil_into(image, coef, block, xlo, xhi, ylo, yhi, span_x, span_y, depth):
    columns = block.shape[0]

    def tile(step, carry):
        rows = pl.ds(pl.multiple_of(step * ROWS, ROWS), ROWS)

        def line(x, y):
            if y < 0:
                ref, at = ylo, x + 1
            elif y >= span_y:
                ref, at = yhi, x + 1
            elif x < 0:
                ref, at = xlo, y
            elif x >= span_x:
                ref, at = xhi, y
            else:
                ref, at = block, x * span_y + y
            return ref[rows, at * depth : (at + 1) * depth].astype(jnp.float32)

        held = {y: [line(x, y) for x in range(-1, span_x + 1)] for y in (-1, 0)}
        for y in range(span_y):
            held[y + 1] = [line(x, y + 1) for x in range(-1, span_x + 1)]
            for x in range(span_x):
                at = x * span_y + y
                sums = [None, None, None]
                for dx in range(3):
                    for dy in range(3):
                        field = held[y + dy - 1][x + dx]
                        for dz in range(3):
                            term = coef[9 * dx + 3 * dy + dz, at : at + 1, :] * field
                            sums[dz] = term if sums[dz] is None else sums[dz] + term
                total = sums[1] + pltpu.roll(sums[0], 1, 1) + pltpu.roll(sums[2], depth - 1, 1)
                image[rows, at * depth : (at + 1) * depth] = total.astype(jnp.bfloat16)
            del held[y - 1]
        return carry

    lax.fori_loop(0, columns // ROWS, tile, 0)


def first_image_kernel(spans, coef, stack, xlo, xhi, ylo, yhi, image, cross):
    columns = image.shape[0]
    fields = stack.shape[0]
    block = stack.at[fields - columns : fields]
    stencil_into(image, coef, block, xlo, xhi, ylo, yhi, *spans)
    w = image[...]
    cross[:, :fields] = dot(w, stack[...], NT)
    cross[:, fields : fields + columns] = dot(w, w, NT)
    at = fields + columns
    for b in range(0, fields, columns):
        width = fields - b
        cross[:, at : at + width] = dot(stack[b : b + columns], stack[b:], NT)
        at += width


def second_image_kernel(spans, coef, stack, block, xlo, xhi, ylo, yhi, image, cross):
    columns = image.shape[0]
    fields = stack.shape[0]
    stencil_into(image, coef, block, xlo, xhi, ylo, yhi, *spans)
    w = image[...]
    cross[:, : fields - columns] = dot(w, stack[columns:], NT)
    cross[:, fields - columns : fields] = dot(w, block[...], NT)
    cross[:, fields:] = dot(w, w, NT)


def factor(square):
    size = square.shape[0]
    lane = lax.broadcasted_iota(jnp.int32, (8, 2 * size), 1)
    sub = lax.broadcasted_iota(jnp.int32, (8, 2 * size), 0)
    blocks = []
    for b in range(size // 8):
        unit = (lax.broadcasted_iota(jnp.int32, (8, size), 1)
                == lax.broadcasted_iota(jnp.int32, (8, size), 0) + 8 * b).astype(jnp.float32)
        blocks.append(jnp.concatenate([square[8 * b : 8 * b + 8], unit], axis=1))
    for k in range(size):
        b, r = divmod(k, 8)
        row = blocks[b][r : r + 1, :]
        row = row * (1.0 / row[:, k : k + 1])
        for later in range(b, size // 8):
            column = blocks[later][:, k : k + 1]
            if later == b:
                column = jnp.where(sub[:, :1] > r, column, 0.0)
            blocks[later] = blocks[later] - column * row
    done = []
    for b, rows in enumerate(blocks):
        diagonal = jnp.sum(jnp.where(lane == sub + 8 * b, rows, 0.0), axis=1, keepdims=True)
        done.append(rows * lax.rsqrt(diagonal))
    whole = jnp.concatenate(done, axis=0)
    return whole[:, :size], whole[:, size:]


def project(cross, own, scale):
    fields = own.shape[0]
    first = cross[:, :fields] * scale
    square = cross[:, fields:] * scale
    first_low = first.astype(jnp.bfloat16)
    second = first - exact(first_low.astype(jnp.float32), own)
    second_low = second.astype(jnp.bfloat16)
    used = first_low.astype(jnp.float32) + second_low.astype(jnp.float32)
    rest = second - exact(second_low.astype(jnp.float32), own)
    square = square - exact(used, first, NT) - exact(rest, used, NT)
    return first_low, second_low, first + second, rest, square


def unpacked(upper, columns, fields):
    rows, at = [], 0
    for b in range(0, fields, columns):
        rows.append((b, upper[:, at : at + fields - b]))
        at += fields - b
    whole = []
    for b, row in rows:
        left = [above[:, b - a : b - a + columns].T for a, above in rows if a < b]
        whole.append(jnp.concatenate(left + [row], axis=1))
    return jnp.concatenate(whole, axis=0)


def first_solve_kernel(scale, cross, stack, image, block, proj, low, own_next):
    columns = image.shape[0]
    fields = stack.shape[0]
    gram = unpacked(cross[:, fields + columns :] * scale, columns, fields)
    first_low, second_low, both, rest, square = project(
        cross[:, : fields + columns], gram, scale
    )
    proj[...] = both
    upper, inverse = factor(square)
    low[...] = upper.T
    inverse = inverse.astype(jnp.bfloat16)
    w = image[...].astype(jnp.float32) - dot(first_low, stack[...]) - dot(second_low, stack[...])
    block[...] = dot(inverse, w.astype(jnp.bfloat16)).astype(jnp.bfloat16)
    kept = stack.shape[0] - columns
    wide = inverse.astype(jnp.float32)
    mixed = exact(wide, rest[:, columns:])
    own_next[:kept, :kept] = gram[columns:, columns:]
    own_next[kept:, :kept] = mixed
    own_next[:kept, kept:] = mixed.T
    own_next[kept:, kept:] = exact(exact(wide, square), wide, NT)


def second_solve_kernel(scale, cross, own, stack, last, image, proj_in, low_in, block, proj, low):
    columns = image.shape[0]
    kept = stack.shape[0] - columns
    first_low, second_low, both, _, square = project(cross[...], own[...], scale)
    proj[0] = proj_in[...]
    proj[1] = both
    upper, inverse = factor(square)
    low[0] = low_in[...]
    low[1] = upper.T
    w = image[...].astype(jnp.float32)
    for part in (first_low, second_low):
        w = w - dot(part[:, :kept], stack[columns:]) - dot(part[:, kept:], last[...])
    block[...] = dot(inverse.astype(jnp.bfloat16), w.astype(jnp.bfloat16)).astype(jnp.bfloat16)


def moved(part, pairs):
    return lax.ppermute(part, ("slab", "col"), pairs)


def whole_sum(part):
    count = lax.axis_size("slab") * lax.axis_size("col")
    second = range(1, count, 2)
    part = part + moved(part, [(i - 1, i) for i in second])
    bit = 2
    while bit < count:
        masks = [mask for mask in (bit, 2 * bit, 3 * bit) if mask < count]
        given = [moved(part, [(i, i ^ mask) for i in second]) for mask in masks]
        part = part + given[0]
        if len(given) == 3:
            part = part + (given[1] + given[2])
        bit *= 4
    back = moved(part, [(i, i - 1) for i in second])
    return jnp.where(lax.axis_index("col") % 2 == 1, part, back)


def call(kernel, name, outs, *args):
    return pl.pallas_call(
        kernel,
        out_shape=[jax.ShapeDtypeStruct(shape, dtype) for shape, dtype in outs],
        in_specs=[pl.BlockSpec(memory_space=pltpu.VMEM)] * len(args),
        out_specs=[pl.BlockSpec(memory_space=pltpu.VMEM)] * len(outs),
        compiler_params=pltpu.CompilerParams(vmem_limit_bytes=24 * 1024 * 1024),
        name=name,
    )(*args)


def shards(basis, cell_map, table):
    span_x, span_y, depth = cell_map.shape
    blocks, columns = basis.shape[:2]
    cells = span_x * span_y * depth
    fields = blocks * columns
    scale = 1.0 / (cells * lax.axis_size("slab") * lax.axis_size("col"))
    spans = (span_x, span_y, depth)
    f32, bf16 = jnp.float32, jnp.bfloat16

    stack = basis.reshape(fields, cells)
    coef = coefficients(table, cell_map)
    around = neighbours(stack[fields - columns :], *spans)
    packed = fields + columns + columns * blocks * (blocks + 1) // 2
    image, cross = call(
        functools.partial(first_image_kernel, spans),
        "first_image",
        [((columns, cells), bf16), ((columns, packed), f32)],
        coef, stack, *around,
    )
    block, proj, low, own = call(
        functools.partial(first_solve_kernel, scale),
        "first_solve",
        [((columns, cells), bf16), ((columns, fields), f32), ((columns, columns), f32),
         ((fields, fields), f32)],
        whole_sum(cross), stack, image,
    )
    around = neighbours(block, *spans)
    image, cross = call(
        functools.partial(second_image_kernel, spans),
        "second_image",
        [((columns, cells), bf16), ((columns, fields + columns), f32)],
        coef, stack, block, *around,
    )
    block, proj, low = call(
        functools.partial(second_solve_kernel, scale),
        "second_solve",
        [((columns, cells), bf16), ((2, columns, fields), f32), ((2, columns, columns), f32)],
        whole_sum(cross), own, stack, block, image, proj, low,
    )
    return block.reshape(columns, *spans), jnp.swapaxes(proj, 1, 2), low


def solution(mesh):
    placed = (P(None, None, "slab", "col", None), P("slab", "col", None), P())
    return jax.shard_map(
        shards,
        mesh=mesh,
        in_specs=placed,
        out_specs=(P(None, "slab", "col", None), P(), P()),
        check_vma=False,
    )
```

```python
import functools
import math

import jax
import jax.numpy as jnp
from jax import lax
from jax.experimental import pallas as pl
from jax.experimental.pallas import tpu as pltpu
from jax.sharding import PartitionSpec as P

HIGHEST = lax.Precision.HIGHEST
NN = (((1,), (0,)), ((), ()))
NT = (((1,), (1,)), ((), ()))
ROWS = 16


def dot(left, right, dims=NN, precision=None):
    return lax.dot_general(
        left, right, dims, precision=precision, preferred_element_type=jnp.float32
    )


def exact(left, right, dims=NN):
    return dot(left, right, dims, HIGHEST)


def neighbours(block, span_x, span_y, depth):
    plane = span_y * depth

    def exchange(axis, upward, downward):
        count = lax.axis_size(axis)
        me = lax.axis_index(axis)
        odd = me % 2 == 1
        inner = swapped(jnp.where(odd, downward, upward), (axis,), lambda i: i ^ 1)
        outer = swapped(
            jnp.where(odd, upward, downward),
            (axis,),
            lambda i: i if i in (0, count - 1) else (i - 1 ^ 1) + 1,
        )
        outer = jnp.where((me == 0) | (me == count - 1), 0, outer)
        return jnp.where(odd, inner, outer), jnp.where(odd, outer, inner)

    xlo, xhi = exchange("slab", block[:, (span_x - 1) * plane :], block[:, :plane])

    def edge(row):
        at = row * depth
        parts = [xlo[:, at : at + depth]]
        parts += [block[:, x * plane + at : x * plane + at + depth] for x in range(span_x)]
        parts += [xhi[:, at : at + depth]]
        return jnp.concatenate(parts, axis=1)

    ylo, yhi = exchange("col", edge(span_y - 1), edge(0))
    return xlo, xhi, ylo, yhi


def coefficients_kernel(table, cells, coef):
    classes = table.shape[0]
    lanes = lax.broadcasted_iota(jnp.int32, cells.shape, 1)
    depth = cells.shape[1]
    here = cells[...]
    below = pltpu.roll(here, depth - 1, 1)
    above = pltpu.roll(here, 1, 1)
    maps = (below, here, above)
    keep = (lanes < depth - 1, None, lanes > 0)
    for dz in range(3):
        masks = [maps[dz] == k for k in range(1, classes)]
        for pair in range(9):
            offset = 3 * pair + dz
            value = jnp.full(cells.shape, table[0, offset], jnp.float32)
            for k in range(1, classes):
                value = jnp.where(masks[k - 1], table[k, offset], value)
            if keep[dz] is not None:
                value = jnp.where(keep[dz], value, 0.0)
            coef[offset] = value


def coefficients(table, cell_map):
    span_x, span_y, depth = cell_map.shape
    lines = span_x * span_y
    return pl.pallas_call(
        coefficients_kernel,
        out_shape=jax.ShapeDtypeStruct((27, lines, depth), jnp.float32),
        in_specs=[
            pl.BlockSpec(memory_space=pltpu.SMEM),
            pl.BlockSpec(memory_space=pltpu.VMEM),
        ],
        out_specs=pl.BlockSpec(memory_space=pltpu.VMEM),
        compiler_params=pltpu.CompilerParams(vmem_limit_bytes=4 * 1024 * 1024),
        name="coefficients",
    )(table, cell_map.reshape(lines, depth))


def stencil_into(image, coef, block, xlo, xhi, ylo, yhi, span_x, span_y, depth):
    columns = block.shape[0]

    def tile(step, carry):
        rows = pl.ds(pl.multiple_of(step * ROWS, ROWS), ROWS)

        def line(x, y):
            if y < 0:
                ref, at = ylo, x + 1
            elif y >= span_y:
                ref, at = yhi, x + 1
            elif x < 0:
                ref, at = xlo, y
            elif x >= span_x:
                ref, at = xhi, y
            else:
                ref, at = block, x * span_y + y
            return ref[rows, at * depth : (at + 1) * depth].astype(jnp.float32)

        held = {y: [line(x, y) for x in range(-1, span_x + 1)] for y in (-1, 0)}
        for y in range(span_y):
            held[y + 1] = [line(x, y + 1) for x in range(-1, span_x + 1)]
            for x in range(span_x):
                at = x * span_y + y
                sums = [None, None, None]
                for dx in range(3):
                    for dy in range(3):
                        field = held[y + dy - 1][x + dx]
                        for dz in range(3):
                            term = coef[9 * dx + 3 * dy + dz, at : at + 1, :] * field
                            sums[dz] = term if sums[dz] is None else sums[dz] + term
                total = sums[1] + pltpu.roll(sums[0], 1, 1) + pltpu.roll(sums[2], depth - 1, 1)
                image[rows, at * depth : (at + 1) * depth] = total.astype(jnp.bfloat16)
            del held[y - 1]
        return carry

    lax.fori_loop(0, columns // ROWS, tile, 0)


def first_image_kernel(spans, coef, stack, xlo, xhi, ylo, yhi, image, cross):
    columns = image.shape[0]
    fields = stack.shape[0]
    block = stack.at[fields - columns : fields]
    stencil_into(image, coef, block, xlo, xhi, ylo, yhi, *spans)
    w = image[...]
    cross[:, :fields] = dot(w, stack[...], NT)
    cross[:, fields : fields + columns] = dot(w, w, NT)
    at = fields + columns
    for b in range(0, fields, columns):
        width = fields - b
        cross[:, at : at + width] = dot(stack[b : b + columns], stack[b:], NT)
        at += width


def second_image_kernel(spans, coef, stack, block, xlo, xhi, ylo, yhi, image, cross):
    columns = image.shape[0]
    fields = stack.shape[0]
    stencil_into(image, coef, block, xlo, xhi, ylo, yhi, *spans)
    w = image[...]
    cross[:, : fields - columns] = dot(w, stack[columns:], NT)
    cross[:, fields - columns : fields] = dot(w, block[...], NT)
    cross[:, fields:] = dot(w, w, NT)


def factor(square):
    size = square.shape[0]
    lane = lax.broadcasted_iota(jnp.int32, (8, 2 * size), 1)
    sub = lax.broadcasted_iota(jnp.int32, (8, 2 * size), 0)
    blocks = []
    for b in range(size // 8):
        unit = (lax.broadcasted_iota(jnp.int32, (8, size), 1)
                == lax.broadcasted_iota(jnp.int32, (8, size), 0) + 8 * b).astype(jnp.float32)
        blocks.append(jnp.concatenate([square[8 * b : 8 * b + 8], unit], axis=1))
    for k in range(size):
        b, r = divmod(k, 8)
        row = blocks[b][r : r + 1, :]
        row = row * (1.0 / row[:, k : k + 1])
        for later in range(b, size // 8):
            column = blocks[later][:, k : k + 1]
            if later == b:
                column = jnp.where(sub[:, :1] > r, column, 0.0)
            blocks[later] = blocks[later] - column * row
    done = []
    for b, rows in enumerate(blocks):
        diagonal = jnp.sum(jnp.where(lane == sub + 8 * b, rows, 0.0), axis=1, keepdims=True)
        done.append(rows * lax.rsqrt(diagonal))
    whole = jnp.concatenate(done, axis=0)
    return whole[:, :size], whole[:, size:]


def project(cross, own, scale):
    fields = own.shape[0]
    first = cross[:, :fields] * scale
    square = cross[:, fields:] * scale
    first_low = first.astype(jnp.bfloat16)
    second = first - exact(first_low.astype(jnp.float32), own)
    second_low = second.astype(jnp.bfloat16)
    used = first_low.astype(jnp.float32) + second_low.astype(jnp.float32)
    rest = second - exact(second_low.astype(jnp.float32), own)
    square = square - exact(used, first, NT) - exact(rest, used, NT)
    return first_low, second_low, first + second, rest, square


def unpacked(upper, columns, fields):
    rows, at = [], 0
    for b in range(0, fields, columns):
        rows.append((b, upper[:, at : at + fields - b]))
        at += fields - b
    whole = []
    for b, row in rows:
        left = [above[:, b - a : b - a + columns].T for a, above in rows if a < b]
        whole.append(jnp.concatenate(left + [row], axis=1))
    return jnp.concatenate(whole, axis=0)


def first_solve_kernel(scale, cross, stack, image, block, proj, low, own_next):
    columns = image.shape[0]
    fields = stack.shape[0]
    gram = unpacked(cross[:, fields + columns :] * scale, columns, fields)
    first_low, second_low, both, rest, square = project(
        cross[:, : fields + columns], gram, scale
    )
    proj[...] = both
    upper, inverse = factor(square)
    low[...] = upper.T
    inverse = inverse.astype(jnp.bfloat16)
    w = image[...].astype(jnp.float32) - dot(first_low, stack[...]) - dot(second_low, stack[...])
    block[...] = dot(inverse, w.astype(jnp.bfloat16)).astype(jnp.bfloat16)
    kept = stack.shape[0] - columns
    wide = inverse.astype(jnp.float32)
    mixed = exact(wide, rest[:, columns:])
    own_next[:kept, :kept] = gram[columns:, columns:]
    own_next[kept:, :kept] = mixed
    own_next[:kept, kept:] = mixed.T
    own_next[kept:, kept:] = exact(exact(wide, square), wide, NT)


def second_solve_kernel(scale, cross, own, stack, last, image, proj_in, low_in, block, proj, low):
    columns = image.shape[0]
    kept = stack.shape[0] - columns
    first_low, second_low, both, _, square = project(cross[...], own[...], scale)
    proj[0] = proj_in[...]
    proj[1] = both
    upper, inverse = factor(square)
    low[0] = low_in[...]
    low[1] = upper.T
    w = image[...].astype(jnp.float32)
    for part in (first_low, second_low):
        w = w - dot(part[:, :kept], stack[columns:]) - dot(part[:, kept:], last[...])
    block[...] = dot(inverse.astype(jnp.bfloat16), w.astype(jnp.bfloat16)).astype(jnp.bfloat16)


def swapped(part, axis, partner):
    count = math.prod(lax.axis_size(name) for name in axis)
    return lax.ppermute(part, axis, [(i, partner(i)) for i in range(count)])


def whole_sum(part):
    axes = ("slab", "col")
    count = lax.axis_size("slab") * lax.axis_size("col")
    part = part + swapped(part, axes, lambda i: i ^ 1)
    bit = 2
    while bit < count:
        masks = [mask for mask in (bit, 2 * bit, 3 * bit) if mask < count]
        given = [swapped(part, axes, lambda i: i ^ mask if i % 2 else i) for mask in masks]
        part = part + given[0]
        if len(given) == 3:
            part = part + (given[1] + given[2])
        bit *= 4
    return jnp.where(
        lax.axis_index("col") % 2 == 1, part, swapped(part, axes, lambda i: i ^ 1)
    )


def call(kernel, name, outs, *args):
    return pl.pallas_call(
        kernel,
        out_shape=[jax.ShapeDtypeStruct(shape, dtype) for shape, dtype in outs],
        in_specs=[pl.BlockSpec(memory_space=pltpu.VMEM)] * len(args),
        out_specs=[pl.BlockSpec(memory_space=pltpu.VMEM)] * len(outs),
        compiler_params=pltpu.CompilerParams(vmem_limit_bytes=24 * 1024 * 1024),
        name=name,
    )(*args)


def shards(basis, cell_map, table):
    span_x, span_y, depth = cell_map.shape
    blocks, columns = basis.shape[:2]
    cells = span_x * span_y * depth
    fields = blocks * columns
    scale = 1.0 / (cells * lax.axis_size("slab") * lax.axis_size("col"))
    spans = (span_x, span_y, depth)
    f32, bf16 = jnp.float32, jnp.bfloat16

    stack = basis.reshape(fields, cells)
    coef = coefficients(table, cell_map)
    around = neighbours(stack[fields - columns :], *spans)
    packed = fields + columns + columns * blocks * (blocks + 1) // 2
    image, cross = call(
        functools.partial(first_image_kernel, spans),
        "first_image",
        [((columns, cells), bf16), ((columns, packed), f32)],
        coef, stack, *around,
    )
    block, proj, low, own = call(
        functools.partial(first_solve_kernel, scale),
        "first_solve",
        [((columns, cells), bf16), ((columns, fields), f32), ((columns, columns), f32),
         ((fields, fields), f32)],
        whole_sum(cross), stack, image,
    )
    around = neighbours(block, *spans)
    image, cross = call(
        functools.partial(second_image_kernel, spans),
        "second_image",
        [((columns, cells), bf16), ((columns, fields + columns), f32)],
        coef, stack, block, *around,
    )
    block, proj, low = call(
        functools.partial(second_solve_kernel, scale),
        "second_solve",
        [((columns, cells), bf16), ((2, columns, fields), f32), ((2, columns, columns), f32)],
        whole_sum(cross), own, stack, block, image, proj, low,
    )
    return block.reshape(columns, *spans), jnp.swapaxes(proj, 1, 2), low


def solution(mesh):
    placed = (P(None, None, "slab", "col", None), P("slab", "col", None), P())
    return jax.shard_map(
        shards,
        mesh=mesh,
        in_specs=placed,
        out_specs=(P(None, "slab", "col", None), P(), P()),
        check_vma=False,
    )
```

```python
import functools

import jax
import jax.numpy as jnp
from jax import lax
from jax.experimental import pallas as pl
from jax.experimental.pallas import tpu as pltpu
from jax.sharding import PartitionSpec as P

NN = (((1,), (0,)), ((), ()))
NT = (((1,), (1,)), ((), ()))
ROWS = 16


def dot(left, right, dims=NN):
    return lax.dot_general(left, right, dims, preferred_element_type=jnp.float32)


def neighbours(block, span_x, span_y, depth):
    plane = span_y * depth

    def exchange(axis, upward, downward):
        count = lax.axis_size(axis)
        odd = lax.axis_index(axis) % 2 == 1
        pairs = [[(i, i + 1) for i in range(first, count - 1, 2)] for first in (0, 1)]
        swaps = [pair + [(b, a) for a, b in pair] for pair in pairs]
        inner = lax.ppermute(jnp.where(odd, downward, upward), axis, swaps[0])
        outer = lax.ppermute(jnp.where(odd, upward, downward), axis, swaps[1])
        return jnp.where(odd, inner, outer), jnp.where(odd, outer, inner)

    xlo, xhi = exchange("slab", block[:, (span_x - 1) * plane :], block[:, :plane])

    def edge(row):
        at = row * depth
        parts = [xlo[:, at : at + depth]]
        parts += [block[:, x * plane + at : x * plane + at + depth] for x in range(span_x)]
        parts += [xhi[:, at : at + depth]]
        return jnp.concatenate(parts, axis=1)

    ylo, yhi = exchange("col", edge(span_y - 1), edge(0))
    return xlo, xhi, ylo, yhi


def coefficients_kernel(table, cells, coef):
    classes = table.shape[0]
    lanes = lax.broadcasted_iota(jnp.int32, cells.shape, 1)
    depth = cells.shape[1]
    here = cells[...]
    below = pltpu.roll(here, depth - 1, 1)
    above = pltpu.roll(here, 1, 1)
    maps = (below, here, above)
    keep = (lanes < depth - 1, None, lanes > 0)
    for dz in range(3):
        masks = [maps[dz] == k for k in range(1, classes)]
        for pair in range(9):
            offset = 3 * pair + dz
            value = jnp.full(cells.shape, table[0, offset], jnp.float32)
            for k in range(1, classes):
                value = jnp.where(masks[k - 1], table[k, offset], value)
            if keep[dz] is not None:
                value = jnp.where(keep[dz], value, 0.0)
            coef[offset] = value


def coefficients(table, cell_map):
    span_x, span_y, depth = cell_map.shape
    lines = span_x * span_y
    return pl.pallas_call(
        coefficients_kernel,
        out_shape=jax.ShapeDtypeStruct((27, lines, depth), jnp.float32),
        in_specs=[
            pl.BlockSpec(memory_space=pltpu.SMEM),
            pl.BlockSpec(memory_space=pltpu.VMEM),
        ],
        out_specs=pl.BlockSpec(memory_space=pltpu.VMEM),
        compiler_params=pltpu.CompilerParams(vmem_limit_bytes=4 * 1024 * 1024),
        name="coefficients",
    )(table, cell_map.reshape(lines, depth))


def stencil_into(image, coef, block, xlo, xhi, ylo, yhi, span_x, span_y, depth):
    columns = block.shape[0]

    def tile(step, carry):
        rows = pl.ds(pl.multiple_of(step * ROWS, ROWS), ROWS)

        def line(x, y):
            if y < 0:
                ref, at = ylo, x + 1
            elif y >= span_y:
                ref, at = yhi, x + 1
            elif x < 0:
                ref, at = xlo, y
            elif x >= span_x:
                ref, at = xhi, y
            else:
                ref, at = block, x * span_y + y
            return ref[rows, at * depth : (at + 1) * depth].astype(jnp.float32)

        held = {y: [line(x, y) for x in range(-1, span_x + 1)] for y in (-1, 0)}
        for y in range(span_y):
            held[y + 1] = [line(x, y + 1) for x in range(-1, span_x + 1)]
            for x in range(span_x):
                at = x * span_y + y
                sums = [None, None, None]
                for dx in range(3):
                    for dy in range(3):
                        field = held[y + dy - 1][x + dx]
                        for dz in range(3):
                            term = coef[9 * dx + 3 * dy + dz, at : at + 1, :] * field
                            sums[dz] = term if sums[dz] is None else sums[dz] + term
                total = sums[1] + pltpu.roll(sums[0], 1, 1) + pltpu.roll(sums[2], depth - 1, 1)
                image[rows, at * depth : (at + 1) * depth] = total.astype(jnp.bfloat16)
            del held[y - 1]
        return carry

    lax.fori_loop(0, columns // ROWS, tile, 0)


def first_image_kernel(spans, coef, stack, xlo, xhi, ylo, yhi, image, cross):
    columns = image.shape[0]
    fields = stack.shape[0]
    block = stack.at[fields - columns : fields]
    stencil_into(image, coef, block, xlo, xhi, ylo, yhi, *spans)
    w = image[...]
    cross[:, :fields] = dot(w, stack[...], NT)
    cross[:, fields : fields + columns] = dot(w, w, NT)
    at = fields + columns
    for b in range(0, fields, columns):
        width = fields - b
        cross[:, at : at + width] = dot(stack[b : b + columns], stack[b:], NT)
        at += width


def second_image_kernel(spans, coef, stack, block, xlo, xhi, ylo, yhi, image, cross):
    columns = image.shape[0]
    fields = stack.shape[0]
    stencil_into(image, coef, block, xlo, xhi, ylo, yhi, *spans)
    w = image[...]
    cross[:, : fields - columns] = dot(w, stack[columns:], NT)
    cross[:, fields - columns : fields] = dot(w, block[...], NT)
    cross[:, fields:] = dot(w, w, NT)


def split(values):
    high = values.astype(jnp.bfloat16)
    return high, (values - high.astype(jnp.float32)).astype(jnp.bfloat16)


def dots(lefts, rights, dims=NN):
    return sum(dot(left, right, dims) for left in lefts for right in rights)


def factor(square):
    size = square.shape[0]
    f32 = jnp.float32
    unit = lax.broadcasted_iota(jnp.int32, (size, size), 0) == lax.broadcasted_iota(
        jnp.int32, (size, size), 1
    )
    diagonal = jnp.where(unit, square, 0.0)
    down = lax.rsqrt(jnp.sum(diagonal, axis=1, keepdims=True))
    across_squared = jnp.sum(diagonal, axis=0, keepdims=True)
    across = lax.rsqrt(across_squared)
    whole = jnp.concatenate([square * down * across, unit.astype(f32)], axis=1)
    sub = lax.broadcasted_iota(jnp.int32, (8, 2 * size), 0)
    blocks = [whole[8 * b : 8 * b + 8] for b in range(size // 8)]
    done = [jnp.zeros((8, 2 * size), f32) for _ in blocks]
    for k in range(0, size, 2):
        b, r = divmod(k, 8)
        here = blocks[b]
        row, next_row = here[r : r + 1, :], here[r + 1 : r + 2, :]
        first, mixed = row[:, k : k + 1], next_row[:, k : k + 1]
        last = next_row[:, k + 1 : k + 2]
        inverse = 1.0 / (first * last - mixed * mixed)
        left = (last * row - mixed * next_row) * inverse
        right = (first * next_row - mixed * row) * inverse
        for later in range(b, size // 8):
            one, two = blocks[later][:, k : k + 1], blocks[later][:, k + 1 : k + 2]
            change = one * left + two * right
            if later == b:
                change = jnp.where(sub > r + 1, change, 0.0)
            blocks[later] = blocks[later] - change
        ratio = mixed * (1.0 / first)
        done[b] = jnp.where(sub == r, row * lax.rsqrt(first), done[b])
        rest = (next_row - ratio * row) * lax.rsqrt(last - ratio * mixed)
        done[b] = jnp.where(sub == r + 1, rest, done[b])
    done = jnp.concatenate(done, axis=0)
    return done[:, :size] * (across_squared * across), done[:, size:] * across


def project(cross, own, scale):
    fields = own[0].shape[0]
    first = cross[:, :fields] * scale
    first_parts = split(first)
    first_low = first_parts[0]
    second = first - dots((first_low,), own)
    second_low = second.astype(jnp.bfloat16)
    used = (first_low, second_low)
    square = cross[:, fields:] * scale - dots(used, first_parts, NT)
    rest = second - dots((second_low,), own)
    square = square - dots(split(rest), used, NT)
    return used, first + second, rest, square


def unpacked(upper, columns, fields):
    rows, at = [], 0
    for b in range(0, fields, columns):
        rows.append((b, upper[:, at : at + fields - b]))
        at += fields - b
    whole = []
    for b, row in rows:
        left = [above[:, b - a : b - a + columns].T for a, above in rows if a < b]
        whole.append(jnp.concatenate(left + [row], axis=1))
    return jnp.concatenate(whole, axis=0)


def first_solve_kernel(scale, cross, stack, image, block, proj, low, rest, square, inverse):
    columns = image.shape[0]
    fields = stack.shape[0]
    gram = unpacked(cross[:, fields + columns :] * scale, columns, fields)
    used, proj[...], rest[...], square_here = project(
        cross[:, : fields + columns], split(gram), scale
    )
    square[...] = square_here
    w = image[...].astype(jnp.float32) - dots(used, (stack[...],))
    block[...] = w.astype(jnp.bfloat16)
    upper, inverse_here = factor(square_here)
    low[...] = upper.T
    inverse_here = inverse_here.astype(jnp.bfloat16)
    inverse[...] = inverse_here
    block[...] = dot(inverse_here, block[...]).astype(jnp.bfloat16)


def next_gram_kernel(scale, cross, rest, square, inverse, high, low):
    columns = square.shape[0]
    fields = rest.shape[1]
    kept = fields - columns
    gram = unpacked(cross[:, fields + columns :] * scale, columns, fields)
    mixed = dots((inverse[...],), split(rest[:, columns:]))
    corner = dots((inverse[...],), split(square[...]))
    corner = dots(split(corner), (inverse[...],), NT)
    for part, (old, side, end) in zip(
        (high, low), zip(split(gram[columns:, columns:]), split(mixed), split(corner))
    ):
        part[:kept, :kept] = old
        part[kept:, :kept] = side
        part[:kept, kept:] = side.T
        part[kept:, kept:] = end


def second_solve_kernel(
    scale, cross, own_high, own_low, stack, last, image, proj_in, low_in, block, proj, low
):
    columns = image.shape[0]
    kept = stack.shape[0] - columns
    used, proj[1], _, square = project(cross[...], (own_high[...], own_low[...]), scale)
    proj[0] = proj_in[...]
    low[0] = low_in[...]
    w = image[...].astype(jnp.float32)
    w = w - dots([part[:, :kept] for part in used], (stack[columns:],))
    w = w - dots([part[:, kept:] for part in used], (last[...],))
    block[...] = w.astype(jnp.bfloat16)
    upper, inverse = factor(square)
    low[1] = upper.T
    block[...] = dot(inverse.astype(jnp.bfloat16), block[...]).astype(jnp.bfloat16)


def partner(part, mask):
    axes = ("slab", "col")
    count = lax.axis_size("slab") * lax.axis_size("col")
    return lax.ppermute(part, axes, [(i, i ^ mask) for i in range(count)])


def whole_sum(part):
    cols = lax.axis_size("col")
    count = lax.axis_size("slab") * cols
    index = lax.axis_index("slab") * cols + lax.axis_index("col")
    bit, upper = 1, 0
    while bit < count:
        upper = upper ^ (index // bit % 2)
        bit *= 2
    upper = upper == 1
    half = part.shape[0] // 2
    low, high = part[:half], part[half:]
    part = jnp.where(upper, high, low) + partner(jnp.where(upper, low, high), 1)
    bit = 2
    while bit < count:
        if 2 * bit < count:
            one, two, both = (partner(part, mask) for mask in (bit + 1, 2 * bit + 1, 3 * bit))
            part = (part + one) + (two + both)
        else:
            part = part + partner(part, bit + 1)
        bit *= 4
    other = partner(part, 1)
    return jnp.concatenate([jnp.where(upper, other, part), jnp.where(upper, part, other)], axis=0)


def call(kernel, name, outs, *args):
    return pl.pallas_call(
        kernel,
        out_shape=[jax.ShapeDtypeStruct(shape, dtype) for shape, dtype in outs],
        in_specs=[pl.BlockSpec(memory_space=pltpu.VMEM)] * len(args),
        out_specs=[pl.BlockSpec(memory_space=pltpu.VMEM)] * len(outs),
        compiler_params=pltpu.CompilerParams(vmem_limit_bytes=24 * 1024 * 1024),
        name=name,
    )(*args)


def shards(basis, cell_map, table):
    span_x, span_y, depth = cell_map.shape
    blocks, columns = basis.shape[:2]
    cells = span_x * span_y * depth
    fields = blocks * columns
    scale = 1.0 / (cells * lax.axis_size("slab") * lax.axis_size("col"))
    spans = (span_x, span_y, depth)
    f32, bf16 = jnp.float32, jnp.bfloat16

    stack = basis.reshape(fields, cells)
    coef = coefficients(table, cell_map)
    around = neighbours(stack[fields - columns :], *spans)
    packed = fields + columns + columns * blocks * (blocks + 1) // 2
    image, cross = call(
        functools.partial(first_image_kernel, spans),
        "first_image",
        [((columns, cells), bf16), ((columns, packed), f32)],
        coef, stack, *around,
    )
    cross = whole_sum(cross)
    block, proj, low, rest, square, inverse = call(
        functools.partial(first_solve_kernel, scale),
        "first_solve",
        [((columns, cells), bf16), ((columns, fields), f32), ((columns, columns), f32),
         ((columns, fields), f32), ((columns, columns), f32), ((columns, columns), bf16)],
        cross, stack, image,
    )
    own = call(
        functools.partial(next_gram_kernel, scale),
        "next_gram",
        [((fields, fields), bf16)] * 2,
        cross, rest, square, inverse,
    )
    around = neighbours(block, *spans)
    image, cross = call(
        functools.partial(second_image_kernel, spans),
        "second_image",
        [((columns, cells), bf16), ((columns, fields + columns), f32)],
        coef, stack, block, *around,
    )
    block, proj, low = call(
        functools.partial(second_solve_kernel, scale),
        "second_solve",
        [((columns, cells), bf16), ((2, columns, fields), f32), ((2, columns, columns), f32)],
        whole_sum(cross), *own, stack, block, image, proj, low,
    )
    return block.reshape(columns, *spans), jnp.swapaxes(proj, 1, 2), low


def solution(mesh):
    placed = (P(None, None, "slab", "col", None), P("slab", "col", None), P())
    return jax.shard_map(
        shards,
        mesh=mesh,
        in_specs=placed,
        out_specs=(P(None, "slab", "col", None), P(), P()),
        check_vma=False,
    )
```

```python
import functools

import jax
import jax.numpy as jnp
from jax import lax
from jax.experimental import pallas as pl
from jax.experimental.pallas import tpu as pltpu
from jax.sharding import PartitionSpec as P

NN = (((1,), (0,)), ((), ()))
NT = (((1,), (1,)), ((), ()))
ROWS = 16


def dot(left, right, dims=NN):
    return lax.dot_general(left, right, dims, preferred_element_type=jnp.float32)


def neighbours(block, span_x, span_y, depth, meanwhile=()):
    plane = span_y * depth

    def exchange(axis, upward, downward):
        count = lax.axis_size(axis)
        odd = lax.axis_index(axis) % 2 == 1
        pairs = [[(i, i + 1) for i in range(first, count - 1, 2)] for first in (0, 1)]
        swaps = [pair + [(b, a) for a, b in pair] for pair in pairs]
        inner = lax.ppermute(jnp.where(odd, downward, upward), axis, swaps[0])
        outer = lax.ppermute(jnp.where(odd, upward, downward), axis, swaps[1])
        return jnp.where(odd, inner, outer), jnp.where(odd, outer, inner)

    xlo, xhi = exchange("slab", block[:, (span_x - 1) * plane :], block[:, :plane])

    xlo, xhi, meanwhile = lax.optimization_barrier((xlo, xhi, meanwhile))

    def edge(row):
        at = row * depth
        parts = [xlo[:, at : at + depth]]
        parts += [block[:, x * plane + at : x * plane + at + depth] for x in range(span_x)]
        parts += [xhi[:, at : at + depth]]
        return jnp.concatenate(parts, axis=1)

    ylo, yhi = exchange("col", edge(span_y - 1), edge(0))
    return (xlo, xhi, ylo, yhi), meanwhile


def coefficients_kernel(table, cells, coef):
    classes = table.shape[0]
    lanes = lax.broadcasted_iota(jnp.int32, cells.shape, 1)
    depth = cells.shape[1]
    here = cells[...]
    below = pltpu.roll(here, depth - 1, 1)
    above = pltpu.roll(here, 1, 1)
    maps = (below, here, above)
    keep = (lanes < depth - 1, None, lanes > 0)
    for dz in range(3):
        masks = [maps[dz] == k for k in range(1, classes)]
        for pair in range(9):
            offset = 3 * pair + dz
            value = jnp.full(cells.shape, table[0, offset], jnp.float32)
            for k in range(1, classes):
                value = jnp.where(masks[k - 1], table[k, offset], value)
            if keep[dz] is not None:
                value = jnp.where(keep[dz], value, 0.0)
            coef[offset] = value


def coefficients(table, cell_map):
    span_x, span_y, depth = cell_map.shape
    lines = span_x * span_y
    return pl.pallas_call(
        coefficients_kernel,
        out_shape=jax.ShapeDtypeStruct((27, lines, depth), jnp.float32),
        in_specs=[
            pl.BlockSpec(memory_space=pltpu.SMEM),
            pl.BlockSpec(memory_space=pltpu.VMEM),
        ],
        out_specs=pl.BlockSpec(memory_space=pltpu.VMEM),
        compiler_params=pltpu.CompilerParams(vmem_limit_bytes=4 * 1024 * 1024),
        name="coefficients",
    )(table, cell_map.reshape(lines, depth))


def stencil_into(image, coef, block, xlo, xhi, ylo, yhi, span_x, span_y, depth):
    columns = block.shape[0]

    def tile(step, carry):
        rows = pl.ds(pl.multiple_of(step * ROWS, ROWS), ROWS)

        def line(x, y):
            if y < 0:
                ref, at = ylo, x + 1
            elif y >= span_y:
                ref, at = yhi, x + 1
            elif x < 0:
                ref, at = xlo, y
            elif x >= span_x:
                ref, at = xhi, y
            else:
                ref, at = block, x * span_y + y
            return ref[rows, at * depth : (at + 1) * depth].astype(jnp.float32)

        held = {y: [line(x, y) for x in range(-1, span_x + 1)] for y in (-1, 0)}
        for y in range(span_y):
            held[y + 1] = [line(x, y + 1) for x in range(-1, span_x + 1)]
            for x in range(span_x):
                at = x * span_y + y
                sums = [None, None, None]
                for dx in range(3):
                    for dy in range(3):
                        field = held[y + dy - 1][x + dx]
                        for dz in range(3):
                            term = coef[9 * dx + 3 * dy + dz, at : at + 1, :] * field
                            sums[dz] = term if sums[dz] is None else sums[dz] + term
                total = sums[1] + pltpu.roll(sums[0], 1, 1) + pltpu.roll(sums[2], depth - 1, 1)
                image[rows, at * depth : (at + 1) * depth] = total.astype(jnp.bfloat16)
            del held[y - 1]
        return carry

    lax.fori_loop(0, columns // ROWS, tile, 0)


def stack_gram_kernel(columns, stack, own):
    at = 0
    for b in range(0, stack.shape[0], columns):
        width = stack.shape[0] - b
        own[:, at : at + width] = dot(stack[b : b + columns], stack[b:], NT)
        at += width


def first_image_kernel(spans, coef, stack, own, xlo, xhi, ylo, yhi, image, cross):
    columns = image.shape[0]
    fields = stack.shape[0]
    block = stack.at[fields - columns : fields]
    stencil_into(image, coef, block, xlo, xhi, ylo, yhi, *spans)
    w = image[...]
    cross[:, :fields] = dot(w, stack[...], NT)
    cross[:, fields : fields + columns] = dot(w, w, NT)
    cross[:, fields + columns :] = own[...]


def second_image_kernel(spans, coef, stack, block, xlo, xhi, ylo, yhi, image, cross):
    columns = image.shape[0]
    fields = stack.shape[0]
    stencil_into(image, coef, block, xlo, xhi, ylo, yhi, *spans)
    w = image[...]
    cross[:, : fields - columns] = dot(w, stack[columns:], NT)
    cross[:, fields - columns : fields] = dot(w, block[...], NT)
    cross[:, fields:] = dot(w, w, NT)


def split(values):
    high = values.astype(jnp.bfloat16)
    return high, (values - high.astype(jnp.float32)).astype(jnp.bfloat16)


def dots(lefts, rights, dims=NN):
    return sum(dot(left, right, dims) for left in lefts for right in rights)


def factor(square):
    size = square.shape[0]
    shape = (8, 2 * size)
    sub = lax.broadcasted_iota(jnp.int32, shape, 0)
    unit = lax.broadcasted_iota(jnp.int32, (size, size), 0) == lax.broadcasted_iota(
        jnp.int32, (size, size), 1
    )
    whole = jnp.concatenate([square, unit.astype(jnp.float32)], axis=1)
    blocks = [whole[b : b + 8] for b in range(0, size, 8)]
    done = []

    def row_of(values, at):
        return jnp.broadcast_to(values[at : at + 1, :], shape)

    def column_of(values, at):
        return jnp.broadcast_to(values[:, at : at + 1], shape)

    for b, here in enumerate(blocks):
        columns = [column_of(here, 8 * b + j) for j in range(8)]
        entry = {(i, j): row_of(columns[j], i) for j in range(8) for i in range(j + 1)}
        rows = [row_of(here, i) for i in range(8)]
        inverse, ratio = [], {}
        for r in range(8):
            inverse.append(1.0 / entry[r, r])
            for j in range(r + 1, 8):
                ratio[r, j] = entry[r, j] * inverse[r]
            for i in range(r + 1, 8):
                for j in range(i, 8):
                    entry[i, j] = entry[i, j] - entry[r, i] * ratio[r, j]
                rows[i] = rows[i] - ratio[r, i] * rows[r]
        solved = {}
        for r in reversed(range(8)):
            solved[r] = rows[r] * inverse[r]
            for j in range(r + 1, 8):
                solved[r] = solved[r] - ratio[r, j] * solved[j]
        for later in range(b + 1, len(blocks)):
            for j in range(8):
                change = column_of(blocks[later], 8 * b + j) * solved[j]
                total = change if j == 0 else total + change
            blocks[later] = blocks[later] - total
        scaled = jnp.zeros(shape, jnp.float32)
        for r in range(8):
            scaled = jnp.where(sub == r, rows[r] * lax.rsqrt(entry[r, r]), scaled)
        done.append(scaled)
    done = jnp.concatenate(done, axis=0)
    return done[:, :size], done[:, size:]


def project(cross, own, scale):
    fields = own[0].shape[0]
    first = cross[:, :fields] * scale
    first_parts = split(first)
    first_low = first_parts[0]
    second = first - dots((first_low,), own)
    second_low = second.astype(jnp.bfloat16)
    used = (first_low, second_low)
    square = cross[:, fields:] * scale - dots(used, first_parts, NT)
    rest = second - dots((second_low,), own)
    square = square - dots(split(rest), used, NT)
    return used, first + second, rest, square


def unpacked(upper, columns, fields):
    rows, at = [], 0
    for b in range(0, fields, columns):
        rows.append((b, upper[:, at : at + fields - b]))
        at += fields - b
    whole = []
    for b, row in rows:
        left = [above[:, b - a : b - a + columns].T for a, above in rows if a < b]
        whole.append(jnp.concatenate(left + [row], axis=1))
    return jnp.concatenate(whole, axis=0)


def first_solve_kernel(scale, cross, stack, image, block, proj, low, rest, square, inverse):
    columns = image.shape[0]
    fields = stack.shape[0]
    gram = unpacked(cross[:, fields + columns :] * scale, columns, fields)
    used, proj[...], rest[...], square_here = project(
        cross[:, : fields + columns], split(gram), scale
    )
    square[...] = square_here
    w = image[...].astype(jnp.float32) - dots(used, (stack[...],))
    block[...] = w.astype(jnp.bfloat16)
    upper, inverse_here = factor(square_here)
    low[...] = upper.T
    inverse_here = inverse_here.astype(jnp.bfloat16)
    inverse[...] = inverse_here
    block[...] = dot(inverse_here, block[...]).astype(jnp.bfloat16)


def next_gram_kernel(scale, cross, rest, square, inverse, high, low):
    columns = square.shape[0]
    fields = rest.shape[1]
    kept = fields - columns
    gram = unpacked(cross[:, fields + columns :] * scale, columns, fields)
    mixed = dots((inverse[...],), split(rest[:, columns:]))
    corner = dots((inverse[...],), split(square[...]))
    corner = dots(split(corner), (inverse[...],), NT)
    for part, (old, side, end) in zip(
        (high, low), zip(split(gram[columns:, columns:]), split(mixed), split(corner))
    ):
        part[:kept, :kept] = old
        part[kept:, :kept] = side
        part[:kept, kept:] = side.T
        part[kept:, kept:] = end


def second_solve_kernel(
    scale, cross, own_high, own_low, stack, last, image, proj_in, low_in, block, proj, low
):
    columns = image.shape[0]
    kept = stack.shape[0] - columns
    used, proj[1], _, square = project(cross[...], (own_high[...], own_low[...]), scale)
    proj[0] = proj_in[...]
    low[0] = low_in[...]
    w = image[...].astype(jnp.float32)
    w = w - dots([part[:, :kept] for part in used], (stack[columns:],))
    w = w - dots([part[:, kept:] for part in used], (last[...],))
    block[...] = w.astype(jnp.bfloat16)
    upper, inverse = factor(square)
    low[1] = upper.T
    block[...] = dot(inverse.astype(jnp.bfloat16), block[...]).astype(jnp.bfloat16)


def partner(part, mask):
    axes = ("slab", "col")
    count = lax.axis_size("slab") * lax.axis_size("col")
    return lax.ppermute(part, axes, [(i, i ^ mask) for i in range(count)])


def whole_sum(part):
    cols = lax.axis_size("col")
    count = lax.axis_size("slab") * cols
    index = lax.axis_index("slab") * cols + lax.axis_index("col")
    bit, upper = 1, 0
    while bit < count:
        upper = upper ^ (index // bit % 2)
        bit *= 2
    upper = upper == 1
    half = part.shape[0] // 2
    low, high = part[:half], part[half:]
    part = jnp.where(upper, high, low) + partner(jnp.where(upper, low, high), 1)
    bit = 2
    while bit < count:
        part = part + partner(part, bit + 1)
        bit *= 2
    other = partner(part, 1)
    return jnp.concatenate([jnp.where(upper, other, part), jnp.where(upper, part, other)], axis=0)


def call(kernel, name, outs, *args):
    return pl.pallas_call(
        kernel,
        out_shape=[jax.ShapeDtypeStruct(shape, dtype) for shape, dtype in outs],
        in_specs=[pl.BlockSpec(memory_space=pltpu.VMEM)] * len(args),
        out_specs=[pl.BlockSpec(memory_space=pltpu.VMEM)] * len(outs),
        compiler_params=pltpu.CompilerParams(vmem_limit_bytes=24 * 1024 * 1024),
        name=name,
    )(*args)


def shards(basis, cell_map, table):
    span_x, span_y, depth = cell_map.shape
    blocks, columns = basis.shape[:2]
    cells = span_x * span_y * depth
    fields = blocks * columns
    scale = 1.0 / (cells * lax.axis_size("slab") * lax.axis_size("col"))
    spans = (span_x, span_y, depth)
    f32, bf16 = jnp.float32, jnp.bfloat16

    stack = basis.reshape(fields, cells)
    coef = coefficients(table, cell_map)
    (own,) = call(
        functools.partial(stack_gram_kernel, columns),
        "stack_gram",
        [((columns, columns * blocks * (blocks + 1) // 2), f32)],
        stack,
    )
    around, (coef, stack, own) = neighbours(
        basis[blocks - 1].reshape(columns, cells), *spans, (coef, stack, own)
    )
    packed = fields + columns + own.shape[1]
    image, cross = call(
        functools.partial(first_image_kernel, spans),
        "first_image",
        [((columns, cells), bf16), ((columns, packed), f32)],
        coef, stack, own, *around,
    )
    cross = whole_sum(cross)
    block, proj, low, rest, square, inverse = call(
        functools.partial(first_solve_kernel, scale),
        "first_solve",
        [((columns, cells), bf16), ((columns, fields), f32), ((columns, columns), f32),
         ((columns, fields), f32), ((columns, columns), f32), ((columns, columns), bf16)],
        cross, stack, image,
    )
    own = call(
        functools.partial(next_gram_kernel, scale),
        "next_gram",
        [((fields, fields), bf16)] * 2,
        cross, rest, square, inverse,
    )
    around, _ = neighbours(block, *spans)
    image, cross = call(
        functools.partial(second_image_kernel, spans),
        "second_image",
        [((columns, cells), bf16), ((columns, fields + columns), f32)],
        coef, stack, block, *around,
    )
    block, proj, low = call(
        functools.partial(second_solve_kernel, scale),
        "second_solve",
        [((columns, cells), bf16), ((2, columns, fields), f32), ((2, columns, columns), f32)],
        whole_sum(cross), *own, stack, block, image, proj, low,
    )
    return block.reshape(columns, *spans), jnp.swapaxes(proj, 1, 2), low


def solution(mesh):
    placed = (P(None, None, "slab", "col", None), P("slab", "col", None), P())
    return jax.shard_map(
        shards,
        mesh=mesh,
        in_specs=placed,
        out_specs=(P(None, "slab", "col", None), P(), P()),
        check_vma=False,
    )
```

```python
import functools

import jax
import jax.numpy as jnp
from jax import lax
from jax.experimental import pallas as pl
from jax.experimental.pallas import tpu as pltpu
from jax.sharding import PartitionSpec as P

NN = (((1,), (0,)), ((), ()))
NT = (((1,), (1,)), ((), ()))
ROWS = 16


def dot(left, right, dims=NN):
    return lax.dot_general(left, right, dims, preferred_element_type=jnp.float32)


def neighbours(block, span_x, span_y, depth, meanwhile=()):
    plane = span_y * depth

    def exchange(axis, upward, downward, closed):
        count = lax.axis_size(axis)
        me = lax.axis_index(axis)
        odd = me % 2 == 1
        pairs = [(i, (i - 1 ^ 1) + 1) for i in range(1, count - 1)]
        if closed:
            pairs += [(0, count - 1), (count - 1, 0)]
        outer = lax.ppermute(jnp.where(odd, upward, downward), axis, pairs)
        inner = lax.ppermute(
            jnp.where(odd, downward, upward), axis, [(i, i ^ 1) for i in range(count)]
        )
        if closed:
            outer = jnp.where((me == 0) | (me == count - 1), 0, outer)
        return jnp.where(odd, inner, outer), jnp.where(odd, outer, inner)

    xlo, xhi = exchange("slab", block[:, (span_x - 1) * plane :], block[:, :plane], False)

    xlo, xhi, meanwhile = lax.optimization_barrier((xlo, xhi, meanwhile))

    def edge(row):
        at = row * depth
        parts = [xlo[:, at : at + depth]]
        parts += [block[:, x * plane + at : x * plane + at + depth] for x in range(span_x)]
        parts += [xhi[:, at : at + depth]]
        return jnp.concatenate(parts, axis=1)

    ylo, yhi = exchange("col", edge(span_y - 1), edge(0), True)
    return (xlo, xhi, ylo, yhi), meanwhile


def coefficients_kernel(table, cells, coef):
    classes = table.shape[0]
    lanes = lax.broadcasted_iota(jnp.int32, cells.shape, 1)
    depth = cells.shape[1]
    here = cells[...]
    below = pltpu.roll(here, depth - 1, 1)
    above = pltpu.roll(here, 1, 1)
    maps = (below, here, above)
    keep = (lanes < depth - 1, None, lanes > 0)
    for dz in range(3):
        masks = [maps[dz] == k for k in range(1, classes)]
        for pair in range(9):
            offset = 3 * pair + dz
            value = jnp.full(cells.shape, table[0, offset], jnp.float32)
            for k in range(1, classes):
                value = jnp.where(masks[k - 1], table[k, offset], value)
            if keep[dz] is not None:
                value = jnp.where(keep[dz], value, 0.0)
            coef[offset] = value


def coefficients(table, cell_map):
    span_x, span_y, depth = cell_map.shape
    lines = span_x * span_y
    return pl.pallas_call(
        coefficients_kernel,
        out_shape=jax.ShapeDtypeStruct((27, lines, depth), jnp.float32),
        in_specs=[
            pl.BlockSpec(memory_space=pltpu.SMEM),
            pl.BlockSpec(memory_space=pltpu.VMEM),
        ],
        out_specs=pl.BlockSpec(memory_space=pltpu.VMEM),
        compiler_params=pltpu.CompilerParams(vmem_limit_bytes=4 * 1024 * 1024),
        name="coefficients",
    )(table, cell_map.reshape(lines, depth))


def stencil(coef, spans, columns, line, inner, write):
    span_x, span_y, depth = spans

    def tile(step, carry):
        rows = pl.ds(pl.multiple_of(step * ROWS, ROWS), ROWS)
        held = {}
        for y in range(span_y):
            for x in range(span_x):
                sums = [None, None, None]
                for pair in range(9):
                    x_there, y_there = x + pair // 3 - 1, y + pair % 3 - 1
                    inside = 0 <= x_there < span_x and 0 <= y_there < span_y
                    if inside != inner:
                        continue
                    if (x_there, y_there) not in held:
                        held[x_there, y_there] = line(rows, x_there, y_there)
                    for dz in range(3):
                        at = x * span_y + y
                        term = coef[3 * pair + dz, at : at + 1, :] * held[x_there, y_there]
                        sums[dz] = term if sums[dz] is None else sums[dz] + term
                total = None
                if sums[0] is not None:
                    total = pltpu.roll(sums[0], 1, 1) + pltpu.roll(sums[2], depth - 1, 1)
                    total = sums[1] + total
                write(rows, x, y, total)
        return carry

    lax.fori_loop(0, columns // ROWS, tile, 0)


def inner_image_kernel(spans, coef, fields, partial):
    _, span_y, depth = spans
    columns = partial.shape[0]
    block = fields.at[fields.shape[0] - columns :]

    def here(x, y):
        return pl.ds((x * span_y + y) * depth, depth)

    def write(rows, x, y, total):
        partial[rows, here(x, y)] = total

    def line(rows, x, y):
        return block[rows, here(x, y)].astype(jnp.float32)

    stencil(coef, spans, columns, line, True, write)


def complete(image, partial, coef, spans, xlo, xhi, ylo, yhi):
    span_x, span_y, depth = spans

    def line(rows, x, y):
        if y < 0:
            ref, at = ylo, x + 1
        elif y >= span_y:
            ref, at = yhi, x + 1
        else:
            ref, at = (xlo, y) if x < 0 else (xhi, y)
        return ref[rows, at * depth : (at + 1) * depth].astype(jnp.float32)

    def write(rows, x, y, total):
        there = pl.ds((x * span_y + y) * depth, depth)
        known = partial[rows, there]
        image[rows, there] = (known if total is None else known + total).astype(jnp.bfloat16)

    stencil(coef, spans, image.shape[0], line, False, write)


def stack_gram_kernel(columns, stack, own):
    at = 0
    for b in range(0, stack.shape[0], columns):
        width = stack.shape[0] - b
        own[:, at : at + width] = dot(stack[b : b + columns], stack[b:], NT)
        at += width


def first_image_kernel(spans, coef, stack, own, partial, xlo, xhi, ylo, yhi, image, cross):
    columns = image.shape[0]
    fields = stack.shape[0]
    complete(image, partial, coef, spans, xlo, xhi, ylo, yhi)
    w = image[...]
    cross[:, :fields] = dot(w, stack[...], NT)
    cross[:, fields : fields + columns] = dot(w, w, NT)
    cross[:, fields + columns :] = own[...]


def second_image_kernel(spans, coef, stack, block, partial, xlo, xhi, ylo, yhi, image, cross):
    columns = image.shape[0]
    fields = stack.shape[0]
    complete(image, partial, coef, spans, xlo, xhi, ylo, yhi)
    w = image[...]
    cross[:, : fields - columns] = dot(w, stack[columns:], NT)
    cross[:, fields - columns : fields] = dot(w, block[...], NT)
    cross[:, fields:] = dot(w, w, NT)


def split(values):
    high = values.astype(jnp.bfloat16)
    return high, (values - high.astype(jnp.float32)).astype(jnp.bfloat16)


def dots(lefts, rights, dims=NN):
    return sum(dot(left, right, dims) for left in lefts for right in rights)


def factor(square):
    size = square.shape[0]
    shape = (8, 2 * size)
    sub = lax.broadcasted_iota(jnp.int32, shape, 0)
    unit = lax.broadcasted_iota(jnp.int32, (size, size), 0) == lax.broadcasted_iota(
        jnp.int32, (size, size), 1
    )
    whole = jnp.concatenate([square, unit.astype(jnp.float32)], axis=1)
    blocks = [whole[b : b + 8] for b in range(0, size, 8)]
    done = []

    def row_of(values, at):
        return jnp.broadcast_to(values[at : at + 1, :], shape)

    def column_of(values, at):
        return jnp.broadcast_to(values[:, at : at + 1], shape)

    for b, here in enumerate(blocks):
        columns = [column_of(here, 8 * b + j) for j in range(8)]
        entry = {(i, j): row_of(columns[j], i) for j in range(8) for i in range(j + 1)}
        rows = [row_of(here, i) for i in range(8)]
        inverse, ratio = [], {}
        for r in range(8):
            inverse.append(1.0 / entry[r, r])
            for j in range(r + 1, 8):
                ratio[r, j] = entry[r, j] * inverse[r]
            for i in range(r + 1, 8):
                for j in range(i, 8):
                    entry[i, j] = entry[i, j] - entry[r, i] * ratio[r, j]
                rows[i] = rows[i] - ratio[r, i] * rows[r]
        solved = {}
        for r in reversed(range(8)):
            solved[r] = rows[r] * inverse[r]
            for j in range(r + 1, 8):
                solved[r] = solved[r] - ratio[r, j] * solved[j]
        for later in range(b + 1, len(blocks)):
            for j in range(8):
                change = column_of(blocks[later], 8 * b + j) * solved[j]
                total = change if j == 0 else total + change
            blocks[later] = blocks[later] - total
        scaled = jnp.zeros(shape, jnp.float32)
        for r in range(8):
            scaled = jnp.where(sub == r, rows[r] * lax.rsqrt(entry[r, r]), scaled)
        done.append(scaled)
    done = jnp.concatenate(done, axis=0)
    return done[:, :size], done[:, size:]


def project(cross, own, scale):
    fields = own[0].shape[0]
    first = cross[:, :fields] * scale
    first_parts = split(first)
    first_low = first_parts[0]
    second = first - dots((first_low,), own)
    second_low = second.astype(jnp.bfloat16)
    used = (first_low, second_low)
    square = cross[:, fields:] * scale - dots(used, first_parts, NT)
    rest = second - dots((second_low,), own)
    square = square - dots(split(rest), used, NT)
    return used, first + second, rest, square


def unpacked(upper, columns, fields):
    rows, at = [], 0
    for b in range(0, fields, columns):
        rows.append((b, upper[:, at : at + fields - b]))
        at += fields - b
    whole = []
    for b, row in rows:
        left = [above[:, b - a : b - a + columns].T for a, above in rows if a < b]
        whole.append(jnp.concatenate(left + [row], axis=1))
    return jnp.concatenate(whole, axis=0)


def first_solve_kernel(scale, cross, stack, image, block, proj, low, rest, square, inverse):
    columns = image.shape[0]
    fields = stack.shape[0]
    gram = unpacked(cross[:, fields + columns :] * scale, columns, fields)
    used, proj[...], rest[...], square_here = project(
        cross[:, : fields + columns], split(gram), scale
    )
    square[...] = square_here
    moved = dot(jnp.concatenate(used, axis=0), stack[...])
    w = image[...].astype(jnp.float32) - moved[:columns] - moved[columns:]
    block[...] = w.astype(jnp.bfloat16)
    upper, inverse_here = factor(square_here)
    low[...] = upper.T
    inverse_here = inverse_here.astype(jnp.bfloat16)
    inverse[...] = inverse_here
    block[...] = dot(inverse_here, block[...]).astype(jnp.bfloat16)


def next_gram_kernel(scale, cross, rest, square, inverse, high, low):
    columns = square.shape[0]
    fields = rest.shape[1]
    kept = fields - columns
    gram = unpacked(cross[:, fields + columns :] * scale, columns, fields)
    mixed = dots((inverse[...],), split(rest[:, columns:]))
    corner = dots((inverse[...],), split(square[...]))
    corner = dots(split(corner), (inverse[...],), NT)
    for part, (old, side, end) in zip(
        (high, low), zip(split(gram[columns:, columns:]), split(mixed), split(corner))
    ):
        part[:kept, :kept] = old
        part[kept:, :kept] = side
        part[:kept, kept:] = side.T
        part[kept:, kept:] = end


def second_solve_kernel(
    scale, cross, own_high, own_low, stack, last, image, proj_in, low_in, block, proj, low
):
    columns = image.shape[0]
    kept = stack.shape[0] - columns
    used, proj[1], _, square = project(cross[...], (own_high[...], own_low[...]), scale)
    proj[0] = proj_in[...]
    low[0] = low_in[...]
    both = jnp.concatenate(used, axis=0)
    moved = dot(both[:, :kept], stack[columns:]) + dot(both[:, kept:], last[...])
    w = image[...].astype(jnp.float32) - moved[:columns] - moved[columns:]
    block[...] = w.astype(jnp.bfloat16)
    upper, inverse = factor(square)
    low[1] = upper.T
    block[...] = dot(inverse.astype(jnp.bfloat16), block[...]).astype(jnp.bfloat16)


def partner(part, mask):
    axes = ("slab", "col")
    count = lax.axis_size("slab") * lax.axis_size("col")
    return lax.ppermute(part, axes, [(i, i ^ mask) for i in range(count)])


def whole_sum(part):
    cols = lax.axis_size("col")
    count = lax.axis_size("slab") * cols
    index = lax.axis_index("slab") * cols + lax.axis_index("col")
    bit, upper = 1, 0
    while bit < count:
        upper = upper ^ (index // bit % 2)
        bit *= 2
    upper = upper == 1
    half = part.shape[0] // 2
    low, high = part[:half], part[half:]
    part = jnp.where(upper, high, low) + partner(jnp.where(upper, low, high), 1)
    bit = 2
    while bit < count:
        if 2 * bit < count:
            one, two, both = (partner(part, mask) for mask in (bit + 1, 2 * bit + 1, 3 * bit))
            part = (part + one) + (two + both)
        else:
            part = part + partner(part, bit + 1)
        bit *= 4
    other = partner(part, 1)
    return jnp.concatenate([jnp.where(upper, other, part), jnp.where(upper, part, other)], axis=0)


def call(kernel, name, outs, *args):
    return pl.pallas_call(
        kernel,
        out_shape=[jax.ShapeDtypeStruct(shape, dtype) for shape, dtype in outs],
        in_specs=[pl.BlockSpec(memory_space=pltpu.VMEM)] * len(args),
        out_specs=[pl.BlockSpec(memory_space=pltpu.VMEM)] * len(outs),
        compiler_params=pltpu.CompilerParams(vmem_limit_bytes=24 * 1024 * 1024),
        name=name,
    )(*args)


def shards(basis, cell_map, table):
    span_x, span_y, depth = cell_map.shape
    blocks, columns = basis.shape[:2]
    cells = span_x * span_y * depth
    fields = blocks * columns
    scale = 1.0 / (cells * lax.axis_size("slab") * lax.axis_size("col"))
    spans = (span_x, span_y, depth)
    f32, bf16 = jnp.float32, jnp.bfloat16

    stack = basis.reshape(fields, cells)
    coef = coefficients(table, cell_map)
    (own,) = call(
        functools.partial(stack_gram_kernel, columns),
        "stack_gram",
        [((columns, columns * blocks * (blocks + 1) // 2), f32)],
        stack,
    )
    inner_image = functools.partial(
        call,
        functools.partial(inner_image_kernel, spans),
        "inner_image",
        [((columns, cells), f32)],
        coef,
    )
    around, (coef, stack, own, partial) = neighbours(
        basis[blocks - 1].reshape(columns, cells), *spans, (coef, stack, own, *inner_image(stack))
    )
    packed = fields + columns + own.shape[1]
    image, cross = call(
        functools.partial(first_image_kernel, spans),
        "first_image",
        [((columns, cells), bf16), ((columns, packed), f32)],
        coef, stack, own, partial, *around,
    )
    cross = whole_sum(cross)
    block, proj, low, rest, square, inverse = call(
        functools.partial(first_solve_kernel, scale),
        "first_solve",
        [((columns, cells), bf16), ((columns, fields), f32), ((columns, columns), f32),
         ((columns, fields), f32), ((columns, columns), f32), ((columns, columns), bf16)],
        cross, stack, image,
    )
    own = call(
        functools.partial(next_gram_kernel, scale),
        "next_gram",
        [((fields, fields), bf16)] * 2,
        cross, rest, square, inverse,
    )
    around, (partial,) = neighbours(block, *spans, tuple(inner_image(block)))
    image, cross = call(
        functools.partial(second_image_kernel, spans),
        "second_image",
        [((columns, cells), bf16), ((columns, fields + columns), f32)],
        coef, stack, block, partial, *around,
    )
    block, proj, low = call(
        functools.partial(second_solve_kernel, scale),
        "second_solve",
        [((columns, cells), bf16), ((2, columns, fields), f32), ((2, columns, columns), f32)],
        whole_sum(cross), *own, stack, block, image, proj, low,
    )
    return block.reshape(columns, *spans), jnp.swapaxes(proj, 1, 2), low


def solution(mesh):
    placed = (P(None, None, "slab", "col", None), P("slab", "col", None), P())
    return jax.shard_map(
        shards,
        mesh=mesh,
        in_specs=placed,
        out_specs=(P(None, "slab", "col", None), P(), P()),
        check_vma=False,
    )
```

```python
import functools
import math

import jax
import jax.numpy as jnp
from jax import lax
from jax.experimental import pallas as pl
from jax.experimental.pallas import tpu as pltpu
from jax.sharding import PartitionSpec as P

NN = (((1,), (0,)), ((), ()))
NT = (((1,), (1,)), ((), ()))
ROWS = 16


def dot(left, right, dims=NN):
    return lax.dot_general(left, right, dims, preferred_element_type=jnp.float32)


def swaps(axis, upward, downward, closed):
    count = lax.axis_size(axis)
    me = lax.axis_index(axis)
    odd = me % 2 == 1
    pairs = [(i, (i - 1 ^ 1) + 1) for i in range(1, count - 1)]
    if closed:
        pairs += [(0, count - 1), (count - 1, 0)]
    inner = lax.ppermute(
        jnp.where(odd, downward, upward), axis, [(i, i ^ 1) for i in range(count)]
    )
    outer = lax.ppermute(jnp.where(odd, upward, downward), axis, pairs)

    def sort(inner, outer):
        if closed:
            outer = jnp.where((me == 0) | (me == count - 1), 0, outer)
        return jnp.where(odd, inner, outer), jnp.where(odd, outer, inner)

    return inner, outer, sort


def neighbours(block, span_x, span_y, depth, inner_image, meanwhile=()):
    plane = span_y * depth
    inner, outer, sort = swaps(
        "slab", block[:, (span_x - 1) * plane :], block[:, :plane], False
    )
    inner, tied = lax.optimization_barrier((inner, block))
    partial = inner_image(tied)
    inner, outer, partial, meanwhile = lax.optimization_barrier((inner, outer, partial, meanwhile))
    xlo, xhi = sort(inner, outer)

    def edge(row):
        at = row * depth
        parts = [xlo[:, at : at + depth]]
        parts += [block[:, x * plane + at : x * plane + at + depth] for x in range(span_x)]
        parts += [xhi[:, at : at + depth]]
        return jnp.concatenate(parts, axis=1)

    inner, outer, sort = swaps("col", edge(span_y - 1), edge(0), True)
    return (xlo, xhi, *sort(inner, outer)), partial, meanwhile


def coefficients_kernel(table, cells, coef):
    classes = table.shape[0]
    lanes = lax.broadcasted_iota(jnp.int32, cells.shape, 1)
    depth = cells.shape[1]
    here = cells[...]
    below = pltpu.roll(here, depth - 1, 1)
    above = pltpu.roll(here, 1, 1)
    maps = (below, here, above)
    keep = (lanes < depth - 1, None, lanes > 0)
    for dz in range(3):
        masks = [maps[dz] == k for k in range(1, classes)]
        for pair in range(9):
            offset = 3 * pair + dz
            value = jnp.full(cells.shape, table[0, offset], jnp.float32)
            for k in range(1, classes):
                value = jnp.where(masks[k - 1], table[k, offset], value)
            if keep[dz] is not None:
                value = jnp.where(keep[dz], value, 0.0)
            coef[offset] = value


def coefficients(table, cell_map):
    span_x, span_y, depth = cell_map.shape
    lines = span_x * span_y
    return pl.pallas_call(
        coefficients_kernel,
        out_shape=jax.ShapeDtypeStruct((27, lines, depth), jnp.float32),
        in_specs=[
            pl.BlockSpec(memory_space=pltpu.SMEM),
            pl.BlockSpec(memory_space=pltpu.VMEM),
        ],
        out_specs=pl.BlockSpec(memory_space=pltpu.VMEM),
        compiler_params=pltpu.CompilerParams(vmem_limit_bytes=4 * 1024 * 1024),
        name="coefficients",
    )(table, cell_map.reshape(lines, depth))


def stencil(coef, spans, columns, line, inner, write):
    span_x, span_y, depth = spans

    def tile(step, carry):
        rows = pl.ds(pl.multiple_of(step * ROWS, ROWS), ROWS)
        held = {}
        for y in range(span_y):
            for x in range(span_x):
                sums = [None, None, None]
                for pair in range(9):
                    x_there, y_there = x + pair // 3 - 1, y + pair % 3 - 1
                    inside = 0 <= x_there < span_x and 0 <= y_there < span_y
                    if inside != inner:
                        continue
                    if (x_there, y_there) not in held:
                        held[x_there, y_there] = line(rows, x_there, y_there)
                    for dz in range(3):
                        at = x * span_y + y
                        term = coef[3 * pair + dz, at : at + 1, :] * held[x_there, y_there]
                        sums[dz] = term if sums[dz] is None else sums[dz] + term
                total = None
                if sums[0] is not None:
                    total = pltpu.roll(sums[0], 1, 1) + pltpu.roll(sums[2], depth - 1, 1)
                    total = sums[1] + total
                write(rows, x, y, total)
        return carry

    lax.fori_loop(0, columns // ROWS, tile, 0)


def inner_image_kernel(spans, coef, fields, partial):
    _, span_y, depth = spans
    columns = partial.shape[0]
    block = fields.at[fields.shape[0] - columns :]

    def here(x, y):
        return pl.ds((x * span_y + y) * depth, depth)

    def write(rows, x, y, total):
        partial[rows, here(x, y)] = total

    def line(rows, x, y):
        return block[rows, here(x, y)].astype(jnp.float32)

    stencil(coef, spans, columns, line, True, write)


def complete(image, partial, coef, spans, xlo, xhi, ylo, yhi):
    span_x, span_y, depth = spans

    def line(rows, x, y):
        if y < 0:
            ref, at = ylo, x + 1
        elif y >= span_y:
            ref, at = yhi, x + 1
        else:
            ref, at = (xlo, y) if x < 0 else (xhi, y)
        return ref[rows, at * depth : (at + 1) * depth].astype(jnp.float32)

    def write(rows, x, y, total):
        there = pl.ds((x * span_y + y) * depth, depth)
        known = partial[rows, there]
        image[rows, there] = (known if total is None else known + total).astype(jnp.bfloat16)

    stencil(coef, spans, image.shape[0], line, False, write)


def stack_gram_kernel(columns, stack, own):
    at = 0
    for b in range(0, stack.shape[0], columns):
        width = stack.shape[0] - b
        own[:, at : at + width] = dot(stack[b : b + columns], stack[b:], NT)
        at += width


def first_image_kernel(spans, coef, stack, own, partial, xlo, xhi, ylo, yhi, image, cross):
    columns = image.shape[0]
    fields = stack.shape[0]
    complete(image, partial, coef, spans, xlo, xhi, ylo, yhi)
    w = image[...]
    cross[:, :fields] = dot(w, stack[...], NT)
    cross[:, fields : fields + columns] = dot(w, w, NT)
    cross[:, fields + columns :] = own[...]


def second_image_kernel(spans, coef, stack, block, partial, xlo, xhi, ylo, yhi, image, cross):
    columns = image.shape[0]
    fields = stack.shape[0]
    complete(image, partial, coef, spans, xlo, xhi, ylo, yhi)
    w = image[...]
    cross[:, : fields - columns] = dot(w, stack[columns:], NT)
    cross[:, fields - columns : fields] = dot(w, block[...], NT)
    cross[:, fields:] = dot(w, w, NT)


def split(values):
    high = values.astype(jnp.bfloat16)
    return high, (values - high.astype(jnp.float32)).astype(jnp.bfloat16)


def dots(lefts, rights, dims=NN):
    return sum(dot(left, right, dims) for left in lefts for right in rights)


def factor(square):
    size = square.shape[0]
    shape = (8, 2 * size)
    sub = lax.broadcasted_iota(jnp.int32, shape, 0)
    unit = lax.broadcasted_iota(jnp.int32, (size, size), 0) == lax.broadcasted_iota(
        jnp.int32, (size, size), 1
    )
    whole = jnp.concatenate([square, unit.astype(jnp.float32)], axis=1)
    blocks = [whole[b : b + 8] for b in range(0, size, 8)]
    done = []

    def row_of(values, at):
        return jnp.broadcast_to(values[at : at + 1, :], shape)

    def column_of(values, at):
        return jnp.broadcast_to(values[:, at : at + 1], shape)

    for b, here in enumerate(blocks):
        columns = [column_of(here, 8 * b + j) for j in range(8)]
        entry = {(i, j): row_of(columns[j], i) for j in range(8) for i in range(j + 1)}
        rows = [row_of(here, i) for i in range(8)]
        inverse, ratio = [], {}
        for r in range(8):
            inverse.append(1.0 / entry[r, r])
            for j in range(r + 1, 8):
                ratio[r, j] = entry[r, j] * inverse[r]
            for i in range(r + 1, 8):
                for j in range(i, 8):
                    entry[i, j] = entry[i, j] - entry[r, i] * ratio[r, j]
                rows[i] = rows[i] - ratio[r, i] * rows[r]
        solved = {}
        for r in reversed(range(8)):
            solved[r] = rows[r] * inverse[r]
            for j in range(r + 1, 8):
                solved[r] = solved[r] - ratio[r, j] * solved[j]
        for later in range(b + 1, len(blocks)):
            for j in range(8):
                change = column_of(blocks[later], 8 * b + j) * solved[j]
                total = change if j == 0 else total + change
            blocks[later] = blocks[later] - total
        scaled = jnp.zeros(shape, jnp.float32)
        for r in range(8):
            scaled = jnp.where(sub == r, rows[r] * lax.rsqrt(entry[r, r]), scaled)
        done.append(scaled)
    done = jnp.concatenate(done, axis=0)
    return done[:, :size], done[:, size:]


def project(cross, own, scale):
    fields = own[0].shape[0]
    first = cross[:, :fields] * scale
    first_parts = split(first)
    first_low = first_parts[0]
    second = first - dots((first_low,), own)
    second_low = second.astype(jnp.bfloat16)
    used = (first_low, second_low)
    square = cross[:, fields:] * scale - dots(used, first_parts, NT)
    rest = second - dots((second_low,), own)
    square = square - dots(split(rest), used, NT)
    return used, first + second, rest, square


def unpacked(upper, columns, fields):
    rows, at = [], 0
    for b in range(0, fields, columns):
        rows.append((b, upper[:, at : at + fields - b]))
        at += fields - b
    whole = []
    for b, row in rows:
        left = [above[:, b - a : b - a + columns].T for a, above in rows if a < b]
        whole.append(jnp.concatenate(left + [row], axis=1))
    return jnp.concatenate(whole, axis=0)


def first_solve_kernel(scale, cross, stack, image, block, proj, low, rest, square, inverse):
    columns = image.shape[0]
    fields = stack.shape[0]
    gram = unpacked(cross[:, fields + columns :] * scale, columns, fields)
    used, proj[...], rest[...], square_here = project(
        cross[:, : fields + columns], split(gram), scale
    )
    square[...] = square_here
    moved = dot(jnp.concatenate(used, axis=0), stack[...])
    w = image[...].astype(jnp.float32) - moved[:columns] - moved[columns:]
    block[...] = w.astype(jnp.bfloat16)
    upper, inverse_here = factor(square_here)
    low[...] = upper.T
    inverse_here = inverse_here.astype(jnp.bfloat16)
    inverse[...] = inverse_here
    block[...] = dot(inverse_here, block[...]).astype(jnp.bfloat16)


def next_gram_kernel(scale, cross, rest, square, inverse, high, low):
    columns = square.shape[0]
    fields = rest.shape[1]
    kept = fields - columns
    gram = unpacked(cross[:, fields + columns :] * scale, columns, fields)
    mixed = dots((inverse[...],), split(rest[:, columns:]))
    corner = dots((inverse[...],), split(square[...]))
    corner = dots(split(corner), (inverse[...],), NT)
    for part, (old, side, end) in zip(
        (high, low), zip(split(gram[columns:, columns:]), split(mixed), split(corner))
    ):
        part[:kept, :kept] = old
        part[kept:, :kept] = side
        part[:kept, kept:] = side.T
        part[kept:, kept:] = end


def second_solve_kernel(
    scale, cross, own_high, own_low, stack, last, image, proj_in, low_in, result, proj, low, block
):
    columns = image.shape[0]
    kept = stack.shape[0] - columns
    used, proj[1], _, square = project(cross[...], (own_high[...], own_low[...]), scale)
    proj[0] = proj_in[...]
    low[0] = low_in[...]
    both = jnp.concatenate(used, axis=0)
    moved = dot(both[:, :kept], stack[columns:]) + dot(both[:, kept:], last[...])
    w = image[...].astype(jnp.float32) - moved[:columns] - moved[columns:]
    block[...] = w.astype(jnp.bfloat16)
    upper, inverse = factor(square)
    low[1] = upper.T
    inverse = inverse.astype(jnp.bfloat16)
    _, span_x, span_y, depth = result.shape
    plane = span_y * depth
    for x in range(span_x):
        part = dot(inverse, block[:, x * plane : (x + 1) * plane])
        result[:, x] = part.reshape(columns, span_y, depth).astype(jnp.bfloat16)


def partner(part, mask):
    axes = ("slab", "col")
    count = lax.axis_size("slab") * lax.axis_size("col")
    return lax.ppermute(part, axes, [(i, i ^ mask) for i in range(count)])


def whole_sum(part, grouped):
    cols = lax.axis_size("col")
    count = lax.axis_size("slab") * cols
    index = lax.axis_index("slab") * cols + lax.axis_index("col")
    bit, upper = 1, 0
    while bit < count:
        upper = upper ^ (index // bit % 2)
        bit *= 2
    upper = upper == 1
    half = part.shape[0] // 2
    low, high = part[:half], part[half:]
    part = jnp.where(upper, high, low) + partner(jnp.where(upper, low, high), 1)
    bit = 2
    while bit < count:
        if 2 * bit < count and (grouped or bit == 2):
            one, two, both = (partner(part, mask) for mask in (bit + 1, 2 * bit + 1, 3 * bit))
            part = (part + one) + (two + both)
            bit *= 4
        else:
            part = part + partner(part, bit + 1)
            bit *= 2
    other = partner(part, 1)
    return jnp.concatenate([jnp.where(upper, other, part), jnp.where(upper, part, other)], axis=0)


def call(kernel, name, outs, *args, flops=0, scratch=()):
    moved = sum(math.prod(arg.shape) * arg.dtype.itemsize for arg in args)
    moved += sum(math.prod(shape) * jnp.dtype(dtype).itemsize for shape, dtype in outs)
    return pl.pallas_call(
        kernel,
        out_shape=[jax.ShapeDtypeStruct(shape, dtype) for shape, dtype in outs],
        in_specs=[pl.BlockSpec(memory_space=pltpu.VMEM)] * len(args),
        out_specs=[pl.BlockSpec(memory_space=pltpu.VMEM)] * len(outs),
        scratch_shapes=scratch,
        compiler_params=pltpu.CompilerParams(vmem_limit_bytes=24 * 1024 * 1024),
        cost_estimate=pl.CostEstimate(flops=flops, bytes_accessed=moved, transcendentals=0),
        name=name,
    )(*args)


def shards(basis, cell_map, table):
    span_x, span_y, depth = cell_map.shape
    blocks, columns = basis.shape[:2]
    cells = span_x * span_y * depth
    fields = blocks * columns
    scale = 1.0 / (cells * lax.axis_size("slab") * lax.axis_size("col"))
    spans = (span_x, span_y, depth)
    f32, bf16 = jnp.float32, jnp.bfloat16

    stack = basis.reshape(fields, cells)
    coef = coefficients(table, cell_map)
    (own,) = call(
        functools.partial(stack_gram_kernel, columns),
        "stack_gram",
        [((columns, columns * blocks * (blocks + 1) // 2), f32)],
        stack,
        flops=2 * fields * fields * cells,
    )
    def inner_image(block):
        return call(
            functools.partial(inner_image_kernel, spans),
            "inner_image",
            [((columns, cells), f32)],
            coef, block,
            flops=2 * 27 * columns * cells,
        )[0]

    around, partial, (coef_ready, stack, own) = neighbours(
        basis[blocks - 1].reshape(columns, cells), *spans, inner_image, (coef, stack, own)
    )
    packed = fields + columns + own.shape[1]
    image, cross = call(
        functools.partial(first_image_kernel, spans),
        "first_image",
        [((columns, cells), bf16), ((columns, packed), f32)],
        coef_ready, stack, own, partial, *around,
    )
    cross = whole_sum(cross, False)
    block, proj, low, rest, square, inverse = call(
        functools.partial(first_solve_kernel, scale),
        "first_solve",
        [((columns, cells), bf16), ((columns, fields), f32), ((columns, columns), f32),
         ((columns, fields), f32), ((columns, columns), f32), ((columns, columns), bf16)],
        cross, stack, image,
    )
    own = call(
        functools.partial(next_gram_kernel, scale),
        "next_gram",
        [((fields, fields), bf16)] * 2,
        cross, rest, square, inverse,
    )
    around, partial, _ = neighbours(block, *spans, inner_image)
    image, cross = call(
        functools.partial(second_image_kernel, spans),
        "second_image",
        [((columns, cells), bf16), ((columns, fields + columns), f32)],
        coef, stack, block, partial, *around,
    )
    block, proj, low = call(
        functools.partial(second_solve_kernel, scale),
        "second_solve",
        [((columns, *spans), bf16), ((2, columns, fields), f32), ((2, columns, columns), f32)],
        whole_sum(cross, True), *own, stack, block, image, proj, low,
        scratch=[pltpu.VMEM((columns, cells), bf16)],
    )
    return block, jnp.swapaxes(proj, 1, 2), low


def solution(mesh):
    placed = (P(None, None, "slab", "col", None), P("slab", "col", None), P())
    return jax.shard_map(
        shards,
        mesh=mesh,
        in_specs=placed,
        out_specs=(P(None, "slab", "col", None), P(), P()),
        check_vma=False,
    )
```

```python
import functools
import math

import jax
import jax.numpy as jnp
from jax import lax
from jax.experimental import pallas as pl
from jax.experimental.pallas import tpu as pltpu
from jax.sharding import PartitionSpec as P

NN = (((1,), (0,)), ((), ()))
NT = (((1,), (1,)), ((), ()))
ROWS = 16


def dot(left, right, dims=NN):
    return lax.dot_general(left, right, dims, preferred_element_type=jnp.float32)


def swaps(axis, upward, downward, closed, beside=None):
    count = lax.axis_size(axis)
    me = lax.axis_index(axis)
    odd = me % 2 == 1
    pairs = [(i, (i - 1 ^ 1) + 1) for i in range(1, count - 1)]
    if closed:
        pairs += [(0, count - 1), (count - 1, 0)]
    near, far = jnp.where(odd, downward, upward), jnp.where(odd, upward, downward)
    inner = lax.ppermute(near, axis, [(i, i ^ 1) for i in range(count)])
    far, beside = lax.optimization_barrier((far, beside))
    outer = lax.ppermute(far, axis, pairs)
    if closed:
        outer = jnp.where((me == 0) | (me == count - 1), 0, outer)
    return jnp.where(odd, inner, outer), jnp.where(odd, outer, inner), beside


def neighbours(block, span_x, span_y, depth, beside=None, meanwhile=None):
    plane = span_y * depth
    xlo, xhi, beside = swaps(
        "slab", block[:, (span_x - 1) * plane :], block[:, :plane], False, beside
    )
    xlo, xhi, meanwhile = lax.optimization_barrier((xlo, xhi, meanwhile))

    def edge(row):
        at = row * depth
        parts = [xlo[:, at : at + depth]]
        parts += [block[:, x * plane + at : x * plane + at + depth] for x in range(span_x)]
        parts += [xhi[:, at : at + depth]]
        return jnp.concatenate(parts, axis=1)

    ylo, yhi, _ = swaps("col", edge(span_y - 1), edge(0), True)
    return (xlo, xhi, ylo, yhi), beside, meanwhile


def coefficients_kernel(table, cells, coef):
    classes = table.shape[0]
    lanes = lax.broadcasted_iota(jnp.int32, cells.shape, 1)
    depth = cells.shape[1]
    here = cells[...]
    below = pltpu.roll(here, depth - 1, 1)
    above = pltpu.roll(here, 1, 1)
    maps = (below, here, above)
    keep = (lanes < depth - 1, None, lanes > 0)
    for dz in range(3):
        masks = [maps[dz] == k for k in range(1, classes)]
        for pair in range(9):
            offset = 3 * pair + dz
            value = jnp.full(cells.shape, table[0, offset], jnp.float32)
            for k in range(1, classes):
                value = jnp.where(masks[k - 1], table[k, offset], value)
            if keep[dz] is not None:
                value = jnp.where(keep[dz], value, 0.0)
            coef[offset] = value


def coefficients(table, cell_map):
    span_x, span_y, depth = cell_map.shape
    lines = span_x * span_y
    return pl.pallas_call(
        coefficients_kernel,
        out_shape=jax.ShapeDtypeStruct((27, lines, depth), jnp.float32),
        in_specs=[
            pl.BlockSpec(memory_space=pltpu.SMEM),
            pl.BlockSpec(memory_space=pltpu.VMEM),
        ],
        out_specs=pl.BlockSpec(memory_space=pltpu.VMEM),
        compiler_params=pltpu.CompilerParams(vmem_limit_bytes=4 * 1024 * 1024),
        name="coefficients",
    )(table, cell_map.reshape(lines, depth))


def stencil(coef, spans, columns, line, inner, write):
    span_x, span_y, depth = spans

    def tile(step, carry):
        rows = pl.ds(pl.multiple_of(step * ROWS, ROWS), ROWS)
        held = {}
        for y in range(span_y):
            for x in range(span_x):
                sums = [None, None, None]
                for pair in range(9):
                    x_there, y_there = x + pair // 3 - 1, y + pair % 3 - 1
                    inside = 0 <= x_there < span_x and 0 <= y_there < span_y
                    if inside != inner:
                        continue
                    if (x_there, y_there) not in held:
                        held[x_there, y_there] = line(rows, x_there, y_there)
                    for dz in range(3):
                        at = x * span_y + y
                        term = coef[3 * pair + dz, at : at + 1, :] * held[x_there, y_there]
                        sums[dz] = term if sums[dz] is None else sums[dz] + term
                total = None
                if sums[0] is not None:
                    total = pltpu.roll(sums[0], 1, 1) + pltpu.roll(sums[2], depth - 1, 1)
                    total = sums[1] + total
                write(rows, x, y, total)
        return carry

    lax.fori_loop(0, columns // ROWS, tile, 0)


def inner_image_kernel(spans, coef, fields, partial):
    _, span_y, depth = spans
    columns = partial.shape[0]
    block = fields.at[fields.shape[0] - columns :]

    def here(x, y):
        return pl.ds((x * span_y + y) * depth, depth)

    def write(rows, x, y, total):
        partial[rows, here(x, y)] = total

    def line(rows, x, y):
        return block[rows, here(x, y)].astype(jnp.float32)

    stencil(coef, spans, columns, line, True, write)


def complete(image, partial, coef, spans, xlo, xhi, ylo, yhi):
    span_x, span_y, depth = spans

    def line(rows, x, y):
        if y < 0:
            ref, at = ylo, x + 1
        elif y >= span_y:
            ref, at = yhi, x + 1
        else:
            ref, at = (xlo, y) if x < 0 else (xhi, y)
        return ref[rows, at * depth : (at + 1) * depth].astype(jnp.float32)

    def write(rows, x, y, total):
        there = pl.ds((x * span_y + y) * depth, depth)
        known = partial[rows, there]
        image[rows, there] = (known if total is None else known + total).astype(jnp.bfloat16)

    stencil(coef, spans, image.shape[0], line, False, write)


def stack_gram_kernel(columns, stack, own):
    at = 0
    for b in range(0, stack.shape[0], columns):
        width = stack.shape[0] - b
        own[:, at : at + width] = dot(stack[b : b + columns], stack[b:], NT)
        at += width


def first_image_kernel(spans, coef, stack, own, partial, xlo, xhi, ylo, yhi, image, cross):
    columns = image.shape[0]
    fields = stack.shape[0]
    complete(image, partial, coef, spans, xlo, xhi, ylo, yhi)
    w = image[...]
    cross[:, :fields] = dot(w, stack[...], NT)
    cross[:, fields : fields + columns] = dot(w, w, NT)
    cross[:, fields + columns :] = own[...]


def second_image_kernel(spans, coef, stack, block, partial, xlo, xhi, ylo, yhi, image, cross):
    columns = image.shape[0]
    fields = stack.shape[0]
    complete(image, partial, coef, spans, xlo, xhi, ylo, yhi)
    w = image[...]
    cross[:, : fields - columns] = dot(w, stack[columns:], NT)
    cross[:, fields - columns : fields] = dot(w, block[...], NT)
    cross[:, fields:] = dot(w, w, NT)


def split(values):
    high = values.astype(jnp.bfloat16)
    return high, (values - high.astype(jnp.float32)).astype(jnp.bfloat16)


def dots(lefts, rights, dims=NN):
    return sum(dot(left, right, dims) for left in lefts for right in rights)


def factor(square):
    size = square.shape[0]
    shape = (8, 2 * size)
    sub = lax.broadcasted_iota(jnp.int32, shape, 0)
    unit = lax.broadcasted_iota(jnp.int32, (size, size), 0) == lax.broadcasted_iota(
        jnp.int32, (size, size), 1
    )
    whole = jnp.concatenate([square, unit.astype(jnp.float32)], axis=1)
    blocks = [whole[b : b + 8] for b in range(0, size, 8)]
    done = []

    def row_of(values, at):
        return jnp.broadcast_to(values[at : at + 1, :], shape)

    def column_of(values, at):
        return jnp.broadcast_to(values[:, at : at + 1], shape)

    for b, here in enumerate(blocks):
        columns = [column_of(here, 8 * b + j) for j in range(8)]
        entry = {(i, j): row_of(columns[j], i) for j in range(8) for i in range(j + 1)}
        rows = [row_of(here, i) for i in range(8)]
        inverse, ratio = [], {}
        for r in range(8):
            inverse.append(1.0 / entry[r, r])
            for j in range(r + 1, 8):
                ratio[r, j] = entry[r, j] * inverse[r]
            for i in range(r + 1, 8):
                for j in range(i, 8):
                    entry[i, j] = entry[i, j] - entry[r, i] * ratio[r, j]
                rows[i] = rows[i] - ratio[r, i] * rows[r]
        solved = {}
        for r in reversed(range(8)):
            solved[r] = rows[r] * inverse[r]
            for j in range(r + 1, 8):
                solved[r] = solved[r] - ratio[r, j] * solved[j]
        for later in range(b + 1, len(blocks)):
            for j in range(8):
                change = column_of(blocks[later], 8 * b + j) * solved[j]
                total = change if j == 0 else total + change
            blocks[later] = blocks[later] - total
        scaled = jnp.zeros(shape, jnp.float32)
        for r in range(8):
            scaled = jnp.where(sub == r, rows[r] * lax.rsqrt(entry[r, r]), scaled)
        done.append(scaled)
    done = jnp.concatenate(done, axis=0)
    return done[:, :size], done[:, size:]


def project(cross, own, scale):
    fields = own[0].shape[0]
    first = cross[:, :fields] * scale
    first_parts = split(first)
    first_low = first_parts[0]
    second = first - dots((first_low,), own)
    second_low = second.astype(jnp.bfloat16)
    used = (first_low, second_low)
    square = cross[:, fields:] * scale - dots(used, first_parts, NT)
    rest = second - dots((second_low,), own)
    square = square - dots(split(rest), used, NT)
    return used, first + second, rest, square


def unpacked(upper, columns, fields):
    rows, at = [], 0
    for b in range(0, fields, columns):
        rows.append((b, upper[:, at : at + fields - b]))
        at += fields - b
    whole = []
    for b, row in rows:
        left = [above[:, b - a : b - a + columns].T for a, above in rows if a < b]
        whole.append(jnp.concatenate(left + [row], axis=1))
    return jnp.concatenate(whole, axis=0)


def first_solve_kernel(scale, cross, stack, image, block, proj, low, rest, square, inverse):
    columns = image.shape[0]
    fields = stack.shape[0]
    gram = unpacked(cross[:, fields + columns :] * scale, columns, fields)
    used, proj[...], rest[...], square_here = project(
        cross[:, : fields + columns], split(gram), scale
    )
    square[...] = square_here
    moved = dot(jnp.concatenate(used, axis=0), stack[...])
    w = image[...].astype(jnp.float32) - moved[:columns] - moved[columns:]
    block[...] = w.astype(jnp.bfloat16)
    upper, inverse_here = factor(square_here)
    low[...] = upper.T
    inverse_here = inverse_here.astype(jnp.bfloat16)
    inverse[...] = inverse_here
    block[...] = dot(inverse_here, block[...]).astype(jnp.bfloat16)


def next_gram_kernel(scale, cross, rest, square, inverse, high, low):
    columns = square.shape[0]
    fields = rest.shape[1]
    kept = fields - columns
    gram = unpacked(cross[:, fields + columns :] * scale, columns, fields)
    mixed = dots((inverse[...],), split(rest[:, columns:]))
    corner = dots((inverse[...],), split(square[...]))
    corner = dots(split(corner), (inverse[...],), NT)
    for part, (old, side, end) in zip(
        (high, low), zip(split(gram[columns:, columns:]), split(mixed), split(corner))
    ):
        part[:kept, :kept] = old
        part[kept:, :kept] = side
        part[:kept, kept:] = side.T
        part[kept:, kept:] = end


def second_solve_kernel(
    scale, cross, own_high, own_low, stack, last, image, proj_in, low_in, result, proj, low, block
):
    columns = image.shape[0]
    kept = stack.shape[0] - columns
    used, proj[1], _, square = project(cross[...], (own_high[...], own_low[...]), scale)
    proj[0] = proj_in[...]
    low[0] = low_in[...]
    both = jnp.concatenate(used, axis=0)
    moved = dot(both[:, :kept], stack[columns:]) + dot(both[:, kept:], last[...])
    w = image[...].astype(jnp.float32) - moved[:columns] - moved[columns:]
    block[...] = w.astype(jnp.bfloat16)
    upper, inverse = factor(square)
    low[1] = upper.T
    inverse = inverse.astype(jnp.bfloat16)
    _, span_x, span_y, depth = result.shape
    plane = span_y * depth
    for x in range(span_x):
        part = dot(inverse, block[:, x * plane : (x + 1) * plane])
        result[:, x] = part.reshape(columns, span_y, depth).astype(jnp.bfloat16)


def partner(part, mask):
    axes = ("slab", "col")
    count = lax.axis_size("slab") * lax.axis_size("col")
    return lax.ppermute(part, axes, [(i, i ^ mask) for i in range(count)])


def whole_sum(part):
    cols = lax.axis_size("col")
    count = lax.axis_size("slab") * cols
    index = lax.axis_index("slab") * cols + lax.axis_index("col")
    bit, upper = 1, 0
    while bit < count:
        upper = upper ^ (index // bit % 2)
        bit *= 2
    upper = upper == 1
    half = part.shape[0] // 2
    low, high = part[:half], part[half:]
    part = jnp.where(upper, high, low) + partner(jnp.where(upper, low, high), 1)
    bit = 2
    while bit < count:
        if 2 * bit < count:
            one, two, both = (partner(part, mask) for mask in (bit + 1, 2 * bit + 1, 3 * bit))
            part = (part + one) + (two + both)
            bit *= 4
        else:
            part = part + partner(part, bit + 1)
            bit *= 2
    other = partner(part, 1)
    return jnp.concatenate([jnp.where(upper, other, part), jnp.where(upper, part, other)], axis=0)


def call(kernel, name, outs, *args, flops=0, scratch=()):
    moved = sum(math.prod(arg.shape) * arg.dtype.itemsize for arg in args)
    moved += sum(math.prod(shape) * jnp.dtype(dtype).itemsize for shape, dtype in outs)
    return pl.pallas_call(
        kernel,
        out_shape=[jax.ShapeDtypeStruct(shape, dtype) for shape, dtype in outs],
        in_specs=[pl.BlockSpec(memory_space=pltpu.VMEM)] * len(args),
        out_specs=[pl.BlockSpec(memory_space=pltpu.VMEM)] * len(outs),
        scratch_shapes=scratch,
        compiler_params=pltpu.CompilerParams(vmem_limit_bytes=24 * 1024 * 1024),
        cost_estimate=pl.CostEstimate(flops=flops, bytes_accessed=moved, transcendentals=0),
        name=name,
    )(*args)


def shards(basis, cell_map, table):
    span_x, span_y, depth = cell_map.shape
    blocks, columns = basis.shape[:2]
    cells = span_x * span_y * depth
    fields = blocks * columns
    scale = 1.0 / (cells * lax.axis_size("slab") * lax.axis_size("col"))
    spans = (span_x, span_y, depth)
    f32, bf16 = jnp.float32, jnp.bfloat16

    stack = basis.reshape(fields, cells)
    coef = coefficients(table, cell_map)
    (own,) = call(
        functools.partial(stack_gram_kernel, columns),
        "stack_gram",
        [((columns, columns * blocks * (blocks + 1) // 2), f32)],
        stack,
        flops=2 * fields * fields * cells,
    )
    def inner_image(block):
        return call(
            functools.partial(inner_image_kernel, spans),
            "inner_image",
            [((columns, cells), f32)],
            coef, block,
            flops=2 * 27 * columns * cells,
        )[0]

    last = basis[blocks - 1].reshape(columns, cells)
    around, partial, (stack, own) = neighbours(last, *spans, inner_image(last), (stack, own))
    packed = fields + columns + own.shape[1]
    image, cross = call(
        functools.partial(first_image_kernel, spans),
        "first_image",
        [((columns, cells), bf16), ((columns, packed), f32)],
        coef, stack, own, partial, *around,
    )
    cross = whole_sum(cross)
    block, proj, low, rest, square, inverse = call(
        functools.partial(first_solve_kernel, scale),
        "first_solve",
        [((columns, cells), bf16), ((columns, fields), f32), ((columns, columns), f32),
         ((columns, fields), f32), ((columns, columns), f32), ((columns, columns), bf16)],
        cross, stack, image,
    )
    own = call(
        functools.partial(next_gram_kernel, scale),
        "next_gram",
        [((fields, fields), bf16)] * 2,
        cross, rest, square, inverse,
    )
    around, _, _ = neighbours(block, *spans)
    image, cross = call(
        functools.partial(second_image_kernel, spans),
        "second_image",
        [((columns, cells), bf16), ((columns, fields + columns), f32)],
        coef, stack, block, inner_image(block), *around,
    )
    block, proj, low = call(
        functools.partial(second_solve_kernel, scale),
        "second_solve",
        [((columns, *spans), bf16), ((2, columns, fields), f32), ((2, columns, columns), f32)],
        whole_sum(cross), *own, stack, block, image, proj, low,
        scratch=[pltpu.VMEM((columns, cells), bf16)],
    )
    return block, jnp.swapaxes(proj, 1, 2), low


def solution(mesh):
    placed = (P(None, None, "slab", "col", None), P("slab", "col", None), P())
    return jax.shard_map(
        shards,
        mesh=mesh,
        in_specs=placed,
        out_specs=(P(None, "slab", "col", None), P(), P()),
        check_vma=False,
    )
```

```python
import functools
import math

import jax
import jax.numpy as jnp
from jax import lax
from jax.experimental import pallas as pl
from jax.experimental.pallas import tpu as pltpu
from jax.sharding import PartitionSpec as P

NN = (((1,), (0,)), ((), ()))
NT = (((1,), (1,)), ((), ()))
ROWS = 16


def dot(left, right, dims=NN):
    return lax.dot_general(left, right, dims, preferred_element_type=jnp.float32)


def swaps(axis, upward, downward, closed, beside=None):
    count = lax.axis_size(axis)
    me = lax.axis_index(axis)
    odd = me % 2 == 1
    pairs = [(i, (i - 1 ^ 1) + 1) for i in range(1, count - 1)]
    if closed:
        pairs += [(0, count - 1), (count - 1, 0)]
    near, far = jnp.where(odd, downward, upward), jnp.where(odd, upward, downward)
    inner = lax.ppermute(near, axis, [(i, i ^ 1) for i in range(count)])
    far, beside = lax.optimization_barrier((far, beside))
    outer = lax.ppermute(far, axis, pairs)
    if closed:
        outer = jnp.where((me == 0) | (me == count - 1), 0, outer)
    return jnp.where(odd, inner, outer), jnp.where(odd, outer, inner), beside


def neighbours(block, span_x, span_y, depth, beside=None, meanwhile=None):
    plane = span_y * depth
    xlo, xhi, beside = swaps(
        "slab", block[:, (span_x - 1) * plane :], block[:, :plane], False, beside
    )
    xlo, xhi, meanwhile = lax.optimization_barrier((xlo, xhi, meanwhile))

    def edge(row):
        at = row * depth
        parts = [xlo[:, at : at + depth]]
        parts += [block[:, x * plane + at : x * plane + at + depth] for x in range(span_x)]
        parts += [xhi[:, at : at + depth]]
        return jnp.concatenate(parts, axis=1)

    ylo, yhi, _ = swaps("col", edge(span_y - 1), edge(0), True)
    return (xlo, xhi, ylo, yhi), beside, meanwhile


def coefficients_kernel(table, cells, coef):
    classes = table.shape[0]
    lanes = lax.broadcasted_iota(jnp.int32, cells.shape, 1)
    depth = cells.shape[1]
    here = cells[...]
    below = pltpu.roll(here, depth - 1, 1)
    above = pltpu.roll(here, 1, 1)
    maps = (below, here, above)
    keep = (lanes < depth - 1, None, lanes > 0)
    for dz in range(3):
        masks = [maps[dz] == k for k in range(1, classes)]
        for pair in range(9):
            offset = 3 * pair + dz
            value = jnp.full(cells.shape, table[0, offset], jnp.float32)
            for k in range(1, classes):
                value = jnp.where(masks[k - 1], table[k, offset], value)
            if keep[dz] is not None:
                value = jnp.where(keep[dz], value, 0.0)
            coef[offset] = value


def coefficients(table, cell_map):
    span_x, span_y, depth = cell_map.shape
    lines = span_x * span_y
    return pl.pallas_call(
        coefficients_kernel,
        out_shape=jax.ShapeDtypeStruct((27, lines, depth), jnp.float32),
        in_specs=[
            pl.BlockSpec(memory_space=pltpu.SMEM),
            pl.BlockSpec(memory_space=pltpu.VMEM),
        ],
        out_specs=pl.BlockSpec(memory_space=pltpu.VMEM),
        compiler_params=pltpu.CompilerParams(vmem_limit_bytes=4 * 1024 * 1024),
        name="coefficients",
    )(table, cell_map.reshape(lines, depth))


def stencil(coef, spans, columns, line, inner, write):
    span_x, span_y, depth = spans

    def tile(step, carry):
        rows = pl.ds(pl.multiple_of(step * ROWS, ROWS), ROWS)
        held = {}
        for y in range(span_y):
            for x in range(span_x):
                sums = [None, None, None]
                for pair in range(9):
                    x_there, y_there = x + pair // 3 - 1, y + pair % 3 - 1
                    inside = 0 <= x_there < span_x and 0 <= y_there < span_y
                    if inside != inner:
                        continue
                    if (x_there, y_there) not in held:
                        held[x_there, y_there] = line(rows, x_there, y_there)
                    for dz in range(3):
                        at = x * span_y + y
                        term = coef[3 * pair + dz, at : at + 1, :] * held[x_there, y_there]
                        sums[dz] = term if sums[dz] is None else sums[dz] + term
                total = None
                if sums[0] is not None:
                    total = pltpu.roll(sums[0], 1, 1) + pltpu.roll(sums[2], depth - 1, 1)
                    total = sums[1] + total
                write(rows, x, y, total)
        return carry

    lax.fori_loop(0, columns // ROWS, tile, 0)


def inner_image_kernel(spans, coef, fields, partial):
    _, span_y, depth = spans
    columns = partial.shape[0]
    block = fields.at[fields.shape[0] - columns :]

    def here(x, y):
        return pl.ds((x * span_y + y) * depth, depth)

    def write(rows, x, y, total):
        partial[rows, here(x, y)] = total

    def line(rows, x, y):
        return block[rows, here(x, y)].astype(jnp.float32)

    stencil(coef, spans, columns, line, True, write)


def complete(image, partial, coef, spans, xlo, xhi, ylo, yhi):
    span_x, span_y, depth = spans

    def line(rows, x, y):
        if y < 0:
            ref, at = ylo, x + 1
        elif y >= span_y:
            ref, at = yhi, x + 1
        else:
            ref, at = (xlo, y) if x < 0 else (xhi, y)
        return ref[rows, at * depth : (at + 1) * depth].astype(jnp.float32)

    def write(rows, x, y, total):
        there = pl.ds((x * span_y + y) * depth, depth)
        known = partial[rows, there]
        image[rows, there] = (known if total is None else known + total).astype(jnp.bfloat16)

    stencil(coef, spans, image.shape[0], line, False, write)


def stack_gram_kernel(columns, stack, own):
    at = 0
    for b in range(0, stack.shape[0], columns):
        width = stack.shape[0] - b
        own[:, at : at + width] = dot(stack[b : b + columns], stack[b:], NT)
        at += width


def first_image_kernel(spans, coef, stack, own, partial, xlo, xhi, ylo, yhi, image, cross):
    columns = image.shape[0]
    fields = stack.shape[0]
    complete(image, partial, coef, spans, xlo, xhi, ylo, yhi)
    w = image[...]
    cross[:, :fields] = dot(w, stack[...], NT)
    cross[:, fields : fields + columns] = dot(w, w, NT)
    cross[:, fields + columns :] = own[...]


def second_image_kernel(spans, coef, stack, block, partial, xlo, xhi, ylo, yhi, image, cross):
    columns = image.shape[0]
    fields = stack.shape[0]
    complete(image, partial, coef, spans, xlo, xhi, ylo, yhi)
    w = image[...]
    cross[:, : fields - columns] = dot(w, stack[columns:], NT)
    cross[:, fields - columns : fields] = dot(w, block[...], NT)
    cross[:, fields:] = dot(w, w, NT)


def split(values):
    high = values.astype(jnp.bfloat16)
    return high, (values - high.astype(jnp.float32)).astype(jnp.bfloat16)


def dots(lefts, rights, dims=NN):
    return sum(dot(left, right, dims) for left in lefts for right in rights)


def factor(square):
    size = square.shape[0]
    shape = (8, 2 * size)
    sub = lax.broadcasted_iota(jnp.int32, shape, 0)
    unit = lax.broadcasted_iota(jnp.int32, (size, size), 0) == lax.broadcasted_iota(
        jnp.int32, (size, size), 1
    )
    whole = jnp.concatenate([square, unit.astype(jnp.float32)], axis=1)
    blocks = [whole[b : b + 8] for b in range(0, size, 8)]
    done = []

    def row_of(values, at):
        return jnp.broadcast_to(values[at : at + 1, :], shape)

    def column_of(values, at):
        return jnp.broadcast_to(values[:, at : at + 1], shape)

    for b, here in enumerate(blocks):
        columns = [column_of(here, 8 * b + j) for j in range(8)]
        entry = {(i, j): row_of(columns[j], i) for j in range(8) for i in range(j + 1)}
        rows = [row_of(here, i) for i in range(8)]
        inverse, ratio = [], {}
        for r in range(8):
            inverse.append(1.0 / entry[r, r])
            for j in range(r + 1, 8):
                ratio[r, j] = entry[r, j] * inverse[r]
            for i in range(r + 1, 8):
                for j in range(i, 8):
                    entry[i, j] = entry[i, j] - entry[r, i] * ratio[r, j]
                rows[i] = rows[i] - ratio[r, i] * rows[r]
        solved = {}
        for r in reversed(range(8)):
            solved[r] = rows[r] * inverse[r]
            for j in range(r + 1, 8):
                solved[r] = solved[r] - ratio[r, j] * solved[j]
        for later in range(b + 1, len(blocks)):
            for j in range(8):
                change = column_of(blocks[later], 8 * b + j) * solved[j]
                total = change if j == 0 else total + change
            blocks[later] = blocks[later] - total
        scaled = jnp.zeros(shape, jnp.float32)
        for r in range(8):
            scaled = jnp.where(sub == r, rows[r] * lax.rsqrt(entry[r, r]), scaled)
        done.append(scaled)
    done = jnp.concatenate(done, axis=0)
    return done[:, :size], done[:, size:]


def project(cross, own, scale):
    fields = own[0].shape[0]
    first = cross[:, :fields] * scale
    first_parts = split(first)
    first_low = first_parts[0]
    second = first - dots((first_low,), own)
    second_low = second.astype(jnp.bfloat16)
    used = (first_low, second_low)
    square = cross[:, fields:] * scale - dots(used, first_parts, NT)
    rest = second - dots((second_low,), own)
    square = square - dots(split(rest), used, NT)
    return used, first + second, rest, square


def unpacked(upper, columns, fields):
    rows, at = [], 0
    for b in range(0, fields, columns):
        rows.append((b, upper[:, at : at + fields - b]))
        at += fields - b
    whole = []
    for b, row in rows:
        left = [above[:, b - a : b - a + columns].T for a, above in rows if a < b]
        whole.append(jnp.concatenate(left + [row], axis=1))
    return jnp.concatenate(whole, axis=0)


def first_solve_kernel(scale, cross, stack, image, block, proj, low, rest, square, inverse):
    columns = image.shape[0]
    fields = stack.shape[0]
    gram = unpacked(cross[:, fields + columns :] * scale, columns, fields)
    used, proj[...], rest[...], square_here = project(
        cross[:, : fields + columns], split(gram), scale
    )
    square[...] = square_here
    moved = dot(jnp.concatenate(used, axis=0), stack[...])
    w = image[...].astype(jnp.float32) - moved[:columns] - moved[columns:]
    block[...] = w.astype(jnp.bfloat16)
    upper, inverse_here = factor(square_here)
    low[...] = upper.T
    inverse_here = inverse_here.astype(jnp.bfloat16)
    inverse[...] = inverse_here
    block[...] = dot(inverse_here, block[...]).astype(jnp.bfloat16)


def next_gram_kernel(scale, cross, rest, square, inverse, high, low):
    columns = square.shape[0]
    fields = rest.shape[1]
    kept = fields - columns
    gram = unpacked(cross[:, fields + columns :] * scale, columns, fields)
    mixed = dots((inverse[...],), split(rest[:, columns:]))
    corner = dots((inverse[...],), split(square[...]))
    corner = dots(split(corner), (inverse[...],), NT)
    for part, (old, side, end) in zip(
        (high, low), zip(split(gram[columns:, columns:]), split(mixed), split(corner))
    ):
        part[:kept, :kept] = old
        part[kept:, :kept] = side
        part[:kept, kept:] = side.T
        part[kept:, kept:] = end


def second_solve_kernel(
    scale, cross, own_high, own_low, stack, last, image, proj_in, low_in, result_out, proj_out,
    low_out, block, result, proj, low, done,
):
    columns = image.shape[0]
    kept = stack.shape[0] - columns
    used, proj[1], _, square = project(cross[...], (own_high[...], own_low[...]), scale)
    proj[0] = proj_in[...]
    copies = [pltpu.make_async_copy(proj, proj_out, done.at[0])]
    copies[0].start()
    both = jnp.concatenate(used, axis=0)
    moved = dot(both[:, :kept], stack[columns:]) + dot(both[:, kept:], last[...])
    w = image[...].astype(jnp.float32) - moved[:columns] - moved[columns:]
    block[...] = w.astype(jnp.bfloat16)
    upper, inverse = factor(square)
    inverse = inverse.astype(jnp.bfloat16)
    _, span_x, span_y, depth = result.shape
    plane = span_y * depth
    for x in range(span_x):
        part = dot(inverse, block[:, x * plane : (x + 1) * plane])
        result[:, x] = part.reshape(columns, span_y, depth).astype(jnp.bfloat16)
        copies.append(
            pltpu.make_async_copy(result.at[:, x], result_out.at[:, x], done.at[2 + x])
        )
        copies[-1].start()
    low[0] = low_in[...]
    low[1] = upper.T
    copies.append(pltpu.make_async_copy(low, low_out, done.at[1]))
    copies[-1].start()
    for copy in copies:
        copy.wait()


def partner(part, mask):
    axes = ("slab", "col")
    count = lax.axis_size("slab") * lax.axis_size("col")
    return lax.ppermute(part, axes, [(i, i ^ mask) for i in range(count)])


def whole_sum(part, scattered):
    cols = lax.axis_size("col")
    count = lax.axis_size("slab") * cols
    index = lax.axis_index("slab") * cols + lax.axis_index("col")
    bit, upper = 1, 0
    while bit < count:
        upper = upper ^ (index // bit % 2)
        bit *= 2
    upper = upper == 1
    half = part.shape[0] // 2
    low, high = part[:half], part[half:]
    part = jnp.where(upper, high, low) + partner(jnp.where(upper, low, high), 1)

    def by_place(four):
        odd, later = index // 2 % 2 == 1, index // 4 % 2 == 1
        four = [jnp.where(odd, four[i ^ 1], four[i]) for i in range(4)]
        return [jnp.where(later, four[i ^ 2], four[i]) for i in range(4)]

    def group(four, bit):
        return [partner(four[i], mask) for i, mask in ((1, bit + 1), (2, 2 * bit + 1), (3, 3 * bit))]

    bit = 2
    if scattered:
        mine = by_place(jnp.split(part, 4, axis=0))
        one, two, both = group(mine, bit)
        part = (mine[0] + one) + (two + both)
        bit = 8
    while bit < count:
        if 2 * bit < count:
            one, two, both = group([part] * 4, bit)
            part = (part + one) + (two + both)
        else:
            part = part + partner(part, bit + 1)
        bit *= 4
    if scattered:
        part = jnp.concatenate(by_place([part, *group([part] * 4, 2)]), axis=0)
    other = partner(part, 1)
    return jnp.concatenate([jnp.where(upper, other, part), jnp.where(upper, part, other)], axis=0)


def call(kernel, name, outs, *args, flops=0, scratch=(), place=pltpu.VMEM):
    moved = sum(math.prod(arg.shape) * arg.dtype.itemsize for arg in args)
    moved += sum(math.prod(shape) * jnp.dtype(dtype).itemsize for shape, dtype in outs)
    return pl.pallas_call(
        kernel,
        out_shape=[jax.ShapeDtypeStruct(shape, dtype) for shape, dtype in outs],
        in_specs=[pl.BlockSpec(memory_space=pltpu.VMEM)] * len(args),
        out_specs=[pl.BlockSpec(memory_space=place)] * len(outs),
        scratch_shapes=scratch,
        compiler_params=pltpu.CompilerParams(vmem_limit_bytes=24 * 1024 * 1024),
        cost_estimate=pl.CostEstimate(flops=flops, bytes_accessed=moved, transcendentals=0),
        name=name,
    )(*args)


def shards(basis, cell_map, table):
    span_x, span_y, depth = cell_map.shape
    blocks, columns = basis.shape[:2]
    cells = span_x * span_y * depth
    fields = blocks * columns
    scale = 1.0 / (cells * lax.axis_size("slab") * lax.axis_size("col"))
    spans = (span_x, span_y, depth)
    f32, bf16 = jnp.float32, jnp.bfloat16

    stack = basis.reshape(fields, cells)
    coef = coefficients(table, cell_map)
    (own,) = call(
        functools.partial(stack_gram_kernel, columns),
        "stack_gram",
        [((columns, columns * blocks * (blocks + 1) // 2), f32)],
        stack,
        flops=2 * fields * fields * cells,
    )
    def inner_image(block):
        return call(
            functools.partial(inner_image_kernel, spans),
            "inner_image",
            [((columns, cells), f32)],
            coef, block,
            flops=2 * 27 * columns * cells,
        )[0]

    last = basis[blocks - 1].reshape(columns, cells)
    around, partial, (stack, own) = neighbours(last, *spans, inner_image(last), (stack, own))
    packed = fields + columns + own.shape[1]
    image, cross = call(
        functools.partial(first_image_kernel, spans),
        "first_image",
        [((columns, cells), bf16), ((columns, packed), f32)],
        coef, stack, own, partial, *around,
    )
    cross = whole_sum(cross, True)
    block, proj, low, rest, square, inverse = call(
        functools.partial(first_solve_kernel, scale),
        "first_solve",
        [((columns, cells), bf16), ((columns, fields), f32), ((columns, columns), f32),
         ((columns, fields), f32), ((columns, columns), f32), ((columns, columns), bf16)],
        cross, stack, image,
    )
    own = call(
        functools.partial(next_gram_kernel, scale),
        "next_gram",
        [((fields, fields), bf16)] * 2,
        cross, rest, square, inverse,
    )
    around, _, _ = neighbours(block, *spans)
    image, cross = call(
        functools.partial(second_image_kernel, spans),
        "second_image",
        [((columns, cells), bf16), ((columns, fields + columns), f32)],
        coef, stack, block, inner_image(block), *around,
    )
    outs = [((columns, *spans), bf16), ((2, columns, fields), f32), ((2, columns, columns), f32)]
    block, proj, low = call(
        functools.partial(second_solve_kernel, scale),
        "second_solve",
        outs,
        whole_sum(cross, False), *own, stack, block, image, proj, low,
        place=pl.ANY,
        scratch=[
            pltpu.VMEM((columns, cells), bf16),
            *(pltpu.VMEM(shape, dtype) for shape, dtype in outs),
            pltpu.SemaphoreType.DMA((2 + span_x,)),
        ],
    )
    return block, jnp.swapaxes(proj, 1, 2), low


def solution(mesh):
    placed = (P(None, None, "slab", "col", None), P("slab", "col", None), P())
    return jax.shard_map(
        shards,
        mesh=mesh,
        in_specs=placed,
        out_specs=(P(None, "slab", "col", None), P(), P()),
        check_vma=False,
    )
```

```python
import functools
import math

import jax
import jax.numpy as jnp
from jax import lax
from jax.experimental import pallas as pl
from jax.experimental.pallas import tpu as pltpu
from jax.sharding import PartitionSpec as P

NN = (((1,), (0,)), ((), ()))
NT = (((1,), (1,)), ((), ()))
ROWS = 16


def dot(left, right, dims=NN):
    return lax.dot_general(left, right, dims, preferred_element_type=jnp.float32)


def swaps(axis, upward, downward, closed, beside=None):
    count = lax.axis_size(axis)
    me = lax.axis_index(axis)
    odd = me % 2 == 1
    pairs = [(i, (i - 1 ^ 1) + 1) for i in range(1, count - 1)]
    if closed:
        pairs += [(0, count - 1), (count - 1, 0)]
    near, far = jnp.where(odd, downward, upward), jnp.where(odd, upward, downward)
    inner = lax.ppermute(near, axis, [(i, i ^ 1) for i in range(count)])
    far, beside = lax.optimization_barrier((far, beside))
    outer = lax.ppermute(far, axis, pairs)
    if closed:
        outer = jnp.where((me == 0) | (me == count - 1), 0, outer)
    return jnp.where(odd, inner, outer), jnp.where(odd, outer, inner), beside


def neighbours(block, span_x, span_y, depth, beside=None, meanwhile=None):
    plane = span_y * depth
    xlo, xhi, beside = swaps(
        "slab", block[:, (span_x - 1) * plane :], block[:, :plane], False, beside
    )
    xlo, xhi, meanwhile = lax.optimization_barrier((xlo, xhi, meanwhile))

    def edge(row):
        at = row * depth
        parts = [xlo[:, at : at + depth]]
        parts += [block[:, x * plane + at : x * plane + at + depth] for x in range(span_x)]
        parts += [xhi[:, at : at + depth]]
        return jnp.concatenate(parts, axis=1)

    ylo, yhi, _ = swaps("col", edge(span_y - 1), edge(0), True)
    return (xlo, xhi, ylo, yhi), beside, meanwhile


def coefficients_kernel(table, cells, coef):
    classes = table.shape[0]
    lanes = lax.broadcasted_iota(jnp.int32, cells.shape, 1)
    depth = cells.shape[1]
    here = cells[...]
    below = pltpu.roll(here, depth - 1, 1)
    above = pltpu.roll(here, 1, 1)
    maps = (below, here, above)
    keep = (lanes < depth - 1, None, lanes > 0)
    for dz in range(3):
        masks = [maps[dz] == k for k in range(1, classes)]
        for pair in range(9):
            offset = 3 * pair + dz
            value = jnp.full(cells.shape, table[0, offset], jnp.float32)
            for k in range(1, classes):
                value = jnp.where(masks[k - 1], table[k, offset], value)
            if keep[dz] is not None:
                value = jnp.where(keep[dz], value, 0.0)
            coef[offset] = value


def coefficients(table, cell_map):
    span_x, span_y, depth = cell_map.shape
    lines = span_x * span_y
    return pl.pallas_call(
        coefficients_kernel,
        out_shape=jax.ShapeDtypeStruct((27, lines, depth), jnp.float32),
        in_specs=[
            pl.BlockSpec(memory_space=pltpu.SMEM),
            pl.BlockSpec(memory_space=pltpu.VMEM),
        ],
        out_specs=pl.BlockSpec(memory_space=pltpu.VMEM),
        compiler_params=pltpu.CompilerParams(vmem_limit_bytes=4 * 1024 * 1024),
        name="coefficients",
    )(table, cell_map.reshape(lines, depth))


def stencil(coef, spans, columns, line, inner, write):
    span_x, span_y, depth = spans

    def tile(step, carry):
        rows = pl.ds(pl.multiple_of(step * ROWS, ROWS), ROWS)
        held = {}
        for y in range(span_y):
            for x in range(span_x):
                sums = [None, None, None]
                for pair in range(9):
                    x_there, y_there = x + pair // 3 - 1, y + pair % 3 - 1
                    inside = 0 <= x_there < span_x and 0 <= y_there < span_y
                    if inside != inner:
                        continue
                    if (x_there, y_there) not in held:
                        held[x_there, y_there] = line(rows, x_there, y_there)
                    for dz in range(3):
                        at = x * span_y + y
                        term = coef[3 * pair + dz, at : at + 1, :] * held[x_there, y_there]
                        sums[dz] = term if sums[dz] is None else sums[dz] + term
                total = None
                if sums[0] is not None:
                    total = pltpu.roll(sums[0], 1, 1) + pltpu.roll(sums[2], depth - 1, 1)
                    total = sums[1] + total
                write(rows, x, y, total)
        return carry

    lax.fori_loop(0, columns // ROWS, tile, 0)


def inner_image_kernel(spans, coef, fields, partial):
    _, span_y, depth = spans
    columns = partial.shape[0]
    block = fields.at[fields.shape[0] - columns :]

    def here(x, y):
        return pl.ds((x * span_y + y) * depth, depth)

    def write(rows, x, y, total):
        partial[rows, here(x, y)] = total

    def line(rows, x, y):
        return block[rows, here(x, y)].astype(jnp.float32)

    stencil(coef, spans, columns, line, True, write)


def complete(image, partial, coef, spans, xlo, xhi, ylo, yhi):
    span_x, span_y, depth = spans

    def line(rows, x, y):
        if y < 0:
            ref, at = ylo, x + 1
        elif y >= span_y:
            ref, at = yhi, x + 1
        else:
            ref, at = (xlo, y) if x < 0 else (xhi, y)
        return ref[rows, at * depth : (at + 1) * depth].astype(jnp.float32)

    def write(rows, x, y, total):
        there = pl.ds((x * span_y + y) * depth, depth)
        known = partial[rows, there]
        image[rows, there] = (known if total is None else known + total).astype(jnp.bfloat16)

    stencil(coef, spans, image.shape[0], line, False, write)


def stack_gram_kernel(columns, stack, own):
    at = 0
    for b in range(0, stack.shape[0], columns):
        width = stack.shape[0] - b
        own[:, at : at + width] = dot(stack[b : b + columns], stack[b:], NT)
        at += width


def first_image_kernel(spans, coef, stack, own, partial, xlo, xhi, ylo, yhi, image, cross):
    columns = image.shape[0]
    fields = stack.shape[0]
    complete(image, partial, coef, spans, xlo, xhi, ylo, yhi)
    w = image[...]
    cross[:, :fields] = dot(w, stack[...], NT)
    cross[:, fields : fields + columns] = dot(w, w, NT)
    cross[:, fields + columns :] = own[...]


def second_image_kernel(spans, coef, stack, block, partial, xlo, xhi, ylo, yhi, image, cross):
    columns = image.shape[0]
    fields = stack.shape[0]
    complete(image, partial, coef, spans, xlo, xhi, ylo, yhi)
    w = image[...]
    cross[:, : fields - columns] = dot(w, stack[columns:], NT)
    cross[:, fields - columns : fields] = dot(w, block[...], NT)
    cross[:, fields:] = dot(w, w, NT)


def split(values):
    high = values.astype(jnp.bfloat16)
    return high, (values - high.astype(jnp.float32)).astype(jnp.bfloat16)


def dots(lefts, rights, dims=NN):
    return sum(dot(left, right, dims) for left in lefts for right in rights)


def factor(square, sizes, across):
    size = square.shape[0]
    shape = (8, 2 * size)
    sub = lax.broadcasted_iota(jnp.int32, shape, 0)
    unit = lax.broadcasted_iota(jnp.int32, (size, size), 0) == lax.broadcasted_iota(
        jnp.int32, (size, size), 1
    )
    scale = lax.rsqrt(across)
    square = square * lax.rsqrt(sizes) * scale
    whole = jnp.concatenate([square, unit.astype(jnp.float32)], axis=1)
    blocks = [whole[b : b + 8] for b in range(0, size, 8)]
    done = []

    def row_of(values, at):
        return jnp.broadcast_to(values[at : at + 1, :], shape)

    def columns_of(values, first):
        return [
            jnp.broadcast_to(values[:, at : at + 1], shape) for at in range(first, first + 8)
        ]

    for b, here in enumerate(blocks):
        columns = columns_of(here, 8 * b)
        entry = {(i, j): row_of(columns[j], i) for j in range(8) for i in range(j + 1)}
        rows = [row_of(here, i) for i in range(8)]
        scaled = jnp.zeros(shape, jnp.float32)
        solved, ratio = [], {}
        if b + 1 < len(blocks):
            below = columns_of(blocks[b + 1], 8 * b)
        for p in range(0, 8, 2):
            q = p + 1
            first, mixed, last = entry[p, p], entry[p, q], entry[q, q]
            inverse = 1.0 / (first * last - mixed * mixed)

            def solve(one, two):
                return (
                    (last * one - mixed * two) * inverse,
                    (first * two - mixed * one) * inverse,
                )

            for j in range(p + 2, 8):
                ratio[p, j], ratio[q, j] = solve(entry[p, j], entry[q, j])
            for i in range(p + 2, 8):
                for j in range(i, 8):
                    change = entry[p, i] * ratio[p, j] + entry[q, i] * ratio[q, j]
                    entry[i, j] = entry[i, j] - change
                rows[i] = rows[i] - (ratio[p, i] * rows[p] + ratio[q, i] * rows[q])
            solved += solve(rows[p], rows[q])
            if b + 1 < len(blocks):
                change = below[p] * solved[p] + below[q] * solved[q]
                blocks[b + 1] = blocks[b + 1] - change
                for j in range(p + 2, 8):
                    below[j] = below[j] - (below[p] * ratio[p, j] + below[q] * ratio[q, j])
            part = mixed * (1.0 / first)
            scaled = jnp.where(sub == p, rows[p] * lax.rsqrt(first), scaled)
            rest = (rows[q] - part * rows[p]) * lax.rsqrt(last - part * mixed)
            scaled = jnp.where(sub == q, rest, scaled)
        done.append(scaled)
        for p in (4, 2, 0):
            for r in (p, p + 1):
                for j in range(p + 2, 8):
                    solved[r] = solved[r] - ratio[r, j] * solved[j]
        for later in range(b + 2, len(blocks)):
            parts = [one * two for one, two in zip(columns_of(blocks[later], 8 * b), solved)]
            while len(parts) > 1:
                parts = [one + two for one, two in zip(parts[::2], parts[1::2])]
            blocks[later] = blocks[later] - parts[0]
    done = jnp.concatenate(done, axis=0)
    above = lax.broadcasted_iota(jnp.int32, (size, size), 0) <= lax.broadcasted_iota(
        jnp.int32, (size, size), 1
    )
    return jnp.where(above, done[:, :size] * (across * scale), 0.0), done[:, size:] * scale


def project(cross, own, scale):
    fields = own[0].shape[0]
    first = cross[:, :fields] * scale
    first_parts = split(first)
    first_low = first_parts[0]
    second = first - dots((first_low,), own)
    second_low = second.astype(jnp.bfloat16)
    used = (first_low, second_low)
    square = cross[:, fields:] * scale
    diagonal = jnp.where(
        lax.broadcasted_iota(jnp.int32, square.shape, 0)
        == lax.broadcasted_iota(jnp.int32, square.shape, 1),
        square,
        0.0,
    )
    sizes = [jnp.sum(diagonal, axis=axis, keepdims=True) for axis in (1, 0)]
    square = square - dots(used, first_parts, NT)
    rest = second - dots((second_low,), own)
    square = square - dots(split(rest), used, NT)
    return used, first + second, rest, square, sizes


def unpacked(upper, columns, fields):
    rows, at = [], 0
    for b in range(0, fields, columns):
        rows.append((b, upper[:, at : at + fields - b]))
        at += fields - b
    whole = []
    for b, row in rows:
        left = [above[:, b - a : b - a + columns].T for a, above in rows if a < b]
        whole.append(jnp.concatenate(left + [row], axis=1))
    return jnp.concatenate(whole, axis=0)


def first_solve_kernel(scale, cross, stack, image, block, proj, low, rest, square, inverse):
    columns = image.shape[0]
    fields = stack.shape[0]
    gram = unpacked(cross[:, fields + columns :] * scale, columns, fields)
    used, proj[...], rest[...], square_here, sizes = project(
        cross[:, : fields + columns], split(gram), scale
    )
    square[...] = square_here
    moved = dot(jnp.concatenate(used, axis=0), stack[...])
    w = image[...].astype(jnp.float32) - moved[:columns] - moved[columns:]
    block[...] = w.astype(jnp.bfloat16)
    upper, inverse_here = factor(square_here, *sizes)
    low[...] = upper.T
    inverse_here = inverse_here.astype(jnp.bfloat16)
    inverse[...] = inverse_here
    block[...] = dot(inverse_here, block[...]).astype(jnp.bfloat16)


def next_gram_kernel(scale, cross, rest, square, inverse, high, low):
    columns = square.shape[0]
    fields = rest.shape[1]
    kept = fields - columns
    gram = unpacked(cross[:, fields + columns :] * scale, columns, fields)
    mixed = dots((inverse[...],), split(rest[:, columns:]))
    corner = dots((inverse[...],), split(square[...]))
    corner = dots(split(corner), (inverse[...],), NT)
    for part, (old, side, end) in zip(
        (high, low), zip(split(gram[columns:, columns:]), split(mixed), split(corner))
    ):
        part[:kept, :kept] = old
        part[kept:, :kept] = side
        part[:kept, kept:] = side.T
        part[kept:, kept:] = end


def second_solve_kernel(
    scale, cross, own_high, own_low, stack, last, image, proj_in, low_in, result, proj, low, block
):
    columns = image.shape[0]
    kept = stack.shape[0] - columns
    used, proj[1], _, square, sizes = project(cross[...], (own_high[...], own_low[...]), scale)
    proj[0] = proj_in[...]
    low[0] = low_in[...]
    both = jnp.concatenate(used, axis=0)
    moved = dot(both[:, :kept], stack[columns:]) + dot(both[:, kept:], last[...])
    w = image[...].astype(jnp.float32) - moved[:columns] - moved[columns:]
    block[...] = w.astype(jnp.bfloat16)
    upper, inverse = factor(square, *sizes)
    low[1] = upper.T
    inverse = inverse.astype(jnp.bfloat16)
    _, span_x, span_y, depth = result.shape
    plane = span_y * depth
    for x in range(span_x):
        part = dot(inverse, block[:, x * plane : (x + 1) * plane])
        result[:, x] = part.reshape(columns, span_y, depth).astype(jnp.bfloat16)


def partner(part, mask):
    axes = ("slab", "col")
    count = lax.axis_size("slab") * lax.axis_size("col")
    return lax.ppermute(part, axes, [(i, i ^ mask) for i in range(count)])


def whole_sum(part):
    cols = lax.axis_size("col")
    count = lax.axis_size("slab") * cols
    index = lax.axis_index("slab") * cols + lax.axis_index("col")
    bit, upper = 1, 0
    while bit < count:
        upper = upper ^ (index // bit % 2)
        bit *= 2
    upper = upper == 1
    half = part.shape[0] // 2
    low, high = part[:half], part[half:]
    part = jnp.where(upper, high, low) + partner(jnp.where(upper, low, high), 1)
    bit = 2
    while bit < count:
        if 2 * bit < count:
            one, two, both = (partner(part, mask) for mask in (bit + 1, 2 * bit + 1, 3 * bit))
            part = (part + one) + (two + both)
            bit *= 4
        else:
            part = part + partner(part, bit + 1)
            bit *= 2
    other = partner(part, 1)
    return jnp.concatenate([jnp.where(upper, other, part), jnp.where(upper, part, other)], axis=0)


def call(kernel, name, outs, *args, flops=0, scratch=()):
    moved = sum(math.prod(arg.shape) * arg.dtype.itemsize for arg in args)
    moved += sum(math.prod(shape) * jnp.dtype(dtype).itemsize for shape, dtype in outs)
    return pl.pallas_call(
        kernel,
        out_shape=[jax.ShapeDtypeStruct(shape, dtype) for shape, dtype in outs],
        in_specs=[pl.BlockSpec(memory_space=pltpu.VMEM)] * len(args),
        out_specs=[pl.BlockSpec(memory_space=pltpu.VMEM)] * len(outs),
        scratch_shapes=scratch,
        compiler_params=pltpu.CompilerParams(vmem_limit_bytes=24 * 1024 * 1024),
        cost_estimate=pl.CostEstimate(flops=flops, bytes_accessed=moved, transcendentals=0),
        name=name,
    )(*args)


def shards(basis, cell_map, table):
    span_x, span_y, depth = cell_map.shape
    blocks, columns = basis.shape[:2]
    cells = span_x * span_y * depth
    fields = blocks * columns
    scale = 1.0 / (cells * lax.axis_size("slab") * lax.axis_size("col"))
    spans = (span_x, span_y, depth)
    f32, bf16 = jnp.float32, jnp.bfloat16

    stack = basis.reshape(fields, cells)
    coef = coefficients(table, cell_map)
    (own,) = call(
        functools.partial(stack_gram_kernel, columns),
        "stack_gram",
        [((columns, columns * blocks * (blocks + 1) // 2), f32)],
        stack,
        flops=2 * fields * fields * cells,
    )
    def inner_image(block):
        return call(
            functools.partial(inner_image_kernel, spans),
            "inner_image",
            [((columns, cells), f32)],
            coef, block,
            flops=2 * 27 * columns * cells,
        )[0]

    last = basis[blocks - 1].reshape(columns, cells)
    around, partial, (stack, own) = neighbours(last, *spans, inner_image(last), (stack, own))
    packed = fields + columns + own.shape[1]
    image, cross = call(
        functools.partial(first_image_kernel, spans),
        "first_image",
        [((columns, cells), bf16), ((columns, packed), f32)],
        coef, stack, own, partial, *around,
    )
    cross = whole_sum(cross)
    block, proj, low, rest, square, inverse = call(
        functools.partial(first_solve_kernel, scale),
        "first_solve",
        [((columns, cells), bf16), ((columns, fields), f32), ((columns, columns), f32),
         ((columns, fields), f32), ((columns, columns), f32), ((columns, columns), bf16)],
        cross, stack, image,
    )
    own = call(
        functools.partial(next_gram_kernel, scale),
        "next_gram",
        [((fields, fields), bf16)] * 2,
        cross, rest, square, inverse,
    )
    around, _, _ = neighbours(block, *spans)
    image, cross = call(
        functools.partial(second_image_kernel, spans),
        "second_image",
        [((columns, cells), bf16), ((columns, fields + columns), f32)],
        coef, stack, block, inner_image(block), *around,
    )
    block, proj, low = call(
        functools.partial(second_solve_kernel, scale),
        "second_solve",
        [((columns, *spans), bf16), ((2, columns, fields), f32), ((2, columns, columns), f32)],
        whole_sum(cross), *own, stack, block, image, proj, low,
        scratch=[pltpu.VMEM((columns, cells), bf16)],
    )
    return block, jnp.swapaxes(proj, 1, 2), low


def solution(mesh):
    placed = (P(None, None, "slab", "col", None), P("slab", "col", None), P())
    return jax.shard_map(
        shards,
        mesh=mesh,
        in_specs=placed,
        out_specs=(P(None, "slab", "col", None), P(), P()),
        check_vma=False,
    )
```

```python
import functools
import math

import jax
import jax.numpy as jnp
from jax import lax
from jax.experimental import pallas as pl
from jax.experimental.pallas import tpu as pltpu
from jax.sharding import PartitionSpec as P

NN = (((1,), (0,)), ((), ()))
NT = (((1,), (1,)), ((), ()))
ROWS = 16


def dot(left, right, dims=NN):
    return lax.dot_general(left, right, dims, preferred_element_type=jnp.float32)


def swaps(axis, upward, downward, closed, beside=None):
    count = lax.axis_size(axis)
    me = lax.axis_index(axis)
    odd = me % 2 == 1
    pairs = [(i, (i - 1 ^ 1) + 1) for i in range(1, count - 1)]
    if closed:
        pairs += [(0, count - 1), (count - 1, 0)]
    near, far = jnp.where(odd, downward, upward), jnp.where(odd, upward, downward)
    inner = lax.ppermute(near, axis, [(i, i ^ 1) for i in range(count)])
    far, beside = lax.optimization_barrier((far, beside))
    outer = lax.ppermute(far, axis, pairs)
    if closed:
        outer = jnp.where((me == 0) | (me == count - 1), 0, outer)
    return jnp.where(odd, inner, outer), jnp.where(odd, outer, inner), beside


def neighbours(block, span_x, span_y, depth, beside=None, meanwhile=None):
    plane = span_y * depth
    xlo, xhi, beside = swaps(
        "slab", block[:, (span_x - 1) * plane :], block[:, :plane], False, beside
    )
    xlo, xhi, meanwhile = lax.optimization_barrier((xlo, xhi, meanwhile))

    def edge(row):
        at = row * depth
        parts = [xlo[:, at : at + depth]]
        parts += [block[:, x * plane + at : x * plane + at + depth] for x in range(span_x)]
        parts += [xhi[:, at : at + depth]]
        return jnp.concatenate(parts, axis=1)

    ylo, yhi, _ = swaps("col", edge(span_y - 1), edge(0), True)
    return (xlo, xhi, ylo, yhi), beside, meanwhile


def coefficients_kernel(table, cells, coef):
    classes = table.shape[0]
    lanes = lax.broadcasted_iota(jnp.int32, cells.shape, 1)
    depth = cells.shape[1]
    here = cells[...]
    below = pltpu.roll(here, depth - 1, 1)
    above = pltpu.roll(here, 1, 1)
    maps = (below, here, above)
    keep = (lanes < depth - 1, None, lanes > 0)
    for dz in range(3):
        masks = [maps[dz] == k for k in range(1, classes)]
        for pair in range(9):
            offset = 3 * pair + dz
            value = jnp.full(cells.shape, table[0, offset], jnp.float32)
            for k in range(1, classes):
                value = jnp.where(masks[k - 1], table[k, offset], value)
            if keep[dz] is not None:
                value = jnp.where(keep[dz], value, 0.0)
            coef[offset] = value


def coefficients(table, cell_map):
    span_x, span_y, depth = cell_map.shape
    lines = span_x * span_y
    return pl.pallas_call(
        coefficients_kernel,
        out_shape=jax.ShapeDtypeStruct((27, lines, depth), jnp.float32),
        in_specs=[
            pl.BlockSpec(memory_space=pltpu.SMEM),
            pl.BlockSpec(memory_space=pltpu.VMEM),
        ],
        out_specs=pl.BlockSpec(memory_space=pltpu.VMEM),
        compiler_params=pltpu.CompilerParams(vmem_limit_bytes=4 * 1024 * 1024),
        name="coefficients",
    )(table, cell_map.reshape(lines, depth))


def stencil(coef, spans, columns, line, inner, write):
    span_x, span_y, depth = spans

    def tile(step, carry):
        rows = pl.ds(pl.multiple_of(step * ROWS, ROWS), ROWS)
        held = {}
        for y in range(span_y):
            for x in range(span_x):
                sums = [None, None, None]
                for pair in range(9):
                    x_there, y_there = x + pair // 3 - 1, y + pair % 3 - 1
                    inside = 0 <= x_there < span_x and 0 <= y_there < span_y
                    if inside != inner:
                        continue
                    if (x_there, y_there) not in held:
                        held[x_there, y_there] = line(rows, x_there, y_there)
                    for dz in range(3):
                        at = x * span_y + y
                        term = coef[3 * pair + dz, at : at + 1, :] * held[x_there, y_there]
                        sums[dz] = term if sums[dz] is None else sums[dz] + term
                total = None
                if sums[0] is not None:
                    total = pltpu.roll(sums[0], 1, 1) + pltpu.roll(sums[2], depth - 1, 1)
                    total = sums[1] + total
                write(rows, x, y, total)
        return carry

    lax.fori_loop(0, columns // ROWS, tile, 0)


def inner_image_kernel(spans, coef, fields, partial):
    _, span_y, depth = spans
    columns = partial.shape[0]
    block = fields.at[fields.shape[0] - columns :]

    def here(x, y):
        return pl.ds((x * span_y + y) * depth, depth)

    def write(rows, x, y, total):
        partial[rows, here(x, y)] = total

    def line(rows, x, y):
        return block[rows, here(x, y)].astype(jnp.float32)

    stencil(coef, spans, columns, line, True, write)


def complete(image, partial, coef, spans, xlo, xhi, ylo, yhi):
    span_x, span_y, depth = spans

    def line(rows, x, y):
        if y < 0:
            ref, at = ylo, x + 1
        elif y >= span_y:
            ref, at = yhi, x + 1
        else:
            ref, at = (xlo, y) if x < 0 else (xhi, y)
        return ref[rows, at * depth : (at + 1) * depth].astype(jnp.float32)

    def write(rows, x, y, total):
        there = pl.ds((x * span_y + y) * depth, depth)
        known = partial[rows, there]
        image[rows, there] = (known if total is None else known + total).astype(jnp.bfloat16)

    stencil(coef, spans, image.shape[0], line, False, write)


def places(size):
    return [lax.broadcasted_iota(jnp.int32, (size, size), dim) for dim in (0, 1)]


def diagonal_of(square, axis):
    row, column = places(square.shape[0])
    return jnp.sum(jnp.where(row == column, square, 0.0), axis=axis, keepdims=True)


def two_in_one(one, two):
    row, column = places(one.shape[0])
    return jnp.where(row >= column, one, two), diagonal_of(two, 0)


def both_of(packed, diagonal):
    row, column = places(packed.shape[0])
    turned = packed.T
    two = jnp.where(row < column, packed, turned)
    return jnp.where(row >= column, packed, turned), jnp.where(row == column, diagonal, two)


def stack_gram_kernel(columns, stack, sides, pair, last, diagonal):
    parts = [stack[b * columns : (b + 1) * columns] for b in range(3)]
    sides[0] = dot(parts[0], parts[1], NT)
    sides[1] = dot(parts[0], parts[2], NT)
    sides[2] = dot(parts[1], parts[2], NT)
    pair[...], diagonal[...] = two_in_one(dot(parts[0], parts[0], NT), dot(parts[1], parts[1], NT))
    last[...] = dot(parts[2], parts[2], NT)


def first_image_kernel(
    spans, coef, stack, sides, pair, last, diagonal, partial, xlo, xhi, ylo, yhi, image, cross
):
    columns = image.shape[0]
    complete(image, partial, coef, spans, xlo, xhi, ylo, yhi)
    w = image[...]
    first = dot(w, stack[...], NT)
    corner, own_diagonal = two_in_one(last[...], dot(w, w, NT))
    rows = [
        first[:, : 2 * columns],
        jnp.concatenate([first[:, 2 * columns :], sides[0]], axis=1),
        jnp.concatenate([sides[1], sides[2]], axis=1),
        jnp.concatenate([pair[...], corner], axis=1),
    ]
    for i, row in enumerate(rows):
        cross[i * columns : (i + 1) * columns] = row
    rest = jnp.concatenate([diagonal[...], own_diagonal], axis=1)
    rest = jnp.broadcast_to(rest, (cross.shape[0] - 4 * columns, 2 * columns))
    cross[4 * columns :] = rest


def opened(cross, columns, scale):
    parts = [cross[i * columns : (i + 1) * columns] * scale for i in range(4)]
    diagonals = cross[4 * columns : 4 * columns + 1] * scale
    first = jnp.concatenate([parts[0], parts[1][:, :columns]], axis=1)
    side = parts[1][:, columns:], parts[2][:, :columns], parts[2][:, columns:]
    one, two = both_of(parts[3][:, :columns], diagonals[:, :columns])
    three, square = both_of(parts[3][:, columns:], diagonals[:, columns:])
    gram = [[one, side[0], side[1]], [side[0].T, two, side[2]], [side[1].T, side[2].T, three]]
    gram = jnp.concatenate([jnp.concatenate(row, axis=1) for row in gram], axis=0)
    return first, square, gram


def second_image_kernel(spans, coef, stack, block, partial, xlo, xhi, ylo, yhi, image, cross):
    columns = image.shape[0]
    fields = stack.shape[0]
    complete(image, partial, coef, spans, xlo, xhi, ylo, yhi)
    w = image[...]
    cross[:, : fields - columns] = dot(w, stack[columns:], NT)
    cross[:, fields - columns : fields] = dot(w, block[...], NT)
    cross[:, fields:] = dot(w, w, NT)


def split(values):
    high = values.astype(jnp.bfloat16)
    return high, (values - high.astype(jnp.float32)).astype(jnp.bfloat16)


def dots(lefts, rights, dims=NN):
    return sum(dot(left, right, dims) for left in lefts for right in rights)


def factor(square, sizes, across):
    size = square.shape[0]
    shape = (8, 2 * size)
    sub = lax.broadcasted_iota(jnp.int32, shape, 0)
    unit = lax.broadcasted_iota(jnp.int32, (size, size), 0) == lax.broadcasted_iota(
        jnp.int32, (size, size), 1
    )
    scale = lax.rsqrt(across)
    square = square * lax.rsqrt(sizes) * scale
    whole = jnp.concatenate([square, unit.astype(jnp.float32)], axis=1)
    blocks = [whole[b : b + 8] for b in range(0, size, 8)]
    done = []

    def row_of(values, at):
        return jnp.broadcast_to(values[at : at + 1, :], shape)

    def columns_of(values, first):
        return [
            jnp.broadcast_to(values[:, at : at + 1], shape) for at in range(first, first + 8)
        ]

    for b, here in enumerate(blocks):
        columns = columns_of(here, 8 * b)
        entry = {(i, j): row_of(columns[j], i) for j in range(8) for i in range(j + 1)}
        rows = [row_of(here, i) for i in range(8)]
        scaled = jnp.zeros(shape, jnp.float32)
        solved, ratio = [], {}
        if b + 1 < len(blocks):
            below = columns_of(blocks[b + 1], 8 * b)
        for p in range(0, 8, 2):
            q = p + 1
            first, mixed, last = entry[p, p], entry[p, q], entry[q, q]
            inverse = 1.0 / (first * last - mixed * mixed)

            def solve(one, two):
                return (
                    (last * one - mixed * two) * inverse,
                    (first * two - mixed * one) * inverse,
                )

            for j in range(p + 2, 8):
                ratio[p, j], ratio[q, j] = solve(entry[p, j], entry[q, j])
            for i in range(p + 2, 8):
                for j in range(i, 8):
                    change = entry[p, i] * ratio[p, j] + entry[q, i] * ratio[q, j]
                    entry[i, j] = entry[i, j] - change
                rows[i] = rows[i] - (ratio[p, i] * rows[p] + ratio[q, i] * rows[q])
            solved += solve(rows[p], rows[q])
            if b + 1 < len(blocks):
                change = below[p] * solved[p] + below[q] * solved[q]
                blocks[b + 1] = blocks[b + 1] - change
                for j in range(p + 2, 8):
                    below[j] = below[j] - (below[p] * ratio[p, j] + below[q] * ratio[q, j])
            part = mixed * (1.0 / first)
            scaled = jnp.where(sub == p, rows[p] * lax.rsqrt(first), scaled)
            rest = (rows[q] - part * rows[p]) * lax.rsqrt(last - part * mixed)
            scaled = jnp.where(sub == q, rest, scaled)
        done.append(scaled)
        for p in (4, 2, 0):
            for r in (p, p + 1):
                for j in range(p + 2, 8):
                    solved[r] = solved[r] - ratio[r, j] * solved[j]
        for later in range(b + 2, len(blocks)):
            parts = [one * two for one, two in zip(columns_of(blocks[later], 8 * b), solved)]
            while len(parts) > 1:
                parts = [one + two for one, two in zip(parts[::2], parts[1::2])]
            blocks[later] = blocks[later] - parts[0]
    done = jnp.concatenate(done, axis=0)
    above = lax.broadcasted_iota(jnp.int32, (size, size), 0) <= lax.broadcasted_iota(
        jnp.int32, (size, size), 1
    )
    return jnp.where(above, done[:, :size] * (across * scale), 0.0), done[:, size:] * scale


def project(first, square, own):
    first_parts = split(first)
    first_low = first_parts[0]
    second = first - dots((first_low,), own)
    second_low = second.astype(jnp.bfloat16)
    used = (first_low, second_low)
    sizes = [diagonal_of(square, axis) for axis in (1, 0)]
    square = square - dots(used, first_parts, NT)
    rest = second - dots((second_low,), own)
    square = square - dots(split(rest), used, NT)
    return used, first + second, rest, square, sizes


def first_solve_kernel(scale, cross, stack, image, block, proj, low, rest, square, inverse):
    columns = image.shape[0]
    first, own_square, gram = opened(cross, columns, scale)
    used, proj[...], rest[...], square_here, sizes = project(first, own_square, split(gram))
    square[...] = square_here
    moved = dot(jnp.concatenate(used, axis=0), stack[...])
    w = image[...].astype(jnp.float32) - moved[:columns] - moved[columns:]
    block[...] = w.astype(jnp.bfloat16)
    upper, inverse_here = factor(square_here, *sizes)
    low[...] = upper.T
    inverse_here = inverse_here.astype(jnp.bfloat16)
    inverse[...] = inverse_here
    block[...] = dot(inverse_here, block[...]).astype(jnp.bfloat16)


def next_gram_kernel(scale, cross, rest, square, inverse, high, low):
    columns = square.shape[0]
    kept = rest.shape[1] - columns
    _, _, gram = opened(cross, columns, scale)
    mixed = dots((inverse[...],), split(rest[:, columns:]))
    corner = dots((inverse[...],), split(square[...]))
    corner = dots(split(corner), (inverse[...],), NT)
    for part, (old, side, end) in zip(
        (high, low), zip(split(gram[columns:, columns:]), split(mixed), split(corner))
    ):
        part[:kept, :kept] = old
        part[kept:, :kept] = side
        part[:kept, kept:] = side.T
        part[kept:, kept:] = end


def second_solve_kernel(
    scale, cross, own_high, own_low, stack, last, image, proj_in, low_in, result, proj, low, block
):
    columns = image.shape[0]
    kept = stack.shape[0] - columns
    fields = stack.shape[0]
    sums = cross[...] * scale
    used, proj[1], _, square, sizes = project(
        sums[:, :fields], sums[:, fields:], (own_high[...], own_low[...])
    )
    proj[0] = proj_in[...]
    low[0] = low_in[...]
    both = jnp.concatenate(used, axis=0)
    moved = dot(both[:, :kept], stack[columns:]) + dot(both[:, kept:], last[...])
    w = image[...].astype(jnp.float32) - moved[:columns] - moved[columns:]
    block[...] = w.astype(jnp.bfloat16)
    upper, inverse = factor(square, *sizes)
    low[1] = upper.T
    inverse = inverse.astype(jnp.bfloat16)
    _, span_x, span_y, depth = result.shape
    plane = span_y * depth
    for x in range(span_x):
        part = dot(inverse, block[:, x * plane : (x + 1) * plane])
        result[:, x] = part.reshape(columns, span_y, depth).astype(jnp.bfloat16)


def partner(part, mask):
    axes = ("slab", "col")
    count = lax.axis_size("slab") * lax.axis_size("col")
    return lax.ppermute(part, axes, [(i, i ^ mask) for i in range(count)])


def whole_sum(part):
    cols = lax.axis_size("col")
    count = lax.axis_size("slab") * cols
    index = lax.axis_index("slab") * cols + lax.axis_index("col")
    bit, upper = 1, 0
    while bit < count:
        upper = upper ^ (index // bit % 2)
        bit *= 2
    upper = upper == 1
    half = part.shape[0] // 2
    low, high = part[:half], part[half:]
    part = jnp.where(upper, high, low) + partner(jnp.where(upper, low, high), 1)
    bit = 2
    while bit < count:
        if 2 * bit < count:
            one, two, both = (partner(part, mask) for mask in (bit + 1, 2 * bit + 1, 3 * bit))
            part = (part + one) + (two + both)
            bit *= 4
        else:
            part = part + partner(part, bit + 1)
            bit *= 2
    other = partner(part, 1)
    return jnp.concatenate([jnp.where(upper, other, part), jnp.where(upper, part, other)], axis=0)


def call(kernel, name, outs, *args, flops=0, scratch=()):
    moved = sum(math.prod(arg.shape) * arg.dtype.itemsize for arg in args)
    moved += sum(math.prod(shape) * jnp.dtype(dtype).itemsize for shape, dtype in outs)
    return pl.pallas_call(
        kernel,
        out_shape=[jax.ShapeDtypeStruct(shape, dtype) for shape, dtype in outs],
        in_specs=[pl.BlockSpec(memory_space=pltpu.VMEM)] * len(args),
        out_specs=[pl.BlockSpec(memory_space=pltpu.VMEM)] * len(outs),
        scratch_shapes=scratch,
        compiler_params=pltpu.CompilerParams(vmem_limit_bytes=24 * 1024 * 1024),
        cost_estimate=pl.CostEstimate(flops=flops, bytes_accessed=moved, transcendentals=0),
        name=name,
    )(*args)


def shards(basis, cell_map, table):
    span_x, span_y, depth = cell_map.shape
    blocks, columns = basis.shape[:2]
    cells = span_x * span_y * depth
    fields = blocks * columns
    scale = 1.0 / (cells * lax.axis_size("slab") * lax.axis_size("col"))
    spans = (span_x, span_y, depth)
    f32, bf16 = jnp.float32, jnp.bfloat16

    stack = basis.reshape(fields, cells)
    coef = coefficients(table, cell_map)
    own = call(
        functools.partial(stack_gram_kernel, columns),
        "stack_gram",
        [((blocks, columns, columns), f32), ((columns, columns), f32), ((columns, columns), f32),
         ((1, columns), f32)],
        stack,
        flops=2 * fields * fields * cells,
    )

    def inner_image(block):
        return call(
            functools.partial(inner_image_kernel, spans),
            "inner_image",
            [((columns, cells), f32)],
            coef, block,
            flops=2 * 27 * columns * cells,
        )[0]

    last = basis[blocks - 1].reshape(columns, cells)
    around, partial, (stack, own) = neighbours(last, *spans, inner_image(last), (stack, own))
    image, cross = call(
        functools.partial(first_image_kernel, spans),
        "first_image",
        [((columns, cells), bf16), ((4 * columns + 16, 2 * columns), f32)],
        coef, stack, *own, partial, *around,
    )
    cross = whole_sum(cross)
    block, proj, low, rest, square, inverse = call(
        functools.partial(first_solve_kernel, scale),
        "first_solve",
        [((columns, cells), bf16), ((columns, fields), f32), ((columns, columns), f32),
         ((columns, fields), f32), ((columns, columns), f32), ((columns, columns), bf16)],
        cross, stack, image,
    )
    own = call(
        functools.partial(next_gram_kernel, scale),
        "next_gram",
        [((fields, fields), bf16)] * 2,
        cross, rest, square, inverse,
    )
    around, _, _ = neighbours(block, *spans)
    image, cross = call(
        functools.partial(second_image_kernel, spans),
        "second_image",
        [((columns, cells), bf16), ((columns, fields + columns), f32)],
        coef, stack, block, inner_image(block), *around,
    )
    block, proj, low = call(
        functools.partial(second_solve_kernel, scale),
        "second_solve",
        [((columns, *spans), bf16), ((2, columns, fields), f32), ((2, columns, columns), f32)],
        whole_sum(cross), *own, stack, block, image, proj, low,
        scratch=[pltpu.VMEM((columns, cells), bf16)],
    )
    return block, jnp.swapaxes(proj, 1, 2), low


def solution(mesh):
    placed = (P(None, None, "slab", "col", None), P("slab", "col", None), P())
    return jax.shard_map(
        shards,
        mesh=mesh,
        in_specs=placed,
        out_specs=(P(None, "slab", "col", None), P(), P()),
        check_vma=False,
    )
```

```python
import functools
import math

import jax
import jax.numpy as jnp
from jax import lax
from jax.experimental import pallas as pl
from jax.experimental.pallas import tpu as pltpu
from jax.sharding import PartitionSpec as P

NN = (((1,), (0,)), ((), ()))
NT = (((1,), (1,)), ((), ()))
ROWS = 16


def dot(left, right, dims=NN):
    return lax.dot_general(left, right, dims, preferred_element_type=jnp.float32)


def swaps(axis, near, far, closed):
    count = lax.axis_size(axis)
    me = lax.axis_index(axis)
    odd = me % 2 == 1
    pairs = [(i, (i - 1 ^ 1) + 1) for i in range(1, count - 1)]
    if closed:
        pairs += [(0, count - 1), (count - 1, 0)]
    inner = lax.ppermute(near, axis, [(i, i ^ 1) for i in range(count)])
    outer = lax.ppermute(far, axis, pairs)
    if closed:
        outer = jnp.where((me == 0) | (me == count - 1), 0, outer)
    return jnp.where(odd, inner, outer), jnp.where(odd, outer, inner)


def cut_kernel(start, block, part):
    part[...] = block[:, pl.ds(pl.multiple_of(start[0], 128), part.shape[1])]


def cut(block, start, width):
    return pl.pallas_call(
        cut_kernel,
        out_shape=jax.ShapeDtypeStruct((block.shape[0], width), block.dtype),
        in_specs=[
            pl.BlockSpec(memory_space=pltpu.SMEM),
            pl.BlockSpec(memory_space=pltpu.VMEM),
        ],
        out_specs=pl.BlockSpec(memory_space=pltpu.VMEM),
        compiler_params=pltpu.CompilerParams(vmem_limit_bytes=4 * 1024 * 1024),
        name="cut",
    )(start.reshape(1), block)


def neighbours(block, span_x, span_y, depth, meanwhile=None):
    plane = span_y * depth
    top = (span_x - 1) * plane
    odd = lax.axis_index("slab") % 2 == 1
    near = jnp.where(odd, block[:, :plane], block[:, top:])
    far = cut(block, jnp.where(odd, top, 0), plane)
    xlo, xhi = swaps("slab", near, far, False)
    xlo, xhi, meanwhile = lax.optimization_barrier((xlo, xhi, meanwhile))

    def edge(row):
        at = row * depth
        parts = [xlo[:, at : at + depth]]
        parts += [block[:, x * plane + at : x * plane + at + depth] for x in range(span_x)]
        parts += [xhi[:, at : at + depth]]
        return jnp.concatenate(parts, axis=1)

    odd = lax.axis_index("col") % 2 == 1
    upward, downward = edge(span_y - 1), edge(0)
    ylo, yhi = swaps(
        "col", jnp.where(odd, downward, upward), jnp.where(odd, upward, downward), True
    )
    return (xlo, xhi, ylo, yhi), meanwhile


def coefficients_kernel(table, cells, coef):
    classes = table.shape[0]
    lanes = lax.broadcasted_iota(jnp.int32, cells.shape, 1)
    depth = cells.shape[1]
    here = cells[...]
    below = pltpu.roll(here, depth - 1, 1)
    above = pltpu.roll(here, 1, 1)
    maps = (below, here, above)
    keep = (lanes < depth - 1, None, lanes > 0)
    for dz in range(3):
        masks = [maps[dz] == k for k in range(1, classes)]
        for pair in range(9):
            offset = 3 * pair + dz
            value = jnp.full(cells.shape, table[0, offset], jnp.float32)
            for k in range(1, classes):
                value = jnp.where(masks[k - 1], table[k, offset], value)
            if keep[dz] is not None:
                value = jnp.where(keep[dz], value, 0.0)
            coef[offset] = value


def coefficients(table, cell_map):
    span_x, span_y, depth = cell_map.shape
    lines = span_x * span_y
    return pl.pallas_call(
        coefficients_kernel,
        out_shape=jax.ShapeDtypeStruct((27, lines, depth), jnp.float32),
        in_specs=[
            pl.BlockSpec(memory_space=pltpu.SMEM),
            pl.BlockSpec(memory_space=pltpu.VMEM),
        ],
        out_specs=pl.BlockSpec(memory_space=pltpu.VMEM),
        compiler_params=pltpu.CompilerParams(vmem_limit_bytes=4 * 1024 * 1024),
        name="coefficients",
    )(table, cell_map.reshape(lines, depth))


def stencil(coef, spans, columns, line, inner, write):
    span_x, span_y, depth = spans

    def tile(step, carry):
        rows = pl.ds(pl.multiple_of(step * ROWS, ROWS), ROWS)
        held = {}
        for y in range(span_y):
            for x in range(span_x):
                sums = [None, None, None]
                for pair in range(9):
                    x_there, y_there = x + pair // 3 - 1, y + pair % 3 - 1
                    inside = 0 <= x_there < span_x and 0 <= y_there < span_y
                    if inside != inner:
                        continue
                    if (x_there, y_there) not in held:
                        held[x_there, y_there] = line(rows, x_there, y_there)
                    for dz in range(3):
                        at = x * span_y + y
                        term = coef[3 * pair + dz, at : at + 1, :] * held[x_there, y_there]
                        sums[dz] = term if sums[dz] is None else sums[dz] + term
                total = None
                if sums[0] is not None:
                    total = pltpu.roll(sums[0], 1, 1) + pltpu.roll(sums[2], depth - 1, 1)
                    total = sums[1] + total
                write(rows, x, y, total)
        return carry

    lax.fori_loop(0, columns // ROWS, tile, 0)


def inner_image_kernel(spans, coef, fields, partial):
    _, span_y, depth = spans
    columns = partial.shape[0]
    block = fields.at[fields.shape[0] - columns :]

    def here(x, y):
        return pl.ds((x * span_y + y) * depth, depth)

    def write(rows, x, y, total):
        partial[rows, here(x, y)] = total

    def line(rows, x, y):
        return block[rows, here(x, y)].astype(jnp.float32)

    stencil(coef, spans, columns, line, True, write)


def complete(image, partial, coef, spans, xlo, xhi, ylo, yhi):
    span_x, span_y, depth = spans

    def line(rows, x, y):
        if y < 0:
            ref, at = ylo, x + 1
        elif y >= span_y:
            ref, at = yhi, x + 1
        else:
            ref, at = (xlo, y) if x < 0 else (xhi, y)
        return ref[rows, at * depth : (at + 1) * depth].astype(jnp.float32)

    def write(rows, x, y, total):
        there = pl.ds((x * span_y + y) * depth, depth)
        known = partial[rows, there]
        image[rows, there] = (known if total is None else known + total).astype(jnp.bfloat16)

    stencil(coef, spans, image.shape[0], line, False, write)


def places(size):
    return [lax.broadcasted_iota(jnp.int32, (size, size), dim) for dim in (0, 1)]


def diagonal_of(square, axis):
    row, column = places(square.shape[0])
    return jnp.sum(jnp.where(row == column, square, 0.0), axis=axis, keepdims=True)


def two_in_one(one, two):
    row, column = places(one.shape[0])
    return jnp.where(row >= column, one, two), diagonal_of(two, 0)


def both_of(packed, diagonal):
    row, column = places(packed.shape[0])
    turned = packed.T
    two = jnp.where(row < column, packed, turned)
    return jnp.where(row >= column, packed, turned), jnp.where(row == column, diagonal, two)


def stack_gram_kernel(columns, stack, sides, pair, last, diagonal):
    parts = [stack[b * columns : (b + 1) * columns] for b in range(3)]
    sides[0] = dot(parts[0], parts[1], NT)
    sides[1] = dot(parts[0], parts[2], NT)
    sides[2] = dot(parts[1], parts[2], NT)
    pair[...], diagonal[...] = two_in_one(dot(parts[0], parts[0], NT), dot(parts[1], parts[1], NT))
    last[...] = dot(parts[2], parts[2], NT)


def first_image_kernel(
    spans, coef, stack, sides, pair, last, diagonal, partial, xlo, xhi, ylo, yhi, image, cross
):
    columns = image.shape[0]
    complete(image, partial, coef, spans, xlo, xhi, ylo, yhi)
    w = image[...]
    first = dot(w, stack[...], NT)
    corner, own_diagonal = two_in_one(last[...], dot(w, w, NT))
    rows = [
        first[:, : 2 * columns],
        jnp.concatenate([first[:, 2 * columns :], sides[0]], axis=1),
        jnp.concatenate([sides[1], sides[2]], axis=1),
        jnp.concatenate([pair[...], corner], axis=1),
    ]
    for i, row in enumerate(rows):
        cross[i * columns : (i + 1) * columns] = row
    rest = jnp.concatenate([diagonal[...], own_diagonal], axis=1)
    rest = jnp.broadcast_to(rest, (cross.shape[0] - 4 * columns, 2 * columns))
    cross[4 * columns :] = rest


def opened(cross, columns, scale):
    parts = [cross[i * columns : (i + 1) * columns] * scale for i in range(4)]
    diagonals = cross[4 * columns : 4 * columns + 1] * scale
    first = jnp.concatenate([parts[0], parts[1][:, :columns]], axis=1)
    side = parts[1][:, columns:], parts[2][:, :columns], parts[2][:, columns:]
    one, two = both_of(parts[3][:, :columns], diagonals[:, :columns])
    three, square = both_of(parts[3][:, columns:], diagonals[:, columns:])
    gram = [[one, side[0], side[1]], [side[0].T, two, side[2]], [side[1].T, side[2].T, three]]
    gram = jnp.concatenate([jnp.concatenate(row, axis=1) for row in gram], axis=0)
    return first, square, gram


def second_image_kernel(spans, coef, stack, block, partial, xlo, xhi, ylo, yhi, image, cross):
    columns = image.shape[0]
    fields = stack.shape[0]
    complete(image, partial, coef, spans, xlo, xhi, ylo, yhi)
    w = image[...]
    cross[:, : fields - columns] = dot(w, stack[columns:], NT)
    cross[:, fields - columns : fields] = dot(w, block[...], NT)
    cross[:, fields:] = dot(w, w, NT)


def split(values):
    high = values.astype(jnp.bfloat16)
    return high, (values - high.astype(jnp.float32)).astype(jnp.bfloat16)


def dots(lefts, rights, dims=NN):
    return sum(dot(left, right, dims) for left in lefts for right in rights)


def factor(square, sizes, across):
    size = square.shape[0]
    shape = (8, 2 * size)
    sub = lax.broadcasted_iota(jnp.int32, shape, 0)
    unit = lax.broadcasted_iota(jnp.int32, (size, size), 0) == lax.broadcasted_iota(
        jnp.int32, (size, size), 1
    )
    scale = lax.rsqrt(across)
    square = square * lax.rsqrt(sizes) * scale
    whole = jnp.concatenate([square, unit.astype(jnp.float32)], axis=1)
    blocks = [whole[b : b + 8] for b in range(0, size, 8)]
    done = []

    def row_of(values, at):
        return jnp.broadcast_to(values[at : at + 1, :], shape)

    def columns_of(values, first):
        return [
            jnp.broadcast_to(values[:, at : at + 1], shape) for at in range(first, first + 8)
        ]

    for b, here in enumerate(blocks):
        columns = columns_of(here, 8 * b)
        entry = {(i, j): row_of(columns[j], i) for j in range(8) for i in range(j + 1)}
        rows = [row_of(here, i) for i in range(8)]
        scaled = jnp.zeros(shape, jnp.float32)
        solved, ratio = [], {}
        if b + 1 < len(blocks):
            below = columns_of(blocks[b + 1], 8 * b)
        for p in range(0, 8, 2):
            q = p + 1
            first, mixed, last = entry[p, p], entry[p, q], entry[q, q]
            inverse = 1.0 / (first * last - mixed * mixed)

            def solve(one, two):
                return (
                    (last * one - mixed * two) * inverse,
                    (first * two - mixed * one) * inverse,
                )

            for j in range(p + 2, 8):
                ratio[p, j], ratio[q, j] = solve(entry[p, j], entry[q, j])
            for i in range(p + 2, 8):
                for j in range(i, 8):
                    change = entry[p, i] * ratio[p, j] + entry[q, i] * ratio[q, j]
                    entry[i, j] = entry[i, j] - change
                rows[i] = rows[i] - (ratio[p, i] * rows[p] + ratio[q, i] * rows[q])
            solved += solve(rows[p], rows[q])
            if b + 1 < len(blocks):
                change = below[p] * solved[p] + below[q] * solved[q]
                blocks[b + 1] = blocks[b + 1] - change
                for j in range(p + 2, 8):
                    below[j] = below[j] - (below[p] * ratio[p, j] + below[q] * ratio[q, j])
            part = mixed * (1.0 / first)
            scaled = jnp.where(sub == p, rows[p] * lax.rsqrt(first), scaled)
            rest = (rows[q] - part * rows[p]) * lax.rsqrt(last - part * mixed)
            scaled = jnp.where(sub == q, rest, scaled)
        done.append(scaled)
        for p in (4, 2, 0):
            for r in (p, p + 1):
                for j in range(p + 2, 8):
                    solved[r] = solved[r] - ratio[r, j] * solved[j]
        for later in range(b + 2, len(blocks)):
            parts = [one * two for one, two in zip(columns_of(blocks[later], 8 * b), solved)]
            while len(parts) > 1:
                parts = [one + two for one, two in zip(parts[::2], parts[1::2])]
            blocks[later] = blocks[later] - parts[0]
    done = jnp.concatenate(done, axis=0)
    above = lax.broadcasted_iota(jnp.int32, (size, size), 0) <= lax.broadcasted_iota(
        jnp.int32, (size, size), 1
    )
    return jnp.where(above, done[:, :size] * (across * scale), 0.0), done[:, size:] * scale


def project(first, square, own):
    first_parts = split(first)
    first_low = first_parts[0]
    second = first - dots((first_low,), own)
    second_low = second.astype(jnp.bfloat16)
    used = (first_low, second_low)
    sizes = [diagonal_of(square, axis) for axis in (1, 0)]
    square = square - dots(used, first_parts, NT)
    rest = second - dots((second_low,), own)
    square = square - dots(split(rest), used, NT)
    return used, first + second, rest, square, sizes


def first_solve_kernel(scale, cross, stack, image, block, proj, low, rest, square, inverse):
    columns = image.shape[0]
    first, own_square, gram = opened(cross, columns, scale)
    used, proj[...], rest[...], square_here, sizes = project(first, own_square, split(gram))
    square[...] = square_here
    moved = dot(jnp.concatenate(used, axis=0), stack[...])
    w = image[...].astype(jnp.float32) - moved[:columns] - moved[columns:]
    block[...] = w.astype(jnp.bfloat16)
    upper, inverse_here = factor(square_here, *sizes)
    low[...] = upper.T
    inverse_here = inverse_here.astype(jnp.bfloat16)
    inverse[...] = inverse_here
    block[...] = dot(inverse_here, block[...]).astype(jnp.bfloat16)


def next_gram_kernel(scale, cross, rest, square, inverse, high, low):
    columns = square.shape[0]
    kept = rest.shape[1] - columns
    _, _, gram = opened(cross, columns, scale)
    mixed = dots((inverse[...],), split(rest[:, columns:]))
    corner = dots((inverse[...],), split(square[...]))
    corner = dots(split(corner), (inverse[...],), NT)
    for part, (old, side, end) in zip(
        (high, low), zip(split(gram[columns:, columns:]), split(mixed), split(corner))
    ):
        part[:kept, :kept] = old
        part[kept:, :kept] = side
        part[:kept, kept:] = side.T
        part[kept:, kept:] = end


def second_solve_kernel(
    scale, cross, own_high, own_low, stack, last, image, proj_in, low_in, result, proj, low, block
):
    columns = image.shape[0]
    kept = stack.shape[0] - columns
    fields = stack.shape[0]
    sums = cross[...] * scale
    used, proj[1], _, square, sizes = project(
        sums[:, :fields], sums[:, fields:], (own_high[...], own_low[...])
    )
    proj[0] = proj_in[...]
    low[0] = low_in[...]
    both = jnp.concatenate(used, axis=0)
    moved = dot(both[:, :kept], stack[columns:]) + dot(both[:, kept:], last[...])
    w = image[...].astype(jnp.float32) - moved[:columns] - moved[columns:]
    block[...] = w.astype(jnp.bfloat16)
    upper, inverse = factor(square, *sizes)
    low[1] = upper.T
    inverse = inverse.astype(jnp.bfloat16)
    _, span_x, span_y, depth = result.shape
    plane = span_y * depth
    for x in range(span_x):
        part = dot(inverse, block[:, x * plane : (x + 1) * plane])
        result[:, x] = part.reshape(columns, span_y, depth).astype(jnp.bfloat16)


def partner(part, mask):
    axes = ("slab", "col")
    count = lax.axis_size("slab") * lax.axis_size("col")
    return lax.ppermute(part, axes, [(i, i ^ mask) for i in range(count)])


def whole_sum(part):
    cols = lax.axis_size("col")
    count = lax.axis_size("slab") * cols
    index = lax.axis_index("slab") * cols + lax.axis_index("col")
    bit, upper = 1, 0
    while bit < count:
        upper = upper ^ (index // bit % 2)
        bit *= 2
    upper = upper == 1
    half = part.shape[0] // 2
    low, high = part[:half], part[half:]
    part = jnp.where(upper, high, low) + partner(jnp.where(upper, low, high), 1)
    bit = 2
    while bit < count:
        if 2 * bit < count:
            one, two, both = (partner(part, mask) for mask in (bit + 1, 2 * bit + 1, 3 * bit))
            part = (part + one) + (two + both)
            bit *= 4
        else:
            part = part + partner(part, bit + 1)
            bit *= 2
    other = partner(part, 1)
    return jnp.concatenate([jnp.where(upper, other, part), jnp.where(upper, part, other)], axis=0)


def call(kernel, name, outs, *args, flops=0, scratch=()):
    moved = sum(math.prod(arg.shape) * arg.dtype.itemsize for arg in args)
    moved += sum(math.prod(shape) * jnp.dtype(dtype).itemsize for shape, dtype in outs)
    return pl.pallas_call(
        kernel,
        out_shape=[jax.ShapeDtypeStruct(shape, dtype) for shape, dtype in outs],
        in_specs=[pl.BlockSpec(memory_space=pltpu.VMEM)] * len(args),
        out_specs=[pl.BlockSpec(memory_space=pltpu.VMEM)] * len(outs),
        scratch_shapes=scratch,
        compiler_params=pltpu.CompilerParams(vmem_limit_bytes=24 * 1024 * 1024),
        cost_estimate=pl.CostEstimate(flops=flops, bytes_accessed=moved, transcendentals=0),
        name=name,
    )(*args)


def shards(basis, cell_map, table):
    span_x, span_y, depth = cell_map.shape
    blocks, columns = basis.shape[:2]
    cells = span_x * span_y * depth
    fields = blocks * columns
    scale = 1.0 / (cells * lax.axis_size("slab") * lax.axis_size("col"))
    spans = (span_x, span_y, depth)
    f32, bf16 = jnp.float32, jnp.bfloat16

    stack = basis.reshape(fields, cells)
    coef = coefficients(table, cell_map)
    own = call(
        functools.partial(stack_gram_kernel, columns),
        "stack_gram",
        [((blocks, columns, columns), f32), ((columns, columns), f32), ((columns, columns), f32),
         ((1, columns), f32)],
        stack,
        flops=2 * fields * fields * cells,
    )

    def inner_image(block):
        return call(
            functools.partial(inner_image_kernel, spans),
            "inner_image",
            [((columns, cells), f32)],
            coef, block,
            flops=2 * 27 * columns * cells,
        )[0]

    last = basis[blocks - 1].reshape(columns, cells)
    around, (stack, own, partial) = neighbours(last, *spans, (stack, own, inner_image(last)))
    image, cross = call(
        functools.partial(first_image_kernel, spans),
        "first_image",
        [((columns, cells), bf16), ((4 * columns + 16, 2 * columns), f32)],
        coef, stack, *own, partial, *around,
    )
    cross = whole_sum(cross)
    block, proj, low, rest, square, inverse = call(
        functools.partial(first_solve_kernel, scale),
        "first_solve",
        [((columns, cells), bf16), ((columns, fields), f32), ((columns, columns), f32),
         ((columns, fields), f32), ((columns, columns), f32), ((columns, columns), bf16)],
        cross, stack, image,
    )
    own = call(
        functools.partial(next_gram_kernel, scale),
        "next_gram",
        [((fields, fields), bf16)] * 2,
        cross, rest, square, inverse,
    )
    around, _ = neighbours(block, *spans)
    image, cross = call(
        functools.partial(second_image_kernel, spans),
        "second_image",
        [((columns, cells), bf16), ((columns, fields + columns), f32)],
        coef, stack, block, inner_image(block), *around,
    )
    block, proj, low = call(
        functools.partial(second_solve_kernel, scale),
        "second_solve",
        [((columns, *spans), bf16), ((2, columns, fields), f32), ((2, columns, columns), f32)],
        whole_sum(cross), *own, stack, block, image, proj, low,
        scratch=[pltpu.VMEM((columns, cells), bf16)],
    )
    return block, jnp.swapaxes(proj, 1, 2), low


def solution(mesh):
    placed = (P(None, None, "slab", "col", None), P("slab", "col", None), P())
    return jax.shard_map(
        shards,
        mesh=mesh,
        in_specs=placed,
        out_specs=(P(None, "slab", "col", None), P(), P()),
        check_vma=False,
    )
```

```python
import functools
import math

import jax
import jax.numpy as jnp
from jax import lax
from jax.experimental import pallas as pl
from jax.experimental.pallas import tpu as pltpu
from jax.sharding import PartitionSpec as P

NN = (((1,), (0,)), ((), ()))
NT = (((1,), (1,)), ((), ()))
ROWS = 16


def dot(left, right, dims=NN):
    return lax.dot_general(left, right, dims, preferred_element_type=jnp.float32)


def swaps(axis, near, far, closed):
    count = lax.axis_size(axis)
    me = lax.axis_index(axis)
    odd = me % 2 == 1
    pairs = [(i, (i - 1 ^ 1) + 1) for i in range(1, count - 1)]
    if closed:
        pairs += [(0, count - 1), (count - 1, 0)]
    inner = lax.ppermute(near, axis, [(i, i ^ 1) for i in range(count)])
    outer = lax.ppermute(far, axis, pairs)
    if closed:
        outer = jnp.where((me == 0) | (me == count - 1), 0, outer)
    return jnp.where(odd, inner, outer), jnp.where(odd, outer, inner)


def cut_kernel(start, block, part):
    part[...] = block[:, pl.ds(pl.multiple_of(start[0], 128), part.shape[1])]


def cut(block, start, width):
    return pl.pallas_call(
        cut_kernel,
        out_shape=jax.ShapeDtypeStruct((block.shape[0], width), block.dtype),
        in_specs=[
            pl.BlockSpec(memory_space=pltpu.SMEM),
            pl.BlockSpec(memory_space=pltpu.VMEM),
        ],
        out_specs=pl.BlockSpec(memory_space=pltpu.VMEM),
        compiler_params=pltpu.CompilerParams(vmem_limit_bytes=4 * 1024 * 1024),
        name="cut",
    )(start.reshape(1), block)


def neighbours(block, span_x, span_y, depth, meanwhile=None):
    plane = span_y * depth
    top = (span_x - 1) * plane
    odd = lax.axis_index("slab") % 2 == 1
    near = jnp.where(odd, block[:, :plane], block[:, top:])
    far = cut(block, jnp.where(odd, top, 0), plane)
    xlo, xhi = swaps("slab", near, far, False)
    xlo, xhi, meanwhile = lax.optimization_barrier((xlo, xhi, meanwhile))

    def edge(row):
        at = row * depth
        parts = [xlo[:, at : at + depth]]
        parts += [block[:, x * plane + at : x * plane + at + depth] for x in range(span_x)]
        parts += [xhi[:, at : at + depth]]
        return jnp.concatenate(parts, axis=1)

    odd = lax.axis_index("col") % 2 == 1
    upward, downward = edge(span_y - 1), edge(0)
    ylo, yhi = swaps(
        "col", jnp.where(odd, downward, upward), jnp.where(odd, upward, downward), True
    )
    return (xlo, xhi, ylo, yhi), meanwhile


def coefficients_kernel(table, cells, coef):
    classes = table.shape[0]
    lanes = lax.broadcasted_iota(jnp.int32, cells.shape, 1)
    depth = cells.shape[1]
    here = cells[...]
    below = pltpu.roll(here, depth - 1, 1)
    above = pltpu.roll(here, 1, 1)
    maps = (below, here, above)
    keep = (lanes < depth - 1, None, lanes > 0)
    for dz in range(3):
        masks = [maps[dz] == k for k in range(1, classes)]
        for pair in range(9):
            offset = 3 * pair + dz
            value = jnp.full(cells.shape, table[0, offset], jnp.float32)
            for k in range(1, classes):
                value = jnp.where(masks[k - 1], table[k, offset], value)
            if keep[dz] is not None:
                value = jnp.where(keep[dz], value, 0.0)
            coef[offset] = value


def coefficients(table, cell_map):
    span_x, span_y, depth = cell_map.shape
    lines = span_x * span_y
    return pl.pallas_call(
        coefficients_kernel,
        out_shape=jax.ShapeDtypeStruct((27, lines, depth), jnp.float32),
        in_specs=[
            pl.BlockSpec(memory_space=pltpu.SMEM),
            pl.BlockSpec(memory_space=pltpu.VMEM),
        ],
        out_specs=pl.BlockSpec(memory_space=pltpu.VMEM),
        compiler_params=pltpu.CompilerParams(vmem_limit_bytes=4 * 1024 * 1024),
        name="coefficients",
    )(table, cell_map.reshape(lines, depth))


def stencil(coef, spans, columns, line, inner, write):
    span_x, span_y, depth = spans

    def tile(step, carry):
        rows = pl.ds(pl.multiple_of(step * ROWS, ROWS), ROWS)
        held = {}
        for y in range(span_y):
            for x in range(span_x):
                sums = [None, None, None]
                for pair in range(9):
                    x_there, y_there = x + pair // 3 - 1, y + pair % 3 - 1
                    inside = 0 <= x_there < span_x and 0 <= y_there < span_y
                    if inside != inner:
                        continue
                    if (x_there, y_there) not in held:
                        held[x_there, y_there] = line(rows, x_there, y_there)
                    for dz in range(3):
                        at = x * span_y + y
                        term = coef[3 * pair + dz, at : at + 1, :] * held[x_there, y_there]
                        sums[dz] = term if sums[dz] is None else sums[dz] + term
                total = None
                if sums[0] is not None:
                    total = pltpu.roll(sums[0], 1, 1) + pltpu.roll(sums[2], depth - 1, 1)
                    total = sums[1] + total
                write(rows, x, y, total)
        return carry

    lax.fori_loop(0, columns // ROWS, tile, 0)


def inner_image_kernel(spans, coef, fields, partial):
    _, span_y, depth = spans
    columns = partial.shape[0]
    block = fields.at[fields.shape[0] - columns :]

    def here(x, y):
        return pl.ds((x * span_y + y) * depth, depth)

    def write(rows, x, y, total):
        partial[rows, here(x, y)] = total

    def line(rows, x, y):
        return block[rows, here(x, y)].astype(jnp.float32)

    stencil(coef, spans, columns, line, True, write)


def complete(image, partial, coef, spans, xlo, xhi, ylo, yhi):
    span_x, span_y, depth = spans

    def line(rows, x, y):
        if y < 0:
            ref, at = ylo, x + 1
        elif y >= span_y:
            ref, at = yhi, x + 1
        else:
            ref, at = (xlo, y) if x < 0 else (xhi, y)
        return ref[rows, at * depth : (at + 1) * depth].astype(jnp.float32)

    def write(rows, x, y, total):
        there = pl.ds((x * span_y + y) * depth, depth)
        known = partial[rows, there]
        image[rows, there] = (known if total is None else known + total).astype(jnp.bfloat16)

    stencil(coef, spans, image.shape[0], line, False, write)


def places(size):
    return [lax.broadcasted_iota(jnp.int32, (size, size), dim) for dim in (0, 1)]


def diagonal_of(square, axis):
    row, column = places(square.shape[0])
    return jnp.sum(jnp.where(row == column, square, 0.0), axis=axis, keepdims=True)


def two_in_one(one, two):
    row, column = places(one.shape[0])
    return jnp.where(row >= column, one, two), diagonal_of(two, 0)


def both_of(packed, diagonal):
    row, column = places(packed.shape[0])
    turned = packed.T
    two = jnp.where(row < column, packed, turned)
    return jnp.where(row >= column, packed, turned), jnp.where(row == column, diagonal, two)


def stack_gram_kernel(columns, stack, sides, pair, last, diagonal):
    parts = [stack[b * columns : (b + 1) * columns] for b in range(3)]
    sides[0] = dot(parts[0], parts[1], NT)
    sides[1] = dot(parts[0], parts[2], NT)
    sides[2] = dot(parts[1], parts[2], NT)
    pair[...], diagonal[...] = two_in_one(dot(parts[0], parts[0], NT), dot(parts[1], parts[1], NT))
    last[...] = dot(parts[2], parts[2], NT)


def first_image_kernel(
    spans, coef, stack, sides, pair, last, diagonal, partial, xlo, xhi, ylo, yhi, image, cross
):
    columns = image.shape[0]
    complete(image, partial, coef, spans, xlo, xhi, ylo, yhi)
    w = image[...]
    first = dot(stack[...], w, NT).T
    corner, own_diagonal = two_in_one(last[...], dot(w, w, NT))
    rows = [
        first[:, : 2 * columns],
        jnp.concatenate([first[:, 2 * columns :], sides[0]], axis=1),
        jnp.concatenate([sides[1], sides[2]], axis=1),
        jnp.concatenate([pair[...], corner], axis=1),
    ]
    for i, row in enumerate(rows):
        cross[i * columns : (i + 1) * columns] = row
    rest = jnp.concatenate([diagonal[...], own_diagonal], axis=1)
    rest = jnp.broadcast_to(rest, (cross.shape[0] - 4 * columns, 2 * columns))
    cross[4 * columns :] = rest


def opened(cross, columns, scale):
    parts = [cross[i * columns : (i + 1) * columns] * scale for i in range(4)]
    diagonals = cross[4 * columns : 4 * columns + 1] * scale
    first = jnp.concatenate([parts[0], parts[1][:, :columns]], axis=1)
    side = parts[1][:, columns:], parts[2][:, :columns], parts[2][:, columns:]
    one, two = both_of(parts[3][:, :columns], diagonals[:, :columns])
    three, square = both_of(parts[3][:, columns:], diagonals[:, columns:])
    gram = [[one, side[0], side[1]], [side[0].T, two, side[2]], [side[1].T, side[2].T, three]]
    gram = jnp.concatenate([jnp.concatenate(row, axis=1) for row in gram], axis=0)
    return first, square, gram


def second_image_kernel(spans, coef, stack, block, partial, xlo, xhi, ylo, yhi, image, cross):
    columns = image.shape[0]
    fields = stack.shape[0]
    complete(image, partial, coef, spans, xlo, xhi, ylo, yhi)
    w = image[...]
    cross[:, : fields - columns] = dot(stack[columns:], w, NT).T
    cross[:, fields - columns : fields] = dot(block[...], w, NT).T
    cross[:, fields:] = dot(w, w, NT)


def split(values):
    high = values.astype(jnp.bfloat16)
    return high, (values - high.astype(jnp.float32)).astype(jnp.bfloat16)


def dots(lefts, rights, dims=NN):
    return sum(dot(left, right, dims) for left in lefts for right in rights)


def factor(square, sizes, across):
    size = square.shape[0]
    shape = (8, 2 * size)
    sub = lax.broadcasted_iota(jnp.int32, shape, 0)
    unit = lax.broadcasted_iota(jnp.int32, (size, size), 0) == lax.broadcasted_iota(
        jnp.int32, (size, size), 1
    )
    scale = lax.rsqrt(across)
    square = square * lax.rsqrt(sizes) * scale
    whole = jnp.concatenate([square, unit.astype(jnp.float32)], axis=1)
    blocks = [whole[b : b + 8] for b in range(0, size, 8)]
    done = []

    def row_of(values, at):
        return jnp.broadcast_to(values[at : at + 1, :], shape)

    def columns_of(values, first):
        return [
            jnp.broadcast_to(values[:, at : at + 1], shape) for at in range(first, first + 8)
        ]

    for b, here in enumerate(blocks):
        columns = columns_of(here, 8 * b)
        entry = {(i, j): row_of(columns[j], i) for j in range(8) for i in range(j + 1)}
        rows = [row_of(here, i) for i in range(8)]
        scaled = jnp.zeros(shape, jnp.float32)
        solved, ratio = [], {}
        if b + 1 < len(blocks):
            below = columns_of(blocks[b + 1], 8 * b)
        for p in range(0, 8, 2):
            q = p + 1
            first, mixed, last = entry[p, p], entry[p, q], entry[q, q]
            inverse = 1.0 / (first * last - mixed * mixed)

            def solve(one, two):
                return (
                    (last * one - mixed * two) * inverse,
                    (first * two - mixed * one) * inverse,
                )

            for j in range(p + 2, 8):
                ratio[p, j], ratio[q, j] = solve(entry[p, j], entry[q, j])
            for i in range(p + 2, 8):
                for j in range(i, 8):
                    change = entry[p, i] * ratio[p, j] + entry[q, i] * ratio[q, j]
                    entry[i, j] = entry[i, j] - change
                rows[i] = rows[i] - (ratio[p, i] * rows[p] + ratio[q, i] * rows[q])
            solved += solve(rows[p], rows[q])
            if b + 1 < len(blocks):
                change = below[p] * solved[p] + below[q] * solved[q]
                blocks[b + 1] = blocks[b + 1] - change
                for j in range(p + 2, 8):
                    below[j] = below[j] - (below[p] * ratio[p, j] + below[q] * ratio[q, j])
            part = mixed * (1.0 / first)
            scaled = jnp.where(sub == p, rows[p] * lax.rsqrt(first), scaled)
            rest = (rows[q] - part * rows[p]) * lax.rsqrt(last - part * mixed)
            scaled = jnp.where(sub == q, rest, scaled)
        done.append(scaled)
        for p in (4, 2, 0):
            for r in (p, p + 1):
                for j in range(p + 2, 8):
                    solved[r] = solved[r] - ratio[r, j] * solved[j]
        for later in range(b + 2, len(blocks)):
            parts = [one * two for one, two in zip(columns_of(blocks[later], 8 * b), solved)]
            while len(parts) > 1:
                parts = [one + two for one, two in zip(parts[::2], parts[1::2])]
            blocks[later] = blocks[later] - parts[0]
    done = jnp.concatenate(done, axis=0)
    above = lax.broadcasted_iota(jnp.int32, (size, size), 0) <= lax.broadcasted_iota(
        jnp.int32, (size, size), 1
    )
    return jnp.where(above, done[:, :size] * (across * scale), 0.0), done[:, size:] * scale


def project(first, square, own):
    first_parts = split(first)
    first_low = first_parts[0]
    second = first - dots((first_low,), own)
    second_low = second.astype(jnp.bfloat16)
    used = (first_low, second_low)
    sizes = [diagonal_of(square, axis) for axis in (1, 0)]
    square = square - dots(used, first_parts, NT)
    rest = second - dots((second_low,), own)
    square = square - dots(split(rest), used, NT)
    return used, first + second, rest, square, sizes


def first_solve_kernel(scale, cross, stack, image, block, proj, low, rest, square, inverse):
    columns = image.shape[0]
    first, own_square, gram = opened(cross, columns, scale)
    used, proj[...], rest[...], square_here, sizes = project(first, own_square, split(gram))
    square[...] = square_here
    moved = dot(jnp.concatenate(used, axis=0), stack[...])
    w = image[...].astype(jnp.float32) - moved[:columns] - moved[columns:]
    block[...] = w.astype(jnp.bfloat16)
    upper, inverse_here = factor(square_here, *sizes)
    low[...] = upper.T
    inverse_here = inverse_here.astype(jnp.bfloat16)
    inverse[...] = inverse_here
    block[...] = dot(inverse_here, block[...]).astype(jnp.bfloat16)


def next_gram_kernel(scale, cross, rest, square, inverse, high, low):
    columns = square.shape[0]
    kept = rest.shape[1] - columns
    _, _, gram = opened(cross, columns, scale)
    mixed = dots((inverse[...],), split(rest[:, columns:]))
    corner = dots((inverse[...],), split(square[...]))
    corner = dots(split(corner), (inverse[...],), NT)
    for part, (old, side, end) in zip(
        (high, low), zip(split(gram[columns:, columns:]), split(mixed), split(corner))
    ):
        part[:kept, :kept] = old
        part[kept:, :kept] = side
        part[:kept, kept:] = side.T
        part[kept:, kept:] = end


def second_solve_kernel(
    scale, cross, own_high, own_low, stack, last, image, proj_in, low_in, result, proj, low, block
):
    columns = image.shape[0]
    kept = stack.shape[0] - columns
    fields = stack.shape[0]
    sums = cross[...] * scale
    used, proj[1], _, square, sizes = project(
        sums[:, :fields], sums[:, fields:], (own_high[...], own_low[...])
    )
    proj[0] = proj_in[...]
    low[0] = low_in[...]
    both = jnp.concatenate(used, axis=0)
    moved = dot(both[:, :kept], stack[columns:]) + dot(both[:, kept:], last[...])
    w = image[...].astype(jnp.float32) - moved[:columns] - moved[columns:]
    block[...] = w.astype(jnp.bfloat16)
    upper, inverse = factor(square, *sizes)
    low[1] = upper.T
    inverse = inverse.astype(jnp.bfloat16)
    _, span_x, span_y, depth = result.shape
    plane = span_y * depth
    for x in range(span_x):
        part = dot(inverse, block[:, x * plane : (x + 1) * plane])
        result[:, x] = part.reshape(columns, span_y, depth).astype(jnp.bfloat16)


def partner(part, mask):
    axes = ("slab", "col")
    count = lax.axis_size("slab") * lax.axis_size("col")
    return lax.ppermute(part, axes, [(i, i ^ mask) for i in range(count)])


def whole_sum(part):
    cols = lax.axis_size("col")
    count = lax.axis_size("slab") * cols
    index = lax.axis_index("slab") * cols + lax.axis_index("col")
    bit, upper = 1, 0
    while bit < count:
        upper = upper ^ (index // bit % 2)
        bit *= 2
    upper = upper == 1
    half = part.shape[0] // 2
    low, high = part[:half], part[half:]
    part = jnp.where(upper, high, low) + partner(jnp.where(upper, low, high), 1)
    bit = 2
    while bit < count:
        if 2 * bit < count:
            one, two, both = (partner(part, mask) for mask in (bit + 1, 2 * bit + 1, 3 * bit))
            part = (part + both) + (two + one)
            bit *= 4
        else:
            part = part + partner(part, bit + 1)
            bit *= 2
    other = partner(part, 1)
    return jnp.concatenate([jnp.where(upper, other, part), jnp.where(upper, part, other)], axis=0)


def call(kernel, name, outs, *args, flops=0, scratch=()):
    moved = sum(math.prod(arg.shape) * arg.dtype.itemsize for arg in args)
    moved += sum(math.prod(shape) * jnp.dtype(dtype).itemsize for shape, dtype in outs)
    return pl.pallas_call(
        kernel,
        out_shape=[jax.ShapeDtypeStruct(shape, dtype) for shape, dtype in outs],
        in_specs=[pl.BlockSpec(memory_space=pltpu.VMEM)] * len(args),
        out_specs=[pl.BlockSpec(memory_space=pltpu.VMEM)] * len(outs),
        scratch_shapes=scratch,
        compiler_params=pltpu.CompilerParams(vmem_limit_bytes=24 * 1024 * 1024),
        cost_estimate=pl.CostEstimate(flops=flops, bytes_accessed=moved, transcendentals=0),
        name=name,
    )(*args)


def shards(basis, cell_map, table):
    span_x, span_y, depth = cell_map.shape
    blocks, columns = basis.shape[:2]
    cells = span_x * span_y * depth
    fields = blocks * columns
    scale = 1.0 / (cells * lax.axis_size("slab") * lax.axis_size("col"))
    spans = (span_x, span_y, depth)
    f32, bf16 = jnp.float32, jnp.bfloat16

    stack = basis.reshape(fields, cells)
    coef = coefficients(table, cell_map)
    own = call(
        functools.partial(stack_gram_kernel, columns),
        "stack_gram",
        [((blocks, columns, columns), f32), ((columns, columns), f32), ((columns, columns), f32),
         ((1, columns), f32)],
        stack,
        flops=2 * fields * fields * cells,
    )

    def inner_image(block):
        return call(
            functools.partial(inner_image_kernel, spans),
            "inner_image",
            [((columns, cells), f32)],
            coef, block,
            flops=2 * 27 * columns * cells,
        )[0]

    last = basis[blocks - 1].reshape(columns, cells)
    around, (stack, own, partial) = neighbours(last, *spans, (stack, own, inner_image(last)))
    image, cross = call(
        functools.partial(first_image_kernel, spans),
        "first_image",
        [((columns, cells), bf16), ((4 * columns + 16, 2 * columns), f32)],
        coef, stack, *own, partial, *around,
    )
    cross = whole_sum(cross)
    block, proj, low, rest, square, inverse = call(
        functools.partial(first_solve_kernel, scale),
        "first_solve",
        [((columns, cells), bf16), ((columns, fields), f32), ((columns, columns), f32),
         ((columns, fields), f32), ((columns, columns), f32), ((columns, columns), bf16)],
        cross, stack, image,
    )
    own = call(
        functools.partial(next_gram_kernel, scale),
        "next_gram",
        [((fields, fields), bf16)] * 2,
        cross, rest, square, inverse,
    )
    around, _ = neighbours(block, *spans)
    image, cross = call(
        functools.partial(second_image_kernel, spans),
        "second_image",
        [((columns, cells), bf16), ((columns, fields + columns), f32)],
        coef, stack, block, inner_image(block), *around,
    )
    block, proj, low = call(
        functools.partial(second_solve_kernel, scale),
        "second_solve",
        [((columns, *spans), bf16), ((2, columns, fields), f32), ((2, columns, columns), f32)],
        whole_sum(cross), *own, stack, block, image, proj, low,
        scratch=[pltpu.VMEM((columns, cells), bf16)],
    )
    return block, jnp.swapaxes(proj, 1, 2), low


def solution(mesh):
    placed = (P(None, None, "slab", "col", None), P("slab", "col", None), P())
    return jax.shard_map(
        shards,
        mesh=mesh,
        in_specs=placed,
        out_specs=(P(None, "slab", "col", None), P(), P()),
        check_vma=False,
    )
```

```python
import functools
import math

import jax
import jax.numpy as jnp
from jax import lax
from jax.experimental import pallas as pl
from jax.experimental.pallas import tpu as pltpu
from jax.sharding import PartitionSpec as P

NN = (((1,), (0,)), ((), ()))
NT = (((1,), (1,)), ((), ()))
ROWS = 16


def dot(left, right, dims=NN):
    return lax.dot_general(left, right, dims, preferred_element_type=jnp.float32)


def swap_pairs(axis, closed):
    count = lax.axis_size(axis)
    near = [(i, i ^ 1) for i in range(count)]
    far = [(i, (i - 1 ^ 1) + 1) for i in range(1, count - 1)]
    if closed:
        far += [(0, count - 1), (count - 1, 0)]
    return near, far


def cut_kernel(depth, start, block, ends, rest):
    lines = rest.shape[1] // depth + 2
    for ref, at, line in ((ends, 0, 0), (ends, 1, lines - 1), (rest, 0, 1)):
        width = depth if ref is ends else rest.shape[1]
        there = pl.ds(pl.multiple_of(start[0] + line * depth, 128), width)
        ref[:, at * depth : at * depth + width] = block[:, there]


def cut(block, start, lines, depth):
    columns = block.shape[0]
    return pl.pallas_call(
        functools.partial(cut_kernel, depth),
        out_shape=[
            jax.ShapeDtypeStruct((columns, count * depth), block.dtype) for count in (2, lines - 2)
        ],
        in_specs=[
            pl.BlockSpec(memory_space=pltpu.SMEM),
            pl.BlockSpec(memory_space=pltpu.VMEM),
        ],
        out_specs=[pl.BlockSpec(memory_space=pltpu.VMEM)] * 2,
        compiler_params=pltpu.CompilerParams(vmem_limit_bytes=4 * 1024 * 1024),
        name="cut",
    )(start.reshape(1), block)


def neighbours(block, span_x, span_y, depth, beside=None, meanwhile=None):
    plane = span_y * depth
    top = (span_x - 1) * plane
    odd = lax.axis_index("slab") % 2 == 1
    near_pairs, far_pairs = swap_pairs("slab", False)
    far_ends, far_rest = cut(block, jnp.where(odd, top, 0), span_y, depth)
    near = lax.ppermute(
        jnp.where(odd, block[:, :plane], block[:, top:]), "slab", near_pairs
    )
    far_ends = lax.ppermute(far_ends, "slab", far_pairs)
    far_rest, beside = lax.optimization_barrier((far_rest, beside))
    far_rest = lax.ppermute(far_rest, "slab", far_pairs)

    def sort(near, far, odd):
        return jnp.where(odd, near, far), jnp.where(odd, far, near)

    far_ends, near = lax.optimization_barrier((far_ends, near))
    near_ends = jnp.concatenate([near[:, :depth], near[:, plane - depth :]], axis=1)
    xlo_ends, xhi_ends = sort(near_ends, far_ends, odd)
    xlo_ends, xhi_ends, meanwhile = lax.optimization_barrier((xlo_ends, xhi_ends, meanwhile))

    def edge(last):
        at = (span_y - 1) * depth * last
        parts = [xlo_ends[:, last * depth : (last + 1) * depth]]
        parts += [block[:, x * plane + at : x * plane + at + depth] for x in range(span_x)]
        parts += [xhi_ends[:, last * depth : (last + 1) * depth]]
        return jnp.concatenate(parts, axis=1)

    me = lax.axis_index("col")
    odd_col = me % 2 == 1
    near_pairs, far_pairs = swap_pairs("col", True)
    upward, downward = edge(1), edge(0)
    near_y = lax.ppermute(jnp.where(odd_col, downward, upward), "col", near_pairs)
    far_y = lax.ppermute(jnp.where(odd_col, upward, downward), "col", far_pairs)
    far_y = jnp.where((me == 0) | (me == lax.axis_size("col") - 1), 0, far_y)
    ylo, yhi = sort(near_y, far_y, odd_col)
    xlo, xhi = sort(near[:, depth : plane - depth], far_rest, odd)
    return (xlo_ends, xlo, xhi_ends, xhi, ylo, yhi), beside, meanwhile


def coefficients_kernel(table, cells, coef):
    classes = table.shape[0]
    lanes = lax.broadcasted_iota(jnp.int32, cells.shape, 1)
    depth = cells.shape[1]
    here = cells[...]
    below = pltpu.roll(here, depth - 1, 1)
    above = pltpu.roll(here, 1, 1)
    maps = (below, here, above)
    keep = (lanes < depth - 1, None, lanes > 0)
    for dz in range(3):
        masks = [maps[dz] == k for k in range(1, classes)]
        for pair in range(9):
            offset = 3 * pair + dz
            value = jnp.full(cells.shape, table[0, offset], jnp.float32)
            for k in range(1, classes):
                value = jnp.where(masks[k - 1], table[k, offset], value)
            if keep[dz] is not None:
                value = jnp.where(keep[dz], value, 0.0)
            coef[offset] = value


def coefficients(table, cell_map):
    span_x, span_y, depth = cell_map.shape
    lines = span_x * span_y
    return pl.pallas_call(
        coefficients_kernel,
        out_shape=jax.ShapeDtypeStruct((27, lines, depth), jnp.float32),
        in_specs=[
            pl.BlockSpec(memory_space=pltpu.SMEM),
            pl.BlockSpec(memory_space=pltpu.VMEM),
        ],
        out_specs=pl.BlockSpec(memory_space=pltpu.VMEM),
        compiler_params=pltpu.CompilerParams(vmem_limit_bytes=4 * 1024 * 1024),
        name="coefficients",
    )(table, cell_map.reshape(lines, depth))


def stencil(coef, spans, columns, line, inner, write):
    span_x, span_y, depth = spans

    def tile(step, carry):
        rows = pl.ds(pl.multiple_of(step * ROWS, ROWS), ROWS)
        held = {}
        for y in range(span_y):
            for x in range(span_x):
                sums = [None, None, None]
                for pair in range(9):
                    x_there, y_there = x + pair // 3 - 1, y + pair % 3 - 1
                    inside = 0 <= x_there < span_x and 0 <= y_there < span_y
                    if inside != inner:
                        continue
                    if (x_there, y_there) not in held:
                        held[x_there, y_there] = line(rows, x_there, y_there)
                    for dz in range(3):
                        at = x * span_y + y
                        term = coef[3 * pair + dz, at : at + 1, :] * held[x_there, y_there]
                        sums[dz] = term if sums[dz] is None else sums[dz] + term
                total = None
                if sums[0] is not None:
                    total = pltpu.roll(sums[0], 1, 1) + pltpu.roll(sums[2], depth - 1, 1)
                    total = sums[1] + total
                write(rows, x, y, total)
        return carry

    lax.fori_loop(0, columns // ROWS, tile, 0)


def inner_image_kernel(spans, coef, fields, partial):
    _, span_y, depth = spans
    columns = partial.shape[0]
    block = fields.at[fields.shape[0] - columns :]

    def here(x, y):
        return pl.ds((x * span_y + y) * depth, depth)

    def write(rows, x, y, total):
        partial[rows, here(x, y)] = total

    def line(rows, x, y):
        return block[rows, here(x, y)].astype(jnp.float32)

    stencil(coef, spans, columns, line, True, write)


def complete(image, partial, coef, spans, xlo_ends, xlo, xhi_ends, xhi, ylo, yhi):
    span_x, span_y, depth = spans

    def line(rows, x, y):
        if y < 0:
            ref, at = ylo, x + 1
        elif y >= span_y:
            ref, at = yhi, x + 1
        elif y in (0, span_y - 1):
            ref, at = (xlo_ends if x < 0 else xhi_ends), int(y > 0)
        else:
            ref, at = (xlo if x < 0 else xhi), y - 1
        return ref[rows, at * depth : (at + 1) * depth].astype(jnp.float32)

    def write(rows, x, y, total):
        there = pl.ds((x * span_y + y) * depth, depth)
        known = partial[rows, there]
        image[rows, there] = (known if total is None else known + total).astype(jnp.bfloat16)

    stencil(coef, spans, image.shape[0], line, False, write)


def places(size):
    return [lax.broadcasted_iota(jnp.int32, (size, size), dim) for dim in (0, 1)]


def diagonal_of(square, axis):
    row, column = places(square.shape[0])
    return jnp.sum(jnp.where(row == column, square, 0.0), axis=axis, keepdims=True)


def two_in_one(one, two):
    row, column = places(one.shape[0])
    return jnp.where(row >= column, one, two), diagonal_of(two, 0)


def both_of(packed, diagonal):
    row, column = places(packed.shape[0])
    turned = packed.T
    two = jnp.where(row < column, packed, turned)
    return jnp.where(row >= column, packed, turned), jnp.where(row == column, diagonal, two)


def stack_gram_kernel(columns, stack, sides, pair, last, diagonal):
    parts = [stack[b * columns : (b + 1) * columns] for b in range(3)]
    sides[0] = dot(parts[0], parts[1], NT)
    sides[1] = dot(parts[0], parts[2], NT)
    sides[2] = dot(parts[1], parts[2], NT)
    pair[...], diagonal[...] = two_in_one(dot(parts[0], parts[0], NT), dot(parts[1], parts[1], NT))
    last[...] = dot(parts[2], parts[2], NT)


def first_image_kernel(
    spans, coef, stack, sides, pair, last, diagonal, partial, *around_and_outs
):
    *around, image, cross = around_and_outs
    columns = image.shape[0]
    complete(image, partial, coef, spans, *around)
    w = image[...]
    first = dot(w, stack[...], NT)
    corner, own_diagonal = two_in_one(last[...], dot(w, w, NT))
    rows = [
        first[:, : 2 * columns],
        jnp.concatenate([first[:, 2 * columns :], sides[0]], axis=1),
        jnp.concatenate([sides[1], sides[2]], axis=1),
        jnp.concatenate([pair[...], corner], axis=1),
    ]
    for i, row in enumerate(rows):
        cross[i * columns : (i + 1) * columns] = row
    rest = jnp.concatenate([diagonal[...], own_diagonal], axis=1)
    rest = jnp.broadcast_to(rest, (cross.shape[0] - 4 * columns, 2 * columns))
    cross[4 * columns :] = rest


def opened(cross, columns, scale):
    parts = [cross[i * columns : (i + 1) * columns] * scale for i in range(4)]
    diagonals = cross[4 * columns : 4 * columns + 1] * scale
    first = jnp.concatenate([parts[0], parts[1][:, :columns]], axis=1)
    side = parts[1][:, columns:], parts[2][:, :columns], parts[2][:, columns:]
    one, two = both_of(parts[3][:, :columns], diagonals[:, :columns])
    three, square = both_of(parts[3][:, columns:], diagonals[:, columns:])
    gram = [[one, side[0], side[1]], [side[0].T, two, side[2]], [side[1].T, side[2].T, three]]
    gram = jnp.concatenate([jnp.concatenate(row, axis=1) for row in gram], axis=0)
    return first, square, gram


def second_image_kernel(spans, coef, stack, block, partial, *around_and_outs):
    *around, image, cross = around_and_outs
    columns = image.shape[0]
    fields = stack.shape[0]
    complete(image, partial, coef, spans, *around)
    w = image[...]
    cross[:, : fields - columns] = dot(w, stack[columns:], NT)
    cross[:, fields - columns : fields] = dot(w, block[...], NT)
    cross[:, fields:] = dot(w, w, NT)


def split(values):
    high = values.astype(jnp.bfloat16)
    return high, (values - high.astype(jnp.float32)).astype(jnp.bfloat16)


def dots(lefts, rights, dims=NN):
    return sum(dot(left, right, dims) for left in lefts for right in rights)


def factor(square, sizes, across):
    size = square.shape[0]
    shape = (8, 2 * size)
    sub = lax.broadcasted_iota(jnp.int32, shape, 0)
    unit = lax.broadcasted_iota(jnp.int32, (size, size), 0) == lax.broadcasted_iota(
        jnp.int32, (size, size), 1
    )
    scale = lax.rsqrt(across)
    square = square * lax.rsqrt(sizes) * scale
    whole = jnp.concatenate([square, unit.astype(jnp.float32)], axis=1)
    blocks = [whole[b : b + 8] for b in range(0, size, 8)]
    done = []

    def row_of(values, at):
        return jnp.broadcast_to(values[at : at + 1, :], shape)

    def columns_of(values, first):
        return [
            jnp.broadcast_to(values[:, at : at + 1], shape) for at in range(first, first + 8)
        ]

    for b, here in enumerate(blocks):
        columns = columns_of(here, 8 * b)
        entry = {(i, j): row_of(columns[j], i) for j in range(8) for i in range(j + 1)}
        rows = [row_of(here, i) for i in range(8)]
        scaled = jnp.zeros(shape, jnp.float32)
        solved, ratio = [], {}
        if b + 1 < len(blocks):
            below = columns_of(blocks[b + 1], 8 * b)
        for p in range(0, 8, 2):
            q = p + 1
            first, mixed, last = entry[p, p], entry[p, q], entry[q, q]
            inverse = 1.0 / (first * last - mixed * mixed)

            def solve(one, two):
                return (
                    (last * one - mixed * two) * inverse,
                    (first * two - mixed * one) * inverse,
                )

            for j in range(p + 2, 8):
                ratio[p, j], ratio[q, j] = solve(entry[p, j], entry[q, j])
            for i in range(p + 2, 8):
                for j in range(i, 8):
                    change = entry[p, i] * ratio[p, j] + entry[q, i] * ratio[q, j]
                    entry[i, j] = entry[i, j] - change
                rows[i] = rows[i] - (ratio[p, i] * rows[p] + ratio[q, i] * rows[q])
            solved += solve(rows[p], rows[q])
            if b + 1 < len(blocks):
                change = below[p] * solved[p] + below[q] * solved[q]
                blocks[b + 1] = blocks[b + 1] - change
                for j in range(p + 2, 8):
                    below[j] = below[j] - (below[p] * ratio[p, j] + below[q] * ratio[q, j])
            part = mixed * (1.0 / first)
            scaled = jnp.where(sub == p, rows[p] * lax.rsqrt(first), scaled)
            rest = (rows[q] - part * rows[p]) * lax.rsqrt(last - part * mixed)
            scaled = jnp.where(sub == q, rest, scaled)
        done.append(scaled)
        for p in (4, 2, 0):
            for r in (p, p + 1):
                for j in range(p + 2, 8):
                    solved[r] = solved[r] - ratio[r, j] * solved[j]
        for later in range(b + 2, len(blocks)):
            parts = [one * two for one, two in zip(columns_of(blocks[later], 8 * b), solved)]
            while len(parts) > 1:
                parts = [one + two for one, two in zip(parts[::2], parts[1::2])]
            blocks[later] = blocks[later] - parts[0]
    done = jnp.concatenate(done, axis=0)
    above = lax.broadcasted_iota(jnp.int32, (size, size), 0) <= lax.broadcasted_iota(
        jnp.int32, (size, size), 1
    )
    return jnp.where(above, done[:, :size] * (across * scale), 0.0), done[:, size:] * scale


def project(first, square, own):
    first_parts = split(first)
    first_low = first_parts[0]
    second = first - dots((first_low,), own)
    second_low = second.astype(jnp.bfloat16)
    used = (first_low, second_low)
    sizes = [diagonal_of(square, axis) for axis in (1, 0)]
    square = square - dots(used, first_parts, NT)
    rest = second - dots((second_low,), own)
    square = square - dots(split(rest), used, NT)
    return used, first + second, rest, square, sizes


def first_solve_kernel(scale, cross, stack, image, block, proj, low, rest, square, inverse):
    columns = image.shape[0]
    first, own_square, gram = opened(cross, columns, scale)
    used, proj[...], rest[...], square_here, sizes = project(first, own_square, split(gram))
    square[...] = square_here
    moved = dot(jnp.concatenate(used, axis=0), stack[...])
    w = image[...].astype(jnp.float32) - moved[:columns] - moved[columns:]
    block[...] = w.astype(jnp.bfloat16)
    upper, inverse_here = factor(square_here, *sizes)
    low[...] = upper.T
    inverse_here = inverse_here.astype(jnp.bfloat16)
    inverse[...] = inverse_here
    block[...] = dot(inverse_here, block[...]).astype(jnp.bfloat16)


def next_gram_kernel(scale, cross, rest, square, inverse, high, low):
    columns = square.shape[0]
    kept = rest.shape[1] - columns
    _, _, gram = opened(cross, columns, scale)
    mixed = dots((inverse[...],), split(rest[:, columns:]))
    corner = dots((inverse[...],), split(square[...]))
    corner = dots(split(corner), (inverse[...],), NT)
    for part, (old, side, end) in zip(
        (high, low), zip(split(gram[columns:, columns:]), split(mixed), split(corner))
    ):
        part[:kept, :kept] = old
        part[kept:, :kept] = side
        part[:kept, kept:] = side.T
        part[kept:, kept:] = end


def second_solve_kernel(
    scale, cross, own_high, own_low, stack, last, image, proj_in, low_in, result, proj, low, block
):
    columns = image.shape[0]
    kept = stack.shape[0] - columns
    fields = stack.shape[0]
    sums = cross[...] * scale
    used, proj[1], _, square, sizes = project(
        sums[:, :fields], sums[:, fields:], (own_high[...], own_low[...])
    )
    proj[0] = proj_in[...]
    low[0] = low_in[...]
    both = jnp.concatenate(used, axis=0)
    moved = dot(both[:, :kept], stack[columns:]) + dot(both[:, kept:], last[...])
    w = image[...].astype(jnp.float32) - moved[:columns] - moved[columns:]
    block[...] = w.astype(jnp.bfloat16)
    upper, inverse = factor(square, *sizes)
    low[1] = upper.T
    inverse = inverse.astype(jnp.bfloat16)
    _, span_x, span_y, depth = result.shape
    plane = span_y * depth
    for x in range(span_x):
        part = dot(inverse, block[:, x * plane : (x + 1) * plane])
        result[:, x] = part.reshape(columns, span_y, depth).astype(jnp.bfloat16)


def partner(part, mask):
    axes = ("slab", "col")
    count = lax.axis_size("slab") * lax.axis_size("col")
    return lax.ppermute(part, axes, [(i, i ^ mask) for i in range(count)])


def whole_sum(part):
    cols = lax.axis_size("col")
    count = lax.axis_size("slab") * cols
    index = lax.axis_index("slab") * cols + lax.axis_index("col")
    bit, upper = 1, 0
    while bit < count:
        upper = upper ^ (index // bit % 2)
        bit *= 2
    upper = upper == 1
    half = part.shape[0] // 2
    low, high = part[:half], part[half:]
    part = jnp.where(upper, high, low) + partner(jnp.where(upper, low, high), 1)
    bit = 2
    while bit < count:
        if 2 * bit < count:
            one, two, both = (partner(part, mask) for mask in (bit + 1, 2 * bit + 1, 3 * bit))
            part = (part + one) + (two + both)
            bit *= 4
        else:
            part = part + partner(part, bit + 1)
            bit *= 2
    other = partner(part, 1)
    return jnp.concatenate([jnp.where(upper, other, part), jnp.where(upper, part, other)], axis=0)


def call(kernel, name, outs, *args, flops=0, scratch=()):
    moved = sum(math.prod(arg.shape) * arg.dtype.itemsize for arg in args)
    moved += sum(math.prod(shape) * jnp.dtype(dtype).itemsize for shape, dtype in outs)
    return pl.pallas_call(
        kernel,
        out_shape=[jax.ShapeDtypeStruct(shape, dtype) for shape, dtype in outs],
        in_specs=[pl.BlockSpec(memory_space=pltpu.VMEM)] * len(args),
        out_specs=[pl.BlockSpec(memory_space=pltpu.VMEM)] * len(outs),
        scratch_shapes=scratch,
        compiler_params=pltpu.CompilerParams(vmem_limit_bytes=24 * 1024 * 1024),
        cost_estimate=pl.CostEstimate(flops=flops, bytes_accessed=moved, transcendentals=0),
        name=name,
    )(*args)


def shards(basis, cell_map, table):
    span_x, span_y, depth = cell_map.shape
    blocks, columns = basis.shape[:2]
    cells = span_x * span_y * depth
    fields = blocks * columns
    scale = 1.0 / (cells * lax.axis_size("slab") * lax.axis_size("col"))
    spans = (span_x, span_y, depth)
    f32, bf16 = jnp.float32, jnp.bfloat16

    stack = basis.reshape(fields, cells)
    coef = coefficients(table, cell_map)
    own = call(
        functools.partial(stack_gram_kernel, columns),
        "stack_gram",
        [((blocks, columns, columns), f32), ((columns, columns), f32), ((columns, columns), f32),
         ((1, columns), f32)],
        stack,
        flops=2 * fields * fields * cells,
    )

    def inner_image(block):
        return call(
            functools.partial(inner_image_kernel, spans),
            "inner_image",
            [((columns, cells), f32)],
            coef, block,
            flops=2 * 27 * columns * cells,
        )[0]

    last = basis[blocks - 1].reshape(columns, cells)
    around, partial, (stack, own) = neighbours(last, *spans, inner_image(last), (stack, own))
    image, cross = call(
        functools.partial(first_image_kernel, spans),
        "first_image",
        [((columns, cells), bf16), ((4 * columns + 16, 2 * columns), f32)],
        coef, stack, *own, partial, *around,
    )
    cross = whole_sum(cross)
    block, proj, low, rest, square, inverse = call(
        functools.partial(first_solve_kernel, scale),
        "first_solve",
        [((columns, cells), bf16), ((columns, fields), f32), ((columns, columns), f32),
         ((columns, fields), f32), ((columns, columns), f32), ((columns, columns), bf16)],
        cross, stack, image,
    )
    own = call(
        functools.partial(next_gram_kernel, scale),
        "next_gram",
        [((fields, fields), bf16)] * 2,
        cross, rest, square, inverse,
    )
    around, _, _ = neighbours(block, *spans)
    image, cross = call(
        functools.partial(second_image_kernel, spans),
        "second_image",
        [((columns, cells), bf16), ((columns, fields + columns), f32)],
        coef, stack, block, inner_image(block), *around,
    )
    block, proj, low = call(
        functools.partial(second_solve_kernel, scale),
        "second_solve",
        [((columns, *spans), bf16), ((2, columns, fields), f32), ((2, columns, columns), f32)],
        whole_sum(cross), *own, stack, block, image, proj, low,
        scratch=[pltpu.VMEM((columns, cells), bf16)],
    )
    return block, jnp.swapaxes(proj, 1, 2), low


def solution(mesh):
    placed = (P(None, None, "slab", "col", None), P("slab", "col", None), P())
    return jax.shard_map(
        shards,
        mesh=mesh,
        in_specs=placed,
        out_specs=(P(None, "slab", "col", None), P(), P()),
        check_vma=False,
    )
```

```python
import functools
import math

import jax
import jax.numpy as jnp
from jax import lax
from jax.experimental import pallas as pl
from jax.experimental.pallas import tpu as pltpu
from jax.sharding import PartitionSpec as P

NN = (((1,), (0,)), ((), ()))
NT = (((1,), (1,)), ((), ()))
ROWS = 16


def dot(left, right, dims=NN):
    return lax.dot_general(left, right, dims, preferred_element_type=jnp.float32)


def swaps(axis, near, far, closed):
    count = lax.axis_size(axis)
    me = lax.axis_index(axis)
    pairs = [(i, (i - 1 ^ 1) + 1) for i in range(1, count - 1)]
    if closed:
        pairs += [(0, count - 1), (count - 1, 0)]
    inner = lax.ppermute(near, axis, [(i, i ^ 1) for i in range(count)])
    outer = lax.ppermute(far, axis, pairs)
    if closed:
        odd = me % 2 == 1
        low, high = jnp.where(odd, inner, outer), jnp.where(odd, outer, inner)
        return jnp.where(me == 0, 0, low), jnp.where(me == count - 1, 0, high)
    even = me % 2 == 0
    return jnp.where(even, outer, inner), jnp.where(even, inner, outer)


def cut_kernel(start, block, part):
    part[...] = block[:, pl.ds(pl.multiple_of(start[0], 128), part.shape[1])]


def cut(block, start, width):
    return pl.pallas_call(
        cut_kernel,
        out_shape=jax.ShapeDtypeStruct((block.shape[0], width), block.dtype),
        in_specs=[
            pl.BlockSpec(memory_space=pltpu.SMEM),
            pl.BlockSpec(memory_space=pltpu.VMEM),
        ],
        out_specs=pl.BlockSpec(memory_space=pltpu.VMEM),
        compiler_params=pltpu.CompilerParams(vmem_limit_bytes=4 * 1024 * 1024),
        name="cut",
    )(start.reshape(1), block)


def neighbours(block, span_x, span_y, depth, meanwhile=None):
    plane = span_y * depth
    top = (span_x - 1) * plane
    odd = lax.axis_index("slab") % 2 == 1
    near = jnp.where(odd, block[:, :plane], block[:, top:])
    far = cut(block, jnp.where(odd, top, 0), plane)
    xlo, xhi = swaps("slab", near, far, False)
    xlo, xhi, meanwhile = lax.optimization_barrier((xlo, xhi, meanwhile))

    def edge(row):
        at = row * depth
        parts = [xlo[:, at : at + depth]]
        parts += [block[:, x * plane + at : x * plane + at + depth] for x in range(span_x)]
        parts += [xhi[:, at : at + depth]]
        return jnp.concatenate(parts, axis=1)

    odd = lax.axis_index("col") % 2 == 1
    upward, downward = edge(span_y - 1), edge(0)
    ylo, yhi = swaps(
        "col", jnp.where(odd, downward, upward), jnp.where(odd, upward, downward), True
    )
    return (xlo, xhi), (ylo, yhi), meanwhile


def coefficients_kernel(table, cells, coef):
    classes = table.shape[0]
    lanes = lax.broadcasted_iota(jnp.int32, cells.shape, 1)
    depth = cells.shape[1]
    here = cells[...]
    below = pltpu.roll(here, depth - 1, 1)
    above = pltpu.roll(here, 1, 1)
    maps = (below, here, above)
    keep = (lanes < depth - 1, None, lanes > 0)
    for dz in range(3):
        masks = [maps[dz] == k for k in range(1, classes)]
        for pair in range(9):
            offset = 3 * pair + dz
            value = jnp.full(cells.shape, table[0, offset], jnp.float32)
            for k in range(1, classes):
                value = jnp.where(masks[k - 1], table[k, offset], value)
            if keep[dz] is not None:
                value = jnp.where(keep[dz], value, 0.0)
            coef[offset] = value


def coefficients(table, cell_map):
    span_x, span_y, depth = cell_map.shape
    lines = span_x * span_y
    return pl.pallas_call(
        coefficients_kernel,
        out_shape=jax.ShapeDtypeStruct((27, lines, depth), jnp.float32),
        in_specs=[
            pl.BlockSpec(memory_space=pltpu.SMEM),
            pl.BlockSpec(memory_space=pltpu.VMEM),
        ],
        out_specs=pl.BlockSpec(memory_space=pltpu.VMEM),
        compiler_params=pltpu.CompilerParams(vmem_limit_bytes=4 * 1024 * 1024),
        name="coefficients",
    )(table, cell_map.reshape(lines, depth))


def stencil(coef, spans, columns, lines, line, wanted, write):
    depth = spans[2]

    def tile(step, carry):
        rows = pl.ds(pl.multiple_of(step * ROWS, ROWS), ROWS)
        held = {}
        for x, y in lines:
            at = x * spans[1] + y
            sums = [None, None, None]
            for pair in range(9):
                there = x + pair // 3 - 1, y + pair % 3 - 1
                if not wanted(there[1]):
                    continue
                if there not in held:
                    held[there] = line(rows, *there)
                for dz in range(3):
                    term = coef[3 * pair + dz, at : at + 1, :] * held[there]
                    sums[dz] = term if sums[dz] is None else sums[dz] + term
            total = pltpu.roll(sums[0], 1, 1) + pltpu.roll(sums[2], depth - 1, 1)
            write(rows, x, y, sums[1] + total)
        return carry

    lax.fori_loop(0, columns // ROWS, tile, 0)


def middle_of(spans, x):
    _, span_y, depth = spans
    inner = (span_y - 2) * depth
    return pl.ds((x * span_y + 1) * depth, inner), pl.ds(x * inner, inner)


def ends_of(spans, x, last):
    _, span_y, depth = spans
    return (
        pl.ds((x * span_y + (span_y - 1) * last) * depth, depth),
        pl.ds((2 * x + last) * depth, depth),
    )


def products(parts, fields):
    total = 0
    for w, cells in parts:
        rows = [dot(w, ref[first:, cells], NT) for ref, first in fields]
        total = total + jnp.concatenate(rows + [dot(w, w, NT)], axis=1)
    return total


def middle_image_kernel(spans, first, coef, stack, block, xlo, xhi, middle, partial, cross):
    span_x, span_y, depth = spans

    def line(rows, x, y):
        ref, at = block, x * span_y + y
        if x < 0 or x >= span_x:
            ref, at = (xlo if x < 0 else xhi), y
        return ref[rows, at * depth : (at + 1) * depth].astype(jnp.float32)

    def write(rows, x, y, total):
        if 0 < y < span_y - 1:
            at = x * (span_y - 2) + y - 1
            middle[rows, at * depth : (at + 1) * depth] = total.astype(jnp.bfloat16)
        else:
            partial[rows, ends_of(spans, x, int(y > 0))[1]] = total

    lines = [(x, y) for y in range(span_y) for x in range(span_x)]
    stencil(coef, spans, block.shape[0], lines, line, lambda y: 0 <= y < span_y, write)
    parts = [
        (middle[:, own], there) for there, own in (middle_of(spans, x) for x in range(span_x))
    ]
    cross[...] = products(parts, [(stack, first)] + ([(block, 0)] if first else []))


def end_lines(spans, coef, stack, block, partial, cross, ylo, yhi, ends):
    span_x, span_y, depth = spans

    def line(rows, x, y):
        return (ylo if y < 0 else yhi)[rows, (x + 1) * depth : (x + 2) * depth].astype(jnp.float32)

    def write(rows, x, y, total):
        own = ends_of(spans, x, int(y > 0))[1]
        ends[rows, own] = (partial[rows, own] + total).astype(jnp.bfloat16)

    lines = [(x, y) for y in (0, span_y - 1) for x in range(span_x)]
    stencil(coef, spans, ends.shape[0], lines, line, lambda y: not 0 <= y < span_y, write)
    parts = []
    for x in range(span_x):
        for last in range(2):
            there, own = ends_of(spans, x, last)
            parts.append((ends[:, own], there))
    fields = [(stack, 0)] if block is None else [(stack, ends.shape[0]), (block, 0)]
    return cross[...] + products(parts, fields)


def subtracted(spans, middle, ends, moved, block):
    columns = ends.shape[0]
    moved = moved[:columns] + moved[columns:]
    pieces = []
    for x in range(spans[0]):
        pieces.append((middle, *middle_of(spans, x)))
        pieces += [(ends, *ends_of(spans, x, last)) for last in range(2)]
    for ref, there, own in pieces:
        less = moved[:, there.start : there.start + there.size]
        block[:, there] = (ref[:, own].astype(jnp.float32) - less).astype(jnp.bfloat16)


def places(size):
    return [lax.broadcasted_iota(jnp.int32, (size, size), dim) for dim in (0, 1)]


def diagonal_of(square, axis):
    row, column = places(square.shape[0])
    return jnp.sum(jnp.where(row == column, square, 0.0), axis=axis, keepdims=True)


def two_in_one(one, two):
    row, column = places(one.shape[0])
    return jnp.where(row >= column, one, two), diagonal_of(two, 0)


def both_of(packed, diagonal):
    row, column = places(packed.shape[0])
    turned = packed.T
    two = jnp.where(row < column, packed, turned)
    return jnp.where(row >= column, packed, turned), jnp.where(row == column, diagonal, two)


def stack_gram_kernel(columns, stack, sides, pair, last, diagonal):
    parts = [stack[b * columns : (b + 1) * columns] for b in range(3)]
    sides[0] = dot(parts[0], parts[1], NT)
    sides[1] = dot(parts[0], parts[2], NT)
    sides[2] = dot(parts[1], parts[2], NT)
    pair[...], diagonal[...] = two_in_one(dot(parts[0], parts[0], NT), dot(parts[1], parts[1], NT))
    last[...] = dot(parts[2], parts[2], NT)


def first_image_kernel(
    spans, coef, stack, sides, pair, last, diagonal, partial, known, ylo, yhi, ends, cross
):
    columns = ends.shape[0]
    fields = stack.shape[0]
    sums = end_lines(spans, coef, stack, None, partial, known, ylo, yhi, ends)
    first, square = sums[:, :fields], sums[:, fields:]
    corner, own_diagonal = two_in_one(last[...], square)
    rows = [
        first[:, : 2 * columns],
        jnp.concatenate([first[:, 2 * columns :], sides[0]], axis=1),
        jnp.concatenate([sides[1], sides[2]], axis=1),
        jnp.concatenate([pair[...], corner], axis=1),
    ]
    for i, row in enumerate(rows):
        cross[i * columns : (i + 1) * columns] = row
    rest = jnp.concatenate([diagonal[...], own_diagonal], axis=1)
    rest = jnp.broadcast_to(rest, (cross.shape[0] - 4 * columns, 2 * columns))
    cross[4 * columns :] = rest


def second_image_kernel(spans, coef, stack, block, partial, known, ylo, yhi, ends, cross):
    cross[...] = end_lines(spans, coef, stack, block, partial, known, ylo, yhi, ends)


def opened(cross, columns, scale):
    parts = [cross[i * columns : (i + 1) * columns] * scale for i in range(4)]
    diagonals = cross[4 * columns : 4 * columns + 1] * scale
    first = jnp.concatenate([parts[0], parts[1][:, :columns]], axis=1)
    side = parts[1][:, columns:], parts[2][:, :columns], parts[2][:, columns:]
    one, two = both_of(parts[3][:, :columns], diagonals[:, :columns])
    three, square = both_of(parts[3][:, columns:], diagonals[:, columns:])
    gram = [[one, side[0], side[1]], [side[0].T, two, side[2]], [side[1].T, side[2].T, three]]
    gram = jnp.concatenate([jnp.concatenate(row, axis=1) for row in gram], axis=0)
    return first, square, gram


def split(values):
    high = values.astype(jnp.bfloat16)
    return high, (values - high.astype(jnp.float32)).astype(jnp.bfloat16)


def dots(lefts, rights, dims=NN):
    return sum(dot(left, right, dims) for left in lefts for right in rights)


def factor(square, sizes, across):
    size = square.shape[0]
    shape = (8, 2 * size)
    sub = lax.broadcasted_iota(jnp.int32, shape, 0)
    unit = lax.broadcasted_iota(jnp.int32, (size, size), 0) == lax.broadcasted_iota(
        jnp.int32, (size, size), 1
    )
    scale = lax.rsqrt(across)
    square = square * lax.rsqrt(sizes) * scale
    whole = jnp.concatenate([square, unit.astype(jnp.float32)], axis=1)
    blocks = [whole[b : b + 8] for b in range(0, size, 8)]
    done = []

    def row_of(values, at):
        return jnp.broadcast_to(values[at : at + 1, :], shape)

    def columns_of(values, first):
        return [
            jnp.broadcast_to(values[:, at : at + 1], shape) for at in range(first, first + 8)
        ]

    for b, here in enumerate(blocks):
        columns = columns_of(here, 8 * b)
        entry = {(i, j): row_of(columns[j], i) for j in range(8) for i in range(j + 1)}
        rows = [row_of(here, i) for i in range(8)]
        scaled = jnp.zeros(shape, jnp.float32)
        solved, ratio = [], {}
        if b + 1 < len(blocks):
            below = columns_of(blocks[b + 1], 8 * b)
        for p in range(0, 8, 2):
            q = p + 1
            first, mixed, last = entry[p, p], entry[p, q], entry[q, q]
            inverse = 1.0 / (first * last - mixed * mixed)

            def solve(one, two):
                return (
                    (last * one - mixed * two) * inverse,
                    (first * two - mixed * one) * inverse,
                )

            for j in range(p + 2, 8):
                ratio[p, j], ratio[q, j] = solve(entry[p, j], entry[q, j])
            for i in range(p + 2, 8):
                for j in range(i, 8):
                    change = entry[p, i] * ratio[p, j] + entry[q, i] * ratio[q, j]
                    entry[i, j] = entry[i, j] - change
                rows[i] = rows[i] - (ratio[p, i] * rows[p] + ratio[q, i] * rows[q])
            solved += solve(rows[p], rows[q])
            if b + 1 < len(blocks):
                change = below[p] * solved[p] + below[q] * solved[q]
                blocks[b + 1] = blocks[b + 1] - change
                for j in range(p + 2, 8):
                    below[j] = below[j] - (below[p] * ratio[p, j] + below[q] * ratio[q, j])
            part = mixed * (1.0 / first)
            scaled = jnp.where(sub == p, rows[p] * lax.rsqrt(first), scaled)
            rest = (rows[q] - part * rows[p]) * lax.rsqrt(last - part * mixed)
            scaled = jnp.where(sub == q, rest, scaled)
        done.append(scaled)
        for p in (4, 2, 0):
            for r in (p, p + 1):
                for j in range(p + 2, 8):
                    solved[r] = solved[r] - ratio[r, j] * solved[j]
        for later in range(b + 2, len(blocks)):
            parts = [one * two for one, two in zip(columns_of(blocks[later], 8 * b), solved)]
            while len(parts) > 1:
                parts = [one + two for one, two in zip(parts[::2], parts[1::2])]
            blocks[later] = blocks[later] - parts[0]
    done = jnp.concatenate(done, axis=0)
    above = lax.broadcasted_iota(jnp.int32, (size, size), 0) <= lax.broadcasted_iota(
        jnp.int32, (size, size), 1
    )
    return jnp.where(above, done[:, :size] * (across * scale), 0.0), done[:, size:] * scale


def project(first, square, own):
    first_parts = split(first)
    first_low = first_parts[0]
    second = first - dots((first_low,), own)
    second_low = second.astype(jnp.bfloat16)
    used = (first_low, second_low)
    sizes = [diagonal_of(square, axis) for axis in (1, 0)]
    square = square - dots(used, first_parts, NT)
    rest = second - dots((second_low,), own)
    square = square - dots(split(rest), used, NT)
    return used, first + second, rest, square, sizes


def first_solve_kernel(
    scale, spans, cross, stack, middle, ends, block, proj, low, rest, square, inverse
):
    columns = ends.shape[0]
    first, own_square, gram = opened(cross, columns, scale)
    used, proj[...], rest[...], square_here, sizes = project(first, own_square, split(gram))
    square[...] = square_here
    moved = dot(jnp.concatenate(used, axis=0), stack[...])
    subtracted(spans, middle, ends, moved, block)
    upper, inverse_here = factor(square_here, *sizes)
    low[...] = upper.T
    inverse_here = inverse_here.astype(jnp.bfloat16)
    inverse[...] = inverse_here
    block[...] = dot(inverse_here, block[...]).astype(jnp.bfloat16)


def next_gram_kernel(scale, cross, rest, square, inverse, high, low):
    columns = square.shape[0]
    kept = rest.shape[1] - columns
    _, _, gram = opened(cross, columns, scale)
    mixed = dots((inverse[...],), split(rest[:, columns:]))
    corner = dots((inverse[...],), split(square[...]))
    corner = dots(split(corner), (inverse[...],), NT)
    for part, (old, side, end) in zip(
        (high, low), zip(split(gram[columns:, columns:]), split(mixed), split(corner))
    ):
        part[:kept, :kept] = old
        part[kept:, :kept] = side
        part[:kept, kept:] = side.T
        part[kept:, kept:] = end


def second_solve_kernel(
    scale, cross, own_high, own_low, stack, last, middle, ends, proj_in, low_in, result, proj, low,
    block,
):
    columns = ends.shape[0]
    kept = stack.shape[0] - columns
    fields = stack.shape[0]
    sums = cross[...] * scale
    used, proj[1], _, square, sizes = project(
        sums[:, :fields], sums[:, fields:], (own_high[...], own_low[...])
    )
    proj[0] = proj_in[...]
    low[0] = low_in[...]
    _, span_x, span_y, depth = result.shape
    both = jnp.concatenate(used, axis=0)
    moved = dot(both[:, :kept], stack[columns:]) + dot(both[:, kept:], last[...])
    subtracted((span_x, span_y, depth), middle, ends, moved, block)
    upper, inverse = factor(square, *sizes)
    low[1] = upper.T
    inverse = inverse.astype(jnp.bfloat16)
    plane = span_y * depth
    for x in range(span_x):
        part = dot(inverse, block[:, x * plane : (x + 1) * plane])
        result[:, x] = part.reshape(columns, span_y, depth).astype(jnp.bfloat16)


def partner(part, mask):
    axes = ("slab", "col")
    count = lax.axis_size("slab") * lax.axis_size("col")
    return lax.ppermute(part, axes, [(i, i ^ mask) for i in range(count)])


def whole_sum(part):
    cols = lax.axis_size("col")
    count = lax.axis_size("slab") * cols
    index = lax.axis_index("slab") * cols + lax.axis_index("col")
    bit, upper = 1, 0
    while bit < count:
        upper = upper ^ (index // bit % 2)
        bit *= 2
    upper = upper == 1
    half = part.shape[0] // 2
    low, high = part[:half], part[half:]
    part = jnp.where(upper, high, low) + partner(jnp.where(upper, low, high), 1)
    bit = 2
    while bit < count:
        if 2 * bit < count:
            one, two, both = (partner(part, mask) for mask in (bit + 1, 2 * bit + 1, 3 * bit))
            part = (part + one) + (both + two)
            bit *= 4
        else:
            part = part + partner(part, bit + 1)
            bit *= 2
    other = partner(part, 1)
    return jnp.concatenate([jnp.where(upper, other, part), jnp.where(upper, part, other)], axis=0)


def call(kernel, name, outs, *args, flops=0, scratch=()):
    moved = sum(math.prod(arg.shape) * arg.dtype.itemsize for arg in args)
    moved += sum(math.prod(shape) * jnp.dtype(dtype).itemsize for shape, dtype in outs)
    return pl.pallas_call(
        kernel,
        out_shape=[jax.ShapeDtypeStruct(shape, dtype) for shape, dtype in outs],
        in_specs=[pl.BlockSpec(memory_space=pltpu.VMEM)] * len(args),
        out_specs=[pl.BlockSpec(memory_space=pltpu.VMEM)] * len(outs),
        scratch_shapes=scratch,
        compiler_params=pltpu.CompilerParams(vmem_limit_bytes=24 * 1024 * 1024),
        cost_estimate=pl.CostEstimate(flops=flops, bytes_accessed=moved, transcendentals=0),
        name=name,
    )(*args)


def shards(basis, cell_map, table):
    span_x, span_y, depth = cell_map.shape
    blocks, columns = basis.shape[:2]
    cells = span_x * span_y * depth
    fields = blocks * columns
    scale = 1.0 / (cells * lax.axis_size("slab") * lax.axis_size("col"))
    spans = (span_x, span_y, depth)
    f32, bf16 = jnp.float32, jnp.bfloat16

    stack = basis.reshape(fields, cells)
    coef = coefficients(table, cell_map)
    own = call(
        functools.partial(stack_gram_kernel, columns),
        "stack_gram",
        [((blocks, columns, columns), f32), ((columns, columns), f32), ((columns, columns), f32),
         ((1, columns), f32)],
        stack,
        flops=2 * fields * fields * cells,
    )

    end_cells = 2 * span_x * depth

    def middle_image(first, stack, block, planes):
        return call(
            functools.partial(middle_image_kernel, spans, first),
            "middle_image",
            [((columns, cells - end_cells), bf16), ((columns, end_cells), f32),
             ((columns, fields + columns), f32)],
            coef, stack, block, *planes,
            flops=2 * 27 * columns * cells,
        )

    last = basis[blocks - 1].reshape(columns, cells)
    planes, lines, (coef, stack, own) = neighbours(last, *spans, (coef, stack, own))
    middle, partial, known = middle_image(0, stack, last, planes)
    ends, cross = call(
        functools.partial(first_image_kernel, spans),
        "first_image",
        [((columns, end_cells), bf16), ((4 * columns + 16, 2 * columns), f32)],
        coef, stack, *own, partial, known, *lines,
    )
    cross = whole_sum(cross)
    block, proj, low, rest, square, inverse = call(
        functools.partial(first_solve_kernel, scale, spans),
        "first_solve",
        [((columns, cells), bf16), ((columns, fields), f32), ((columns, columns), f32),
         ((columns, fields), f32), ((columns, columns), f32), ((columns, columns), bf16)],
        cross, stack, middle, ends,
    )
    own = call(
        functools.partial(next_gram_kernel, scale),
        "next_gram",
        [((fields, fields), bf16)] * 2,
        cross, rest, square, inverse,
    )
    planes, lines, _ = neighbours(block, *spans)
    middle, partial, known = middle_image(columns, stack, block, planes)
    ends, cross = call(
        functools.partial(second_image_kernel, spans),
        "second_image",
        [((columns, end_cells), bf16), ((columns, fields + columns), f32)],
        coef, stack, block, partial, known, *lines,
    )
    block, proj, low = call(
        functools.partial(second_solve_kernel, scale),
        "second_solve",
        [((columns, *spans), bf16), ((2, columns, fields), f32), ((2, columns, columns), f32)],
        whole_sum(cross), *own, stack, block, middle, ends, proj, low,
        scratch=[pltpu.VMEM((columns, cells), bf16)],
    )
    return block, jnp.swapaxes(proj, 1, 2), low


def solution(mesh):
    placed = (P(None, None, "slab", "col", None), P("slab", "col", None), P())
    return jax.shard_map(
        shards,
        mesh=mesh,
        in_specs=placed,
        out_specs=(P(None, "slab", "col", None), P(), P()),
        check_vma=False,
    )
```

```python
import functools
import math

import jax
import jax.numpy as jnp
from jax import lax
from jax.experimental import pallas as pl
from jax.experimental.pallas import tpu as pltpu
from jax.sharding import PartitionSpec as P

NN = (((1,), (0,)), ((), ()))
NT = (((1,), (1,)), ((), ()))
ROWS = 16


def dot(left, right, dims=NN):
    return lax.dot_general(left, right, dims, preferred_element_type=jnp.float32)


def swaps(axis, near, far, closed):
    count = lax.axis_size(axis)
    me = lax.axis_index(axis)
    pairs = [(i, (i - 1 ^ 1) + 1) for i in range(1, count - 1)]
    if closed:
        pairs += [(0, count - 1), (count - 1, 0)]
    inner = lax.ppermute(near, axis, [(i, i ^ 1) for i in range(count)])
    outer = lax.ppermute(far, axis, pairs)
    if closed:
        odd = me % 2 == 1
        low, high = jnp.where(odd, inner, outer), jnp.where(odd, outer, inner)
        return jnp.where(me == 0, 0, low), jnp.where(me == count - 1, 0, high)
    even = me % 2 == 0
    return jnp.where(even, outer, inner), jnp.where(even, inner, outer)


def cut_kernel(start, block, part):
    part[...] = block[:, pl.ds(pl.multiple_of(start[0], 128), part.shape[1])]


def cut(block, start, width):
    return pl.pallas_call(
        cut_kernel,
        out_shape=jax.ShapeDtypeStruct((block.shape[0], width), block.dtype),
        in_specs=[
            pl.BlockSpec(memory_space=pltpu.SMEM),
            pl.BlockSpec(memory_space=pltpu.VMEM),
        ],
        out_specs=pl.BlockSpec(memory_space=pltpu.VMEM),
        compiler_params=pltpu.CompilerParams(vmem_limit_bytes=4 * 1024 * 1024),
        name="cut",
    )(start.reshape(1), block)


def neighbours(block, span_x, span_y, depth, meanwhile=None):
    plane = span_y * depth
    top = (span_x - 1) * plane
    odd = lax.axis_index("slab") % 2 == 1
    near = jnp.where(odd, block[:, :plane], block[:, top:])
    far = cut(block, jnp.where(odd, top, 0), plane)
    xlo, xhi = swaps("slab", near, far, False)
    xlo, xhi, meanwhile = lax.optimization_barrier((xlo, xhi, meanwhile))

    def edge(row):
        at = row * depth
        parts = [xlo[:, at : at + depth]]
        parts += [block[:, x * plane + at : x * plane + at + depth] for x in range(span_x)]
        parts += [xhi[:, at : at + depth]]
        return jnp.concatenate(parts, axis=1)

    odd = lax.axis_index("col") % 2 == 1
    upward, downward = edge(span_y - 1), edge(0)
    ylo, yhi = swaps(
        "col", jnp.where(odd, downward, upward), jnp.where(odd, upward, downward), True
    )
    return (xlo, xhi), (ylo, yhi), meanwhile


def coefficients_kernel(table, cells, coef):
    classes = table.shape[0]
    lanes = lax.broadcasted_iota(jnp.int32, cells.shape, 1)
    depth = cells.shape[1]
    here = cells[...]
    below = pltpu.roll(here, depth - 1, 1)
    above = pltpu.roll(here, 1, 1)
    maps = (below, here, above)
    keep = (lanes < depth - 1, None, lanes > 0)
    for dz in range(3):
        masks = [maps[dz] == k for k in range(1, classes)]
        for pair in range(9):
            offset = 3 * pair + dz
            value = jnp.full(cells.shape, table[0, offset], jnp.float32)
            for k in range(1, classes):
                value = jnp.where(masks[k - 1], table[k, offset], value)
            if keep[dz] is not None:
                value = jnp.where(keep[dz], value, 0.0)
            coef[offset] = value


def coefficients(table, cell_map):
    span_x, span_y, depth = cell_map.shape
    lines = span_x * span_y
    return pl.pallas_call(
        coefficients_kernel,
        out_shape=jax.ShapeDtypeStruct((27, lines, depth), jnp.float32),
        in_specs=[
            pl.BlockSpec(memory_space=pltpu.SMEM),
            pl.BlockSpec(memory_space=pltpu.VMEM),
        ],
        out_specs=pl.BlockSpec(memory_space=pltpu.VMEM),
        compiler_params=pltpu.CompilerParams(vmem_limit_bytes=4 * 1024 * 1024),
        name="coefficients",
    )(table, cell_map.reshape(lines, depth))


def stencil(coef, spans, columns, lines, line, wanted, write):
    depth = spans[2]

    def tile(step, carry):
        rows = pl.ds(pl.multiple_of(step * ROWS, ROWS), ROWS)
        held = {}
        for x, y in lines:
            at = x * spans[1] + y
            sums = [None, None, None]
            for pair in range(9):
                there = x + pair // 3 - 1, y + pair % 3 - 1
                if not wanted(there[1]):
                    continue
                if there not in held:
                    held[there] = line(rows, *there)
                for dz in range(3):
                    term = coef[3 * pair + dz, at : at + 1, :] * held[there]
                    sums[dz] = term if sums[dz] is None else sums[dz] + term
            total = pltpu.roll(sums[0], 1, 1) + pltpu.roll(sums[2], depth - 1, 1)
            write(rows, x, y, sums[1] + total)
        return carry

    lax.fori_loop(0, columns // ROWS, tile, 0)


def middle_of(spans, x):
    _, span_y, depth = spans
    inner = (span_y - 2) * depth
    return pl.ds((x * span_y + 1) * depth, inner), pl.ds(x * inner, inner)


def ends_of(spans, x, last):
    _, span_y, depth = spans
    return (
        pl.ds((x * span_y + (span_y - 1) * last) * depth, depth),
        pl.ds((2 * x + last) * depth, depth),
    )


def products(image, cells, fields):
    w = image[...]
    rows = [jnp.concatenate([ref[first:, there] for there in cells], axis=1) for ref, first in fields]
    return dot(w, jnp.concatenate(rows + [w], axis=0), NT)


def middle_image_kernel(spans, first, coef, stack, block, xlo, xhi, middle, partial, cross):
    span_x, span_y, depth = spans

    def line(rows, x, y):
        ref, at = block, x * span_y + y
        if x < 0 or x >= span_x:
            ref, at = (xlo if x < 0 else xhi), y
        return ref[rows, at * depth : (at + 1) * depth].astype(jnp.float32)

    def write(rows, x, y, total):
        if 0 < y < span_y - 1:
            at = x * (span_y - 2) + y - 1
            middle[rows, at * depth : (at + 1) * depth] = total.astype(jnp.bfloat16)
        else:
            partial[rows, ends_of(spans, x, int(y > 0))[1]] = total

    lines = [(x, y) for y in range(span_y) for x in range(span_x)]
    stencil(coef, spans, block.shape[0], lines, line, lambda y: 0 <= y < span_y, write)
    cells = [middle_of(spans, x)[0] for x in range(span_x)]
    cross[...] = products(middle, cells, [(stack, first)] + ([(block, 0)] if first else []))


def end_lines(spans, coef, stack, block, partial, cross, ylo, yhi, ends):
    span_x, span_y, depth = spans

    def line(rows, x, y):
        return (ylo if y < 0 else yhi)[rows, (x + 1) * depth : (x + 2) * depth].astype(jnp.float32)

    def write(rows, x, y, total):
        own = ends_of(spans, x, int(y > 0))[1]
        ends[rows, own] = (partial[rows, own] + total).astype(jnp.bfloat16)

    lines = [(x, y) for y in (0, span_y - 1) for x in range(span_x)]
    stencil(coef, spans, ends.shape[0], lines, line, lambda y: not 0 <= y < span_y, write)
    cells = [ends_of(spans, x, last)[0] for x in range(span_x) for last in range(2)]
    fields = [(stack, 0)] if block is None else [(stack, ends.shape[0]), (block, 0)]
    return cross[...] + products(ends, cells, fields)


def subtracted(spans, middle, ends, moved, block):
    columns = ends.shape[0]
    moved = moved[:columns] + moved[columns:]
    pieces = []
    for x in range(spans[0]):
        pieces.append((middle, *middle_of(spans, x)))
        pieces += [(ends, *ends_of(spans, x, last)) for last in range(2)]
    for ref, there, own in pieces:
        less = moved[:, there.start : there.start + there.size]
        block[:, there] = (ref[:, own].astype(jnp.float32) - less).astype(jnp.bfloat16)


def places(size):
    return [lax.broadcasted_iota(jnp.int32, (size, size), dim) for dim in (0, 1)]


def diagonal_of(square, axis):
    row, column = places(square.shape[0])
    return jnp.sum(jnp.where(row == column, square, 0.0), axis=axis, keepdims=True)


def both_of(packed, diagonal):
    row, column = places(packed.shape[0])
    turned = packed.T
    two = jnp.where(row < column, packed, turned)
    return jnp.where(row >= column, packed, turned), jnp.where(row == column, diagonal, two)


def stack_gram_kernel(columns, stack, sides, right, diagonal):
    parts = [stack[b * columns : (b + 1) * columns] for b in range(3)]
    row, column = places(columns)
    second = dot(parts[1], parts[1], NT)
    pair = jnp.where(row >= column, dot(parts[0], parts[0], NT), second)
    sides[0] = jnp.concatenate(
        [dot(parts[0], parts[2], NT), dot(parts[1], parts[2], NT)], axis=1
    )
    sides[1] = jnp.concatenate([pair, dot(parts[0], parts[1], NT)], axis=1)
    nothing = jnp.zeros((columns, columns), jnp.float32)
    right[...] = jnp.concatenate([nothing, dot(parts[2], parts[2], NT)], axis=1)
    diagonal[...] = jnp.concatenate([diagonal_of(second, 0), nothing[:1]], axis=1)


def first_image_kernel(
    spans, coef, stack, sides, right, diagonal, partial, known, ylo, yhi, ends, cross
):
    columns = ends.shape[0]
    sums = end_lines(spans, coef, stack, None, partial, known, ylo, yhi, ends)
    cross[:columns] = sums[:, : 2 * columns]
    sums = sums[:, 2 * columns :]
    row, lane = (lax.broadcasted_iota(jnp.int32, sums.shape, dim) for dim in (0, 1))
    cross[columns : 2 * columns] = jnp.where(
        (lane >= columns) & (row >= lane - columns), right[...], sums
    )
    for i in range(2):
        cross[(2 + i) * columns : (3 + i) * columns] = sides[i]
    own = jnp.sum(jnp.where(row == lane - columns, sums, 0.0), axis=0, keepdims=True)
    cross[4 * columns :] = jnp.broadcast_to(
        diagonal[...] + own, (cross.shape[0] - 4 * columns, 2 * columns)
    )


def second_image_kernel(spans, coef, stack, block, partial, known, ylo, yhi, ends, cross):
    cross[...] = end_lines(spans, coef, stack, block, partial, known, ylo, yhi, ends)


def opened(cross, columns, scale):
    parts = [cross[i * columns : (i + 1) * columns] * scale for i in range(4)]
    left, right = ([part[:, at : at + columns] for part in parts] for at in (0, columns))
    diagonals = cross[4 * columns : 4 * columns + 1] * scale
    first = jnp.concatenate([parts[0], left[1]], axis=1)
    one, two = both_of(left[3], diagonals[:, :columns])
    three, square = both_of(right[1], diagonals[:, columns:])
    gram = [
        [one, right[3], left[2]],
        [right[3].T, two, right[2]],
        [left[2].T, right[2].T, three],
    ]
    gram = jnp.concatenate([jnp.concatenate(row, axis=1) for row in gram], axis=0)
    return first, square, gram


def split(values):
    high = values.astype(jnp.bfloat16)
    return high, (values - high.astype(jnp.float32)).astype(jnp.bfloat16)


def dots(lefts, rights, dims=NN):
    return sum(dot(left, right, dims) for left in lefts for right in rights)


def factor(square, sizes, across):
    size = square.shape[0]
    shape = (8, 2 * size)
    sub = lax.broadcasted_iota(jnp.int32, shape, 0)
    unit = lax.broadcasted_iota(jnp.int32, (size, size), 0) == lax.broadcasted_iota(
        jnp.int32, (size, size), 1
    )
    scale = lax.rsqrt(across)
    square = square * lax.rsqrt(sizes) * scale
    whole = jnp.concatenate([square, unit.astype(jnp.float32)], axis=1)
    blocks = [whole[b : b + 8] for b in range(0, size, 8)]
    done = []

    def row_of(values, at):
        return jnp.broadcast_to(values[at : at + 1, :], shape)

    def columns_of(values, first):
        return [
            jnp.broadcast_to(values[:, at : at + 1], shape) for at in range(first, first + 8)
        ]

    for b, here in enumerate(blocks):
        columns = columns_of(here, 8 * b)
        entry = {(i, j): row_of(columns[j], i) for j in range(8) for i in range(j + 1)}
        rows = [row_of(here, i) for i in range(8)]
        scaled = jnp.zeros(shape, jnp.float32)
        solved, ratio = [], {}
        if b + 1 < len(blocks):
            below = columns_of(blocks[b + 1], 8 * b)
        for p in range(0, 8, 2):
            q = p + 1
            first, mixed, last = entry[p, p], entry[p, q], entry[q, q]
            inverse = 1.0 / (first * last - mixed * mixed)

            def solve(one, two):
                return (
                    (last * one - mixed * two) * inverse,
                    (first * two - mixed * one) * inverse,
                )

            for j in range(p + 2, 8):
                ratio[p, j], ratio[q, j] = solve(entry[p, j], entry[q, j])
            for i in range(p + 2, 8):
                for j in range(i, 8):
                    change = entry[p, i] * ratio[p, j] + entry[q, i] * ratio[q, j]
                    entry[i, j] = entry[i, j] - change
                rows[i] = rows[i] - (ratio[p, i] * rows[p] + ratio[q, i] * rows[q])
            solved += solve(rows[p], rows[q])
            if b + 1 < len(blocks):
                change = below[p] * solved[p] + below[q] * solved[q]
                blocks[b + 1] = blocks[b + 1] - change
                for j in range(p + 2, 8):
                    below[j] = below[j] - (below[p] * ratio[p, j] + below[q] * ratio[q, j])
            part = mixed * (1.0 / first)
            scaled = jnp.where(sub == p, rows[p] * lax.rsqrt(first), scaled)
            rest = (rows[q] - part * rows[p]) * lax.rsqrt(last - part * mixed)
            scaled = jnp.where(sub == q, rest, scaled)
        done.append(scaled)
        for p in (4, 2, 0):
            for r in (p, p + 1):
                for j in range(p + 2, 8):
                    solved[r] = solved[r] - ratio[r, j] * solved[j]
        for later in range(b + 2, len(blocks)):
            parts = [one * two for one, two in zip(columns_of(blocks[later], 8 * b), solved)]
            while len(parts) > 1:
                parts = [one + two for one, two in zip(parts[::2], parts[1::2])]
            blocks[later] = blocks[later] - parts[0]
    done = jnp.concatenate(done, axis=0)
    above = lax.broadcasted_iota(jnp.int32, (size, size), 0) <= lax.broadcasted_iota(
        jnp.int32, (size, size), 1
    )
    return jnp.where(above, done[:, :size] * (across * scale), 0.0), done[:, size:] * scale


def project(first, square, own):
    first_parts = split(first)
    first_low = first_parts[0]
    second = first - dots((first_low,), own)
    second_low = second.astype(jnp.bfloat16)
    used = (first_low, second_low)
    sizes = [diagonal_of(square, axis) for axis in (1, 0)]
    square = square - dots(used, first_parts, NT)
    rest = second - dots((second_low,), own)
    square = square - dots(split(rest), used, NT)
    return used, first + second, rest, square, sizes


def first_solve_kernel(
    scale, spans, cross, stack, middle, ends, block, proj, low, rest, square, inverse
):
    columns = ends.shape[0]
    first, own_square, gram = opened(cross, columns, scale)
    used, proj[...], rest[...], square_here, sizes = project(first, own_square, split(gram))
    square[...] = square_here
    moved = dot(jnp.concatenate(used, axis=0), stack[...])
    subtracted(spans, middle, ends, moved, block)
    upper, inverse_here = factor(square_here, *sizes)
    low[...] = upper.T
    inverse_here = inverse_here.astype(jnp.bfloat16)
    inverse[...] = inverse_here
    block[...] = dot(inverse_here, block[...]).astype(jnp.bfloat16)


def next_gram_kernel(scale, cross, rest, square, inverse, high, low):
    columns = square.shape[0]
    kept = rest.shape[1] - columns
    _, _, gram = opened(cross, columns, scale)
    mixed = dots((inverse[...],), split(rest[:, columns:]))
    corner = dots((inverse[...],), split(square[...]))
    corner = dots(split(corner), (inverse[...],), NT)
    for part, (old, side, end) in zip(
        (high, low), zip(split(gram[columns:, columns:]), split(mixed), split(corner))
    ):
        part[:kept, :kept] = old
        part[kept:, :kept] = side
        part[:kept, kept:] = side.T
        part[kept:, kept:] = end


def second_solve_kernel(
    scale, cross, own_high, own_low, stack, last, middle, ends, proj_in, low_in, result, proj, low,
    block,
):
    columns = ends.shape[0]
    kept = stack.shape[0] - columns
    fields = stack.shape[0]
    sums = cross[...] * scale
    used, proj[1], _, square, sizes = project(
        sums[:, :fields], sums[:, fields:], (own_high[...], own_low[...])
    )
    proj[0] = proj_in[...]
    low[0] = low_in[...]
    _, span_x, span_y, depth = result.shape
    both = jnp.concatenate(used, axis=0)
    moved = dot(both[:, :kept], stack[columns:]) + dot(both[:, kept:], last[...])
    subtracted((span_x, span_y, depth), middle, ends, moved, block)
    upper, inverse = factor(square, *sizes)
    low[1] = upper.T
    inverse = inverse.astype(jnp.bfloat16)
    plane = span_y * depth
    for x in range(span_x):
        part = dot(inverse, block[:, x * plane : (x + 1) * plane])
        result[:, x] = part.reshape(columns, span_y, depth).astype(jnp.bfloat16)


def partner(part, mask):
    axes = ("slab", "col")
    count = lax.axis_size("slab") * lax.axis_size("col")
    return lax.ppermute(part, axes, [(i, i ^ mask) for i in range(count)])


def whole_sum(part):
    cols = lax.axis_size("col")
    count = lax.axis_size("slab") * cols
    index = lax.axis_index("slab") * cols + lax.axis_index("col")
    bit, upper = 1, 0
    while bit < count:
        upper = upper ^ (index // bit % 2)
        bit *= 2
    upper = upper == 1
    half = part.shape[0] // 2
    low, high = part[:half], part[half:]
    part = jnp.where(upper, high, low) + partner(jnp.where(upper, low, high), 1)
    bit = 2
    while bit < count:
        if 2 * bit < count:
            one, two, both = (partner(part, mask) for mask in (bit + 1, 2 * bit + 1, 3 * bit))
            part = (part + one) + (both + two)
            bit *= 4
        else:
            part = part + partner(part, bit + 1)
            bit *= 2
    other = partner(part, 1)
    return jnp.concatenate([jnp.where(upper, other, part), jnp.where(upper, part, other)], axis=0)


def call(kernel, name, outs, *args, flops=0, scratch=()):
    moved = sum(math.prod(arg.shape) * arg.dtype.itemsize for arg in args)
    moved += sum(math.prod(shape) * jnp.dtype(dtype).itemsize for shape, dtype in outs)
    return pl.pallas_call(
        kernel,
        out_shape=[jax.ShapeDtypeStruct(shape, dtype) for shape, dtype in outs],
        in_specs=[pl.BlockSpec(memory_space=pltpu.VMEM)] * len(args),
        out_specs=[pl.BlockSpec(memory_space=pltpu.VMEM)] * len(outs),
        scratch_shapes=scratch,
        compiler_params=pltpu.CompilerParams(vmem_limit_bytes=24 * 1024 * 1024),
        cost_estimate=pl.CostEstimate(flops=flops, bytes_accessed=moved, transcendentals=0),
        name=name,
    )(*args)


def shards(basis, cell_map, table):
    span_x, span_y, depth = cell_map.shape
    blocks, columns = basis.shape[:2]
    cells = span_x * span_y * depth
    fields = blocks * columns
    scale = 1.0 / (cells * lax.axis_size("slab") * lax.axis_size("col"))
    spans = (span_x, span_y, depth)
    f32, bf16 = jnp.float32, jnp.bfloat16

    stack = basis.reshape(fields, cells)
    coef = coefficients(table, cell_map)
    own = call(
        functools.partial(stack_gram_kernel, columns),
        "stack_gram",
        [((2, columns, 2 * columns), f32), ((columns, 2 * columns), f32), ((1, 2 * columns), f32)],
        stack,
        flops=2 * fields * fields * cells,
    )

    end_cells = 2 * span_x * depth

    def middle_image(first, stack, block, planes):
        return call(
            functools.partial(middle_image_kernel, spans, first),
            "middle_image",
            [((columns, cells - end_cells), bf16), ((columns, end_cells), f32),
             ((columns, fields + columns), f32)],
            coef, stack, block, *planes,
            flops=2 * 27 * columns * cells,
        )

    last = basis[blocks - 1].reshape(columns, cells)
    planes, lines, (coef, stack, own) = neighbours(last, *spans, (coef, stack, own))
    middle, partial, known = middle_image(0, stack, last, planes)
    ends, cross = call(
        functools.partial(first_image_kernel, spans),
        "first_image",
        [((columns, end_cells), bf16), ((4 * columns + 16, 2 * columns), f32)],
        coef, stack, *own, partial, known, *lines,
    )
    cross = whole_sum(cross)
    block, proj, low, rest, square, inverse = call(
        functools.partial(first_solve_kernel, scale, spans),
        "first_solve",
        [((columns, cells), bf16), ((columns, fields), f32), ((columns, columns), f32),
         ((columns, fields), f32), ((columns, columns), f32), ((columns, columns), bf16)],
        cross, stack, middle, ends,
    )
    own = call(
        functools.partial(next_gram_kernel, scale),
        "next_gram",
        [((fields, fields), bf16)] * 2,
        cross, rest, square, inverse,
    )
    planes, lines, _ = neighbours(block, *spans)
    middle, partial, known = middle_image(columns, stack, block, planes)
    ends, cross = call(
        functools.partial(second_image_kernel, spans),
        "second_image",
        [((columns, end_cells), bf16), ((columns, fields + columns), f32)],
        coef, stack, block, partial, known, *lines,
    )
    block, proj, low = call(
        functools.partial(second_solve_kernel, scale),
        "second_solve",
        [((columns, *spans), bf16), ((2, columns, fields), f32), ((2, columns, columns), f32)],
        whole_sum(cross), *own, stack, block, middle, ends, proj, low,
        scratch=[pltpu.VMEM((columns, cells), bf16)],
    )
    return block, jnp.swapaxes(proj, 1, 2), low


def solution(mesh):
    placed = (P(None, None, "slab", "col", None), P("slab", "col", None), P())
    return jax.shard_map(
        shards,
        mesh=mesh,
        in_specs=placed,
        out_specs=(P(None, "slab", "col", None), P(), P()),
        check_vma=False,
    )
```

```python
import functools
import math

import jax
import jax.numpy as jnp
from jax import lax
from jax.experimental import pallas as pl
from jax.experimental.pallas import tpu as pltpu
from jax.sharding import PartitionSpec as P

NN = (((1,), (0,)), ((), ()))
NT = (((1,), (1,)), ((), ()))
ROWS = 16


def dot(left, right, dims=NN):
    return lax.dot_general(left, right, dims, preferred_element_type=jnp.float32)


def swaps(axis, near, far, closed):
    count = lax.axis_size(axis)
    me = lax.axis_index(axis)
    pairs = [(i, (i - 1 ^ 1) + 1) for i in range(1, count - 1)]
    if closed:
        pairs += [(0, count - 1), (count - 1, 0)]
    inner = lax.ppermute(near, axis, [(i, i ^ 1) for i in range(count)])
    outer = lax.ppermute(far, axis, pairs)
    if closed:
        odd = me % 2 == 1
        low, high = jnp.where(odd, inner, outer), jnp.where(odd, outer, inner)
        return jnp.where(me == 0, 0, low), jnp.where(me == count - 1, 0, high)
    even = me % 2 == 0
    return jnp.where(even, outer, inner), jnp.where(even, inner, outer)


def cut_kernel(start, block, part):
    part[...] = block[:, pl.ds(pl.multiple_of(start[0], 128), part.shape[1])]


def cut(block, start, width):
    return pl.pallas_call(
        cut_kernel,
        out_shape=jax.ShapeDtypeStruct((block.shape[0], width), block.dtype),
        in_specs=[
            pl.BlockSpec(memory_space=pltpu.SMEM),
            pl.BlockSpec(memory_space=pltpu.VMEM),
        ],
        out_specs=pl.BlockSpec(memory_space=pltpu.VMEM),
        compiler_params=pltpu.CompilerParams(vmem_limit_bytes=4 * 1024 * 1024),
        name="cut",
    )(start.reshape(1), block)


def neighbours(block, span_x, span_y, depth, meanwhile=None):
    plane = span_y * depth
    top = (span_x - 1) * plane
    odd = lax.axis_index("slab") % 2 == 1
    near = jnp.where(odd, block[:, :plane], block[:, top:])
    far = cut(block, jnp.where(odd, top, 0), plane)
    xlo, xhi = swaps("slab", near, far, False)
    xlo, xhi, meanwhile = lax.optimization_barrier((xlo, xhi, meanwhile))

    def edge(row):
        at = row * depth
        parts = [xlo[:, at : at + depth]]
        parts += [block[:, x * plane + at : x * plane + at + depth] for x in range(span_x)]
        parts += [xhi[:, at : at + depth]]
        return jnp.concatenate(parts, axis=1)

    odd = lax.axis_index("col") % 2 == 1
    upward, downward = edge(span_y - 1), edge(0)
    ylo, yhi = swaps(
        "col", jnp.where(odd, downward, upward), jnp.where(odd, upward, downward), True
    )
    return (xlo, xhi), (ylo, yhi), meanwhile


def coefficients_kernel(table, cells, coef):
    classes = table.shape[0]
    lanes = lax.broadcasted_iota(jnp.int32, cells.shape, 1)
    depth = cells.shape[1]
    here = cells[...]
    below = pltpu.roll(here, depth - 1, 1)
    above = pltpu.roll(here, 1, 1)
    maps = (below, here, above)
    keep = (lanes < depth - 1, None, lanes > 0)
    for dz in range(3):
        masks = [maps[dz] == k for k in range(1, classes)]
        for pair in range(9):
            offset = 3 * pair + dz
            value = jnp.full(cells.shape, table[0, offset], jnp.float32)
            for k in range(1, classes):
                value = jnp.where(masks[k - 1], table[k, offset], value)
            if keep[dz] is not None:
                value = jnp.where(keep[dz], value, 0.0)
            coef[offset] = value


def coefficients(table, cell_map):
    span_x, span_y, depth = cell_map.shape
    lines = span_x * span_y
    return pl.pallas_call(
        coefficients_kernel,
        out_shape=jax.ShapeDtypeStruct((27, lines, depth), jnp.float32),
        in_specs=[
            pl.BlockSpec(memory_space=pltpu.SMEM),
            pl.BlockSpec(memory_space=pltpu.VMEM),
        ],
        out_specs=pl.BlockSpec(memory_space=pltpu.VMEM),
        compiler_params=pltpu.CompilerParams(vmem_limit_bytes=4 * 1024 * 1024),
        name="coefficients",
    )(table, cell_map.reshape(lines, depth))


def stencil(coef, spans, columns, lines, line, wanted, write):
    depth = spans[2]

    def tile(step, carry):
        rows = pl.ds(pl.multiple_of(step * ROWS, ROWS), ROWS)
        held = {}
        for x, y in lines:
            at = x * spans[1] + y
            sums = [None, None, None]
            for pair in range(9):
                there = x + pair // 3 - 1, y + pair % 3 - 1
                if not wanted(there[1]):
                    continue
                if there not in held:
                    held[there] = line(rows, *there)
                for dz in range(3):
                    term = coef[3 * pair + dz, at : at + 1, :] * held[there]
                    sums[dz] = term if sums[dz] is None else sums[dz] + term
            total = pltpu.roll(sums[0], 1, 1) + pltpu.roll(sums[2], depth - 1, 1)
            write(rows, x, y, sums[1] + total)
        return carry

    lax.fori_loop(0, columns // ROWS, tile, 0)


def middle_of(spans, x):
    _, span_y, depth = spans
    inner = (span_y - 2) * depth
    return pl.ds((x * span_y + 1) * depth, inner), pl.ds(x * inner, inner)


def ends_of(spans, x, last):
    _, span_y, depth = spans
    return (
        pl.ds((x * span_y + (span_y - 1) * last) * depth, depth),
        pl.ds((2 * x + last) * depth, depth),
    )


def products(image, cells, fields):
    w = image[...]
    rows = [jnp.concatenate([ref[first:, there] for there in cells], axis=1) for ref, first in fields]
    return dot(w, jnp.concatenate(rows + [w], axis=0), NT)


def middle_image_kernel(spans, first, coef, stack, block, xlo, xhi, middle, partial, cross):
    span_x, span_y, depth = spans

    def line(rows, x, y):
        ref, at = block, x * span_y + y
        if x < 0 or x >= span_x:
            ref, at = (xlo if x < 0 else xhi), y
        return ref[rows, at * depth : (at + 1) * depth].astype(jnp.float32)

    def write(rows, x, y, total):
        if 0 < y < span_y - 1:
            at = x * (span_y - 2) + y - 1
            middle[rows, at * depth : (at + 1) * depth] = total.astype(jnp.bfloat16)
        else:
            partial[rows, ends_of(spans, x, int(y > 0))[1]] = total

    lines = [(x, y) for y in range(span_y) for x in range(span_x)]
    stencil(coef, spans, block.shape[0], lines, line, lambda y: 0 <= y < span_y, write)
    cells = [middle_of(spans, x)[0] for x in range(span_x)]
    cross[...] = products(middle, cells, [(stack, first)] + ([(block, 0)] if first else []))


def end_lines(spans, coef, stack, block, partial, cross, ylo, yhi, ends):
    span_x, span_y, depth = spans

    def line(rows, x, y):
        return (ylo if y < 0 else yhi)[rows, (x + 1) * depth : (x + 2) * depth].astype(jnp.float32)

    def write(rows, x, y, total):
        own = ends_of(spans, x, int(y > 0))[1]
        ends[rows, own] = (partial[rows, own] + total).astype(jnp.bfloat16)

    lines = [(x, y) for y in (0, span_y - 1) for x in range(span_x)]
    stencil(coef, spans, ends.shape[0], lines, line, lambda y: not 0 <= y < span_y, write)
    cells = [ends_of(spans, x, last)[0] for x in range(span_x) for last in range(2)]
    fields = [(stack, 0)] if block is None else [(stack, ends.shape[0]), (block, 0)]
    return cross[...] + products(ends, cells, fields)


def subtracted(spans, middle, ends, moved, block):
    columns = ends.shape[0]
    moved = moved[:columns] + moved[columns:]
    pieces = []
    for x in range(spans[0]):
        pieces.append((middle, *middle_of(spans, x)))
        pieces += [(ends, *ends_of(spans, x, last)) for last in range(2)]
    for ref, there, own in pieces:
        less = moved[:, there.start : there.start + there.size]
        block[:, there] = (ref[:, own].astype(jnp.float32) - less).astype(jnp.bfloat16)


def places(size):
    return [lax.broadcasted_iota(jnp.int32, (size, size), dim) for dim in (0, 1)]


def diagonal_of(square, axis):
    row, column = places(square.shape[0])
    return jnp.sum(jnp.where(row == column, square, 0.0), axis=axis, keepdims=True)


def both_of(packed, diagonal):
    row, column = places(packed.shape[0])
    turned = packed.T
    two = jnp.where(row < column, packed, turned)
    return jnp.where(row >= column, packed, turned), jnp.where(row == column, diagonal, two)


def stack_gram_kernel(columns, stack, sides, right, diagonal):
    parts = [stack[b * columns : (b + 1) * columns] for b in range(3)]
    row, column = places(columns)
    second = dot(parts[1], parts[1], NT)
    pair = jnp.where(row >= column, dot(parts[0], parts[0], NT), second)
    sides[0] = jnp.concatenate(
        [dot(parts[0], parts[2], NT), dot(parts[1], parts[2], NT)], axis=1
    )
    sides[1] = jnp.concatenate([pair, dot(parts[0], parts[1], NT)], axis=1)
    nothing = jnp.zeros((columns, columns), jnp.float32)
    right[...] = jnp.concatenate([nothing, dot(parts[2], parts[2], NT)], axis=1)
    diagonal[...] = jnp.concatenate([diagonal_of(second, 0), nothing[:1]], axis=1)


def first_image_kernel(
    spans, coef, stack, sides, right, diagonal, partial, known, ylo, yhi, ends, cross
):
    columns = ends.shape[0]
    sums = end_lines(spans, coef, stack, None, partial, known, ylo, yhi, ends)
    cross[:columns] = sums[:, : 2 * columns]
    sums = sums[:, 2 * columns :]
    row, lane = (lax.broadcasted_iota(jnp.int32, sums.shape, dim) for dim in (0, 1))
    cross[columns : 2 * columns] = jnp.where(
        (lane >= columns) & (row >= lane - columns), right[...], sums
    )
    for i in range(2):
        cross[(2 + i) * columns : (3 + i) * columns] = sides[i]
    own = jnp.sum(jnp.where(row == lane - columns, sums, 0.0), axis=0, keepdims=True)
    cross[4 * columns :] = jnp.broadcast_to(
        diagonal[...] + own, (cross.shape[0] - 4 * columns, 2 * columns)
    )


def second_image_kernel(spans, coef, stack, block, partial, known, ylo, yhi, ends, cross):
    cross[...] = end_lines(spans, coef, stack, block, partial, known, ylo, yhi, ends)


def opened(cross, columns, scale):
    parts = [cross[i * columns : (i + 1) * columns] * scale for i in range(4)]
    left, right = ([part[:, at : at + columns] for part in parts] for at in (0, columns))
    diagonals = cross[4 * columns : 4 * columns + 1] * scale
    first = jnp.concatenate([parts[0], left[1]], axis=1)
    one, two = both_of(left[3], diagonals[:, :columns])
    three, square = both_of(right[1], diagonals[:, columns:])
    gram = [
        [one, right[3], left[2]],
        [right[3].T, two, right[2]],
        [left[2].T, right[2].T, three],
    ]
    gram = jnp.concatenate([jnp.concatenate(row, axis=1) for row in gram], axis=0)
    return first, square, gram


def split(values):
    high = values.astype(jnp.bfloat16)
    return high, (values - high.astype(jnp.float32)).astype(jnp.bfloat16)


def dots(lefts, rights, dims=NN):
    return sum(dot(left, right, dims) for left in lefts for right in rights)


def factor(square, sizes, across):
    size = square.shape[0]
    shape = (8, 2 * size)
    sub = lax.broadcasted_iota(jnp.int32, shape, 0)
    unit = lax.broadcasted_iota(jnp.int32, (size, size), 0) == lax.broadcasted_iota(
        jnp.int32, (size, size), 1
    )
    scale = lax.rsqrt(across)
    square = square * lax.rsqrt(sizes) * scale
    whole = jnp.concatenate([square, unit.astype(jnp.float32)], axis=1)
    blocks = [whole[b : b + 8] for b in range(0, size, 8)]
    done = []

    def row_of(values, at):
        return jnp.broadcast_to(values[at : at + 1, :], shape)

    def columns_of(values, first):
        return [
            jnp.broadcast_to(values[:, at : at + 1], shape) for at in range(first, first + 8)
        ]

    for b, here in enumerate(blocks):
        columns = columns_of(here, 8 * b)
        entry = {(i, j): row_of(columns[j], i) for j in range(8) for i in range(j + 1)}
        rows = [row_of(here, i) for i in range(8)]
        scaled = jnp.zeros(shape, jnp.float32)
        solved, ratio = [], {}
        if b + 1 < len(blocks):
            below = columns_of(blocks[b + 1], 8 * b)
        for p in range(0, 8, 2):
            q = p + 1
            first, mixed, last = entry[p, p], entry[p, q], entry[q, q]
            inverse = pltpu.reciprocal(first * last - mixed * mixed, approx=True)

            def solve(one, two):
                return (
                    (last * one - mixed * two) * inverse,
                    (first * two - mixed * one) * inverse,
                )

            for j in range(p + 2, 8):
                ratio[p, j], ratio[q, j] = solve(entry[p, j], entry[q, j])
            for i in range(p + 2, 8):
                for j in range(i, 8):
                    change = entry[p, i] * ratio[p, j] + entry[q, i] * ratio[q, j]
                    entry[i, j] = entry[i, j] - change
                rows[i] = rows[i] - (ratio[p, i] * rows[p] + ratio[q, i] * rows[q])
            solved += solve(rows[p], rows[q])
            if b + 1 < len(blocks):
                change = below[p] * solved[p] + below[q] * solved[q]
                blocks[b + 1] = blocks[b + 1] - change
                for j in range(p + 2, 8):
                    below[j] = below[j] - (below[p] * ratio[p, j] + below[q] * ratio[q, j])
            part = mixed * (1.0 / first)
            scaled = jnp.where(sub == p, rows[p] * lax.rsqrt(first), scaled)
            rest = (rows[q] - part * rows[p]) * lax.rsqrt(last - part * mixed)
            scaled = jnp.where(sub == q, rest, scaled)
        done.append(scaled)
        for p in (4, 2, 0):
            for r in (p, p + 1):
                for j in range(p + 2, 8):
                    solved[r] = solved[r] - ratio[r, j] * solved[j]
        for later in range(b + 2, len(blocks)):
            parts = [one * two for one, two in zip(columns_of(blocks[later], 8 * b), solved)]
            while len(parts) > 1:
                parts = [one + two for one, two in zip(parts[::2], parts[1::2])]
            blocks[later] = blocks[later] - parts[0]
    done = jnp.concatenate(done, axis=0)
    above = lax.broadcasted_iota(jnp.int32, (size, size), 0) <= lax.broadcasted_iota(
        jnp.int32, (size, size), 1
    )
    return jnp.where(above, done[:, :size] * (across * scale), 0.0), done[:, size:] * scale


def project(first, square, own):
    first_parts = split(first)
    first_low = first_parts[0]
    second = first - dots((first_low,), own)
    second_low = second.astype(jnp.bfloat16)
    used = (first_low, second_low)
    sizes = [diagonal_of(square, axis) for axis in (1, 0)]
    square = square - dots(used, first_parts, NT)
    rest = second - dots((second_low,), own)
    square = square - dots(split(rest), used, NT)
    return used, first + second, rest, square, sizes


def first_solve_kernel(
    scale, spans, cross, stack, middle, ends, block, proj, low, rest, square, inverse
):
    columns = ends.shape[0]
    first, own_square, gram = opened(cross, columns, scale)
    used, proj[...], rest[...], square_here, sizes = project(first, own_square, split(gram))
    square[...] = square_here
    moved = dot(jnp.concatenate(used, axis=0), stack[...])
    subtracted(spans, middle, ends, moved, block)
    upper, inverse_here = factor(square_here, *sizes)
    low[...] = upper.T
    inverse_here = inverse_here.astype(jnp.bfloat16)
    inverse[...] = inverse_here
    block[...] = dot(inverse_here, block[...]).astype(jnp.bfloat16)


def next_gram_kernel(scale, cross, rest, square, inverse, high, low):
    columns = square.shape[0]
    kept = rest.shape[1] - columns
    _, _, gram = opened(cross, columns, scale)
    mixed = dots((inverse[...],), split(rest[:, columns:]))
    corner = dots((inverse[...],), split(square[...]))
    corner = dots(split(corner), (inverse[...],), NT)
    for part, (old, side, end) in zip(
        (high, low), zip(split(gram[columns:, columns:]), split(mixed), split(corner))
    ):
        part[:kept, :kept] = old
        part[kept:, :kept] = side
        part[:kept, kept:] = side.T
        part[kept:, kept:] = end


def second_solve_kernel(
    scale, cross, own_high, own_low, stack, last, middle, ends, proj_in, low_in, result, proj, low,
    block,
):
    columns = ends.shape[0]
    kept = stack.shape[0] - columns
    fields = stack.shape[0]
    sums = cross[...] * scale
    used, proj[1], _, square, sizes = project(
        sums[:, :fields], sums[:, fields:], (own_high[...], own_low[...])
    )
    proj[0] = proj_in[...]
    low[0] = low_in[...]
    _, span_x, span_y, depth = result.shape
    both = jnp.concatenate(used, axis=0)
    moved = dot(both[:, :kept], stack[columns:]) + dot(both[:, kept:], last[...])
    subtracted((span_x, span_y, depth), middle, ends, moved, block)
    upper, inverse = factor(square, *sizes)
    low[1] = upper.T
    inverse = inverse.astype(jnp.bfloat16)
    plane = span_y * depth
    for x in range(span_x):
        part = dot(inverse, block[:, x * plane : (x + 1) * plane])
        result[:, x] = part.reshape(columns, span_y, depth).astype(jnp.bfloat16)


def partner(part, mask):
    axes = ("slab", "col")
    count = lax.axis_size("slab") * lax.axis_size("col")
    return lax.ppermute(part, axes, [(i, i ^ mask) for i in range(count)])


def whole_sum(part):
    cols = lax.axis_size("col")
    count = lax.axis_size("slab") * cols
    index = lax.axis_index("slab") * cols + lax.axis_index("col")
    bit, upper = 1, 0
    while bit < count:
        upper = upper ^ (index // bit % 2)
        bit *= 2
    upper = upper == 1
    half = part.shape[0] // 2
    low, high = part[:half], part[half:]
    part = jnp.where(upper, high, low) + partner(jnp.where(upper, low, high), 1)
    bit = 2
    while bit < count:
        if 2 * bit < count:
            one, two, both = (partner(part, mask) for mask in (bit + 1, 2 * bit + 1, 3 * bit))
            part = (part + one) + (two + both)
            bit *= 4
        else:
            part = part + partner(part, bit + 1)
            bit *= 2
    other = partner(part, 1)
    return jnp.concatenate([jnp.where(upper, other, part), jnp.where(upper, part, other)], axis=0)


def call(kernel, name, outs, *args, flops=0, scratch=()):
    moved = sum(math.prod(arg.shape) * arg.dtype.itemsize for arg in args)
    moved += sum(math.prod(shape) * jnp.dtype(dtype).itemsize for shape, dtype in outs)
    return pl.pallas_call(
        kernel,
        out_shape=[jax.ShapeDtypeStruct(shape, dtype) for shape, dtype in outs],
        in_specs=[pl.BlockSpec(memory_space=pltpu.VMEM)] * len(args),
        out_specs=[pl.BlockSpec(memory_space=pltpu.VMEM)] * len(outs),
        scratch_shapes=scratch,
        compiler_params=pltpu.CompilerParams(vmem_limit_bytes=24 * 1024 * 1024),
        cost_estimate=pl.CostEstimate(flops=flops, bytes_accessed=moved, transcendentals=0),
        name=name,
    )(*args)


def shards(basis, cell_map, table):
    span_x, span_y, depth = cell_map.shape
    blocks, columns = basis.shape[:2]
    cells = span_x * span_y * depth
    fields = blocks * columns
    scale = 1.0 / (cells * lax.axis_size("slab") * lax.axis_size("col"))
    spans = (span_x, span_y, depth)
    f32, bf16 = jnp.float32, jnp.bfloat16

    stack = basis.reshape(fields, cells)
    coef = coefficients(table, cell_map)
    own = call(
        functools.partial(stack_gram_kernel, columns),
        "stack_gram",
        [((2, columns, 2 * columns), f32), ((columns, 2 * columns), f32), ((1, 2 * columns), f32)],
        stack,
        flops=2 * fields * fields * cells,
    )

    end_cells = 2 * span_x * depth

    def middle_image(first, stack, block, planes):
        return call(
            functools.partial(middle_image_kernel, spans, first),
            "middle_image",
            [((columns, cells - end_cells), bf16), ((columns, end_cells), f32),
             ((columns, fields + columns), f32)],
            coef, stack, block, *planes,
            flops=2 * 27 * columns * cells,
        )

    last = basis[blocks - 1].reshape(columns, cells)
    planes, lines, (coef, stack, own) = neighbours(last, *spans, (coef, stack, own))
    middle, partial, known = middle_image(0, stack, last, planes)
    ends, cross = call(
        functools.partial(first_image_kernel, spans),
        "first_image",
        [((columns, end_cells), bf16), ((4 * columns + 16, 2 * columns), f32)],
        coef, stack, *own, partial, known, *lines,
    )
    cross = whole_sum(cross)
    block, proj, low, rest, square, inverse = call(
        functools.partial(first_solve_kernel, scale, spans),
        "first_solve",
        [((columns, cells), bf16), ((columns, fields), f32), ((columns, columns), f32),
         ((columns, fields), f32), ((columns, columns), f32), ((columns, columns), bf16)],
        cross, stack, middle, ends,
    )
    own = call(
        functools.partial(next_gram_kernel, scale),
        "next_gram",
        [((fields, fields), bf16)] * 2,
        cross, rest, square, inverse,
    )
    planes, lines, _ = neighbours(block, *spans)
    middle, partial, known = middle_image(columns, stack, block, planes)
    ends, cross = call(
        functools.partial(second_image_kernel, spans),
        "second_image",
        [((columns, end_cells), bf16), ((columns, fields + columns), f32)],
        coef, stack, block, partial, known, *lines,
    )
    block, proj, low = call(
        functools.partial(second_solve_kernel, scale),
        "second_solve",
        [((columns, *spans), bf16), ((2, columns, fields), f32), ((2, columns, columns), f32)],
        whole_sum(cross), *own, stack, block, middle, ends, proj, low,
        scratch=[pltpu.VMEM((columns, cells), bf16)],
    )
    return block, jnp.swapaxes(proj, 1, 2), low


def solution(mesh):
    placed = (P(None, None, "slab", "col", None), P("slab", "col", None), P())
    return jax.shard_map(
        shards,
        mesh=mesh,
        in_specs=placed,
        out_specs=(P(None, "slab", "col", None), P(), P()),
        check_vma=False,
    )
```

```python
import functools
import math

import jax
import jax.numpy as jnp
from jax import lax
from jax.experimental import pallas as pl
from jax.experimental.pallas import tpu as pltpu
from jax.sharding import PartitionSpec as P

NN = (((1,), (0,)), ((), ()))
NT = (((1,), (1,)), ((), ()))
ROWS = 16


def dot(left, right, dims=NN):
    return lax.dot_general(left, right, dims, preferred_element_type=jnp.float32)


def swaps(axis, near, far, closed):
    count = lax.axis_size(axis)
    me = lax.axis_index(axis)
    pairs = [(i, (i - 1 ^ 1) + 1) for i in range(1, count - 1)]
    if closed:
        pairs += [(0, count - 1), (count - 1, 0)]
    inner = lax.ppermute(near, axis, [(i, i ^ 1) for i in range(count)])
    outer = lax.ppermute(far, axis, pairs)
    if closed:
        odd = me % 2 == 1
        low, high = jnp.where(odd, inner, outer), jnp.where(odd, outer, inner)
        return jnp.where(me == 0, 0, low), jnp.where(me == count - 1, 0, high)
    even = me % 2 == 0
    return jnp.where(even, outer, inner), jnp.where(even, inner, outer)


def cut_kernel(start, block, part):
    part[...] = block[:, pl.ds(pl.multiple_of(start[0], 128), part.shape[1])]


def cut(block, start, width):
    return pl.pallas_call(
        cut_kernel,
        out_shape=jax.ShapeDtypeStruct((block.shape[0], width), block.dtype),
        in_specs=[
            pl.BlockSpec(memory_space=pltpu.SMEM),
            pl.BlockSpec(memory_space=pltpu.VMEM),
        ],
        out_specs=pl.BlockSpec(memory_space=pltpu.VMEM),
        compiler_params=pltpu.CompilerParams(vmem_limit_bytes=4 * 1024 * 1024),
        name="cut",
    )(start.reshape(1), block)


def neighbours(block, span_x, span_y, depth, meanwhile=None):
    plane = span_y * depth
    top = (span_x - 1) * plane
    odd = lax.axis_index("slab") % 2 == 1
    near = jnp.where(odd, block[:, :plane], block[:, top:])
    far = cut(block, jnp.where(odd, top, 0), plane)
    xlo, xhi = swaps("slab", near, far, False)
    xlo, xhi, meanwhile = lax.optimization_barrier((xlo, xhi, meanwhile))

    def edge(row):
        at = row * depth
        parts = [xlo[:, at : at + depth]]
        parts += [block[:, x * plane + at : x * plane + at + depth] for x in range(span_x)]
        parts += [xhi[:, at : at + depth]]
        return jnp.concatenate(parts, axis=1)

    odd = lax.axis_index("col") % 2 == 1
    upward, downward = edge(span_y - 1), edge(0)
    ylo, yhi = swaps(
        "col", jnp.where(odd, downward, upward), jnp.where(odd, upward, downward), True
    )
    return (xlo, xhi), (ylo, yhi), meanwhile


def coefficients_kernel(table, cells, coef):
    classes = table.shape[0]
    lanes = lax.broadcasted_iota(jnp.int32, cells.shape, 1)
    depth = cells.shape[1]
    here = cells[...]
    below = pltpu.roll(here, depth - 1, 1)
    above = pltpu.roll(here, 1, 1)
    maps = (below, here, above)
    keep = (lanes < depth - 1, None, lanes > 0)
    for dz in range(3):
        masks = [maps[dz] == k for k in range(1, classes)]
        for pair in range(9):
            offset = 3 * pair + dz
            value = jnp.full(cells.shape, table[0, offset], jnp.float32)
            for k in range(1, classes):
                value = jnp.where(masks[k - 1], table[k, offset], value)
            if keep[dz] is not None:
                value = jnp.where(keep[dz], value, 0.0)
            coef[offset] = value


def coefficients(table, cell_map):
    span_x, span_y, depth = cell_map.shape
    lines = span_x * span_y
    return pl.pallas_call(
        coefficients_kernel,
        out_shape=jax.ShapeDtypeStruct((27, lines, depth), jnp.float32),
        in_specs=[
            pl.BlockSpec(memory_space=pltpu.SMEM),
            pl.BlockSpec(memory_space=pltpu.VMEM),
        ],
        out_specs=pl.BlockSpec(memory_space=pltpu.VMEM),
        compiler_params=pltpu.CompilerParams(vmem_limit_bytes=4 * 1024 * 1024),
        name="coefficients",
    )(table, cell_map.reshape(lines, depth))


def stencil(coef, spans, columns, lines, line, wanted, write):
    depth = spans[2]

    def tile(step, carry):
        rows = pl.ds(pl.multiple_of(step * ROWS, ROWS), ROWS)
        held = {}
        for x, y in lines:
            at = x * spans[1] + y
            sums = [None, None, None]
            for pair in range(9):
                there = x + pair // 3 - 1, y + pair % 3 - 1
                if not wanted(there[1]):
                    continue
                if there not in held:
                    held[there] = line(rows, *there)
                for dz in range(3):
                    term = coef[3 * pair + dz, at : at + 1, :] * held[there]
                    sums[dz] = term if sums[dz] is None else sums[dz] + term
            total = pltpu.roll(sums[0], 1, 1) + pltpu.roll(sums[2], depth - 1, 1)
            write(rows, x, y, sums[1] + total)
        return carry

    lax.fori_loop(0, columns // ROWS, tile, 0)


def middle_of(spans, x):
    _, span_y, depth = spans
    inner = (span_y - 2) * depth
    return pl.ds((x * span_y + 1) * depth, inner), pl.ds(x * inner, inner)


def ends_of(spans, x, last):
    _, span_y, depth = spans
    return (
        pl.ds((x * span_y + (span_y - 1) * last) * depth, depth),
        pl.ds((2 * x + last) * depth, depth),
    )


def products(image, cells, fields):
    w = image[...]
    rows = [jnp.concatenate([ref[first:, there] for there in cells], axis=1) for ref, first in fields]
    return dot(w, jnp.concatenate(rows + [w], axis=0), NT)


def middle_image_kernel(spans, first, coef, stack, block, xlo, xhi, middle, partial, cross):
    span_x, span_y, depth = spans

    def line(rows, x, y):
        ref, at = block, x * span_y + y
        if x < 0 or x >= span_x:
            ref, at = (xlo if x < 0 else xhi), y
        return ref[rows, at * depth : (at + 1) * depth].astype(jnp.float32)

    def write(rows, x, y, total):
        if 0 < y < span_y - 1:
            at = x * (span_y - 2) + y - 1
            middle[rows, at * depth : (at + 1) * depth] = total.astype(jnp.bfloat16)
        else:
            partial[rows, ends_of(spans, x, int(y > 0))[1]] = total

    lines = [(x, y) for y in range(span_y) for x in range(span_x)]
    stencil(coef, spans, block.shape[0], lines, line, lambda y: 0 <= y < span_y, write)
    cells = [middle_of(spans, x)[0] for x in range(span_x)]
    cross[...] = products(middle, cells, [(stack, first)] + ([(block, 0)] if first else []))


def end_lines(spans, coef, stack, block, partial, cross, ylo, yhi, ends):
    span_x, span_y, depth = spans

    def line(rows, x, y):
        return (ylo if y < 0 else yhi)[rows, (x + 1) * depth : (x + 2) * depth].astype(jnp.float32)

    def write(rows, x, y, total):
        own = ends_of(spans, x, int(y > 0))[1]
        ends[rows, own] = (partial[rows, own] + total).astype(jnp.bfloat16)

    lines = [(x, y) for y in (0, span_y - 1) for x in range(span_x)]
    stencil(coef, spans, ends.shape[0], lines, line, lambda y: not 0 <= y < span_y, write)
    cells = [ends_of(spans, x, last)[0] for x in range(span_x) for last in range(2)]
    fields = [(stack, 0)] if block is None else [(stack, ends.shape[0]), (block, 0)]
    return cross[...] + products(ends, cells, fields)


def subtracted(spans, middle, ends, moved, block):
    columns = ends.shape[0]
    moved = moved[:columns] + moved[columns:]
    pieces = []
    for x in range(spans[0]):
        pieces.append((middle, *middle_of(spans, x)))
        pieces += [(ends, *ends_of(spans, x, last)) for last in range(2)]
    for ref, there, own in pieces:
        less = moved[:, there.start : there.start + there.size]
        block[:, there] = (ref[:, own].astype(jnp.float32) - less).astype(jnp.bfloat16)


def places(size):
    return [lax.broadcasted_iota(jnp.int32, (size, size), dim) for dim in (0, 1)]


def diagonal_of(square, axis):
    row, column = places(square.shape[0])
    return jnp.sum(jnp.where(row == column, square, 0.0), axis=axis, keepdims=True)


def both_of(packed, diagonal):
    row, column = places(packed.shape[0])
    turned = packed.T
    two = jnp.where(row < column, packed, turned)
    return jnp.where(row >= column, packed, turned), jnp.where(row == column, diagonal, two)


def stack_gram_kernel(columns, stack, sides, right, diagonal):
    parts = [stack[b * columns : (b + 1) * columns] for b in range(3)]
    row, column = places(columns)
    second = dot(parts[1], parts[1], NT)
    pair = jnp.where(row >= column, dot(parts[0], parts[0], NT), second)
    sides[0] = jnp.concatenate(
        [dot(parts[0], parts[2], NT), dot(parts[1], parts[2], NT)], axis=1
    )
    sides[1] = jnp.concatenate([pair, dot(parts[0], parts[1], NT)], axis=1)
    nothing = jnp.zeros((columns, columns), jnp.float32)
    right[...] = jnp.concatenate([nothing, dot(parts[2], parts[2], NT)], axis=1)
    diagonal[...] = jnp.concatenate([diagonal_of(second, 0), nothing[:1]], axis=1)


def first_image_kernel(
    spans, coef, stack, sides, right, diagonal, partial, known, ylo, yhi, ends, cross
):
    columns = ends.shape[0]
    sums = end_lines(spans, coef, stack, None, partial, known, ylo, yhi, ends)
    cross[:columns] = sums[:, : 2 * columns]
    sums = sums[:, 2 * columns :]
    row, lane = (lax.broadcasted_iota(jnp.int32, sums.shape, dim) for dim in (0, 1))
    cross[columns : 2 * columns] = jnp.where(
        (lane >= columns) & (row >= lane - columns), right[...], sums
    )
    for i in range(2):
        cross[(2 + i) * columns : (3 + i) * columns] = sides[i]
    own = jnp.sum(jnp.where(row == lane - columns, sums, 0.0), axis=0, keepdims=True)
    cross[4 * columns :] = jnp.broadcast_to(
        diagonal[...] + own, (cross.shape[0] - 4 * columns, 2 * columns)
    )


def second_image_kernel(spans, coef, stack, block, partial, known, ylo, yhi, ends, cross):
    cross[...] = end_lines(spans, coef, stack, block, partial, known, ylo, yhi, ends)


def opened(cross, columns, scale):
    parts = [cross[i * columns : (i + 1) * columns] * scale for i in range(4)]
    left, right = ([part[:, at : at + columns] for part in parts] for at in (0, columns))
    diagonals = cross[4 * columns : 4 * columns + 1] * scale
    first = jnp.concatenate([parts[0], left[1]], axis=1)
    one, two = both_of(left[3], diagonals[:, :columns])
    three, square = both_of(right[1], diagonals[:, columns:])
    gram = [
        [one, right[3], left[2]],
        [right[3].T, two, right[2]],
        [left[2].T, right[2].T, three],
    ]
    gram = jnp.concatenate([jnp.concatenate(row, axis=1) for row in gram], axis=0)
    return first, square, gram


def split(values):
    high = values.astype(jnp.bfloat16)
    return high, (values - high.astype(jnp.float32)).astype(jnp.bfloat16)


def dots(lefts, rights, dims=NN):
    return sum(dot(left, right, dims) for left in lefts for right in rights)


def factor(square, sizes, across):
    size = square.shape[0]
    shape = (8, 2 * size)
    sub = lax.broadcasted_iota(jnp.int32, shape, 0)
    unit = lax.broadcasted_iota(jnp.int32, (size, size), 0) == lax.broadcasted_iota(
        jnp.int32, (size, size), 1
    )
    scale = lax.rsqrt(across)
    square = square * lax.rsqrt(sizes) * scale
    whole = jnp.concatenate([square, unit.astype(jnp.float32)], axis=1)
    blocks = [whole[b : b + 8] for b in range(0, size, 8)]
    done = []

    def row_of(values, at):
        return jnp.broadcast_to(values[at : at + 1, :], shape)

    def columns_of(values, first):
        return [
            jnp.broadcast_to(values[:, at : at + 1], shape) for at in range(first, first + 8)
        ]

    for b, here in enumerate(blocks):
        columns = columns_of(here, 8 * b)
        entry = {(i, j): row_of(columns[j], i) for j in range(8) for i in range(j + 1)}
        rows = [row_of(here, i) for i in range(8)]
        scaled = jnp.zeros(shape, jnp.float32)
        solved, ratio = [], {}
        if b + 1 < len(blocks):
            below = columns_of(blocks[b + 1], 8 * b)
        for p in range(0, 8, 2):
            q = p + 1
            first, mixed, last = entry[p, p], entry[p, q], entry[q, q]
            inverse = 1.0 / (first * last - mixed * mixed)

            def solve(one, two):
                return (
                    (last * one - mixed * two) * inverse,
                    (first * two - mixed * one) * inverse,
                )

            for j in range(p + 2, 8):
                ratio[p, j], ratio[q, j] = solve(entry[p, j], entry[q, j])
            for i in range(p + 2, 8):
                for j in range(i, 8):
                    change = entry[p, i] * ratio[p, j] + entry[q, i] * ratio[q, j]
                    entry[i, j] = entry[i, j] - change
                rows[i] = rows[i] - (ratio[p, i] * rows[p] + ratio[q, i] * rows[q])
            solved += solve(rows[p], rows[q])
            if b + 1 < len(blocks):
                change = below[p] * solved[p] + below[q] * solved[q]
                blocks[b + 1] = blocks[b + 1] - change
                for j in range(p + 2, 8):
                    below[j] = below[j] - (below[p] * ratio[p, j] + below[q] * ratio[q, j])
            part = mixed * (1.0 / first)
            scaled = jnp.where(sub == p, rows[p] * lax.rsqrt(first), scaled)
            rest = (rows[q] - part * rows[p]) * lax.rsqrt(last - part * mixed)
            scaled = jnp.where(sub == q, rest, scaled)
        done.append(scaled)
        for p in (4, 2, 0):
            for r in (p, p + 1):
                for j in range(p + 2, 8):
                    solved[r] = solved[r] - ratio[r, j] * solved[j]
        for later in range(b + 2, len(blocks)):
            parts = [one * two for one, two in zip(columns_of(blocks[later], 8 * b), solved)]
            while len(parts) > 1:
                parts = [one + two for one, two in zip(parts[::2], parts[1::2])]
            blocks[later] = blocks[later] - parts[0]
    done = jnp.concatenate(done, axis=0)
    above = lax.broadcasted_iota(jnp.int32, (size, size), 0) <= lax.broadcasted_iota(
        jnp.int32, (size, size), 1
    )
    return jnp.where(above, done[:, :size] * (across * scale), 0.0), done[:, size:] * scale


def project(first, square, own):
    first_parts = split(first)
    first_low = first_parts[0]
    second = first - dots((first_low,), own)
    second_low = second.astype(jnp.bfloat16)
    used = (first_low, second_low)
    sizes = [diagonal_of(square, axis) for axis in (1, 0)]
    square = square - dots(used, first_parts, NT)
    rest = second - dots((second_low,), own)
    square = square - dots(split(rest), used, NT)
    return used, first + second, rest, square, sizes


def first_solve_kernel(
    scale, spans, cross, stack, middle, ends, block, proj, low, rest, square, inverse
):
    columns = ends.shape[0]
    first, own_square, gram = opened(cross, columns, scale)
    used, proj[...], rest[...], square_here, sizes = project(first, own_square, split(gram))
    square[...] = square_here
    moved = dot(jnp.concatenate(used, axis=0), stack[...])
    subtracted(spans, middle, ends, moved, block)
    upper, inverse_here = factor(square_here, *sizes)
    low[...] = upper.T
    inverse_here = inverse_here.astype(jnp.bfloat16)
    inverse[...] = inverse_here
    block[...] = dot(inverse_here, block[...]).astype(jnp.bfloat16)


def next_gram_kernel(scale, cross, rest, square, inverse, high, low):
    columns = square.shape[0]
    kept = rest.shape[1] - columns
    _, _, gram = opened(cross, columns, scale)
    mixed = dots((inverse[...],), split(rest[:, columns:]))
    corner = dots((inverse[...],), split(square[...]))
    corner = dots(split(corner), (inverse[...],), NT)
    for part, (old, side, end) in zip(
        (high, low), zip(split(gram[columns:, columns:]), split(mixed), split(corner))
    ):
        part[:kept, :kept] = old
        part[kept:, :kept] = side
        part[:kept, kept:] = side.T
        part[kept:, kept:] = end


def second_solve_kernel(
    scale, cross, own_high, own_low, stack, last, middle, ends, proj_in, low_in, result, proj, low,
    block,
):
    columns = ends.shape[0]
    kept = stack.shape[0] - columns
    fields = stack.shape[0]
    sums = cross[...] * scale
    used, proj[1], _, square, sizes = project(
        sums[:, :fields], sums[:, fields:], (own_high[...], own_low[...])
    )
    proj[0] = proj_in[...]
    low[0] = low_in[...]
    _, span_x, span_y, depth = result.shape
    both = jnp.concatenate(used, axis=0)
    moved = dot(both[:, :kept], stack[columns:]) + dot(both[:, kept:], last[...])
    subtracted((span_x, span_y, depth), middle, ends, moved, block)
    upper, inverse = factor(square, *sizes)
    low[1] = upper.T
    inverse = inverse.astype(jnp.bfloat16)
    plane = span_y * depth
    for x in range(span_x):
        part = dot(inverse, block[:, x * plane : (x + 1) * plane])
        result[:, x] = part.reshape(columns, span_y, depth).astype(jnp.bfloat16)


def partner(part, mask):
    axes = ("slab", "col")
    count = lax.axis_size("slab") * lax.axis_size("col")
    return lax.ppermute(part, axes, [(i, i ^ mask) for i in range(count)])


def whole_sum(part):
    cols = lax.axis_size("col")
    count = lax.axis_size("slab") * cols
    index = lax.axis_index("slab") * cols + lax.axis_index("col")
    bit, upper = 1, 0
    while bit < count:
        upper = upper ^ (index // bit % 2)
        bit *= 4
    upper = upper == 1
    half = part.shape[0] // 2
    low, high = part[:half], part[half:]
    part = jnp.where(upper, high, low) + partner(jnp.where(upper, low, high), 1)
    bit = 2
    while bit < count:
        if 2 * bit < count:
            one, two, both = (partner(part, mask) for mask in (bit, 2 * bit + 1, 3 * bit + 1))
            part = (part + one) + (both + two)
            bit *= 4
        else:
            part = part + partner(part, bit)
            bit *= 2
    other = partner(part, 1)
    return jnp.concatenate([jnp.where(upper, other, part), jnp.where(upper, part, other)], axis=0)


def call(kernel, name, outs, *args, flops=0, scratch=()):
    moved = sum(math.prod(arg.shape) * arg.dtype.itemsize for arg in args)
    moved += sum(math.prod(shape) * jnp.dtype(dtype).itemsize for shape, dtype in outs)
    return pl.pallas_call(
        kernel,
        out_shape=[jax.ShapeDtypeStruct(shape, dtype) for shape, dtype in outs],
        in_specs=[pl.BlockSpec(memory_space=pltpu.VMEM)] * len(args),
        out_specs=[pl.BlockSpec(memory_space=pltpu.VMEM)] * len(outs),
        scratch_shapes=scratch,
        compiler_params=pltpu.CompilerParams(vmem_limit_bytes=24 * 1024 * 1024),
        cost_estimate=pl.CostEstimate(flops=flops, bytes_accessed=moved, transcendentals=0),
        name=name,
    )(*args)


def shards(basis, cell_map, table):
    span_x, span_y, depth = cell_map.shape
    blocks, columns = basis.shape[:2]
    cells = span_x * span_y * depth
    fields = blocks * columns
    scale = 1.0 / (cells * lax.axis_size("slab") * lax.axis_size("col"))
    spans = (span_x, span_y, depth)
    f32, bf16 = jnp.float32, jnp.bfloat16

    stack = basis.reshape(fields, cells)
    coef = coefficients(table, cell_map)
    own = call(
        functools.partial(stack_gram_kernel, columns),
        "stack_gram",
        [((2, columns, 2 * columns), f32), ((columns, 2 * columns), f32), ((1, 2 * columns), f32)],
        stack,
        flops=2 * fields * fields * cells,
    )

    end_cells = 2 * span_x * depth

    def middle_image(first, stack, block, planes):
        return call(
            functools.partial(middle_image_kernel, spans, first),
            "middle_image",
            [((columns, cells - end_cells), bf16), ((columns, end_cells), f32),
             ((columns, fields + columns), f32)],
            coef, stack, block, *planes,
            flops=2 * 27 * columns * cells,
        )

    last = basis[blocks - 1].reshape(columns, cells)
    planes, lines, (coef, stack, own) = neighbours(last, *spans, (coef, stack, own))
    middle, partial, known = middle_image(0, stack, last, planes)
    ends, cross = call(
        functools.partial(first_image_kernel, spans),
        "first_image",
        [((columns, end_cells), bf16), ((4 * columns + 16, 2 * columns), f32)],
        coef, stack, *own, partial, known, *lines,
    )
    cross = whole_sum(cross)
    block, proj, low, rest, square, inverse = call(
        functools.partial(first_solve_kernel, scale, spans),
        "first_solve",
        [((columns, cells), bf16), ((columns, fields), f32), ((columns, columns), f32),
         ((columns, fields), f32), ((columns, columns), f32), ((columns, columns), bf16)],
        cross, stack, middle, ends,
    )
    own = call(
        functools.partial(next_gram_kernel, scale),
        "next_gram",
        [((fields, fields), bf16)] * 2,
        cross, rest, square, inverse,
    )
    planes, lines, _ = neighbours(block, *spans)
    middle, partial, known = middle_image(columns, stack, block, planes)
    ends, cross = call(
        functools.partial(second_image_kernel, spans),
        "second_image",
        [((columns, end_cells), bf16), ((columns, fields + columns), f32)],
        coef, stack, block, partial, known, *lines,
    )
    block, proj, low = call(
        functools.partial(second_solve_kernel, scale),
        "second_solve",
        [((columns, *spans), bf16), ((2, columns, fields), f32), ((2, columns, columns), f32)],
        whole_sum(cross), *own, stack, block, middle, ends, proj, low,
        scratch=[pltpu.VMEM((columns, cells), bf16)],
    )
    return block, jnp.swapaxes(proj, 1, 2), low


def solution(mesh):
    placed = (P(None, None, "slab", "col", None), P("slab", "col", None), P())
    return jax.shard_map(
        shards,
        mesh=mesh,
        in_specs=placed,
        out_specs=(P(None, "slab", "col", None), P(), P()),
        check_vma=False,
    )
```

```python
import functools
import math

import jax
import jax.numpy as jnp
from jax import lax
from jax.experimental import pallas as pl
from jax.experimental.pallas import tpu as pltpu
from jax.sharding import PartitionSpec as P

NN = (((1,), (0,)), ((), ()))
NT = (((1,), (1,)), ((), ()))
ROWS = 16


def dot(left, right, dims=NN):
    return lax.dot_general(left, right, dims, preferred_element_type=jnp.float32)


def swaps(axis, near, far):
    count = lax.axis_size(axis)
    me = lax.axis_index(axis)
    pairs = [(i, (i - 1 ^ 1) + 1) for i in range(1, count - 1)]
    inner = lax.ppermute(near, axis, [(i, i ^ 1) for i in range(count)])
    outer = lax.ppermute(far, axis, pairs + [(0, count - 1), (count - 1, 0)])
    if axis == "slab":
        even = me % 2 == 0
        low, high = jnp.where(even, outer, inner), jnp.where(even, inner, outer)
    else:
        odd = me % 2 == 1
        low, high = jnp.where(odd, inner, outer), jnp.where(odd, outer, inner)
    return jnp.where(me == 0, 0, low), jnp.where(me == count - 1, 0, high)


def cut_kernel(start, block, part):
    part[...] = block[:, pl.ds(pl.multiple_of(start[0], 128), part.shape[1])]


def cut(block, start, width):
    return pl.pallas_call(
        cut_kernel,
        out_shape=jax.ShapeDtypeStruct((block.shape[0], width), block.dtype),
        in_specs=[
            pl.BlockSpec(memory_space=pltpu.SMEM),
            pl.BlockSpec(memory_space=pltpu.VMEM),
        ],
        out_specs=pl.BlockSpec(memory_space=pltpu.VMEM),
        compiler_params=pltpu.CompilerParams(vmem_limit_bytes=4 * 1024 * 1024),
        name="cut",
    )(start.reshape(1), block)


def neighbours(block, span_x, span_y, depth, meanwhile=None):
    plane = span_y * depth
    top = (span_x - 1) * plane
    odd = lax.axis_index("slab") % 2 == 1
    near = jnp.where(odd, block[:, :plane], block[:, top:])
    far = cut(block, jnp.where(odd, top, 0), plane)
    xlo, xhi = swaps("slab", near, far)
    xlo, xhi, meanwhile = lax.optimization_barrier((xlo, xhi, meanwhile))

    def edge(row):
        at = row * depth
        parts = [xlo[:, at : at + depth]]
        parts += [block[:, x * plane + at : x * plane + at + depth] for x in range(span_x)]
        parts += [xhi[:, at : at + depth]]
        return jnp.concatenate(parts, axis=1)

    odd = lax.axis_index("col") % 2 == 1
    upward, downward = edge(span_y - 1), edge(0)
    ylo, yhi = swaps(
        "col", jnp.where(odd, downward, upward), jnp.where(odd, upward, downward)
    )
    return (xlo, xhi), (ylo, yhi), meanwhile


def coefficients_kernel(table, cells, coef):
    classes = table.shape[0]
    lanes = lax.broadcasted_iota(jnp.int32, cells.shape, 1)
    depth = cells.shape[1]
    here = cells[...]
    below = pltpu.roll(here, depth - 1, 1)
    above = pltpu.roll(here, 1, 1)
    maps = (below, here, above)
    keep = (lanes < depth - 1, None, lanes > 0)
    for dz in range(3):
        masks = [maps[dz] == k for k in range(1, classes)]
        for pair in range(9):
            offset = 3 * pair + dz
            value = jnp.full(cells.shape, table[0, offset], jnp.float32)
            for k in range(1, classes):
                value = jnp.where(masks[k - 1], table[k, offset], value)
            if keep[dz] is not None:
                value = jnp.where(keep[dz], value, 0.0)
            coef[offset] = value


def coefficients(table, cell_map):
    span_x, span_y, depth = cell_map.shape
    lines = span_x * span_y
    return pl.pallas_call(
        coefficients_kernel,
        out_shape=jax.ShapeDtypeStruct((27, lines, depth), jnp.float32),
        in_specs=[
            pl.BlockSpec(memory_space=pltpu.SMEM),
            pl.BlockSpec(memory_space=pltpu.VMEM),
        ],
        out_specs=pl.BlockSpec(memory_space=pltpu.VMEM),
        compiler_params=pltpu.CompilerParams(vmem_limit_bytes=4 * 1024 * 1024),
        name="coefficients",
    )(table, cell_map.reshape(lines, depth))


def stencil(coef, spans, columns, lines, line, wanted, write):
    depth = spans[2]

    def tile(step, carry):
        rows = pl.ds(pl.multiple_of(step * ROWS, ROWS), ROWS)
        held = {}
        for x, y in lines:
            at = x * spans[1] + y
            sums = [None, None, None]
            for pair in range(9):
                there = x + pair // 3 - 1, y + pair % 3 - 1
                if not wanted(there[1]):
                    continue
                if there not in held:
                    held[there] = line(rows, *there)
                for dz in range(3):
                    term = coef[3 * pair + dz, at : at + 1, :] * held[there]
                    sums[dz] = term if sums[dz] is None else sums[dz] + term
            total = pltpu.roll(sums[0], 1, 1) + pltpu.roll(sums[2], depth - 1, 1)
            write(rows, x, y, sums[1] + total)
        return carry

    lax.fori_loop(0, columns // ROWS, tile, 0)


def middle_of(spans, x):
    _, span_y, depth = spans
    inner = (span_y - 2) * depth
    return pl.ds((x * span_y + 1) * depth, inner), pl.ds(x * inner, inner)


def ends_of(spans, x, last):
    _, span_y, depth = spans
    return (
        pl.ds((x * span_y + (span_y - 1) * last) * depth, depth),
        pl.ds((2 * x + last) * depth, depth),
    )


def products(image, cells, fields):
    w = image[...]
    rows = [jnp.concatenate([ref[first:, there] for there in cells], axis=1) for ref, first in fields]
    return dot(w, jnp.concatenate(rows + [w], axis=0), NT)


def middle_image_kernel(spans, first, coef, stack, block, xlo, xhi, middle, partial, cross):
    span_x, span_y, depth = spans

    def line(rows, x, y):
        ref, at = block, x * span_y + y
        if x < 0 or x >= span_x:
            ref, at = (xlo if x < 0 else xhi), y
        return ref[rows, at * depth : (at + 1) * depth].astype(jnp.float32)

    def write(rows, x, y, total):
        if 0 < y < span_y - 1:
            at = x * (span_y - 2) + y - 1
            middle[rows, at * depth : (at + 1) * depth] = total.astype(jnp.bfloat16)
        else:
            partial[rows, ends_of(spans, x, int(y > 0))[1]] = total

    lines = [(x, y) for y in range(span_y) for x in range(span_x)]
    stencil(coef, spans, block.shape[0], lines, line, lambda y: 0 <= y < span_y, write)
    cells = [middle_of(spans, x)[0] for x in range(span_x)]
    cross[...] = products(middle, cells, [(stack, first)] + ([(block, 0)] if first else []))


def end_lines(spans, coef, stack, block, partial, cross, ylo, yhi, ends):
    span_x, span_y, depth = spans

    def line(rows, x, y):
        return (ylo if y < 0 else yhi)[rows, (x + 1) * depth : (x + 2) * depth].astype(jnp.float32)

    def write(rows, x, y, total):
        own = ends_of(spans, x, int(y > 0))[1]
        ends[rows, own] = (partial[rows, own] + total).astype(jnp.bfloat16)

    lines = [(x, y) for y in (0, span_y - 1) for x in range(span_x)]
    stencil(coef, spans, ends.shape[0], lines, line, lambda y: not 0 <= y < span_y, write)
    cells = [ends_of(spans, x, last)[0] for x in range(span_x) for last in range(2)]
    fields = [(stack, 0)] if block is None else [(stack, ends.shape[0]), (block, 0)]
    return cross[...] + products(ends, cells, fields)


def subtracted(spans, middle, ends, moved, block):
    columns = ends.shape[0]
    moved = moved[:columns] + moved[columns:]
    pieces = []
    for x in range(spans[0]):
        pieces.append((middle, *middle_of(spans, x)))
        pieces += [(ends, *ends_of(spans, x, last)) for last in range(2)]
    for ref, there, own in pieces:
        less = moved[:, there.start : there.start + there.size]
        block[:, there] = (ref[:, own].astype(jnp.float32) - less).astype(jnp.bfloat16)


def places(size):
    return [lax.broadcasted_iota(jnp.int32, (size, size), dim) for dim in (0, 1)]


def diagonal_of(square, axis):
    row, column = places(square.shape[0])
    return jnp.sum(jnp.where(row == column, square, 0.0), axis=axis, keepdims=True)


def both_of(packed, diagonal):
    row, column = places(packed.shape[0])
    turned = packed.T
    two = jnp.where(row < column, packed, turned)
    return jnp.where(row >= column, packed, turned), jnp.where(row == column, diagonal, two)


def stack_gram_kernel(columns, stack, sides, right, diagonal):
    parts = [stack[b * columns : (b + 1) * columns] for b in range(3)]
    row, column = places(columns)
    second = dot(parts[1], parts[1], NT)
    pair = jnp.where(row >= column, dot(parts[0], parts[0], NT), second)
    sides[0] = jnp.concatenate(
        [dot(parts[0], parts[2], NT), dot(parts[1], parts[2], NT)], axis=1
    )
    sides[1] = jnp.concatenate([pair, dot(parts[0], parts[1], NT)], axis=1)
    nothing = jnp.zeros((columns, columns), jnp.float32)
    right[...] = jnp.concatenate([nothing, dot(parts[2], parts[2], NT)], axis=1)
    diagonal[...] = jnp.concatenate([diagonal_of(second, 0), nothing[:1]], axis=1)


def first_image_kernel(
    spans, coef, stack, sides, right, diagonal, partial, known, ylo, yhi, ends, cross
):
    columns = ends.shape[0]
    sums = end_lines(spans, coef, stack, None, partial, known, ylo, yhi, ends)
    cross[:columns] = sums[:, : 2 * columns]
    sums = sums[:, 2 * columns :]
    row, lane = (lax.broadcasted_iota(jnp.int32, sums.shape, dim) for dim in (0, 1))
    cross[columns : 2 * columns] = jnp.where(
        (lane >= columns) & (row >= lane - columns), right[...], sums
    )
    for i in range(2):
        cross[(2 + i) * columns : (3 + i) * columns] = sides[i]
    own = jnp.sum(jnp.where(row == lane - columns, sums, 0.0), axis=0, keepdims=True)
    cross[4 * columns :] = jnp.broadcast_to(
        diagonal[...] + own, (cross.shape[0] - 4 * columns, 2 * columns)
    )


def second_image_kernel(spans, coef, stack, block, partial, known, ylo, yhi, ends, cross):
    cross[...] = end_lines(spans, coef, stack, block, partial, known, ylo, yhi, ends)


def opened(cross, columns, scale):
    parts = [cross[i * columns : (i + 1) * columns] * scale for i in range(4)]
    left, right = ([part[:, at : at + columns] for part in parts] for at in (0, columns))
    diagonals = cross[4 * columns : 4 * columns + 1] * scale
    first = jnp.concatenate([parts[0], left[1]], axis=1)
    one, two = both_of(left[3], diagonals[:, :columns])
    three, square = both_of(right[1], diagonals[:, columns:])
    gram = [
        [one, right[3], left[2]],
        [right[3].T, two, right[2]],
        [left[2].T, right[2].T, three],
    ]
    gram = jnp.concatenate([jnp.concatenate(row, axis=1) for row in gram], axis=0)
    return first, square, gram


def split(values):
    high = values.astype(jnp.bfloat16)
    return high, (values - high.astype(jnp.float32)).astype(jnp.bfloat16)


def dots(lefts, rights, dims=NN):
    return sum(dot(left, right, dims) for left in lefts for right in rights)


def factor(square, sizes, across):
    size = square.shape[0]
    shape = (8, 2 * size)
    sub = lax.broadcasted_iota(jnp.int32, shape, 0)
    unit = lax.broadcasted_iota(jnp.int32, (size, size), 0) == lax.broadcasted_iota(
        jnp.int32, (size, size), 1
    )
    scale = lax.rsqrt(across)
    square = square * lax.rsqrt(sizes) * scale
    whole = jnp.concatenate([square, unit.astype(jnp.float32)], axis=1)
    blocks = [whole[b : b + 8] for b in range(0, size, 8)]
    done = []

    def row_of(values, at):
        return jnp.broadcast_to(values[at : at + 1, :], shape)

    def columns_of(values, first):
        return [
            jnp.broadcast_to(values[:, at : at + 1], shape) for at in range(first, first + 8)
        ]

    for b, here in enumerate(blocks):
        columns = columns_of(here, 8 * b)
        entry = {(i, j): row_of(columns[j], i) for j in range(8) for i in range(j + 1)}
        rows = [row_of(here, i) for i in range(8)]
        scaled = jnp.zeros(shape, jnp.float32)
        solved, ratio = [], {}
        if b + 1 < len(blocks):
            below = columns_of(blocks[b + 1], 8 * b)
        for p in range(0, 8, 2):
            q = p + 1
            first, mixed, last = entry[p, p], entry[p, q], entry[q, q]
            inverse = 1.0 / (first * last - mixed * mixed)

            def solve(one, two):
                return (
                    (last * one - mixed * two) * inverse,
                    (first * two - mixed * one) * inverse,
                )

            for j in range(p + 2, 8):
                ratio[p, j], ratio[q, j] = solve(entry[p, j], entry[q, j])
            for i in range(p + 2, 8):
                for j in range(i, 8):
                    change = entry[p, i] * ratio[p, j] + entry[q, i] * ratio[q, j]
                    entry[i, j] = entry[i, j] - change
                rows[i] = rows[i] - (ratio[p, i] * rows[p] + ratio[q, i] * rows[q])
            solved += solve(rows[p], rows[q])
            if b + 1 < len(blocks):
                change = below[p] * solved[p] + below[q] * solved[q]
                blocks[b + 1] = blocks[b + 1] - change
                for j in range(p + 2, 8):
                    below[j] = below[j] - (below[p] * ratio[p, j] + below[q] * ratio[q, j])
            part = mixed * (1.0 / first)
            scaled = jnp.where(sub == p, rows[p] * lax.rsqrt(first), scaled)
            rest = (rows[q] - part * rows[p]) * lax.rsqrt(last - part * mixed)
            scaled = jnp.where(sub == q, rest, scaled)
        done.append(scaled)
        for p in (4, 2, 0):
            for r in (p, p + 1):
                for j in range(p + 2, 8):
                    solved[r] = solved[r] - ratio[r, j] * solved[j]
        for later in range(b + 2, len(blocks)):
            parts = [one * two for one, two in zip(columns_of(blocks[later], 8 * b), solved)]
            while len(parts) > 1:
                parts = [one + two for one, two in zip(parts[::2], parts[1::2])]
            blocks[later] = blocks[later] - parts[0]
    done = jnp.concatenate(done, axis=0)
    above = lax.broadcasted_iota(jnp.int32, (size, size), 0) <= lax.broadcasted_iota(
        jnp.int32, (size, size), 1
    )
    return jnp.where(above, done[:, :size] * (across * scale), 0.0), done[:, size:] * scale


def project(first, square, own):
    first_parts = split(first)
    first_low = first_parts[0]
    second = first - dots((first_low,), own)
    second_low = second.astype(jnp.bfloat16)
    used = (first_low, second_low)
    sizes = [diagonal_of(square, axis) for axis in (1, 0)]
    square = square - dots(used, first_parts, NT)
    rest = second - dots((second_low,), own)
    square = square - dots(split(rest), used, NT)
    return used, first + second, rest, square, sizes


def first_solve_kernel(
    scale, spans, cross, stack, middle, ends, block, proj, low, rest, square, inverse
):
    columns = ends.shape[0]
    first, own_square, gram = opened(cross, columns, scale)
    used, proj[...], rest[...], square_here, sizes = project(first, own_square, split(gram))
    square[...] = square_here
    moved = dot(jnp.concatenate(used, axis=0), stack[...])
    subtracted(spans, middle, ends, moved, block)
    upper, inverse_here = factor(square_here, *sizes)
    low[...] = upper.T
    inverse_here = inverse_here.astype(jnp.bfloat16)
    inverse[...] = inverse_here
    block[...] = dot(inverse_here, block[...]).astype(jnp.bfloat16)


def next_gram_kernel(scale, cross, rest, square, inverse, high, low):
    columns = square.shape[0]
    kept = rest.shape[1] - columns
    _, _, gram = opened(cross, columns, scale)
    mixed = dots((inverse[...],), split(rest[:, columns:]))
    corner = dots((inverse[...],), split(square[...]))
    corner = dots(split(corner), (inverse[...],), NT)
    for part, (old, side, end) in zip(
        (high, low), zip(split(gram[columns:, columns:]), split(mixed), split(corner))
    ):
        part[:kept, :kept] = old
        part[kept:, :kept] = side
        part[:kept, kept:] = side.T
        part[kept:, kept:] = end


def second_solve_kernel(
    scale, cross, own_high, own_low, stack, last, middle, ends, proj_in, low_in, result, proj, low,
    block,
):
    columns = ends.shape[0]
    kept = stack.shape[0] - columns
    fields = stack.shape[0]
    sums = cross[...] * scale
    used, proj[1], _, square, sizes = project(
        sums[:, :fields], sums[:, fields:], (own_high[...], own_low[...])
    )
    proj[0] = proj_in[...]
    low[0] = low_in[...]
    _, span_x, span_y, depth = result.shape
    both = jnp.concatenate(used, axis=0)
    moved = dot(both[:, :kept], stack[columns:]) + dot(both[:, kept:], last[...])
    subtracted((span_x, span_y, depth), middle, ends, moved, block)
    upper, inverse = factor(square, *sizes)
    low[1] = upper.T
    inverse = inverse.astype(jnp.bfloat16)
    plane = span_y * depth
    for x in range(span_x):
        part = dot(inverse, block[:, x * plane : (x + 1) * plane])
        result[:, x] = part.reshape(columns, span_y, depth).astype(jnp.bfloat16)


def partner(part, mask):
    axes = ("slab", "col")
    count = lax.axis_size("slab") * lax.axis_size("col")
    return lax.ppermute(part, axes, [(i, i ^ mask) for i in range(count)])


def whole_sum(part):
    cols = lax.axis_size("col")
    count = lax.axis_size("slab") * cols
    index = lax.axis_index("slab") * cols + lax.axis_index("col")
    bit, upper = 1, 0
    while bit < count:
        upper = upper ^ (index // bit % 2)
        bit *= 2
    upper = upper == 1
    half = part.shape[0] // 2
    low, high = part[:half], part[half:]
    part = jnp.where(upper, high, low) + partner(jnp.where(upper, low, high), 1)
    bit = 2
    while bit < count:
        if 2 * bit < count:
            one, two, both = (partner(part, mask) for mask in (bit + 1, 2 * bit + 1, 3 * bit))
            part = (part + one) + (both + two)
            bit *= 4
        else:
            part = part + partner(part, bit + 1)
            bit *= 2
    other = partner(part, 1)
    return jnp.concatenate([jnp.where(upper, other, part), jnp.where(upper, part, other)], axis=0)


def call(kernel, name, outs, *args, flops=0, scratch=()):
    moved = sum(math.prod(arg.shape) * arg.dtype.itemsize for arg in args)
    moved += sum(math.prod(shape) * jnp.dtype(dtype).itemsize for shape, dtype in outs)
    return pl.pallas_call(
        kernel,
        out_shape=[jax.ShapeDtypeStruct(shape, dtype) for shape, dtype in outs],
        in_specs=[pl.BlockSpec(memory_space=pltpu.VMEM)] * len(args),
        out_specs=[pl.BlockSpec(memory_space=pltpu.VMEM)] * len(outs),
        scratch_shapes=scratch,
        compiler_params=pltpu.CompilerParams(vmem_limit_bytes=24 * 1024 * 1024),
        cost_estimate=pl.CostEstimate(flops=flops, bytes_accessed=moved, transcendentals=0),
        name=name,
    )(*args)


def shards(basis, cell_map, table):
    span_x, span_y, depth = cell_map.shape
    blocks, columns = basis.shape[:2]
    cells = span_x * span_y * depth
    fields = blocks * columns
    scale = 1.0 / (cells * lax.axis_size("slab") * lax.axis_size("col"))
    spans = (span_x, span_y, depth)
    f32, bf16 = jnp.float32, jnp.bfloat16

    stack = basis.reshape(fields, cells)
    coef = coefficients(table, cell_map)
    own = call(
        functools.partial(stack_gram_kernel, columns),
        "stack_gram",
        [((2, columns, 2 * columns), f32), ((columns, 2 * columns), f32), ((1, 2 * columns), f32)],
        stack,
        flops=2 * fields * fields * cells,
    )

    end_cells = 2 * span_x * depth

    def middle_image(first, stack, block, planes):
        return call(
            functools.partial(middle_image_kernel, spans, first),
            "middle_image",
            [((columns, cells - end_cells), bf16), ((columns, end_cells), f32),
             ((columns, fields + columns), f32)],
            coef, stack, block, *planes,
            flops=2 * 27 * columns * cells,
        )

    last = basis[blocks - 1].reshape(columns, cells)
    planes, lines, (coef, stack, own) = neighbours(last, *spans, (coef, stack, own))
    middle, partial, known = middle_image(0, stack, last, planes)
    ends, cross = call(
        functools.partial(first_image_kernel, spans),
        "first_image",
        [((columns, end_cells), bf16), ((4 * columns + 16, 2 * columns), f32)],
        coef, stack, *own, partial, known, *lines,
    )
    cross = whole_sum(cross)
    block, proj, low, rest, square, inverse = call(
        functools.partial(first_solve_kernel, scale, spans),
        "first_solve",
        [((columns, cells), bf16), ((columns, fields), f32), ((columns, columns), f32),
         ((columns, fields), f32), ((columns, columns), f32), ((columns, columns), bf16)],
        cross, stack, middle, ends,
    )
    own = call(
        functools.partial(next_gram_kernel, scale),
        "next_gram",
        [((fields, fields), bf16)] * 2,
        cross, rest, square, inverse,
    )
    planes, lines, _ = neighbours(block, *spans)
    middle, partial, known = middle_image(columns, stack, block, planes)
    ends, cross = call(
        functools.partial(second_image_kernel, spans),
        "second_image",
        [((columns, end_cells), bf16), ((columns, fields + columns), f32)],
        coef, stack, block, partial, known, *lines,
    )
    block, proj, low = call(
        functools.partial(second_solve_kernel, scale),
        "second_solve",
        [((columns, *spans), bf16), ((2, columns, fields), f32), ((2, columns, columns), f32)],
        whole_sum(cross), *own, stack, block, middle, ends, proj, low,
        scratch=[pltpu.VMEM((columns, cells), bf16)],
    )
    return block, jnp.swapaxes(proj, 1, 2), low


def solution(mesh):
    placed = (P(None, None, "slab", "col", None), P("slab", "col", None), P())
    return jax.shard_map(
        shards,
        mesh=mesh,
        in_specs=placed,
        out_specs=(P(None, "slab", "col", None), P(), P()),
        check_vma=False,
    )
```

```python
import functools
import math

import jax
import jax.numpy as jnp
from jax import lax
from jax.experimental import pallas as pl
from jax.experimental.pallas import tpu as pltpu
from jax.sharding import PartitionSpec as P

NN = (((1,), (0,)), ((), ()))
NT = (((1,), (1,)), ((), ()))
ROWS = 16


def dot(left, right, dims=NN):
    return lax.dot_general(left, right, dims, preferred_element_type=jnp.float32)


def swaps(axis, near, far):
    count = lax.axis_size(axis)
    me = lax.axis_index(axis)
    pairs = [(i, (i - 1 ^ 1) + 1) for i in range(1, count - 1)]
    inner = lax.ppermute(near, axis, [(i, i ^ 1) for i in range(count)])
    outer = lax.ppermute(far, axis, pairs + [(0, count - 1), (count - 1, 0)])
    if axis == "slab":
        odd = me % 2 == 1
        low, high = jnp.where(odd, inner, outer), jnp.where(odd, outer, inner)
    else:
        odd = me % 2 == 1
        low, high = jnp.where(odd, inner, outer), jnp.where(odd, outer, inner)
    return jnp.where(me == 0, 0, low), jnp.where(me == count - 1, 0, high)


def cut_kernel(start, block, part):
    part[...] = block[:, pl.ds(pl.multiple_of(start[0], 128), part.shape[1])]


def cut(block, start, width):
    return pl.pallas_call(
        cut_kernel,
        out_shape=jax.ShapeDtypeStruct((block.shape[0], width), block.dtype),
        in_specs=[
            pl.BlockSpec(memory_space=pltpu.SMEM),
            pl.BlockSpec(memory_space=pltpu.VMEM),
        ],
        out_specs=pl.BlockSpec(memory_space=pltpu.VMEM),
        compiler_params=pltpu.CompilerParams(vmem_limit_bytes=4 * 1024 * 1024),
        name="cut",
    )(start.reshape(1), block)


def neighbours(block, span_x, span_y, depth, meanwhile=None):
    plane = span_y * depth
    top = (span_x - 1) * plane
    odd = lax.axis_index("slab") % 2 == 1
    near = jnp.where(odd, block[:, :plane], block[:, top:])
    far = cut(block, jnp.where(odd, top, 0), plane)
    xlo, xhi = swaps("slab", near, far)
    xlo, xhi, meanwhile = lax.optimization_barrier((xlo, xhi, meanwhile))

    def edge(row):
        at = row * depth
        parts = [xlo[:, at : at + depth]]
        parts += [block[:, x * plane + at : x * plane + at + depth] for x in range(span_x)]
        parts += [xhi[:, at : at + depth]]
        return jnp.concatenate(parts, axis=1)

    odd = lax.axis_index("col") % 2 == 1
    upward, downward = edge(span_y - 1), edge(0)
    ylo, yhi = swaps(
        "col", jnp.where(odd, downward, upward), jnp.where(odd, upward, downward)
    )
    return (xlo, xhi), (ylo, yhi), meanwhile


def coefficients_kernel(table, cells, coef):
    classes = table.shape[0]
    lanes = lax.broadcasted_iota(jnp.int32, cells.shape, 1)
    depth = cells.shape[1]
    here = cells[...]
    below = pltpu.roll(here, depth - 1, 1)
    above = pltpu.roll(here, 1, 1)
    maps = (below, here, above)
    keep = (lanes < depth - 1, None, lanes > 0)
    for dz in range(3):
        masks = [maps[dz] == k for k in range(1, classes)]
        for pair in range(9):
            offset = 3 * pair + dz
            value = jnp.full(cells.shape, table[0, offset], jnp.float32)
            for k in range(1, classes):
                value = jnp.where(masks[k - 1], table[k, offset], value)
            if keep[dz] is not None:
                value = jnp.where(keep[dz], value, 0.0)
            coef[offset] = value


def coefficients(table, cell_map):
    span_x, span_y, depth = cell_map.shape
    lines = span_x * span_y
    return pl.pallas_call(
        coefficients_kernel,
        out_shape=jax.ShapeDtypeStruct((27, lines, depth), jnp.float32),
        in_specs=[
            pl.BlockSpec(memory_space=pltpu.SMEM),
            pl.BlockSpec(memory_space=pltpu.VMEM),
        ],
        out_specs=pl.BlockSpec(memory_space=pltpu.VMEM),
        compiler_params=pltpu.CompilerParams(vmem_limit_bytes=4 * 1024 * 1024),
        name="coefficients",
    )(table, cell_map.reshape(lines, depth))


def stencil(coef, spans, columns, lines, line, wanted, write):
    depth = spans[2]

    def tile(step, carry):
        rows = pl.ds(pl.multiple_of(step * ROWS, ROWS), ROWS)
        held = {}
        for x, y in lines:
            at = x * spans[1] + y
            sums = [None, None, None]
            for pair in range(9):
                there = x + pair // 3 - 1, y + pair % 3 - 1
                if not wanted(there[1]):
                    continue
                if there not in held:
                    held[there] = line(rows, *there)
                for dz in range(3):
                    term = coef[3 * pair + dz, at : at + 1, :] * held[there]
                    sums[dz] = term if sums[dz] is None else sums[dz] + term
            total = pltpu.roll(sums[0], 1, 1) + pltpu.roll(sums[2], depth - 1, 1)
            write(rows, x, y, sums[1] + total)
        return carry

    lax.fori_loop(0, columns // ROWS, tile, 0)


def middle_of(spans, x):
    _, span_y, depth = spans
    inner = (span_y - 2) * depth
    return pl.ds((x * span_y + 1) * depth, inner), pl.ds(x * inner, inner)


def ends_of(spans, x, last):
    _, span_y, depth = spans
    return (
        pl.ds((x * span_y + (span_y - 1) * last) * depth, depth),
        pl.ds((2 * x + last) * depth, depth),
    )


def products(image, cells, fields):
    w = image[...]
    rows = [jnp.concatenate([ref[first:, there] for there in cells], axis=1) for ref, first in fields]
    return dot(w, jnp.concatenate(rows + [w], axis=0), NT)


def middle_image_kernel(spans, first, coef, stack, block, xlo, xhi, middle, partial, cross):
    span_x, span_y, depth = spans

    def line(rows, x, y):
        ref, at = block, x * span_y + y
        if x < 0 or x >= span_x:
            ref, at = (xlo if x < 0 else xhi), y
        return ref[rows, at * depth : (at + 1) * depth].astype(jnp.float32)

    def write(rows, x, y, total):
        if 0 < y < span_y - 1:
            at = x * (span_y - 2) + y - 1
            middle[rows, at * depth : (at + 1) * depth] = total.astype(jnp.bfloat16)
        else:
            partial[rows, ends_of(spans, x, int(y > 0))[1]] = total

    lines = [(x, y) for y in range(span_y) for x in range(span_x)]
    stencil(coef, spans, block.shape[0], lines, line, lambda y: 0 <= y < span_y, write)
    cells = [middle_of(spans, x)[0] for x in range(span_x)]
    cross[...] = products(middle, cells, [(stack, first)] + ([(block, 0)] if first else []))


def end_lines(spans, coef, stack, block, partial, cross, ylo, yhi, ends):
    span_x, span_y, depth = spans

    def line(rows, x, y):
        return (ylo if y < 0 else yhi)[rows, (x + 1) * depth : (x + 2) * depth].astype(jnp.float32)

    def write(rows, x, y, total):
        own = ends_of(spans, x, int(y > 0))[1]
        ends[rows, own] = (partial[rows, own] + total).astype(jnp.bfloat16)

    lines = [(x, y) for y in (0, span_y - 1) for x in range(span_x)]
    stencil(coef, spans, ends.shape[0], lines, line, lambda y: not 0 <= y < span_y, write)
    cells = [ends_of(spans, x, last)[0] for x in range(span_x) for last in range(2)]
    fields = [(stack, 0)] if block is None else [(stack, ends.shape[0]), (block, 0)]
    return cross[...] + products(ends, cells, fields)


def subtracted(spans, middle, ends, moved, block):
    columns = ends.shape[0]
    moved = moved[:columns] + moved[columns:]
    pieces = []
    for x in range(spans[0]):
        pieces.append((middle, *middle_of(spans, x)))
        pieces += [(ends, *ends_of(spans, x, last)) for last in range(2)]
    for ref, there, own in pieces:
        less = moved[:, there.start : there.start + there.size]
        block[:, there] = (ref[:, own].astype(jnp.float32) - less).astype(jnp.bfloat16)


def places(size):
    return [lax.broadcasted_iota(jnp.int32, (size, size), dim) for dim in (0, 1)]


def diagonal_of(square, axis):
    row, column = places(square.shape[0])
    return jnp.sum(jnp.where(row == column, square, 0.0), axis=axis, keepdims=True)


def both_of(packed, diagonal):
    row, column = places(packed.shape[0])
    turned = packed.T
    two = jnp.where(row < column, packed, turned)
    return jnp.where(row >= column, packed, turned), jnp.where(row == column, diagonal, two)


def stack_gram_kernel(columns, stack, sides, right, diagonal):
    parts = [stack[b * columns : (b + 1) * columns] for b in range(3)]
    row, column = places(columns)
    second = dot(parts[1], parts[1], NT)
    pair = jnp.where(row >= column, dot(parts[0], parts[0], NT), second)
    sides[0] = jnp.concatenate(
        [dot(parts[0], parts[2], NT), dot(parts[1], parts[2], NT)], axis=1
    )
    sides[1] = jnp.concatenate([pair, dot(parts[0], parts[1], NT)], axis=1)
    nothing = jnp.zeros((columns, columns), jnp.float32)
    right[...] = jnp.concatenate([nothing, dot(parts[2], parts[2], NT)], axis=1)
    diagonal[...] = jnp.concatenate([diagonal_of(second, 0), nothing[:1]], axis=1)


def first_image_kernel(
    spans, coef, stack, sides, right, diagonal, partial, known, ylo, yhi, ends, cross
):
    columns = ends.shape[0]
    sums = end_lines(spans, coef, stack, None, partial, known, ylo, yhi, ends)
    cross[:columns] = sums[:, : 2 * columns]
    sums = sums[:, 2 * columns :]
    row, lane = (lax.broadcasted_iota(jnp.int32, sums.shape, dim) for dim in (0, 1))
    cross[columns : 2 * columns] = jnp.where(
        (lane >= columns) & (row >= lane - columns), right[...], sums
    )
    for i in range(2):
        cross[(2 + i) * columns : (3 + i) * columns] = sides[i]
    own = jnp.sum(jnp.where(row == lane - columns, sums, 0.0), axis=0, keepdims=True)
    cross[4 * columns :] = jnp.broadcast_to(
        diagonal[...] + own, (cross.shape[0] - 4 * columns, 2 * columns)
    )


def second_image_kernel(spans, coef, stack, block, partial, known, ylo, yhi, ends, cross):
    cross[...] = end_lines(spans, coef, stack, block, partial, known, ylo, yhi, ends)


def opened(cross, columns, scale):
    parts = [cross[i * columns : (i + 1) * columns] * scale for i in range(4)]
    left, right = ([part[:, at : at + columns] for part in parts] for at in (0, columns))
    diagonals = cross[4 * columns : 4 * columns + 1] * scale
    first = jnp.concatenate([parts[0], left[1]], axis=1)
    one, two = both_of(left[3], diagonals[:, :columns])
    three, square = both_of(right[1], diagonals[:, columns:])
    gram = [
        [one, right[3], left[2]],
        [right[3].T, two, right[2]],
        [left[2].T, right[2].T, three],
    ]
    gram = jnp.concatenate([jnp.concatenate(row, axis=1) for row in gram], axis=0)
    return first, square, gram


def split(values):
    high = values.astype(jnp.bfloat16)
    return high, (values - high.astype(jnp.float32)).astype(jnp.bfloat16)


def dots(lefts, rights, dims=NN):
    return sum(dot(left, right, dims) for left in lefts for right in rights)


def factor(square, sizes, across):
    size = square.shape[0]
    shape = (8, 2 * size)
    sub = lax.broadcasted_iota(jnp.int32, shape, 0)
    unit = lax.broadcasted_iota(jnp.int32, (size, size), 0) == lax.broadcasted_iota(
        jnp.int32, (size, size), 1
    )
    scale = lax.rsqrt(across)
    square = square * lax.rsqrt(sizes) * scale
    whole = jnp.concatenate([square, unit.astype(jnp.float32)], axis=1)
    blocks = [whole[b : b + 8] for b in range(0, size, 8)]
    done = []

    def row_of(values, at):
        return jnp.broadcast_to(values[at : at + 1, :], shape)

    def columns_of(values, first):
        return [
            jnp.broadcast_to(values[:, at : at + 1], shape) for at in range(first, first + 8)
        ]

    for b, here in enumerate(blocks):
        columns = columns_of(here, 8 * b)
        entry = {(i, j): row_of(columns[j], i) for j in range(8) for i in range(j + 1)}
        rows = [row_of(here, i) for i in range(8)]
        scaled = jnp.zeros(shape, jnp.float32)
        solved, ratio = [], {}
        if b + 1 < len(blocks):
            below = columns_of(blocks[b + 1], 8 * b)
        for p in range(0, 8, 2):
            q = p + 1
            first, mixed, last = entry[p, p], entry[p, q], entry[q, q]
            inverse = 1.0 / (first * last - mixed * mixed)

            def solve(one, two):
                return (
                    (last * one - mixed * two) * inverse,
                    (first * two - mixed * one) * inverse,
                )

            for j in range(p + 2, 8):
                ratio[p, j], ratio[q, j] = solve(entry[p, j], entry[q, j])
            for i in range(p + 2, 8):
                for j in range(i, 8):
                    change = entry[p, i] * ratio[p, j] + entry[q, i] * ratio[q, j]
                    entry[i, j] = entry[i, j] - change
                rows[i] = rows[i] - (ratio[p, i] * rows[p] + ratio[q, i] * rows[q])
            solved += solve(rows[p], rows[q])
            if b + 1 < len(blocks):
                change = below[p] * solved[p] + below[q] * solved[q]
                blocks[b + 1] = blocks[b + 1] - change
                for j in range(p + 2, 8):
                    below[j] = below[j] - (below[p] * ratio[p, j] + below[q] * ratio[q, j])
            part = mixed * (1.0 / first)
            scaled = jnp.where(sub == p, rows[p] * lax.rsqrt(first), scaled)
            rest = (rows[q] - part * rows[p]) * lax.rsqrt(last - part * mixed)
            scaled = jnp.where(sub == q, rest, scaled)
        done.append(scaled)
        for p in (4, 2, 0):
            for r in (p, p + 1):
                for j in range(p + 2, 8):
                    solved[r] = solved[r] - ratio[r, j] * solved[j]
        for later in range(b + 2, len(blocks)):
            parts = [one * two for one, two in zip(columns_of(blocks[later], 8 * b), solved)]
            while len(parts) > 1:
                parts = [one + two for one, two in zip(parts[::2], parts[1::2])]
            blocks[later] = blocks[later] - parts[0]
    done = jnp.concatenate(done, axis=0)
    above = lax.broadcasted_iota(jnp.int32, (size, size), 0) <= lax.broadcasted_iota(
        jnp.int32, (size, size), 1
    )
    return jnp.where(above, done[:, :size] * (across * scale), 0.0), done[:, size:] * scale


def project(first, square, own):
    first_parts = split(first)
    first_low = first_parts[0]
    second = first - dots((first_low,), own)
    second_low = second.astype(jnp.bfloat16)
    used = (first_low, second_low)
    sizes = [diagonal_of(square, axis) for axis in (1, 0)]
    square = square - dots(used, first_parts, NT)
    rest = second - dots((second_low,), own)
    square = square - dots(split(rest), used, NT)
    return used, first + second, rest, square, sizes


def first_solve_kernel(
    scale, spans, cross, stack, middle, ends, block, proj, low, rest, square, inverse
):
    columns = ends.shape[0]
    first, own_square, gram = opened(cross, columns, scale)
    used, proj[...], rest[...], square_here, sizes = project(first, own_square, split(gram))
    square[...] = square_here
    moved = dot(jnp.concatenate(used, axis=0), stack[...])
    subtracted(spans, middle, ends, moved, block)
    upper, inverse_here = factor(square_here, *sizes)
    low[...] = upper.T
    inverse_here = inverse_here.astype(jnp.bfloat16)
    inverse[...] = inverse_here
    block[...] = dot(inverse_here, block[...]).astype(jnp.bfloat16)


def next_gram_kernel(scale, cross, rest, square, inverse, high, low):
    columns = square.shape[0]
    kept = rest.shape[1] - columns
    _, _, gram = opened(cross, columns, scale)
    mixed = dots((inverse[...],), split(rest[:, columns:]))
    corner = dots((inverse[...],), split(square[...]))
    corner = dots(split(corner), (inverse[...],), NT)
    for part, (old, side, end) in zip(
        (high, low), zip(split(gram[columns:, columns:]), split(mixed), split(corner))
    ):
        part[:kept, :kept] = old
        part[kept:, :kept] = side
        part[:kept, kept:] = side.T
        part[kept:, kept:] = end


def second_solve_kernel(
    scale, cross, own_high, own_low, stack, last, middle, ends, proj_in, low_in, result, proj, low,
    block,
):
    columns = ends.shape[0]
    kept = stack.shape[0] - columns
    fields = stack.shape[0]
    sums = cross[...] * scale
    used, proj[1], _, square, sizes = project(
        sums[:, :fields], sums[:, fields:], (own_high[...], own_low[...])
    )
    proj[0] = proj_in[...]
    low[0] = low_in[...]
    _, span_x, span_y, depth = result.shape
    both = jnp.concatenate(used, axis=0)
    moved = dot(both[:, :kept], stack[columns:]) + dot(both[:, kept:], last[...])
    subtracted((span_x, span_y, depth), middle, ends, moved, block)
    upper, inverse = factor(square, *sizes)
    low[1] = upper.T
    inverse = inverse.astype(jnp.bfloat16)
    plane = span_y * depth
    for x in range(span_x):
        part = dot(inverse, block[:, x * plane : (x + 1) * plane])
        result[:, x] = part.reshape(columns, span_y, depth).astype(jnp.bfloat16)


def partner(part, mask):
    axes = ("slab", "col")
    count = lax.axis_size("slab") * lax.axis_size("col")
    return lax.ppermute(part, axes, [(i, i ^ mask) for i in range(count)])


def whole_sum(part):
    cols = lax.axis_size("col")
    count = lax.axis_size("slab") * cols
    index = lax.axis_index("slab") * cols + lax.axis_index("col")
    bit, upper = 1, 0
    while bit < count:
        upper = upper ^ (index // bit % 2)
        bit *= 2
    upper = upper == 1
    half = part.shape[0] // 2
    low, high = part[:half], part[half:]
    part = jnp.where(upper, high, low) + partner(jnp.where(upper, low, high), 1)
    bit = 2
    while bit < count:
        if 2 * bit < count:
            one, two, both = (partner(part, mask) for mask in (bit + 1, 2 * bit + 1, 3 * bit))
            part = (part + one) + (both + two)
            bit *= 4
        else:
            part = part + partner(part, bit + 1)
            bit *= 2
    other = partner(part, 1)
    return jnp.concatenate([jnp.where(upper, other, part), jnp.where(upper, part, other)], axis=0)


def call(kernel, name, outs, *args, flops=0, scratch=()):
    moved = sum(math.prod(arg.shape) * arg.dtype.itemsize for arg in args)
    moved += sum(math.prod(shape) * jnp.dtype(dtype).itemsize for shape, dtype in outs)
    return pl.pallas_call(
        kernel,
        out_shape=[jax.ShapeDtypeStruct(shape, dtype) for shape, dtype in outs],
        in_specs=[pl.BlockSpec(memory_space=pltpu.VMEM)] * len(args),
        out_specs=[pl.BlockSpec(memory_space=pltpu.VMEM)] * len(outs),
        scratch_shapes=scratch,
        compiler_params=pltpu.CompilerParams(vmem_limit_bytes=24 * 1024 * 1024),
        cost_estimate=pl.CostEstimate(flops=flops, bytes_accessed=moved, transcendentals=0),
        name=name,
    )(*args)


def shards(basis, cell_map, table):
    span_x, span_y, depth = cell_map.shape
    blocks, columns = basis.shape[:2]
    cells = span_x * span_y * depth
    fields = blocks * columns
    scale = 1.0 / (cells * lax.axis_size("slab") * lax.axis_size("col"))
    spans = (span_x, span_y, depth)
    f32, bf16 = jnp.float32, jnp.bfloat16

    stack = basis.reshape(fields, cells)
    coef = coefficients(table, cell_map)
    own = call(
        functools.partial(stack_gram_kernel, columns),
        "stack_gram",
        [((2, columns, 2 * columns), f32), ((columns, 2 * columns), f32), ((1, 2 * columns), f32)],
        stack,
        flops=2 * fields * fields * cells,
    )

    end_cells = 2 * span_x * depth

    def middle_image(first, stack, block, planes):
        return call(
            functools.partial(middle_image_kernel, spans, first),
            "middle_image",
            [((columns, cells - end_cells), bf16), ((columns, end_cells), f32),
             ((columns, fields + columns), f32)],
            coef, stack, block, *planes,
            flops=2 * 27 * columns * cells,
        )

    last = basis[blocks - 1].reshape(columns, cells)
    planes, lines, (coef, stack, own) = neighbours(last, *spans, (coef, stack, own))
    middle, partial, known = middle_image(0, stack, last, planes)
    ends, cross = call(
        functools.partial(first_image_kernel, spans),
        "first_image",
        [((columns, end_cells), bf16), ((4 * columns + 16, 2 * columns), f32)],
        coef, stack, *own, partial, known, *lines,
    )
    cross = whole_sum(cross)
    block, proj, low, rest, square, inverse = call(
        functools.partial(first_solve_kernel, scale, spans),
        "first_solve",
        [((columns, cells), bf16), ((columns, fields), f32), ((columns, columns), f32),
         ((columns, fields), f32), ((columns, columns), f32), ((columns, columns), bf16)],
        cross, stack, middle, ends,
    )
    own = call(
        functools.partial(next_gram_kernel, scale),
        "next_gram",
        [((fields, fields), bf16)] * 2,
        cross, rest, square, inverse,
    )
    planes, lines, _ = neighbours(block, *spans)
    middle, partial, known = middle_image(columns, stack, block, planes)
    ends, cross = call(
        functools.partial(second_image_kernel, spans),
        "second_image",
        [((columns, end_cells), bf16), ((columns, fields + columns), f32)],
        coef, stack, block, partial, known, *lines,
    )
    block, proj, low = call(
        functools.partial(second_solve_kernel, scale),
        "second_solve",
        [((columns, *spans), bf16), ((2, columns, fields), f32), ((2, columns, columns), f32)],
        whole_sum(cross), *own, stack, block, middle, ends, proj, low,
        scratch=[pltpu.VMEM((columns, cells), bf16)],
    )
    return block, jnp.swapaxes(proj, 1, 2), low


def solution(mesh):
    placed = (P(None, None, "slab", "col", None), P("slab", "col", None), P())
    return jax.shard_map(
        shards,
        mesh=mesh,
        in_specs=placed,
        out_specs=(P(None, "slab", "col", None), P(), P()),
        check_vma=False,
    )
```

```python
import functools
import math

import jax
import jax.numpy as jnp
from jax import lax
from jax.experimental import pallas as pl
from jax.experimental.pallas import tpu as pltpu
from jax.sharding import PartitionSpec as P

NN = (((1,), (0,)), ((), ()))
NT = (((1,), (1,)), ((), ()))
ROWS = 16


def dot(left, right, dims=NN):
    return lax.dot_general(left, right, dims, preferred_element_type=jnp.float32)


def swaps(axis, near, far):
    count = lax.axis_size(axis)
    me = lax.axis_index(axis)
    pairs = [(i, (i - 1 ^ 1) + 1) for i in range(1, count - 1)]
    inner = lax.ppermute(near, axis, [(i, i ^ 1) for i in range(count)])
    outer = lax.ppermute(far, axis, pairs + [(0, count - 1), (count - 1, 0)])
    if axis == "slab":
        even = me % 2 == 0
        low, high = jnp.where(even, outer, inner), jnp.where(even, inner, outer)
    else:
        odd = me % 2 == 1
        low, high = jnp.where(odd, inner, outer), jnp.where(odd, outer, inner)
    return jnp.where(me == 0, 0, low), jnp.where(me == count - 1, 0, high)


def cut_kernel(start, block, part):
    part[...] = block[:, pl.ds(pl.multiple_of(start[0], 128), part.shape[1])]


def cut(block, start, width):
    return pl.pallas_call(
        cut_kernel,
        out_shape=jax.ShapeDtypeStruct((block.shape[0], width), block.dtype),
        in_specs=[
            pl.BlockSpec(memory_space=pltpu.SMEM),
            pl.BlockSpec(memory_space=pltpu.VMEM),
        ],
        out_specs=pl.BlockSpec(memory_space=pltpu.VMEM),
        compiler_params=pltpu.CompilerParams(vmem_limit_bytes=4 * 1024 * 1024),
        name="cut",
    )(start.reshape(1), block)


def neighbours(block, span_x, span_y, depth, meanwhile=None):
    plane = span_y * depth
    top = (span_x - 1) * plane
    odd = lax.axis_index("slab") % 2 == 1
    near = jnp.where(odd, block[:, :plane], block[:, top:])
    far = cut(block, jnp.where(odd, top, 0), plane)
    xlo, xhi = swaps("slab", near, far)
    xlo, xhi, meanwhile = lax.optimization_barrier((xlo, xhi, meanwhile))

    def edge(row):
        at = row * depth
        parts = [xlo[:, at : at + depth]]
        parts += [block[:, x * plane + at : x * plane + at + depth] for x in range(span_x)]
        parts += [xhi[:, at : at + depth]]
        return jnp.concatenate(parts, axis=1)

    odd = lax.axis_index("col") % 2 == 1
    upward, downward = edge(span_y - 1), edge(0)
    ylo, yhi = swaps(
        "col", jnp.where(odd, downward, upward), jnp.where(odd, upward, downward)
    )
    return (xlo, xhi), (ylo, yhi), meanwhile


def coefficients_kernel(table, cells, coef):
    classes = table.shape[0]
    lanes = lax.broadcasted_iota(jnp.int32, cells.shape, 1)
    depth = cells.shape[1]
    here = cells[...]
    below = pltpu.roll(here, depth - 1, 1)
    above = pltpu.roll(here, 1, 1)
    maps = (below, here, above)
    keep = (lanes < depth - 1, None, lanes > 0)
    for dz in range(3):
        masks = [maps[dz] == k for k in range(1, classes)]
        for pair in range(9):
            offset = 3 * pair + dz
            value = jnp.full(cells.shape, table[0, offset], jnp.float32)
            for k in range(1, classes):
                value = jnp.where(masks[k - 1], table[k, offset], value)
            if keep[dz] is not None:
                value = jnp.where(keep[dz], value, 0.0)
            coef[offset] = value


def coefficients(table, cell_map):
    span_x, span_y, depth = cell_map.shape
    lines = span_x * span_y
    return pl.pallas_call(
        coefficients_kernel,
        out_shape=jax.ShapeDtypeStruct((27, lines, depth), jnp.float32),
        in_specs=[
            pl.BlockSpec(memory_space=pltpu.SMEM),
            pl.BlockSpec(memory_space=pltpu.VMEM),
        ],
        out_specs=pl.BlockSpec(memory_space=pltpu.VMEM),
        compiler_params=pltpu.CompilerParams(vmem_limit_bytes=4 * 1024 * 1024),
        name="coefficients",
    )(table, cell_map.reshape(lines, depth))


def stencil(coef, spans, columns, lines, line, wanted, write):
    depth = spans[2]

    def tile(step, carry):
        rows = pl.ds(pl.multiple_of(step * ROWS, ROWS), ROWS)
        held = {}
        for x, y in lines:
            at = x * spans[1] + y
            sums = [None, None, None]
            for pair in range(9):
                there = x + pair // 3 - 1, y + pair % 3 - 1
                if not wanted(there[1]):
                    continue
                if there not in held:
                    held[there] = line(rows, *there)
                for dz in range(3):
                    term = coef[3 * pair + dz, at : at + 1, :] * held[there]
                    sums[dz] = term if sums[dz] is None else sums[dz] + term
            total = pltpu.roll(sums[0], 1, 1) + pltpu.roll(sums[2], depth - 1, 1)
            write(rows, x, y, sums[1] + total)
        return carry

    lax.fori_loop(0, columns // ROWS, tile, 0)


def middle_of(spans, x):
    _, span_y, depth = spans
    inner = (span_y - 2) * depth
    return pl.ds((x * span_y + 1) * depth, inner), pl.ds(x * inner, inner)


def ends_of(spans, x, last):
    _, span_y, depth = spans
    return (
        pl.ds((x * span_y + (span_y - 1) * last) * depth, depth),
        pl.ds((2 * x + last) * depth, depth),
    )


def products(image, cells, fields):
    w = image[...]
    rows = [jnp.concatenate([ref[first:, there] for there in cells], axis=1) for ref, first in fields]
    return dot(w, jnp.concatenate(rows + [w], axis=0), NT)


def middle_image_kernel(spans, first, coef, stack, block, xlo, xhi, middle, partial, cross):
    span_x, span_y, depth = spans

    def line(rows, x, y):
        ref, at = block, x * span_y + y
        if x < 0 or x >= span_x:
            ref, at = (xlo if x < 0 else xhi), y
        return ref[rows, at * depth : (at + 1) * depth].astype(jnp.float32)

    def write(rows, x, y, total):
        if 0 < y < span_y - 1:
            at = x * (span_y - 2) + y - 1
            middle[rows, at * depth : (at + 1) * depth] = total.astype(jnp.bfloat16)
        else:
            partial[rows, ends_of(spans, x, int(y > 0))[1]] = total

    lines = [(x, y) for y in range(span_y) for x in range(span_x)]
    stencil(coef, spans, block.shape[0], lines, line, lambda y: 0 <= y < span_y, write)
    cells = [middle_of(spans, x)[0] for x in range(span_x)]
    cross[...] = products(middle, cells, [(stack, first)] + ([(block, 0)] if first else []))


def end_lines(spans, coef, stack, block, partial, cross, ylo, yhi, ends):
    span_x, span_y, depth = spans

    def line(rows, x, y):
        return (ylo if y < 0 else yhi)[rows, (x + 1) * depth : (x + 2) * depth].astype(jnp.float32)

    def write(rows, x, y, total):
        own = ends_of(spans, x, int(y > 0))[1]
        ends[rows, own] = (partial[rows, own] + total).astype(jnp.bfloat16)

    lines = [(x, y) for y in (0, span_y - 1) for x in range(span_x)]
    stencil(coef, spans, ends.shape[0], lines, line, lambda y: not 0 <= y < span_y, write)
    cells = [ends_of(spans, x, last)[0] for x in range(span_x) for last in range(2)]
    fields = [(stack, 0)] if block is None else [(stack, ends.shape[0]), (block, 0)]
    return cross[...] + products(ends, cells, fields)


def subtracted(spans, middle, ends, moved, block):
    columns = ends.shape[0]
    moved = moved[:columns] + moved[columns:]
    pieces = []
    for x in range(spans[0]):
        pieces.append((middle, *middle_of(spans, x)))
        pieces += [(ends, *ends_of(spans, x, last)) for last in range(2)]
    for ref, there, own in pieces:
        less = moved[:, there.start : there.start + there.size]
        block[:, there] = (ref[:, own].astype(jnp.float32) - less).astype(jnp.bfloat16)


def places(size):
    return [lax.broadcasted_iota(jnp.int32, (size, size), dim) for dim in (0, 1)]


def diagonal_of(square, axis):
    row, column = places(square.shape[0])
    return jnp.sum(jnp.where(row == column, square, 0.0), axis=axis, keepdims=True)


def both_of(packed, diagonal):
    row, column = places(packed.shape[0])
    turned = packed.T
    two = jnp.where(row < column, packed, turned)
    return jnp.where(row >= column, packed, turned), jnp.where(row == column, diagonal, two)


def stack_gram_kernel(columns, stack, sides, right, diagonal):
    parts = [stack[b * columns : (b + 1) * columns] for b in range(3)]
    row, column = places(columns)
    second = dot(parts[1], parts[1], NT)
    pair = jnp.where(row >= column, dot(parts[0], parts[0], NT), second)
    sides[0] = jnp.concatenate(
        [dot(parts[0], parts[2], NT), dot(parts[1], parts[2], NT)], axis=1
    )
    sides[1] = jnp.concatenate([pair, dot(parts[0], parts[1], NT)], axis=1)
    nothing = jnp.zeros((columns, columns), jnp.float32)
    right[...] = jnp.concatenate([nothing, dot(parts[2], parts[2], NT)], axis=1)
    diagonal[...] = jnp.concatenate([diagonal_of(second, 0), nothing[:1]], axis=1)


def first_image_kernel(
    spans, coef, stack, sides, right, diagonal, partial, known, ylo, yhi, ends, cross
):
    columns = ends.shape[0]
    sums = end_lines(spans, coef, stack, None, partial, known, ylo, yhi, ends)
    cross[:columns] = sums[:, : 2 * columns]
    sums = sums[:, 2 * columns :]
    row, lane = (lax.broadcasted_iota(jnp.int32, sums.shape, dim) for dim in (0, 1))
    cross[columns : 2 * columns] = jnp.where(
        (lane >= columns) & (row >= lane - columns), right[...], sums
    )
    for i in range(2):
        cross[(2 + i) * columns : (3 + i) * columns] = sides[i]
    own = jnp.sum(jnp.where(row == lane - columns, sums, 0.0), axis=0, keepdims=True)
    cross[4 * columns :] = jnp.broadcast_to(
        diagonal[...] + own, (cross.shape[0] - 4 * columns, 2 * columns)
    )


def second_image_kernel(spans, coef, stack, block, partial, known, ylo, yhi, ends, cross):
    cross[...] = end_lines(spans, coef, stack, block, partial, known, ylo, yhi, ends)


def opened(cross, columns, scale):
    parts = [cross[i * columns : (i + 1) * columns] * scale for i in range(4)]
    left, right = ([part[:, at : at + columns] for part in parts] for at in (0, columns))
    diagonals = cross[4 * columns : 4 * columns + 1] * scale
    first = jnp.concatenate([parts[0], left[1]], axis=1)
    one, two = both_of(left[3], diagonals[:, :columns])
    three, square = both_of(right[1], diagonals[:, columns:])
    gram = [
        [one, right[3], left[2]],
        [right[3].T, two, right[2]],
        [left[2].T, right[2].T, three],
    ]
    gram = jnp.concatenate([jnp.concatenate(row, axis=1) for row in gram], axis=0)
    return first, square, gram


def split(values):
    high = values.astype(jnp.bfloat16)
    return high, (values - high.astype(jnp.float32)).astype(jnp.bfloat16)


def dots(lefts, rights, dims=NN):
    return sum(dot(left, right, dims) for left in lefts for right in rights)


def factor(square, sizes, across):
    size = square.shape[0]
    shape = (8, 2 * size)
    sub = lax.broadcasted_iota(jnp.int32, shape, 0)
    unit = lax.broadcasted_iota(jnp.int32, (size, size), 0) == lax.broadcasted_iota(
        jnp.int32, (size, size), 1
    )
    scale = lax.rsqrt(across)
    square = square * lax.rsqrt(sizes) * scale
    whole = jnp.concatenate([square, unit.astype(jnp.float32)], axis=1)
    blocks = [whole[b : b + 8] for b in range(0, size, 8)]
    done = []

    def row_of(values, at):
        return jnp.broadcast_to(values[at : at + 1, :], shape)

    def columns_of(values, first):
        return [
            jnp.broadcast_to(values[:, at : at + 1], shape) for at in range(first, first + 8)
        ]

    for b, here in enumerate(blocks):
        columns = columns_of(here, 8 * b)
        entry = {(i, j): row_of(columns[j], i) for j in range(8) for i in range(j + 1)}
        rows = [row_of(here, i) for i in range(8)]
        scaled = jnp.zeros(shape, jnp.float32)
        solved, ratio = [], {}
        if b + 1 < len(blocks):
            below = columns_of(blocks[b + 1], 8 * b)
        for p in range(0, 8, 2):
            q = p + 1
            first, mixed, last = entry[p, p], entry[p, q], entry[q, q]
            inverse = 1.0 / (first * last - mixed * mixed)

            def solve(one, two):
                return (
                    (last * one - mixed * two) * inverse,
                    (first * two - mixed * one) * inverse,
                )

            for j in range(p + 2, 8):
                ratio[p, j], ratio[q, j] = solve(entry[p, j], entry[q, j])
            for i in range(p + 2, 8):
                for j in range(i, 8):
                    change = entry[p, i] * ratio[p, j] + entry[q, i] * ratio[q, j]
                    entry[i, j] = entry[i, j] - change
                rows[i] = rows[i] - (ratio[p, i] * rows[p] + ratio[q, i] * rows[q])
            solved += solve(rows[p], rows[q])
            if b + 1 < len(blocks):
                change = below[p] * solved[p] + below[q] * solved[q]
                blocks[b + 1] = blocks[b + 1] - change
                for j in range(p + 2, 8):
                    below[j] = below[j] - (below[p] * ratio[p, j] + below[q] * ratio[q, j])
            part = mixed * (1.0 / first)
            scaled = jnp.where(sub == p, rows[p] * lax.rsqrt(first), scaled)
            rest = (rows[q] - part * rows[p]) * lax.rsqrt(last - part * mixed)
            scaled = jnp.where(sub == q, rest, scaled)
        done.append(scaled)
        for p in (4, 2, 0):
            for r in (p, p + 1):
                for j in range(p + 2, 8):
                    solved[r] = solved[r] - ratio[r, j] * solved[j]
        for later in range(b + 2, len(blocks)):
            parts = [one * two for one, two in zip(columns_of(blocks[later], 8 * b), solved)]
            while len(parts) > 1:
                parts = [one + two for one, two in zip(parts[::2], parts[1::2])]
            blocks[later] = blocks[later] - parts[0]
    done = jnp.concatenate(done, axis=0)
    above = lax.broadcasted_iota(jnp.int32, (size, size), 0) <= lax.broadcasted_iota(
        jnp.int32, (size, size), 1
    )
    return jnp.where(above, done[:, :size] * (across * scale), 0.0), done[:, size:] * scale


def project(first, square, own):
    first_parts = split(first)
    first_low = first_parts[0]
    second = first - dots((first_low,), own)
    second_low = second.astype(jnp.bfloat16)
    used = (first_low, second_low)
    square = square - dots(used, first_parts, NT)
    rest = second - dots((second_low,), own)
    square = square - dots(split(rest), used, NT)
    sizes = [diagonal_of(square, axis) for axis in (1, 0)]
    return used, first + second, rest, square, sizes


def first_solve_kernel(
    scale, spans, cross, stack, middle, ends, block, proj, low, rest, square, inverse
):
    columns = ends.shape[0]
    first, own_square, gram = opened(cross, columns, scale)
    used, proj[...], rest[...], square_here, sizes = project(first, own_square, split(gram))
    square[...] = square_here
    moved = dot(jnp.concatenate(used, axis=0), stack[...])
    subtracted(spans, middle, ends, moved, block)
    upper, inverse_here = factor(square_here, *sizes)
    low[...] = upper.T
    inverse_here = inverse_here.astype(jnp.bfloat16)
    inverse[...] = inverse_here
    block[...] = dot(inverse_here, block[...]).astype(jnp.bfloat16)


def next_gram_kernel(scale, cross, rest, square, inverse, high, low):
    columns = square.shape[0]
    kept = rest.shape[1] - columns
    _, _, gram = opened(cross, columns, scale)
    mixed = dots((inverse[...],), split(rest[:, columns:]))
    corner = dots((inverse[...],), split(square[...]))
    corner = dots(split(corner), (inverse[...],), NT)
    for part, (old, side, end) in zip(
        (high, low), zip(split(gram[columns:, columns:]), split(mixed), split(corner))
    ):
        part[:kept, :kept] = old
        part[kept:, :kept] = side
        part[:kept, kept:] = side.T
        part[kept:, kept:] = end


def second_solve_kernel(
    scale, cross, own_high, own_low, stack, last, middle, ends, proj_in, low_in, result, proj, low,
    block,
):
    columns = ends.shape[0]
    kept = stack.shape[0] - columns
    fields = stack.shape[0]
    sums = cross[...] * scale
    used, proj[1], _, square, sizes = project(
        sums[:, :fields], sums[:, fields:], (own_high[...], own_low[...])
    )
    proj[0] = proj_in[...]
    low[0] = low_in[...]
    _, span_x, span_y, depth = result.shape
    both = jnp.concatenate(used, axis=0)
    moved = dot(both[:, :kept], stack[columns:]) + dot(both[:, kept:], last[...])
    subtracted((span_x, span_y, depth), middle, ends, moved, block)
    upper, inverse = factor(square, *sizes)
    low[1] = upper.T
    inverse = inverse.astype(jnp.bfloat16)
    plane = span_y * depth
    for x in range(span_x):
        part = dot(inverse, block[:, x * plane : (x + 1) * plane])
        result[:, x] = part.reshape(columns, span_y, depth).astype(jnp.bfloat16)


def partner(part, mask):
    axes = ("slab", "col")
    count = lax.axis_size("slab") * lax.axis_size("col")
    return lax.ppermute(part, axes, [(i, i ^ mask) for i in range(count)])


def whole_sum(part):
    cols = lax.axis_size("col")
    count = lax.axis_size("slab") * cols
    index = lax.axis_index("slab") * cols + lax.axis_index("col")
    bit, upper = 1, 0
    while bit < count:
        upper = upper ^ (index // bit % 2)
        bit *= 2
    upper = upper == 1
    half = part.shape[0] // 2
    low, high = part[:half], part[half:]
    part = jnp.where(upper, high, low) + partner(jnp.where(upper, low, high), 1)
    bit = 2
    while bit < count:
        if 2 * bit < count:
            one, two, both = (partner(part, mask) for mask in (bit + 1, 2 * bit + 1, 3 * bit))
            part = (part + one) + (both + two)
            bit *= 4
        else:
            part = part + partner(part, bit + 1)
            bit *= 2
    other = partner(part, 1)
    return jnp.concatenate([jnp.where(upper, other, part), jnp.where(upper, part, other)], axis=0)


def call(kernel, name, outs, *args, flops=0, scratch=()):
    moved = sum(math.prod(arg.shape) * arg.dtype.itemsize for arg in args)
    moved += sum(math.prod(shape) * jnp.dtype(dtype).itemsize for shape, dtype in outs)
    return pl.pallas_call(
        kernel,
        out_shape=[jax.ShapeDtypeStruct(shape, dtype) for shape, dtype in outs],
        in_specs=[pl.BlockSpec(memory_space=pltpu.VMEM)] * len(args),
        out_specs=[pl.BlockSpec(memory_space=pltpu.VMEM)] * len(outs),
        scratch_shapes=scratch,
        compiler_params=pltpu.CompilerParams(vmem_limit_bytes=24 * 1024 * 1024),
        cost_estimate=pl.CostEstimate(flops=flops, bytes_accessed=moved, transcendentals=0),
        name=name,
    )(*args)


def shards(basis, cell_map, table):
    span_x, span_y, depth = cell_map.shape
    blocks, columns = basis.shape[:2]
    cells = span_x * span_y * depth
    fields = blocks * columns
    scale = 1.0 / (cells * lax.axis_size("slab") * lax.axis_size("col"))
    spans = (span_x, span_y, depth)
    f32, bf16 = jnp.float32, jnp.bfloat16

    stack = basis.reshape(fields, cells)
    coef = coefficients(table, cell_map)
    own = call(
        functools.partial(stack_gram_kernel, columns),
        "stack_gram",
        [((2, columns, 2 * columns), f32), ((columns, 2 * columns), f32), ((1, 2 * columns), f32)],
        stack,
        flops=2 * fields * fields * cells,
    )

    end_cells = 2 * span_x * depth

    def middle_image(first, stack, block, planes):
        return call(
            functools.partial(middle_image_kernel, spans, first),
            "middle_image",
            [((columns, cells - end_cells), bf16), ((columns, end_cells), f32),
             ((columns, fields + columns), f32)],
            coef, stack, block, *planes,
            flops=2 * 27 * columns * cells,
        )

    last = basis[blocks - 1].reshape(columns, cells)
    planes, lines, (coef, stack, own) = neighbours(last, *spans, (coef, stack, own))
    middle, partial, known = middle_image(0, stack, last, planes)
    ends, cross = call(
        functools.partial(first_image_kernel, spans),
        "first_image",
        [((columns, end_cells), bf16), ((4 * columns + 16, 2 * columns), f32)],
        coef, stack, *own, partial, known, *lines,
    )
    cross = whole_sum(cross)
    block, proj, low, rest, square, inverse = call(
        functools.partial(first_solve_kernel, scale, spans),
        "first_solve",
        [((columns, cells), bf16), ((columns, fields), f32), ((columns, columns), f32),
         ((columns, fields), f32), ((columns, columns), f32), ((columns, columns), bf16)],
        cross, stack, middle, ends,
    )
    own = call(
        functools.partial(next_gram_kernel, scale),
        "next_gram",
        [((fields, fields), bf16)] * 2,
        cross, rest, square, inverse,
    )
    planes, lines, _ = neighbours(block, *spans)
    middle, partial, known = middle_image(columns, stack, block, planes)
    ends, cross = call(
        functools.partial(second_image_kernel, spans),
        "second_image",
        [((columns, end_cells), bf16), ((columns, fields + columns), f32)],
        coef, stack, block, partial, known, *lines,
    )
    block, proj, low = call(
        functools.partial(second_solve_kernel, scale),
        "second_solve",
        [((columns, *spans), bf16), ((2, columns, fields), f32), ((2, columns, columns), f32)],
        whole_sum(cross), *own, stack, block, middle, ends, proj, low,
        scratch=[pltpu.VMEM((columns, cells), bf16)],
    )
    return block, jnp.swapaxes(proj, 1, 2), low


def solution(mesh):
    placed = (P(None, None, "slab", "col", None), P("slab", "col", None), P())
    return jax.shard_map(
        shards,
        mesh=mesh,
        in_specs=placed,
        out_specs=(P(None, "slab", "col", None), P(), P()),
        check_vma=False,
    )
```

```python
import functools
import math

import jax
import jax.numpy as jnp
from jax import lax
from jax.experimental import pallas as pl
from jax.experimental.pallas import tpu as pltpu
from jax.sharding import PartitionSpec as P

NN = (((1,), (0,)), ((), ()))
NT = (((1,), (1,)), ((), ()))
ROWS = 16


def dot(left, right, dims=NN):
    return lax.dot_general(left, right, dims, preferred_element_type=jnp.float32)


def swaps(axis, near, far):
    count = lax.axis_size(axis)
    me = lax.axis_index(axis)
    pairs = [(i, (i - 1 ^ 1) + 1) for i in range(1, count - 1)]
    inner = lax.ppermute(near, axis, [(i, i ^ 1) for i in range(count)])
    outer = lax.ppermute(far, axis, pairs + [(0, count - 1), (count - 1, 0)])
    if axis == "slab":
        even = me % 2 == 0
        low, high = jnp.where(even, outer, inner), jnp.where(even, inner, outer)
    else:
        odd = me % 2 == 1
        low, high = jnp.where(odd, inner, outer), jnp.where(odd, outer, inner)
    return jnp.where(me == 0, 0, low), jnp.where(me == count - 1, 0, high)


def cut_kernel(start, block, part):
    part[...] = block[:, pl.ds(pl.multiple_of(start[0], 128), part.shape[1])]


def cut(block, start, width):
    return pl.pallas_call(
        cut_kernel,
        out_shape=jax.ShapeDtypeStruct((block.shape[0], width), block.dtype),
        in_specs=[
            pl.BlockSpec(memory_space=pltpu.SMEM),
            pl.BlockSpec(memory_space=pltpu.VMEM),
        ],
        out_specs=pl.BlockSpec(memory_space=pltpu.VMEM),
        compiler_params=pltpu.CompilerParams(vmem_limit_bytes=4 * 1024 * 1024),
        name="cut",
    )(start.reshape(1), block)


def neighbours(block, span_x, span_y, depth, meanwhile=None):
    plane = span_y * depth
    top = (span_x - 1) * plane
    odd = lax.axis_index("slab") % 2 == 1
    near = jnp.where(odd, block[:, :plane], block[:, top:])
    far = cut(block, jnp.where(odd, top, 0), plane)
    xlo, xhi = swaps("slab", near, far)
    xlo, xhi, meanwhile = lax.optimization_barrier((xlo, xhi, meanwhile))

    def edge(row):
        at = row * depth
        parts = [xlo[:, at : at + depth]]
        parts += [block[:, x * plane + at : x * plane + at + depth] for x in range(span_x)]
        parts += [xhi[:, at : at + depth]]
        return jnp.concatenate(parts, axis=1)

    odd = lax.axis_index("col") % 2 == 1
    upward, downward = edge(span_y - 1), edge(0)
    ylo, yhi = swaps(
        "col", jnp.where(odd, downward, upward), jnp.where(odd, upward, downward)
    )
    return (xlo, xhi), (ylo, yhi), meanwhile


def coefficients_kernel(table, cells, coef):
    classes = table.shape[0]
    lanes = lax.broadcasted_iota(jnp.int32, cells.shape, 1)
    depth = cells.shape[1]
    here = cells[...]
    below = pltpu.roll(here, depth - 1, 1)
    above = pltpu.roll(here, 1, 1)
    maps = (below, here, above)
    keep = (lanes < depth - 1, None, lanes > 0)
    for dz in range(3):
        masks = [maps[dz] == k for k in range(1, classes)]
        for pair in range(9):
            offset = 3 * pair + dz
            value = jnp.full(cells.shape, table[0, offset], jnp.float32)
            for k in range(1, classes):
                value = jnp.where(masks[k - 1], table[k, offset], value)
            if keep[dz] is not None:
                value = jnp.where(keep[dz], value, 0.0)
            coef[offset] = value


def coefficients(table, cell_map):
    span_x, span_y, depth = cell_map.shape
    lines = span_x * span_y
    return pl.pallas_call(
        coefficients_kernel,
        out_shape=jax.ShapeDtypeStruct((27, lines, depth), jnp.float32),
        in_specs=[
            pl.BlockSpec(memory_space=pltpu.SMEM),
            pl.BlockSpec(memory_space=pltpu.VMEM),
        ],
        out_specs=pl.BlockSpec(memory_space=pltpu.VMEM),
        compiler_params=pltpu.CompilerParams(vmem_limit_bytes=4 * 1024 * 1024),
        name="coefficients",
    )(table, cell_map.reshape(lines, depth))


def stencil(coef, spans, columns, lines, line, wanted, write):
    depth = spans[2]

    def tile(step, carry):
        rows = pl.ds(pl.multiple_of(step * ROWS, ROWS), ROWS)
        held = {}
        for x, y in lines:
            at = x * spans[1] + y
            sums = [None, None, None]
            for pair in range(9):
                there = x + pair // 3 - 1, y + pair % 3 - 1
                if not wanted(there[1]):
                    continue
                if there not in held:
                    held[there] = line(rows, *there)
                for dz in range(3):
                    term = coef[3 * pair + dz, at : at + 1, :] * held[there]
                    sums[dz] = term if sums[dz] is None else sums[dz] + term
            total = pltpu.roll(sums[0], 1, 1) + pltpu.roll(sums[2], depth - 1, 1)
            write(rows, x, y, sums[1] + total)
        return carry

    lax.fori_loop(0, columns // ROWS, tile, 0)


def middle_of(spans, x):
    _, span_y, depth = spans
    inner = (span_y - 2) * depth
    return pl.ds((x * span_y + 1) * depth, inner), pl.ds(x * inner, inner)


def ends_of(spans, x, last):
    _, span_y, depth = spans
    return (
        pl.ds((x * span_y + (span_y - 1) * last) * depth, depth),
        pl.ds((2 * x + last) * depth, depth),
    )


def products(image, cells, fields):
    w = image[...]
    rows = [jnp.concatenate([ref[first:, there] for there in cells], axis=1) for ref, first in fields]
    return dot(w, jnp.concatenate(rows + [w], axis=0), NT)


def middle_image_kernel(spans, first, coef, stack, block, xlo, xhi, middle, partial, cross):
    span_x, span_y, depth = spans

    def line(rows, x, y):
        ref, at = block, x * span_y + y
        if x < 0 or x >= span_x:
            ref, at = (xlo if x < 0 else xhi), y
        return ref[rows, at * depth : (at + 1) * depth].astype(jnp.float32)

    def write(rows, x, y, total):
        if 0 < y < span_y - 1:
            at = x * (span_y - 2) + y - 1
            middle[rows, at * depth : (at + 1) * depth] = total.astype(jnp.bfloat16)
        else:
            partial[rows, ends_of(spans, x, int(y > 0))[1]] = total

    lines = [(x, y) for y in range(span_y) for x in range(span_x)]
    stencil(coef, spans, block.shape[0], lines, line, lambda y: 0 <= y < span_y, write)
    cells = [middle_of(spans, x)[0] for x in range(span_x)]
    cross[...] = products(middle, cells, [(stack, first)] + ([(block, 0)] if first else []))


def end_lines(spans, coef, stack, block, partial, cross, ylo, yhi, ends):
    span_x, span_y, depth = spans

    def line(rows, x, y):
        return (ylo if y < 0 else yhi)[rows, (x + 1) * depth : (x + 2) * depth].astype(jnp.float32)

    def write(rows, x, y, total):
        own = ends_of(spans, x, int(y > 0))[1]
        ends[rows, own] = (partial[rows, own] + total).astype(jnp.bfloat16)

    lines = [(x, y) for y in (0, span_y - 1) for x in range(span_x)]
    stencil(coef, spans, ends.shape[0], lines, line, lambda y: not 0 <= y < span_y, write)
    cells = [ends_of(spans, x, last)[0] for x in range(span_x) for last in range(2)]
    fields = [(stack, 0)] if block is None else [(stack, ends.shape[0]), (block, 0)]
    return cross[...] + products(ends, cells, fields)


def subtracted(spans, middle, ends, moved, block):
    columns = ends.shape[0]
    moved = moved[:columns] + moved[columns:]
    pieces = []
    for x in range(spans[0]):
        pieces.append((middle, *middle_of(spans, x)))
        pieces += [(ends, *ends_of(spans, x, last)) for last in range(2)]
    for ref, there, own in pieces:
        less = moved[:, there.start : there.start + there.size]
        block[:, there] = (ref[:, own].astype(jnp.float32) - less).astype(jnp.bfloat16)


def places(size):
    return [lax.broadcasted_iota(jnp.int32, (size, size), dim) for dim in (0, 1)]


def diagonal_of(square, axis):
    row, column = places(square.shape[0])
    return jnp.sum(jnp.where(row == column, square, 0.0), axis=axis, keepdims=True)


def both_of(packed, diagonal):
    row, column = places(packed.shape[0])
    turned = packed.T
    two = jnp.where(row < column, packed, turned)
    return jnp.where(row >= column, packed, turned), jnp.where(row == column, diagonal, two)


def stack_gram_kernel(columns, stack, sides, right, diagonal):
    parts = [stack[b * columns : (b + 1) * columns] for b in range(3)]
    row, column = places(columns)
    second = dot(parts[1], parts[1], NT)
    pair = jnp.where(row >= column, dot(parts[0], parts[0], NT), second)
    sides[0] = jnp.concatenate(
        [dot(parts[0], parts[2], NT), dot(parts[1], parts[2], NT)], axis=1
    )
    sides[1] = jnp.concatenate([pair, dot(parts[0], parts[1], NT)], axis=1)
    nothing = jnp.zeros((columns, columns), jnp.float32)
    right[...] = jnp.concatenate([nothing, dot(parts[2], parts[2], NT)], axis=1)
    diagonal[...] = jnp.concatenate([diagonal_of(second, 0), nothing[:1]], axis=1)


def first_image_kernel(
    spans, coef, stack, sides, right, diagonal, partial, known, ylo, yhi, ends, cross
):
    columns = ends.shape[0]
    sums = end_lines(spans, coef, stack, None, partial, known, ylo, yhi, ends)
    cross[:columns] = sums[:, : 2 * columns]
    sums = sums[:, 2 * columns :]
    row, lane = (lax.broadcasted_iota(jnp.int32, sums.shape, dim) for dim in (0, 1))
    cross[columns : 2 * columns] = jnp.where(
        (lane >= columns) & (row >= lane - columns), right[...], sums
    )
    for i in range(2):
        cross[(2 + i) * columns : (3 + i) * columns] = sides[i]
    own = jnp.sum(jnp.where(row == lane - columns, sums, 0.0), axis=0, keepdims=True)
    cross[4 * columns :] = jnp.broadcast_to(
        diagonal[...] + own, (cross.shape[0] - 4 * columns, 2 * columns)
    )


def second_image_kernel(spans, coef, stack, block, partial, known, ylo, yhi, ends, cross):
    cross[...] = end_lines(spans, coef, stack, block, partial, known, ylo, yhi, ends)


def opened(cross, columns, scale):
    parts = [cross[i * columns : (i + 1) * columns] * scale for i in range(4)]
    left, right = ([part[:, at : at + columns] for part in parts] for at in (0, columns))
    diagonals = cross[4 * columns : 4 * columns + 1] * scale
    first = jnp.concatenate([parts[0], left[1]], axis=1)
    one, two = both_of(left[3], diagonals[:, :columns])
    three, square = both_of(right[1], diagonals[:, columns:])
    gram = [
        [one, right[3], left[2]],
        [right[3].T, two, right[2]],
        [left[2].T, right[2].T, three],
    ]
    gram = jnp.concatenate([jnp.concatenate(row, axis=1) for row in gram], axis=0)
    return first, square, gram


def split(values):
    high = values.astype(jnp.bfloat16)
    return high, (values - high.astype(jnp.float32)).astype(jnp.bfloat16)


def dots(lefts, rights, dims=NN):
    stacked = lefts[0] if len(lefts) == 1 else jnp.concatenate(lefts, axis=0)
    total = sum(dot(stacked, right, dims) for right in rights)
    rows = lefts[0].shape[0]
    return sum(total[i * rows : (i + 1) * rows] for i in range(len(lefts)))


def factor(square, sizes, across):
    size = square.shape[0]
    shape = (8, 2 * size)
    sub = lax.broadcasted_iota(jnp.int32, shape, 0)
    unit = lax.broadcasted_iota(jnp.int32, (size, size), 0) == lax.broadcasted_iota(
        jnp.int32, (size, size), 1
    )
    scale = lax.rsqrt(across)
    square = square * lax.rsqrt(sizes) * scale
    whole = jnp.concatenate([square, unit.astype(jnp.float32)], axis=1)
    blocks = [whole[b : b + 8] for b in range(0, size, 8)]
    done = []

    def row_of(values, at):
        return jnp.broadcast_to(values[at : at + 1, :], shape)

    def columns_of(values, first):
        return [
            jnp.broadcast_to(values[:, at : at + 1], shape) for at in range(first, first + 8)
        ]

    for b, here in enumerate(blocks):
        columns = columns_of(here, 8 * b)
        entry = {(i, j): row_of(columns[j], i) for j in range(8) for i in range(j + 1)}
        rows = [row_of(here, i) for i in range(8)]
        scaled = jnp.zeros(shape, jnp.float32)
        solved, ratio = [], {}
        if b + 1 < len(blocks):
            below = columns_of(blocks[b + 1], 8 * b)
        for p in range(0, 8, 2):
            q = p + 1
            first, mixed, last = entry[p, p], entry[p, q], entry[q, q]
            inverse = 1.0 / (first * last - mixed * mixed)

            def solve(one, two):
                return (
                    (last * one - mixed * two) * inverse,
                    (first * two - mixed * one) * inverse,
                )

            for j in range(p + 2, 8):
                ratio[p, j], ratio[q, j] = solve(entry[p, j], entry[q, j])
            for i in range(p + 2, 8):
                for j in range(i, 8):
                    change = entry[p, i] * ratio[p, j] + entry[q, i] * ratio[q, j]
                    entry[i, j] = entry[i, j] - change
                rows[i] = rows[i] - (ratio[p, i] * rows[p] + ratio[q, i] * rows[q])
            solved += solve(rows[p], rows[q])
            if b + 1 < len(blocks):
                change = below[p] * solved[p] + below[q] * solved[q]
                blocks[b + 1] = blocks[b + 1] - change
                for j in range(p + 2, 8):
                    below[j] = below[j] - (below[p] * ratio[p, j] + below[q] * ratio[q, j])
            part = mixed * (1.0 / first)
            scaled = jnp.where(sub == p, rows[p] * lax.rsqrt(first), scaled)
            rest = (rows[q] - part * rows[p]) * lax.rsqrt(last - part * mixed)
            scaled = jnp.where(sub == q, rest, scaled)
        done.append(scaled)
        for p in (4, 2, 0):
            for r in (p, p + 1):
                for j in range(p + 2, 8):
                    solved[r] = solved[r] - ratio[r, j] * solved[j]
        for later in range(b + 2, len(blocks)):
            parts = [one * two for one, two in zip(columns_of(blocks[later], 8 * b), solved)]
            while len(parts) > 1:
                parts = [one + two for one, two in zip(parts[::2], parts[1::2])]
            blocks[later] = blocks[later] - parts[0]
    done = jnp.concatenate(done, axis=0)
    above = lax.broadcasted_iota(jnp.int32, (size, size), 0) <= lax.broadcasted_iota(
        jnp.int32, (size, size), 1
    )
    return jnp.where(above, done[:, :size] * (across * scale), 0.0), done[:, size:] * scale


def project(first, square, own):
    first_parts = split(first)
    first_low = first_parts[0]
    second = first - dots((first_low,), own)
    second_low = second.astype(jnp.bfloat16)
    used = (first_low, second_low)
    square = square - dots(used, first_parts, NT)
    rest = second - dots((second_low,), own)
    square = square - dots(split(rest), used, NT)
    sizes = [diagonal_of(square, axis) for axis in (1, 0)]
    return used, first + second, rest, square, sizes


def first_solve_kernel(
    scale, spans, cross, stack, middle, ends, block, proj, low, rest, square, inverse
):
    columns = ends.shape[0]
    first, own_square, gram = opened(cross, columns, scale)
    used, proj[...], rest[...], square_here, sizes = project(first, own_square, split(gram))
    square[...] = square_here
    moved = dot(jnp.concatenate(used, axis=0), stack[...])
    subtracted(spans, middle, ends, moved, block)
    upper, inverse_here = factor(square_here, *sizes)
    low[...] = upper.T
    inverse_here = inverse_here.astype(jnp.bfloat16)
    inverse[...] = inverse_here
    block[...] = dot(inverse_here, block[...]).astype(jnp.bfloat16)


def next_gram_kernel(scale, cross, rest, square, inverse, high, low):
    columns = square.shape[0]
    kept = rest.shape[1] - columns
    _, _, gram = opened(cross, columns, scale)
    mixed = dots((inverse[...],), split(rest[:, columns:]))
    corner = dots((inverse[...],), split(square[...]))
    corner = dots(split(corner), (inverse[...],), NT)
    for part, (old, side, end) in zip(
        (high, low), zip(split(gram[columns:, columns:]), split(mixed), split(corner))
    ):
        part[:kept, :kept] = old
        part[kept:, :kept] = side
        part[:kept, kept:] = side.T
        part[kept:, kept:] = end


def second_solve_kernel(
    scale, cross, own_high, own_low, stack, last, middle, ends, proj_in, low_in, result, proj, low,
    block,
):
    columns = ends.shape[0]
    kept = stack.shape[0] - columns
    fields = stack.shape[0]
    sums = cross[...] * scale
    used, proj[1], _, square, sizes = project(
        sums[:, :fields], sums[:, fields:], (own_high[...], own_low[...])
    )
    proj[0] = proj_in[...]
    low[0] = low_in[...]
    _, span_x, span_y, depth = result.shape
    both = jnp.concatenate(used, axis=0)
    moved = dot(both[:, :kept], stack[columns:]) + dot(both[:, kept:], last[...])
    subtracted((span_x, span_y, depth), middle, ends, moved, block)
    upper, inverse = factor(square, *sizes)
    low[1] = upper.T
    inverse = inverse.astype(jnp.bfloat16)
    plane = span_y * depth
    for x in range(span_x):
        part = dot(inverse, block[:, x * plane : (x + 1) * plane])
        result[:, x] = part.reshape(columns, span_y, depth).astype(jnp.bfloat16)


def partner(part, mask):
    axes = ("slab", "col")
    count = lax.axis_size("slab") * lax.axis_size("col")
    return lax.ppermute(part, axes, [(i, i ^ mask) for i in range(count)])


def whole_sum(part):
    cols = lax.axis_size("col")
    count = lax.axis_size("slab") * cols
    index = lax.axis_index("slab") * cols + lax.axis_index("col")
    bit, upper = 1, 0
    while bit < count:
        upper = upper ^ (index // bit % 2)
        bit *= 2
    upper = upper == 1
    half = part.shape[0] // 2
    low, high = part[:half], part[half:]
    part = jnp.where(upper, high, low) + partner(jnp.where(upper, low, high), 1)
    bit = 2
    while bit < count:
        if 2 * bit < count:
            one, two, both = (partner(part, mask) for mask in (bit + 1, 2 * bit + 1, 3 * bit))
            part = (part + one) + (both + two)
            bit *= 4
        else:
            part = part + partner(part, bit + 1)
            bit *= 2
    other = partner(part, 1)
    return jnp.concatenate([jnp.where(upper, other, part), jnp.where(upper, part, other)], axis=0)


def call(kernel, name, outs, *args, flops=0, scratch=()):
    moved = sum(math.prod(arg.shape) * arg.dtype.itemsize for arg in args)
    moved += sum(math.prod(shape) * jnp.dtype(dtype).itemsize for shape, dtype in outs)
    return pl.pallas_call(
        kernel,
        out_shape=[jax.ShapeDtypeStruct(shape, dtype) for shape, dtype in outs],
        in_specs=[pl.BlockSpec(memory_space=pltpu.VMEM)] * len(args),
        out_specs=[pl.BlockSpec(memory_space=pltpu.VMEM)] * len(outs),
        scratch_shapes=scratch,
        compiler_params=pltpu.CompilerParams(vmem_limit_bytes=24 * 1024 * 1024),
        cost_estimate=pl.CostEstimate(flops=flops, bytes_accessed=moved, transcendentals=0),
        name=name,
    )(*args)


def shards(basis, cell_map, table):
    span_x, span_y, depth = cell_map.shape
    blocks, columns = basis.shape[:2]
    cells = span_x * span_y * depth
    fields = blocks * columns
    scale = 1.0 / (cells * lax.axis_size("slab") * lax.axis_size("col"))
    spans = (span_x, span_y, depth)
    f32, bf16 = jnp.float32, jnp.bfloat16

    stack = basis.reshape(fields, cells)
    coef = coefficients(table, cell_map)
    own = call(
        functools.partial(stack_gram_kernel, columns),
        "stack_gram",
        [((2, columns, 2 * columns), f32), ((columns, 2 * columns), f32), ((1, 2 * columns), f32)],
        stack,
        flops=2 * fields * fields * cells,
    )

    end_cells = 2 * span_x * depth

    def middle_image(first, stack, block, planes):
        return call(
            functools.partial(middle_image_kernel, spans, first),
            "middle_image",
            [((columns, cells - end_cells), bf16), ((columns, end_cells), f32),
             ((columns, fields + columns), f32)],
            coef, stack, block, *planes,
            flops=2 * 27 * columns * cells,
        )

    last = basis[blocks - 1].reshape(columns, cells)
    planes, lines, (coef, stack, own) = neighbours(last, *spans, (coef, stack, own))
    middle, partial, known = middle_image(0, stack, last, planes)
    ends, cross = call(
        functools.partial(first_image_kernel, spans),
        "first_image",
        [((columns, end_cells), bf16), ((4 * columns + 16, 2 * columns), f32)],
        coef, stack, *own, partial, known, *lines,
    )
    cross = whole_sum(cross)
    block, proj, low, rest, square, inverse = call(
        functools.partial(first_solve_kernel, scale, spans),
        "first_solve",
        [((columns, cells), bf16), ((columns, fields), f32), ((columns, columns), f32),
         ((columns, fields), f32), ((columns, columns), f32), ((columns, columns), bf16)],
        cross, stack, middle, ends,
    )
    own = call(
        functools.partial(next_gram_kernel, scale),
        "next_gram",
        [((fields, fields), bf16)] * 2,
        cross, rest, square, inverse,
    )
    planes, lines, _ = neighbours(block, *spans)
    middle, partial, known = middle_image(columns, stack, block, planes)
    ends, cross = call(
        functools.partial(second_image_kernel, spans),
        "second_image",
        [((columns, end_cells), bf16), ((columns, fields + columns), f32)],
        coef, stack, block, partial, known, *lines,
    )
    block, proj, low = call(
        functools.partial(second_solve_kernel, scale),
        "second_solve",
        [((columns, *spans), bf16), ((2, columns, fields), f32), ((2, columns, columns), f32)],
        whole_sum(cross), *own, stack, block, middle, ends, proj, low,
        scratch=[pltpu.VMEM((columns, cells), bf16)],
    )
    return block, jnp.swapaxes(proj, 1, 2), low


def solution(mesh):
    placed = (P(None, None, "slab", "col", None), P("slab", "col", None), P())
    return jax.shard_map(
        shards,
        mesh=mesh,
        in_specs=placed,
        out_specs=(P(None, "slab", "col", None), P(), P()),
        check_vma=False,
    )
```

```python
import functools
import math

import jax
import jax.numpy as jnp
from jax import lax
from jax.experimental import pallas as pl
from jax.experimental.pallas import tpu as pltpu
from jax.sharding import PartitionSpec as P

NN = (((1,), (0,)), ((), ()))
NT = (((1,), (1,)), ((), ()))
ROWS = 16


def dot(left, right, dims=NN):
    return lax.dot_general(left, right, dims, preferred_element_type=jnp.float32)


def swaps(axis, near, far):
    count = lax.axis_size(axis)
    me = lax.axis_index(axis)
    pairs = [(i, (i - 1 ^ 1) + 1) for i in range(1, count - 1)]
    inner = lax.ppermute(near, axis, [(i, i ^ 1) for i in range(count)])
    outer = lax.ppermute(far, axis, pairs + [(0, count - 1), (count - 1, 0)])
    if axis == "slab":
        even = me % 2 == 0
        low, high = jnp.where(even, outer, inner), jnp.where(even, inner, outer)
    else:
        odd = me % 2 == 1
        low, high = jnp.where(odd, inner, outer), jnp.where(odd, outer, inner)
    return jnp.where(me == 0, 0, low), jnp.where(me == count - 1, 0, high)


def cut_kernel(start, block, part):
    part[...] = block[:, pl.ds(pl.multiple_of(start[0], 128), part.shape[1])]


def cut(block, start, width):
    return pl.pallas_call(
        cut_kernel,
        out_shape=jax.ShapeDtypeStruct((block.shape[0], width), block.dtype),
        in_specs=[
            pl.BlockSpec(memory_space=pltpu.SMEM),
            pl.BlockSpec(memory_space=pltpu.VMEM),
        ],
        out_specs=pl.BlockSpec(memory_space=pltpu.VMEM),
        compiler_params=pltpu.CompilerParams(vmem_limit_bytes=4 * 1024 * 1024),
        name="cut",
    )(start.reshape(1), block)


def neighbours(block, span_x, span_y, depth, meanwhile=None):
    plane = span_y * depth
    top = (span_x - 1) * plane
    odd = lax.axis_index("slab") % 2 == 1
    near = jnp.where(odd, block[:, :plane], block[:, top:])
    far = cut(block, jnp.where(odd, top, 0), plane)
    xlo, xhi = swaps("slab", near, far)
    xlo, xhi, meanwhile = lax.optimization_barrier((xlo, xhi, meanwhile))

    def edge(row):
        at = row * depth
        parts = [xlo[:, at : at + depth]]
        parts += [block[:, x * plane + at : x * plane + at + depth] for x in range(span_x)]
        parts += [xhi[:, at : at + depth]]
        return jnp.concatenate(parts, axis=1)

    odd = lax.axis_index("col") % 2 == 1
    upward, downward = edge(span_y - 1), edge(0)
    ylo, yhi = swaps(
        "col", jnp.where(odd, downward, upward), jnp.where(odd, upward, downward)
    )
    return (xlo, xhi), (ylo, yhi), meanwhile


def coefficients_kernel(table, cells, coef):
    classes = table.shape[0]
    lanes = lax.broadcasted_iota(jnp.int32, cells.shape, 1)
    depth = cells.shape[1]
    here = cells[...]
    below = pltpu.roll(here, depth - 1, 1)
    above = pltpu.roll(here, 1, 1)
    maps = (below, here, above)
    keep = (lanes < depth - 1, None, lanes > 0)
    for dz in range(3):
        masks = [maps[dz] == k for k in range(1, classes)]
        for pair in range(9):
            offset = 3 * pair + dz
            value = jnp.full(cells.shape, table[0, offset], jnp.float32)
            for k in range(1, classes):
                value = jnp.where(masks[k - 1], table[k, offset], value)
            if keep[dz] is not None:
                value = jnp.where(keep[dz], value, 0.0)
            coef[offset] = value


def coefficients(table, cell_map):
    span_x, span_y, depth = cell_map.shape
    lines = span_x * span_y
    return pl.pallas_call(
        coefficients_kernel,
        out_shape=jax.ShapeDtypeStruct((27, lines, depth), jnp.float32),
        in_specs=[
            pl.BlockSpec(memory_space=pltpu.SMEM),
            pl.BlockSpec(memory_space=pltpu.VMEM),
        ],
        out_specs=pl.BlockSpec(memory_space=pltpu.VMEM),
        compiler_params=pltpu.CompilerParams(vmem_limit_bytes=4 * 1024 * 1024),
        name="coefficients",
    )(table, cell_map.reshape(lines, depth))


def stencil(coef, spans, columns, lines, line, wanted, write):
    depth = spans[2]

    def tile(step, carry):
        rows = pl.ds(pl.multiple_of(step * ROWS, ROWS), ROWS)
        held = {}
        for x, y in lines:
            at = x * spans[1] + y
            sums = [None, None, None]
            for pair in range(9):
                there = x + pair // 3 - 1, y + pair % 3 - 1
                if not wanted(there[1]):
                    continue
                if there not in held:
                    held[there] = line(rows, *there)
                for dz in range(3):
                    term = coef[3 * pair + dz, at : at + 1, :] * held[there]
                    sums[dz] = term if sums[dz] is None else sums[dz] + term
            total = pltpu.roll(sums[0], 1, 1) + pltpu.roll(sums[2], depth - 1, 1)
            write(rows, x, y, sums[1] + total)
        return carry

    lax.fori_loop(0, columns // ROWS, tile, 0)


def middle_of(spans, x):
    _, span_y, depth = spans
    inner = (span_y - 2) * depth
    return pl.ds((x * span_y + 1) * depth, inner), pl.ds(x * inner, inner)


def ends_of(spans, x, last):
    _, span_y, depth = spans
    return (
        pl.ds((x * span_y + (span_y - 1) * last) * depth, depth),
        pl.ds((2 * x + last) * depth, depth),
    )


def products(image, cells, fields):
    w = image[...]
    rows = [jnp.concatenate([ref[first:, there] for there in cells], axis=1) for ref, first in fields]
    return dot(w, jnp.concatenate(rows + [w], axis=0), NT)


def middle_image_kernel(spans, first, coef, stack, block, xlo, xhi, middle, partial, cross):
    span_x, span_y, depth = spans

    def line(rows, x, y):
        ref, at = block, x * span_y + y
        if x < 0 or x >= span_x:
            ref, at = (xlo if x < 0 else xhi), y
        return ref[rows, at * depth : (at + 1) * depth].astype(jnp.float32)

    def write(rows, x, y, total):
        if 0 < y < span_y - 1:
            at = x * (span_y - 2) + y - 1
            middle[rows, at * depth : (at + 1) * depth] = total.astype(jnp.bfloat16)
        else:
            partial[rows, ends_of(spans, x, int(y > 0))[1]] = total

    lines = [(x, y) for y in range(span_y) for x in range(span_x)]
    stencil(coef, spans, block.shape[0], lines, line, lambda y: 0 <= y < span_y, write)
    cells = [middle_of(spans, x)[0] for x in range(span_x)]
    cross[...] = products(middle, cells, [(stack, first)] + ([(block, 0)] if first else []))


def end_lines(spans, coef, stack, block, partial, cross, ylo, yhi, ends):
    span_x, span_y, depth = spans

    def line(rows, x, y):
        return (ylo if y < 0 else yhi)[rows, (x + 1) * depth : (x + 2) * depth].astype(jnp.float32)

    def write(rows, x, y, total):
        own = ends_of(spans, x, int(y > 0))[1]
        ends[rows, own] = (partial[rows, own] + total).astype(jnp.bfloat16)

    lines = [(x, y) for y in (0, span_y - 1) for x in range(span_x)]
    stencil(coef, spans, ends.shape[0], lines, line, lambda y: not 0 <= y < span_y, write)
    cells = [ends_of(spans, x, last)[0] for x in range(span_x) for last in range(2)]
    fields = [(stack, 0)] if block is None else [(stack, ends.shape[0]), (block, 0)]
    return cross[...] + products(ends, cells, fields)


def subtracted(spans, middle, ends, moved, block):
    columns = ends.shape[0]
    moved = moved[:columns] + moved[columns:]
    pieces = []
    for x in range(spans[0]):
        pieces.append((middle, *middle_of(spans, x)))
        pieces += [(ends, *ends_of(spans, x, last)) for last in range(2)]
    for ref, there, own in pieces:
        less = moved[:, there.start : there.start + there.size]
        block[:, there] = (ref[:, own].astype(jnp.float32) - less).astype(jnp.bfloat16)


def places(size):
    return [lax.broadcasted_iota(jnp.int32, (size, size), dim) for dim in (0, 1)]


def diagonal_of(square, axis):
    row, column = places(square.shape[0])
    return jnp.sum(jnp.where(row == column, square, 0.0), axis=axis, keepdims=True)


def both_of(packed, diagonal):
    row, column = places(packed.shape[0])
    turned = packed.T
    two = jnp.where(row < column, packed, turned)
    return jnp.where(row >= column, packed, turned), jnp.where(row == column, diagonal, two)


def stack_gram_kernel(columns, stack, sides, right, diagonal):
    parts = [stack[b * columns : (b + 1) * columns] for b in range(3)]
    row, column = places(columns)
    second = dot(parts[1], parts[1], NT)
    pair = jnp.where(row >= column, dot(parts[0], parts[0], NT), second)
    sides[0] = jnp.concatenate(
        [dot(parts[0], parts[2], NT), dot(parts[1], parts[2], NT)], axis=1
    )
    sides[1] = jnp.concatenate([pair, dot(parts[0], parts[1], NT)], axis=1)
    nothing = jnp.zeros((columns, columns), jnp.float32)
    right[...] = jnp.concatenate([nothing, dot(parts[2], parts[2], NT)], axis=1)
    diagonal[...] = jnp.concatenate([diagonal_of(second, 0), nothing[:1]], axis=1)


def first_image_kernel(
    spans, coef, stack, sides, right, diagonal, partial, known, ylo, yhi, ends, cross
):
    columns = ends.shape[0]
    sums = end_lines(spans, coef, stack, None, partial, known, ylo, yhi, ends)
    cross[:columns] = sums[:, : 2 * columns]
    sums = sums[:, 2 * columns :]
    row, lane = (lax.broadcasted_iota(jnp.int32, sums.shape, dim) for dim in (0, 1))
    cross[columns : 2 * columns] = jnp.where(
        (lane >= columns) & (row >= lane - columns), right[...], sums
    )
    for i in range(2):
        cross[(2 + i) * columns : (3 + i) * columns] = sides[i]
    own = jnp.sum(jnp.where(row == lane - columns, sums, 0.0), axis=0, keepdims=True)
    cross[4 * columns :] = jnp.broadcast_to(
        diagonal[...] + own, (cross.shape[0] - 4 * columns, 2 * columns)
    )


def second_image_kernel(spans, coef, stack, block, partial, known, ylo, yhi, ends, cross):
    cross[...] = end_lines(spans, coef, stack, block, partial, known, ylo, yhi, ends)


def opened(cross, columns, scale):
    parts = [cross[i * columns : (i + 1) * columns] * scale for i in range(4)]
    left, right = ([part[:, at : at + columns] for part in parts] for at in (0, columns))
    diagonals = cross[4 * columns : 4 * columns + 1] * scale
    first = jnp.concatenate([parts[0], left[1]], axis=1)
    one, two = both_of(left[3], diagonals[:, :columns])
    three, square = both_of(right[1], diagonals[:, columns:])
    gram = [
        [one, right[3], left[2]],
        [right[3].T, two, right[2]],
        [left[2].T, right[2].T, three],
    ]
    gram = jnp.concatenate([jnp.concatenate(row, axis=1) for row in gram], axis=0)
    return first, square, gram


def split(values):
    high = values.astype(jnp.bfloat16)
    return high, (values - high.astype(jnp.float32)).astype(jnp.bfloat16)


def dots(lefts, rights, dims=NN):
    stacked = lefts[0] if len(lefts) == 1 else jnp.concatenate(lefts, axis=0)
    total = sum(dot(stacked, right, dims) for right in rights)
    rows = lefts[0].shape[0]
    return sum(total[i * rows : (i + 1) * rows] for i in range(len(lefts)))


def factor(square, sizes, across):
    size = square.shape[0]
    shape = (8, 2 * size)
    sub = lax.broadcasted_iota(jnp.int32, shape, 0)
    unit = lax.broadcasted_iota(jnp.int32, (size, size), 0) == lax.broadcasted_iota(
        jnp.int32, (size, size), 1
    )
    scale = lax.rsqrt(across)
    square = square * lax.rsqrt(sizes) * scale
    whole = jnp.concatenate([square, unit.astype(jnp.float32)], axis=1)
    blocks = [whole[b : b + 8] for b in range(0, size, 8)]
    done = []

    def row_of(values, at):
        return jnp.broadcast_to(values[at : at + 1, :], shape)

    def columns_of(values, first):
        return [
            jnp.broadcast_to(values[:, at : at + 1], shape) for at in range(first, first + 8)
        ]

    for b, here in enumerate(blocks):
        columns = columns_of(here, 8 * b)
        entry = {(i, j): row_of(columns[j], i) for j in range(8) for i in range(j + 1)}
        rows = [row_of(here, i) for i in range(8)]
        scaled = jnp.zeros(shape, jnp.float32)
        solved, ratio = [], {}
        if b + 1 < len(blocks):
            below = columns_of(blocks[b + 1], 8 * b)
        for p in range(0, 8, 2):
            q = p + 1
            first, mixed, last = entry[p, p], entry[p, q], entry[q, q]
            inverse = 1.0 / (first * last - mixed * mixed)

            def solve(one, two):
                return (
                    (last * one - mixed * two) * inverse,
                    (first * two - mixed * one) * inverse,
                )

            for j in range(p + 2, 8):
                ratio[p, j], ratio[q, j] = solve(entry[p, j], entry[q, j])
            for i in range(p + 2, 8):
                for j in range(i, 8):
                    change = entry[p, i] * ratio[p, j] + entry[q, i] * ratio[q, j]
                    entry[i, j] = entry[i, j] - change
                rows[i] = rows[i] - (ratio[p, i] * rows[p] + ratio[q, i] * rows[q])
            solved += solve(rows[p], rows[q])
            if b + 1 < len(blocks):
                change = below[p] * solved[p] + below[q] * solved[q]
                blocks[b + 1] = blocks[b + 1] - change
                for j in range(p + 2, 8):
                    below[j] = below[j] - (below[p] * ratio[p, j] + below[q] * ratio[q, j])
            part = mixed * (1.0 / first)
            scaled = jnp.where(sub == p, rows[p] * lax.rsqrt(first), scaled)
            rest = (rows[q] - part * rows[p]) * lax.rsqrt(last - part * mixed)
            scaled = jnp.where(sub == q, rest, scaled)
        done.append(scaled)
        for p in (4, 2, 0):
            for r in (p, p + 1):
                for j in range(p + 2, 8):
                    solved[r] = solved[r] - ratio[r, j] * solved[j]
        for later in range(b + 2, len(blocks)):
            parts = [one * two for one, two in zip(columns_of(blocks[later], 8 * b), solved)]
            while len(parts) > 1:
                parts = [one + two for one, two in zip(parts[::2], parts[1::2])]
            blocks[later] = blocks[later] - parts[0]
    done = jnp.concatenate(done, axis=0)
    above = lax.broadcasted_iota(jnp.int32, (size, size), 0) <= lax.broadcasted_iota(
        jnp.int32, (size, size), 1
    )
    return jnp.where(above, done[:, :size] * (across * scale), 0.0), done[:, size:] * scale


def project(first, square, own):
    first_parts = split(first)
    first_low = first_parts[0]
    second = first - dots((first_low,), own)
    second_low = second.astype(jnp.bfloat16)
    used = (first_low, second_low)
    square = square - dots(used, first_parts, NT)
    rest = second - dots((second_low,), own)
    square = square - dots(split(rest), used, NT)
    sizes = [diagonal_of(square, axis) for axis in (1, 0)]
    return used, first + second, rest, square, sizes


def first_solve_kernel(
    scale, spans, cross, stack, middle, ends, block, proj, low, rest, square, inverse
):
    columns = ends.shape[0]
    first, own_square, gram = opened(cross, columns, scale)
    used, proj[...], rest[...], square_here, sizes = project(first, own_square, split(gram))
    square[...] = square_here
    moved = dot(jnp.concatenate(used, axis=0), stack[...])
    subtracted(spans, middle, ends, moved, block)
    upper, inverse_here = factor(square_here, *sizes)
    low[...] = upper.T
    inverse_here = inverse_here.astype(jnp.bfloat16)
    inverse[...] = inverse_here
    block[...] = dot(inverse_here, block[...]).astype(jnp.bfloat16)


def next_gram_kernel(scale, cross, rest, square, inverse, high, low):
    columns = square.shape[0]
    kept = rest.shape[1] - columns
    _, _, gram = opened(cross, columns, scale)
    mixed = dots((inverse[...],), split(rest[:, columns:]))
    corner = dots((inverse[...],), split(square[...]))
    corner = dots(split(corner), (inverse[...],), NT)
    for part, (old, side, end) in zip(
        (high, low), zip(split(gram[columns:, columns:]), split(mixed), split(corner))
    ):
        part[:kept, :kept] = old
        part[kept:, :kept] = side
        part[:kept, kept:] = side.T
        part[kept:, kept:] = end


def second_solve_kernel(
    scale, cross, own_high, own_low, stack, last, middle, ends, proj_in, low_in, result, proj, low,
    block,
):
    columns = ends.shape[0]
    fields = stack.shape[0]
    sums = cross[...] * scale
    used, proj[1], _, square, sizes = project(
        sums[:, :fields], sums[:, fields:], (own_high[...], own_low[...])
    )
    proj[0] = proj_in[...]
    low[0] = low_in[...]
    _, span_x, span_y, depth = result.shape
    both = jnp.concatenate(used, axis=0)
    moved = dot(both, jnp.concatenate([stack[columns:], last[...]], axis=0))
    subtracted((span_x, span_y, depth), middle, ends, moved, block)
    upper, inverse = factor(square, *sizes)
    low[1] = upper.T
    inverse = inverse.astype(jnp.bfloat16)
    plane = span_y * depth
    for x in range(span_x):
        part = dot(inverse, block[:, x * plane : (x + 1) * plane])
        result[:, x] = part.reshape(columns, span_y, depth).astype(jnp.bfloat16)


def partner(part, mask):
    axes = ("slab", "col")
    count = lax.axis_size("slab") * lax.axis_size("col")
    return lax.ppermute(part, axes, [(i, i ^ mask) for i in range(count)])


def whole_sum(part):
    cols = lax.axis_size("col")
    count = lax.axis_size("slab") * cols
    index = lax.axis_index("slab") * cols + lax.axis_index("col")
    bit, upper = 1, 0
    while bit < count:
        upper = upper ^ (index // bit % 2)
        bit *= 2
    upper = upper == 1
    half = part.shape[0] // 2
    low, high = part[:half], part[half:]
    part = jnp.where(upper, high, low) + partner(jnp.where(upper, low, high), 1)
    bit = 2
    while bit < count:
        if 2 * bit < count:
            one, two, both = (partner(part, mask) for mask in (bit + 1, 2 * bit + 1, 3 * bit))
            part = (part + one) + (both + two)
            bit *= 4
        else:
            part = part + partner(part, bit + 1)
            bit *= 2
    other = partner(part, 1)
    return jnp.concatenate([jnp.where(upper, other, part), jnp.where(upper, part, other)], axis=0)


def call(kernel, name, outs, *args, flops=0, scratch=()):
    moved = sum(math.prod(arg.shape) * arg.dtype.itemsize for arg in args)
    moved += sum(math.prod(shape) * jnp.dtype(dtype).itemsize for shape, dtype in outs)
    return pl.pallas_call(
        kernel,
        out_shape=[jax.ShapeDtypeStruct(shape, dtype) for shape, dtype in outs],
        in_specs=[pl.BlockSpec(memory_space=pltpu.VMEM)] * len(args),
        out_specs=[pl.BlockSpec(memory_space=pltpu.VMEM)] * len(outs),
        scratch_shapes=scratch,
        compiler_params=pltpu.CompilerParams(vmem_limit_bytes=24 * 1024 * 1024),
        cost_estimate=pl.CostEstimate(flops=flops, bytes_accessed=moved, transcendentals=0),
        name=name,
    )(*args)


def shards(basis, cell_map, table):
    span_x, span_y, depth = cell_map.shape
    blocks, columns = basis.shape[:2]
    cells = span_x * span_y * depth
    fields = blocks * columns
    scale = 1.0 / (cells * lax.axis_size("slab") * lax.axis_size("col"))
    spans = (span_x, span_y, depth)
    f32, bf16 = jnp.float32, jnp.bfloat16

    stack = basis.reshape(fields, cells)
    coef = coefficients(table, cell_map)
    own = call(
        functools.partial(stack_gram_kernel, columns),
        "stack_gram",
        [((2, columns, 2 * columns), f32), ((columns, 2 * columns), f32), ((1, 2 * columns), f32)],
        stack,
        flops=2 * fields * fields * cells,
    )

    end_cells = 2 * span_x * depth

    def middle_image(first, stack, block, planes):
        return call(
            functools.partial(middle_image_kernel, spans, first),
            "middle_image",
            [((columns, cells - end_cells), bf16), ((columns, end_cells), f32),
             ((columns, fields + columns), f32)],
            coef, stack, block, *planes,
            flops=2 * 27 * columns * cells,
        )

    last = basis[blocks - 1].reshape(columns, cells)
    planes, lines, (coef, stack, own) = neighbours(last, *spans, (coef, stack, own))
    middle, partial, known = middle_image(0, stack, last, planes)
    ends, cross = call(
        functools.partial(first_image_kernel, spans),
        "first_image",
        [((columns, end_cells), bf16), ((4 * columns + 16, 2 * columns), f32)],
        coef, stack, *own, partial, known, *lines,
    )
    cross = whole_sum(cross)
    block, proj, low, rest, square, inverse = call(
        functools.partial(first_solve_kernel, scale, spans),
        "first_solve",
        [((columns, cells), bf16), ((columns, fields), f32), ((columns, columns), f32),
         ((columns, fields), f32), ((columns, columns), f32), ((columns, columns), bf16)],
        cross, stack, middle, ends,
    )
    own = call(
        functools.partial(next_gram_kernel, scale),
        "next_gram",
        [((fields, fields), bf16)] * 2,
        cross, rest, square, inverse,
    )
    planes, lines, _ = neighbours(block, *spans)
    middle, partial, known = middle_image(columns, stack, block, planes)
    ends, cross = call(
        functools.partial(second_image_kernel, spans),
        "second_image",
        [((columns, end_cells), bf16), ((columns, fields + columns), f32)],
        coef, stack, block, partial, known, *lines,
    )
    block, proj, low = call(
        functools.partial(second_solve_kernel, scale),
        "second_solve",
        [((columns, *spans), bf16), ((2, columns, fields), f32), ((2, columns, columns), f32)],
        whole_sum(cross), *own, stack, block, middle, ends, proj, low,
        scratch=[pltpu.VMEM((columns, cells), bf16)],
    )
    return block, jnp.swapaxes(proj, 1, 2), low


def solution(mesh):
    placed = (P(None, None, "slab", "col", None), P("slab", "col", None), P())
    return jax.shard_map(
        shards,
        mesh=mesh,
        in_specs=placed,
        out_specs=(P(None, "slab", "col", None), P(), P()),
        check_vma=False,
    )
```

```python
import functools
import math

import jax
import jax.numpy as jnp
from jax import lax
from jax.experimental import pallas as pl
from jax.experimental.pallas import tpu as pltpu
from jax.sharding import PartitionSpec as P

NN = (((1,), (0,)), ((), ()))
NT = (((1,), (1,)), ((), ()))
ROWS = 16


def dot(left, right, dims=NN):
    return lax.dot_general(left, right, dims, preferred_element_type=jnp.float32)


def swaps(axis, near, far):
    count = lax.axis_size(axis)
    me = lax.axis_index(axis)
    pairs = [(i, (i - 1 ^ 1) + 1) for i in range(1, count - 1)]
    inner = lax.ppermute(near, axis, [(i, i ^ 1) for i in range(count)])
    outer = lax.ppermute(far, axis, pairs + [(0, count - 1), (count - 1, 0)])
    if axis == "slab":
        even = me % 2 == 0
        low, high = jnp.where(even, outer, inner), jnp.where(even, inner, outer)
    else:
        even = me % 2 == 0
        low, high = jnp.where(even, outer, inner), jnp.where(even, inner, outer)
    return jnp.where(me == 0, 0, low), jnp.where(me == count - 1, 0, high)


def cut_kernel(start, block, part):
    part[...] = block[:, pl.ds(pl.multiple_of(start[0], 128), part.shape[1])]


def cut(block, start, width):
    return pl.pallas_call(
        cut_kernel,
        out_shape=jax.ShapeDtypeStruct((block.shape[0], width), block.dtype),
        in_specs=[
            pl.BlockSpec(memory_space=pltpu.SMEM),
            pl.BlockSpec(memory_space=pltpu.VMEM),
        ],
        out_specs=pl.BlockSpec(memory_space=pltpu.VMEM),
        compiler_params=pltpu.CompilerParams(vmem_limit_bytes=4 * 1024 * 1024),
        name="cut",
    )(start.reshape(1), block)


def neighbours(block, span_x, span_y, depth, meanwhile=None):
    plane = span_y * depth
    top = (span_x - 1) * plane
    odd = lax.axis_index("slab") % 2 == 1
    near = jnp.where(odd, block[:, :plane], block[:, top:])
    far = cut(block, jnp.where(odd, top, 0), plane)
    xlo, xhi = swaps("slab", near, far)
    xlo, xhi, meanwhile = lax.optimization_barrier((xlo, xhi, meanwhile))

    def edge(row):
        at = row * depth
        parts = [xlo[:, at : at + depth]]
        parts += [block[:, x * plane + at : x * plane + at + depth] for x in range(span_x)]
        parts += [xhi[:, at : at + depth]]
        return jnp.concatenate(parts, axis=1)

    odd = lax.axis_index("col") % 2 == 1
    upward, downward = edge(span_y - 1), edge(0)
    ylo, yhi = swaps(
        "col", jnp.where(odd, downward, upward), jnp.where(odd, upward, downward)
    )
    return (xlo, xhi), (ylo, yhi), meanwhile


def coefficients_kernel(table, cells, coef):
    classes = table.shape[0]
    lanes = lax.broadcasted_iota(jnp.int32, cells.shape, 1)
    depth = cells.shape[1]
    here = cells[...]
    below = pltpu.roll(here, depth - 1, 1)
    above = pltpu.roll(here, 1, 1)
    maps = (below, here, above)
    keep = (lanes < depth - 1, None, lanes > 0)
    for dz in range(3):
        masks = [maps[dz] == k for k in range(1, classes)]
        for pair in range(9):
            offset = 3 * pair + dz
            value = jnp.full(cells.shape, table[0, offset], jnp.float32)
            for k in range(1, classes):
                value = jnp.where(masks[k - 1], table[k, offset], value)
            if keep[dz] is not None:
                value = jnp.where(keep[dz], value, 0.0)
            coef[offset] = value


def coefficients(table, cell_map):
    span_x, span_y, depth = cell_map.shape
    lines = span_x * span_y
    return pl.pallas_call(
        coefficients_kernel,
        out_shape=jax.ShapeDtypeStruct((27, lines, depth), jnp.float32),
        in_specs=[
            pl.BlockSpec(memory_space=pltpu.SMEM),
            pl.BlockSpec(memory_space=pltpu.VMEM),
        ],
        out_specs=pl.BlockSpec(memory_space=pltpu.VMEM),
        compiler_params=pltpu.CompilerParams(vmem_limit_bytes=4 * 1024 * 1024),
        name="coefficients",
    )(table, cell_map.reshape(lines, depth))


def stencil(coef, spans, columns, lines, line, wanted, write):
    depth = spans[2]

    def tile(step, carry):
        rows = pl.ds(pl.multiple_of(step * ROWS, ROWS), ROWS)
        held = {}
        for x, y in lines:
            at = x * spans[1] + y
            sums = [None, None, None]
            for pair in range(9):
                there = x + pair // 3 - 1, y + pair % 3 - 1
                if not wanted(there[1]):
                    continue
                if there not in held:
                    held[there] = line(rows, *there)
                for dz in range(3):
                    term = coef[3 * pair + dz, at : at + 1, :] * held[there]
                    sums[dz] = term if sums[dz] is None else sums[dz] + term
            total = pltpu.roll(sums[0], 1, 1) + pltpu.roll(sums[2], depth - 1, 1)
            write(rows, x, y, sums[1] + total)
        return carry

    lax.fori_loop(0, columns // ROWS, tile, 0)


def middle_of(spans, x):
    _, span_y, depth = spans
    inner = (span_y - 2) * depth
    return pl.ds((x * span_y + 1) * depth, inner), pl.ds(x * inner, inner)


def ends_of(spans, x, last):
    _, span_y, depth = spans
    return (
        pl.ds((x * span_y + (span_y - 1) * last) * depth, depth),
        pl.ds((2 * x + last) * depth, depth),
    )


def products(image, cells, fields):
    w = image[...]
    rows = [jnp.concatenate([ref[first:, there] for there in cells], axis=1) for ref, first in fields]
    return dot(w, jnp.concatenate(rows + [w], axis=0), NT)


def middle_image_kernel(spans, first, coef, stack, block, xlo, xhi, middle, partial, cross):
    span_x, span_y, depth = spans

    def line(rows, x, y):
        ref, at = block, x * span_y + y
        if x < 0 or x >= span_x:
            ref, at = (xlo if x < 0 else xhi), y
        return ref[rows, at * depth : (at + 1) * depth].astype(jnp.float32)

    def write(rows, x, y, total):
        if 0 < y < span_y - 1:
            at = x * (span_y - 2) + y - 1
            middle[rows, at * depth : (at + 1) * depth] = total.astype(jnp.bfloat16)
        else:
            partial[rows, ends_of(spans, x, int(y > 0))[1]] = total

    lines = [(x, y) for y in range(span_y) for x in range(span_x)]
    stencil(coef, spans, block.shape[0], lines, line, lambda y: 0 <= y < span_y, write)
    cells = [middle_of(spans, x)[0] for x in range(span_x)]
    cross[...] = products(middle, cells, [(stack, first)] + ([(block, 0)] if first else []))


def end_lines(spans, coef, stack, block, partial, cross, ylo, yhi, ends):
    span_x, span_y, depth = spans

    def line(rows, x, y):
        return (ylo if y < 0 else yhi)[rows, (x + 1) * depth : (x + 2) * depth].astype(jnp.float32)

    def write(rows, x, y, total):
        own = ends_of(spans, x, int(y > 0))[1]
        ends[rows, own] = (partial[rows, own] + total).astype(jnp.bfloat16)

    lines = [(x, y) for y in (0, span_y - 1) for x in range(span_x)]
    stencil(coef, spans, ends.shape[0], lines, line, lambda y: not 0 <= y < span_y, write)
    cells = [ends_of(spans, x, last)[0] for x in range(span_x) for last in range(2)]
    fields = [(stack, 0)] if block is None else [(stack, ends.shape[0]), (block, 0)]
    return cross[...] + products(ends, cells, fields)


def subtracted(spans, middle, ends, moved, block):
    columns = ends.shape[0]
    moved = moved[:columns] + moved[columns:]
    pieces = []
    for x in range(spans[0]):
        pieces.append((middle, *middle_of(spans, x)))
        pieces += [(ends, *ends_of(spans, x, last)) for last in range(2)]
    for ref, there, own in pieces:
        less = moved[:, there.start : there.start + there.size]
        block[:, there] = (ref[:, own].astype(jnp.float32) - less).astype(jnp.bfloat16)


def places(size):
    return [lax.broadcasted_iota(jnp.int32, (size, size), dim) for dim in (0, 1)]


def diagonal_of(square, axis):
    row, column = places(square.shape[0])
    return jnp.sum(jnp.where(row == column, square, 0.0), axis=axis, keepdims=True)


def both_of(packed, diagonal):
    row, column = places(packed.shape[0])
    turned = packed.T
    two = jnp.where(row < column, packed, turned)
    return jnp.where(row >= column, packed, turned), jnp.where(row == column, diagonal, two)


def stack_gram_kernel(columns, stack, sides, right, diagonal):
    parts = [stack[b * columns : (b + 1) * columns] for b in range(3)]
    row, column = places(columns)
    second = dot(parts[1], parts[1], NT)
    pair = jnp.where(row >= column, dot(parts[0], parts[0], NT), second)
    sides[0] = jnp.concatenate(
        [dot(parts[0], parts[2], NT), dot(parts[1], parts[2], NT)], axis=1
    )
    sides[1] = jnp.concatenate([pair, dot(parts[0], parts[1], NT)], axis=1)
    nothing = jnp.zeros((columns, columns), jnp.float32)
    right[...] = jnp.concatenate([nothing, dot(parts[2], parts[2], NT)], axis=1)
    diagonal[...] = jnp.concatenate([diagonal_of(second, 0), nothing[:1]], axis=1)


def first_image_kernel(
    spans, coef, stack, sides, right, diagonal, partial, known, ylo, yhi, ends, cross
):
    columns = ends.shape[0]
    sums = end_lines(spans, coef, stack, None, partial, known, ylo, yhi, ends)
    cross[:columns] = sums[:, : 2 * columns]
    sums = sums[:, 2 * columns :]
    row, lane = (lax.broadcasted_iota(jnp.int32, sums.shape, dim) for dim in (0, 1))
    cross[columns : 2 * columns] = jnp.where(
        (lane >= columns) & (row >= lane - columns), right[...], sums
    )
    for i in range(2):
        cross[(2 + i) * columns : (3 + i) * columns] = sides[i]
    own = jnp.sum(jnp.where(row == lane - columns, sums, 0.0), axis=0, keepdims=True)
    cross[4 * columns :] = jnp.broadcast_to(
        diagonal[...] + own, (cross.shape[0] - 4 * columns, 2 * columns)
    )


def second_image_kernel(spans, coef, stack, block, partial, known, ylo, yhi, ends, cross):
    cross[...] = end_lines(spans, coef, stack, block, partial, known, ylo, yhi, ends)


def opened(cross, columns, scale):
    parts = [cross[i * columns : (i + 1) * columns] * scale for i in range(4)]
    left, right = ([part[:, at : at + columns] for part in parts] for at in (0, columns))
    diagonals = cross[4 * columns : 4 * columns + 1] * scale
    first = jnp.concatenate([parts[0], left[1]], axis=1)
    one, two = both_of(left[3], diagonals[:, :columns])
    three, square = both_of(right[1], diagonals[:, columns:])
    gram = [
        [one, right[3], left[2]],
        [right[3].T, two, right[2]],
        [left[2].T, right[2].T, three],
    ]
    gram = jnp.concatenate([jnp.concatenate(row, axis=1) for row in gram], axis=0)
    return first, square, gram


def split(values):
    high = values.astype(jnp.bfloat16)
    return high, (values - high.astype(jnp.float32)).astype(jnp.bfloat16)


def dots(lefts, rights, dims=NN):
    stacked = lefts[0] if len(lefts) == 1 else jnp.concatenate(lefts, axis=0)
    total = sum(dot(stacked, right, dims) for right in rights)
    rows = lefts[0].shape[0]
    return sum(total[i * rows : (i + 1) * rows] for i in range(len(lefts)))


def factor(square, sizes, across):
    size = square.shape[0]
    shape = (8, 2 * size)
    sub = lax.broadcasted_iota(jnp.int32, shape, 0)
    unit = lax.broadcasted_iota(jnp.int32, (size, size), 0) == lax.broadcasted_iota(
        jnp.int32, (size, size), 1
    )
    scale = lax.rsqrt(across)
    square = square * lax.rsqrt(sizes) * scale
    whole = jnp.concatenate([square, unit.astype(jnp.float32)], axis=1)
    blocks = [whole[b : b + 8] for b in range(0, size, 8)]
    done = []

    def row_of(values, at):
        return jnp.broadcast_to(values[at : at + 1, :], shape)

    def columns_of(values, first):
        return [
            jnp.broadcast_to(values[:, at : at + 1], shape) for at in range(first, first + 8)
        ]

    for b, here in enumerate(blocks):
        columns = columns_of(here, 8 * b)
        entry = {(i, j): row_of(columns[j], i) for j in range(8) for i in range(j + 1)}
        rows = [row_of(here, i) for i in range(8)]
        scaled = jnp.zeros(shape, jnp.float32)
        solved, ratio = [], {}
        if b + 1 < len(blocks):
            below = columns_of(blocks[b + 1], 8 * b)
        for p in range(0, 8, 2):
            q = p + 1
            first, mixed, last = entry[p, p], entry[p, q], entry[q, q]
            inverse = 1.0 / (first * last - mixed * mixed)

            def solve(one, two):
                return (
                    (last * one - mixed * two) * inverse,
                    (first * two - mixed * one) * inverse,
                )

            for j in range(p + 2, 8):
                ratio[p, j], ratio[q, j] = solve(entry[p, j], entry[q, j])
            for i in range(p + 2, 8):
                for j in range(i, 8):
                    change = entry[p, i] * ratio[p, j] + entry[q, i] * ratio[q, j]
                    entry[i, j] = entry[i, j] - change
                rows[i] = rows[i] - (ratio[p, i] * rows[p] + ratio[q, i] * rows[q])
            solved += solve(rows[p], rows[q])
            if b + 1 < len(blocks):
                change = below[p] * solved[p] + below[q] * solved[q]
                blocks[b + 1] = blocks[b + 1] - change
                for j in range(p + 2, 8):
                    below[j] = below[j] - (below[p] * ratio[p, j] + below[q] * ratio[q, j])
            part = mixed * (1.0 / first)
            scaled = jnp.where(sub == p, rows[p] * lax.rsqrt(first), scaled)
            rest = (rows[q] - part * rows[p]) * lax.rsqrt(last - part * mixed)
            scaled = jnp.where(sub == q, rest, scaled)
        done.append(scaled)
        for p in (4, 2, 0):
            for r in (p, p + 1):
                for j in range(p + 2, 8):
                    solved[r] = solved[r] - ratio[r, j] * solved[j]
        for later in range(b + 2, len(blocks)):
            parts = [one * two for one, two in zip(columns_of(blocks[later], 8 * b), solved)]
            while len(parts) > 1:
                parts = [one + two for one, two in zip(parts[::2], parts[1::2])]
            blocks[later] = blocks[later] - parts[0]
    done = jnp.concatenate(done, axis=0)
    above = lax.broadcasted_iota(jnp.int32, (size, size), 0) <= lax.broadcasted_iota(
        jnp.int32, (size, size), 1
    )
    return jnp.where(above, done[:, :size] * (across * scale), 0.0), done[:, size:] * scale


def project(first, square, own):
    first_parts = split(first)
    first_low = first_parts[0]
    second = first - dots((first_low,), own)
    second_low = second.astype(jnp.bfloat16)
    used = (first_low, second_low)
    square = square - dots(used, first_parts, NT)
    rest = second - dots((second_low,), own)
    square = square - dots(split(rest), used, NT)
    sizes = [diagonal_of(square, axis) for axis in (1, 0)]
    return used, first + second, rest, square, sizes


def first_solve_kernel(
    scale, spans, cross, stack, middle, ends, block, proj, low, rest, square, inverse
):
    columns = ends.shape[0]
    first, own_square, gram = opened(cross, columns, scale)
    used, proj[...], rest[...], square_here, sizes = project(first, own_square, split(gram))
    square[...] = square_here
    moved = dot(jnp.concatenate(used, axis=0), stack[...])
    subtracted(spans, middle, ends, moved, block)
    upper, inverse_here = factor(square_here, *sizes)
    low[...] = upper.T
    inverse_here = inverse_here.astype(jnp.bfloat16)
    inverse[...] = inverse_here
    block[...] = dot(inverse_here, block[...]).astype(jnp.bfloat16)


def next_gram_kernel(scale, cross, rest, square, inverse, high, low):
    columns = square.shape[0]
    kept = rest.shape[1] - columns
    _, _, gram = opened(cross, columns, scale)
    mixed = dots((inverse[...],), split(rest[:, columns:]))
    corner = dots((inverse[...],), split(square[...]))
    corner = dots(split(corner), (inverse[...],), NT)
    for part, (old, side, end) in zip(
        (high, low), zip(split(gram[columns:, columns:]), split(mixed), split(corner))
    ):
        part[:kept, :kept] = old
        part[kept:, :kept] = side
        part[:kept, kept:] = side.T
        part[kept:, kept:] = end


def second_solve_kernel(
    scale, cross, own_high, own_low, stack, last, middle, ends, proj_in, low_in, result, proj, low,
    block,
):
    columns = ends.shape[0]
    kept = stack.shape[0] - columns
    fields = stack.shape[0]
    sums = cross[...] * scale
    used, proj[1], _, square, sizes = project(
        sums[:, :fields], sums[:, fields:], (own_high[...], own_low[...])
    )
    proj[0] = proj_in[...]
    low[0] = low_in[...]
    _, span_x, span_y, depth = result.shape
    both = jnp.concatenate(used, axis=0)
    moved = dot(both[:, :kept], stack[columns:]) + dot(both[:, kept:], last[...])
    subtracted((span_x, span_y, depth), middle, ends, moved, block)
    upper, inverse = factor(square, *sizes)
    low[1] = upper.T
    inverse = inverse.astype(jnp.bfloat16)
    plane = span_y * depth
    for x in range(span_x):
        part = dot(inverse, block[:, x * plane : (x + 1) * plane])
        result[:, x] = part.reshape(columns, span_y, depth).astype(jnp.bfloat16)


def partner(part, mask):
    axes = ("slab", "col")
    count = lax.axis_size("slab") * lax.axis_size("col")
    return lax.ppermute(part, axes, [(i, i ^ mask) for i in range(count)])


def whole_sum(part):
    cols = lax.axis_size("col")
    count = lax.axis_size("slab") * cols
    index = lax.axis_index("slab") * cols + lax.axis_index("col")
    bit, upper = 1, 0
    while bit < count:
        upper = upper ^ (index // bit % 2)
        bit *= 2
    upper = upper == 1
    half = part.shape[0] // 2
    low, high = part[:half], part[half:]
    part = jnp.where(upper, high, low) + partner(jnp.where(upper, low, high), 1)
    bit = 2
    while bit < count:
        if 2 * bit < count:
            one, two, both = (partner(part, mask) for mask in (bit + 1, 2 * bit + 1, 3 * bit))
            part = (part + one) + (both + two)
            bit *= 4
        else:
            part = part + partner(part, bit + 1)
            bit *= 2
    other = partner(part, 1)
    return jnp.concatenate([jnp.where(upper, other, part), jnp.where(upper, part, other)], axis=0)


def call(kernel, name, outs, *args, flops=0, scratch=()):
    moved = sum(math.prod(arg.shape) * arg.dtype.itemsize for arg in args)
    moved += sum(math.prod(shape) * jnp.dtype(dtype).itemsize for shape, dtype in outs)
    return pl.pallas_call(
        kernel,
        out_shape=[jax.ShapeDtypeStruct(shape, dtype) for shape, dtype in outs],
        in_specs=[pl.BlockSpec(memory_space=pltpu.VMEM)] * len(args),
        out_specs=[pl.BlockSpec(memory_space=pltpu.VMEM)] * len(outs),
        scratch_shapes=scratch,
        compiler_params=pltpu.CompilerParams(vmem_limit_bytes=24 * 1024 * 1024),
        cost_estimate=pl.CostEstimate(flops=flops, bytes_accessed=moved, transcendentals=0),
        name=name,
    )(*args)


def shards(basis, cell_map, table):
    span_x, span_y, depth = cell_map.shape
    blocks, columns = basis.shape[:2]
    cells = span_x * span_y * depth
    fields = blocks * columns
    scale = 1.0 / (cells * lax.axis_size("slab") * lax.axis_size("col"))
    spans = (span_x, span_y, depth)
    f32, bf16 = jnp.float32, jnp.bfloat16

    stack = basis.reshape(fields, cells)
    coef = coefficients(table, cell_map)
    own = call(
        functools.partial(stack_gram_kernel, columns),
        "stack_gram",
        [((2, columns, 2 * columns), f32), ((columns, 2 * columns), f32), ((1, 2 * columns), f32)],
        stack,
        flops=2 * fields * fields * cells,
    )

    end_cells = 2 * span_x * depth

    def middle_image(first, stack, block, planes):
        return call(
            functools.partial(middle_image_kernel, spans, first),
            "middle_image",
            [((columns, cells - end_cells), bf16), ((columns, end_cells), f32),
             ((columns, fields + columns), f32)],
            coef, stack, block, *planes,
            flops=2 * 27 * columns * cells,
        )

    last = basis[blocks - 1].reshape(columns, cells)
    planes, lines, (coef, stack, own) = neighbours(last, *spans, (coef, stack, own))
    middle, partial, known = middle_image(0, stack, last, planes)
    ends, cross = call(
        functools.partial(first_image_kernel, spans),
        "first_image",
        [((columns, end_cells), bf16), ((4 * columns + 16, 2 * columns), f32)],
        coef, stack, *own, partial, known, *lines,
    )
    cross = whole_sum(cross)
    block, proj, low, rest, square, inverse = call(
        functools.partial(first_solve_kernel, scale, spans),
        "first_solve",
        [((columns, cells), bf16), ((columns, fields), f32), ((columns, columns), f32),
         ((columns, fields), f32), ((columns, columns), f32), ((columns, columns), bf16)],
        cross, stack, middle, ends,
    )
    own = call(
        functools.partial(next_gram_kernel, scale),
        "next_gram",
        [((fields, fields), bf16)] * 2,
        cross, rest, square, inverse,
    )
    planes, lines, _ = neighbours(block, *spans)
    middle, partial, known = middle_image(columns, stack, block, planes)
    ends, cross = call(
        functools.partial(second_image_kernel, spans),
        "second_image",
        [((columns, end_cells), bf16), ((columns, fields + columns), f32)],
        coef, stack, block, partial, known, *lines,
    )
    block, proj, low = call(
        functools.partial(second_solve_kernel, scale),
        "second_solve",
        [((columns, *spans), bf16), ((2, columns, fields), f32), ((2, columns, columns), f32)],
        whole_sum(cross), *own, stack, block, middle, ends, proj, low,
        scratch=[pltpu.VMEM((columns, cells), bf16)],
    )
    return block, jnp.swapaxes(proj, 1, 2), low


def solution(mesh):
    placed = (P(None, None, "slab", "col", None), P("slab", "col", None), P())
    return jax.shard_map(
        shards,
        mesh=mesh,
        in_specs=placed,
        out_specs=(P(None, "slab", "col", None), P(), P()),
        check_vma=False,
    )
```
